32 devices in a mesh: blk: 8 (over z, y), sub: 4 (over x, core).
Axes of the slice: x: 2, y: 2, z: 4, core: 2. Of those that a mesh axis runs over, the one named last changes fastest.
Arguments:
- node_input: float32 [512, 16384], P(('blk', 'sub')), may hold values from -6 to 6
- edge_input: bfloat16 [147456, 512], P(('blk', 'sub')), may hold values from -6 to 6
- senders: int32 [147456], P(('blk', 'sub')), may hold values from 0 to 16383, as said below
- receivers: int32 [147456], P(('blk', 'sub')), may hold values from 0 to 16383, as said below
- edge_count: int32 [32], P(('blk', 'sub')), may hold values from 1 to 4608, 110592 in all
- edge_w_one: bfloat16 [1536, 512], replicated, may hold values from -0.15625 to 0.15625
- edge_b_one: float32 [512], replicated, may hold values from -3 to 3
- edge_w_two: bfloat16 [512, 512], replicated, may hold values from -0.25 to 0.25
- edge_b_two: float32 [512], replicated, may hold values from -3 to 3
- edge_gain: float32 [512], replicated, may hold values from 0.1 to 1.9
- edge_shift: float32 [512], replicated, may hold values from -2 to 2
- node_w_one: bfloat16 [1024, 512], replicated, may hold values from -0.1875 to 0.1875
- node_b_one: float32 [512], replicated, may hold values from -3 to 3
- node_w_two: bfloat16 [512, 512], replicated, may hold values from -0.25 to 0.25
- node_b_two: float32 [512], replicated, may hold values from -3 to 3
- node_gain: float32 [512], replicated, may hold values from 0.1 to 1.9
- node_shift: float32 [512], replicated, may hold values from -2 to 2
- node_cotangent: float32 [512, 16384], P(('blk', 'sub')), may hold values from -6 to 6
- edge_cotangent: bfloat16 [147456, 512], P(('blk', 'sub')), may hold values from -6 to 6
Outputs:
- node_out: float32 [512, 16384], P(('blk', 'sub'))
- edge_out: float32 [147456, 512], P(('blk', 'sub'))
- node_grad: float32 [512, 16384], P(('blk', 'sub'))
- edge_grad: float32 [147456, 512], P(('blk', 'sub'))
- grad_edge_w_one: float32 [1536, 512], replicated
- grad_edge_b_one: float32 [512], replicated
- grad_edge_w_two: float32 [512, 512], replicated
- grad_edge_b_two: float32 [512], replicated
- grad_edge_gain: float32 [512], replicated
- grad_edge_shift: float32 [512], replicated
- grad_node_w_one: float32 [1024, 512], replicated
- grad_node_b_one: float32 [512], replicated
- grad_node_w_two: float32 [512, 512], replicated
- grad_node_b_two: float32 [512], replicated
- grad_node_gain: float32 [512], replicated
- grad_node_shift: float32 [512], replicated
The draws below stay inside these ranges and needn't reach their ends.
Inputs may be any that keep to these rules, and one draw needn't show every extreme that they name: `senders`: an edge slot of device d (slots d * 4608 to d * 4608 + 4607) has its sender among nodes d * 512 to d * 512 + 511. `receivers`: with device d = g * 4 + s, an edge slot of device d has its receiver in node group g - 1, g or g + 1 modulo 8, where group k holds nodes k * 4 * 512 to (k + 1) * 4 * 512 - 1.
All inputs are finite; a program needn't handle non-finite values. No bound on the sum of `edge_count` on one device may be relied on, other than what follows from the above.
Results may differ from the reference program's by a relative error of at most 0.0079.
Values may be sent and summed in bfloat16 or wider, within the bound.
A program may use at most 256 MiB of HBM per device.

```python
import math
import jax
import jax.numpy as jnp
import numpy as np
from jax import lax

D = 512
NODE_DEV = 512
EDGE_DEV = 4608
GROUPS = 8
SUBS = 4
NODES = 16384
EDGES = 147456
DEVICES = 32


def draw_senders(key, part):
    key = jax.random.fold_in(key, 11)
    positions = jnp.arange(EDGES, dtype=jnp.int32)
    device = positions // EDGE_DEV
    slot_index = positions % EDGE_DEV
    local = jax.random.randint(key, (EDGES,), 0, NODE_DEV, dtype=jnp.int32)
    local = jnp.where(slot_index == 1, 0, local)
    local = jnp.where(slot_index == 2, NODE_DEV - 1, local)
    return device * NODE_DEV + local


def draw_receivers(key, part):
    key = jax.random.fold_in(key, 23)
    step_key, local_key = jax.random.split(key)
    positions = jnp.arange(EDGES, dtype=jnp.int32)
    device = positions // EDGE_DEV
    slot_index = positions % EDGE_DEV
    group = device // SUBS
    step = jax.random.randint(step_key, (EDGES,), -1, 2, dtype=jnp.int32)
    local = jax.random.randint(local_key, (EDGES,), 0, SUBS * NODE_DEV, dtype=jnp.int32)
    step = jnp.where(slot_index == 1, 0, step)
    local = jnp.where(slot_index == 1, 0, local)
    step = jnp.where(slot_index == 2, -1, step)
    local = jnp.where(slot_index == 2, SUBS * NODE_DEV - 1, local)
    target = (group + step + GROUPS) % GROUPS
    return target * SUBS * NODE_DEV + local


def levels(rng, extent, cuts, least, largest):
    factor_of, own = 1.0, jax.random.fold_in(rng, 6)
    for axis_at, shards_of in cuts:
        heights = jnp.exp(jax.random.uniform(jax.random.fold_in(own, axis_at), (shards_of,), jnp.float32, least / len(cuts), largest / len(cuts)))
        factor_of = factor_of * jnp.repeat(heights, extent[axis_at] // shards_of).reshape([-1 if axis == axis_at else 1 for axis in range(len(extent))])
    return factor_of


def profile(count, total, bound, lean):
    weights = [(1 << 20) // math.isqrt(rank ** lean) + 1 for rank in range(2, count + 1)]
    surplus, given = total - bound - (count - 1), [1] * (count - 1)
    while surplus > 0:
        free = [i for i in range(count - 1) if given[i] < bound]
        whole, remaining = sum([weights[i] for i in free]), surplus
        for i in free:
            more = min(bound - given[i], max(1, remaining * weights[i] // whole), surplus)
            given[i] = given[i] + more
            surplus = surplus - more
    return np.array([bound] + given)


def ragged_sizes(stream_key, number_of, total, bound, skew):
    if number_of == 2:
        one = jax.random.randint(stream_key, (), max(1, total - bound), min(bound, total - 1) + 1)
        return jnp.stack([one, total - one])
    lengths = jnp.asarray(profile(number_of, total, bound, skew), jnp.int32)
    twos = (number_of - 1) // 2
    giver, taker = lengths[1:1 + 2 * twos:2], lengths[2:2 + 2 * twos:2]
    room = jnp.minimum(giver - 1, bound - taker)
    passed = jax.random.randint(jax.random.fold_in(stream_key, 1), (twos,), 0, 1 << 20) % (room + 1)
    lengths = lengths.at[1:1 + 2 * twos:2].set(giver - passed).at[2:2 + 2 * twos:2].set(taker + passed)
    return lengths[jax.random.permutation(jax.random.fold_in(stream_key, 2), number_of)]


def bell_draw(stream_key, extent, width, reach, cuts=(), kind=jnp.bfloat16):
    entries = width * jax.random.normal(stream_key, extent, jnp.float32)
    if cuts:
        entries = entries * levels(stream_key, extent, cuts, -0.22, 0.18)
    return jnp.clip(entries, -reach, reach).astype(kind)


def setup_inputs(seed: int = 0) -> dict:
    key_of = jax.random.split(jax.random.key(seed), 20)
    return {
        "node_input": bell_draw(key_of[0], (D, NODES), 1.0, 6.0, ((0, 32),), jnp.float32),
        "edge_input": bell_draw(key_of[1], (EDGES, D), 1.0, 6.0, ((0, 32),)),
        "senders": draw_senders(jax.random.fold_in(key_of[19], 71), 0),
        "receivers": draw_receivers(jax.random.fold_in(key_of[19], 71), 0),
        "edge_count": ragged_sizes(key_of[4], DEVICES, DEVICES * EDGE_DEV * 3 // 4, EDGE_DEV, 1).astype(jnp.int32),
        "edge_w_one": bell_draw(key_of[5], (3 * D, D), (3 * D) ** -0.5, 0.15625),
        "edge_b_one": bell_draw(key_of[6], (D,), 0.5, 3.0, (), jnp.float32),
        "edge_w_two": bell_draw(key_of[7], (D, D), D ** -0.5, 0.25),
        "edge_b_two": bell_draw(key_of[8], (D,), 0.5, 3.0, (), jnp.float32),
        "edge_gain": jnp.clip(1.0 + 0.18 * jax.random.normal(key_of[9], (D,), jnp.float32), 0.1, 1.9),
        "edge_shift": bell_draw(key_of[10], (D,), 0.3, 2.0, (), jnp.float32),
        "node_w_one": bell_draw(key_of[11], (2 * D, D), (2 * D) ** -0.5, 0.1875),
        "node_b_one": bell_draw(key_of[12], (D,), 0.5, 3.0, (), jnp.float32),
        "node_w_two": bell_draw(key_of[13], (D, D), D ** -0.5, 0.25),
        "node_b_two": bell_draw(key_of[14], (D,), 0.5, 3.0, (), jnp.float32),
        "node_gain": jnp.clip(1.0 + 0.18 * jax.random.normal(key_of[15], (D,), jnp.float32), 0.1, 1.9),
        "node_shift": bell_draw(key_of[16], (D,), 0.3, 2.0, (), jnp.float32),
        "node_cotangent": bell_draw(key_of[17], (D, NODES), 1.0, 6.0, ((0, 32),), jnp.float32),
        "edge_cotangent": bell_draw(key_of[18], (EDGES, D), 1.0, 6.0, ((0, 32),)),
    }


@jax.custom_vjp
def low(v):
    return lax.optimization_barrier(v.astype(jnp.bfloat16)).astype(jnp.float32)

@jax.custom_vjp
def low_back(v):
    return v

def low_keep(v):
    return (low(v), None)

def low_pass(kept, grad):
    return (grad,)

def back_keep(v):
    return (v, None)

def back_low(kept, grad):
    return (low(grad),)
low.defvjp(low_keep, low_pass)
low_back.defvjp(back_keep, back_low)
EPSILON = 1e-05
HIGHEST = lax.Precision.HIGHEST

def norm_apply(values, gain, shift):
    average = lax.optimization_barrier(jnp.mean(values, -1, keepdims=True))
    centred = values - average
    variance = lax.optimization_barrier(jnp.mean(centred * centred, -1, keepdims=True))
    return centred * lax.rsqrt(variance + EPSILON) * gain + shift

def perceptron(inputs, weight_one, bias_one, weight_two, bias_two):
    primary = low_back(jnp.dot(inputs, weight_one, precision=HIGHEST) + bias_one)
    activated = low(jax.nn.silu(primary))
    return low_back(jnp.dot(activated, weight_two, precision=HIGHEST) + bias_two)

def layer(node_rows, edge_rows, weights, senders, receivers, live):
    edge_w_one, edge_b_one, edge_w_two, edge_b_two, edge_gain, edge_shift, node_w_one, node_b_one, node_w_two, node_b_two, node_gain, node_shift = weights
    node_low = low(node_rows)

    def edge_block(pieces):
        edge_piece, send_piece, recv_piece, live_piece = pieces
        stacked = jnp.concatenate([edge_piece, jnp.take(node_low, send_piece, axis=0), jnp.take(node_low, recv_piece, axis=0)], axis=1)
        branch = norm_apply(perceptron(stacked, edge_w_one, edge_b_one, edge_w_two, edge_b_two), edge_gain, edge_shift)
        return edge_piece + live_piece[:, None] * branch
    blocks = lax.map(jax.checkpoint(edge_block), (edge_rows.reshape(DEVICES, EDGE_DEV, D), senders.reshape(DEVICES, EDGE_DEV), receivers.reshape(DEVICES, EDGE_DEV), live.reshape(DEVICES, EDGE_DEV)))
    edge_result = blocks.reshape(EDGES, D)
    summed = jax.ops.segment_sum(live[:, None] * edge_result, receivers, num_segments=NODES)
    joined = jnp.concatenate([node_low, low(summed)], axis=1)
    node_result = node_rows + norm_apply(perceptron(joined, node_w_one, node_b_one, node_w_two, node_b_two), node_gain, node_shift)
    return (node_result, edge_result)

def reference(node_input, edge_input, senders, receivers, edge_count, edge_w_one, edge_b_one, edge_w_two, edge_b_two, edge_gain, edge_shift, node_w_one, node_b_one, node_w_two, node_b_two, node_gain, node_shift, node_cotangent, edge_cotangent):
    positions = jnp.arange(EDGES)
    owners = positions // EDGE_DEV
    slot_index = positions % EDGE_DEV
    live = jnp.where(slot_index < edge_count[owners], 1.0, 0.0).astype(jnp.float32)
    weights = tuple((item.astype(jnp.float32) for item in (edge_w_one, edge_b_one, edge_w_two, edge_b_two, edge_gain, edge_shift, node_w_one, node_b_one, node_w_two, node_b_two, node_gain, node_shift)))

    def forward(node_rows, edge_rows, params):
        return layer(node_rows, edge_rows, params, senders, receivers, live)
    primal, pullback = jax.vjp(forward, node_input.T, edge_input.astype(jnp.float32), weights)
    grad_nodes, grad_edges, grads = pullback((node_cotangent.T, edge_cotangent.astype(jnp.float32)))
    return (primal[0].T, primal[1], grad_nodes.T, grad_edges, grads[0], grads[1], grads[2], grads[3], grads[4], grads[5], grads[6], grads[7], grads[8], grads[9], grads[10], grads[11])
```

```python
import jax
import jax.numpy as jnp
from jax import lax
from jax.sharding import PartitionSpec as P

EPSILON = 1e-05


def shifted(block, axis, distance):
    devices = range(lax.axis_size(axis))
    route = [((i - distance) % len(devices), i) for i in devices]
    return lax.ppermute(block, axis, route)


def norm_apply(values, gain, shift):
    average = jnp.mean(values, -1, keepdims=True)
    centred = values - average
    variance = jnp.mean(centred * centred, -1, keepdims=True)
    return centred * lax.rsqrt(variance + EPSILON) * gain + shift


def silu_slope(values):
    logistic = jax.nn.sigmoid(values)
    return logistic * (1.0 + values * (1.0 - logistic))


def matmul(left, right):
    return jnp.dot(left, right, preferred_element_type=jnp.float32)


def left_matmul(left, right):
    return lax.dot_general(
        left, right, (((0,), (0,)), ((), ())), preferred_element_type=jnp.float32
    )


def right_matmul(left, right):
    return lax.dot_general(
        left, right, (((1,), (1,)), ((), ())), preferred_element_type=jnp.float32
    )


def to_nodes(channels):
    return lax.all_to_all(
        channels.astype(jnp.bfloat16), ("blk", "sub"), split_axis=1, concat_axis=0, tiled=True
    )


def to_channels(values):
    return lax.all_to_all(
        values.astype(jnp.bfloat16), ("blk", "sub"), split_axis=0, concat_axis=1, tiled=True
    ).astype(jnp.float32)


def widened(rows):
    below = shifted(rows, "blk", 1)
    above = shifted(rows, "blk", -1)
    return lax.all_gather(jnp.concatenate([below, rows, above], 0), "sub", axis=0, tiled=True)


def combine_sums(wide_sums, per_device):
    mine = lax.psum_scatter(
        wide_sums.astype(jnp.bfloat16), "sub", scatter_dimension=0, tiled=True
    )
    from_above = shifted(mine[:per_device], "blk", -1)
    from_below = shifted(mine[2 * per_device :], "blk", 1)
    return (
        mine[per_device : 2 * per_device].astype(jnp.float32)
        + from_above.astype(jnp.float32)
        + from_below.astype(jnp.float32)
    )


def shards(
    node_input,
    edge_input,
    senders,
    receivers,
    edge_count,
    edge_w_one,
    edge_b_one,
    edge_w_two,
    edge_b_two,
    edge_gain,
    edge_shift,
    node_w_one,
    node_b_one,
    node_w_two,
    node_b_two,
    node_gain,
    node_shift,
    node_cotangent,
    edge_cotangent,
):
    groups = lax.axis_size("blk")
    sub_count = lax.axis_size("sub")
    block_index = lax.axis_index("blk")
    sub_index = lax.axis_index("sub")
    width = edge_input.shape[1]
    node_low = to_nodes(node_input).T
    node_upstream = to_nodes(node_cotangent).T.astype(jnp.float32)
    per_device = node_low.shape[0]
    per_group = per_device * sub_count
    my_start = (block_index * sub_count + sub_index) * per_device
    send_local = senders - my_start
    relative = (receivers // per_group - block_index + 1 + groups) % groups
    recv_sub = receivers % per_group // per_device
    recv_wide = (recv_sub * 3 + relative) * per_device + receivers % per_device
    slot_index = jnp.arange(edge_input.shape[0], dtype=jnp.int32)
    live = jnp.where(slot_index < edge_count[0], 1.0, 0.0).astype(jnp.float32)[:, None]
    wide_low = widened(node_low)
    stacked = jnp.concatenate(
        [edge_input, jnp.take(node_low, send_local, axis=0), jnp.take(wide_low, recv_wide, axis=0)],
        axis=1,
    )
    first_pre = matmul(stacked, edge_w_one) + edge_b_one
    first_act = jax.nn.silu(first_pre).astype(jnp.bfloat16)
    second_pre = matmul(first_act, edge_w_two) + edge_b_two
    edge_branch, edge_norm_back = jax.vjp(norm_apply, second_pre, edge_gain, edge_shift)
    edge_result = edge_input.astype(jnp.float32) + live * edge_branch
    wide_sums = jax.ops.segment_sum(live * edge_result, recv_wide, num_segments=3 * per_group)
    gathered = combine_sums(wide_sums, per_device)
    joined = jnp.concatenate([node_low, gathered.astype(jnp.bfloat16)], axis=1)
    third_pre = matmul(joined, node_w_one) + node_b_one
    third_act = jax.nn.silu(third_pre).astype(jnp.bfloat16)
    fourth_pre = matmul(third_act, node_w_two) + node_b_two
    node_branch, node_norm_back = jax.vjp(norm_apply, fourth_pre, node_gain, node_shift)
    grad_fourth, grad_node_gain, grad_node_shift = node_norm_back(node_upstream)
    fourth_low = grad_fourth.astype(jnp.bfloat16)
    grad_node_w_two = left_matmul(third_act, fourth_low)
    grad_node_b_two = jnp.sum(fourth_low.astype(jnp.float32), 0)
    grad_third = right_matmul(fourth_low, node_w_two) * silu_slope(third_pre)
    third_low = grad_third.astype(jnp.bfloat16)
    grad_node_w_one = left_matmul(joined, third_low)
    grad_node_b_one = jnp.sum(third_low.astype(jnp.float32), 0)
    grad_joined = right_matmul(third_low, node_w_one)
    grad_nodes = grad_joined[:, :width]
    grad_gathered = grad_joined[:, width:]
    wide_grad = widened(grad_gathered.astype(jnp.bfloat16))
    node_summed = lax.psum(
        (grad_node_w_one, grad_node_b_one, grad_node_w_two, grad_node_b_two, grad_node_gain, grad_node_shift),
        ("blk", "sub"),
    )
    node_out = node_input + to_channels(node_branch.T)
    edge_total = edge_cotangent.astype(jnp.float32) + live * jnp.take(wide_grad, recv_wide, axis=0).astype(jnp.float32)
    grad_second, grad_edge_gain, grad_edge_shift = edge_norm_back(live * edge_total)
    second_low = grad_second.astype(jnp.bfloat16)
    grad_edge_w_two = left_matmul(first_act, second_low)
    grad_edge_b_two = jnp.sum(second_low.astype(jnp.float32), 0)
    grad_first = right_matmul(second_low, edge_w_two) * silu_slope(first_pre)
    first_low = grad_first.astype(jnp.bfloat16)
    grad_edge_w_one = left_matmul(stacked, first_low)
    grad_edge_b_one = jnp.sum(first_low.astype(jnp.float32), 0)
    grad_stacked = right_matmul(first_low, edge_w_one)
    edge_grad = edge_total + grad_stacked[:, :width]
    sender_grad = jax.ops.segment_sum(
        grad_stacked[:, width : 2 * width], send_local, num_segments=per_device
    )
    receiver_wide = jax.ops.segment_sum(
        grad_stacked[:, 2 * width :], recv_wide, num_segments=3 * per_group
    )
    receiver_grad = combine_sums(receiver_wide, per_device)
    node_total = grad_nodes + sender_grad + receiver_grad
    summed = lax.psum(
        (
            grad_edge_w_one,
            grad_edge_b_one,
            grad_edge_w_two,
            grad_edge_b_two,
            grad_edge_gain,
            grad_edge_shift,
        ),
        ("blk", "sub"),
    )
    node_grad = node_cotangent + to_channels(node_total.T)
    return (
        node_out,
        edge_result,
        node_grad,
        edge_grad,
        summed[0],
        summed[1],
        summed[2],
        summed[3],
        summed[4],
        summed[5],
        node_summed[0],
        node_summed[1],
        node_summed[2],
        node_summed[3],
        node_summed[4],
        node_summed[5],
    )


def solution(mesh):
    placed = (
        P(("blk", "sub"), None),
        P(("blk", "sub"), None),
        P(("blk", "sub")),
        P(("blk", "sub")),
        P(("blk", "sub")),
        P(),
        P(),
        P(),
        P(),
        P(),
        P(),
        P(),
        P(),
        P(),
        P(),
        P(),
        P(),
        P(("blk", "sub"), None),
        P(("blk", "sub"), None),
    )
    return jax.shard_map(
        shards,
        mesh=mesh,
        in_specs=placed,
        out_specs=(
            P(("blk", "sub"), None),
            P(("blk", "sub"), None),
            P(("blk", "sub"), None),
            P(("blk", "sub"), None),
            P(),
            P(),
            P(),
            P(),
            P(),
            P(),
            P(),
            P(),
            P(),
            P(),
            P(),
            P(),
        ),
        check_vma=False,
    )
```

```python
import jax
import jax.numpy as jnp
from jax import lax
from jax.experimental import pallas as pl
from jax.experimental.pallas import tpu as pltpu
from jax.sharding import PartitionSpec as P

EPSILON = 1e-05


def shifted(block, axis, distance):
    devices = range(lax.axis_size(axis))
    route = [((i - distance) % len(devices), i) for i in devices]
    return lax.ppermute(block, axis, route)


def norm_apply(values, gain, shift):
    average = jnp.mean(values, -1, keepdims=True)
    centred = values - average
    variance = jnp.mean(centred * centred, -1, keepdims=True)
    return centred * lax.rsqrt(variance + EPSILON) * gain + shift


def silu_slope(values):
    logistic = jax.nn.sigmoid(values)
    return logistic * (1.0 + values * (1.0 - logistic))


def matmul(left, right):
    return jnp.dot(left, right, preferred_element_type=jnp.float32)


def left_matmul(left, right):
    return lax.dot_general(
        left, right, (((0,), (0,)), ((), ())), preferred_element_type=jnp.float32
    )


def right_matmul(left, right):
    return lax.dot_general(
        left, right, (((1,), (1,)), ((), ())), preferred_element_type=jnp.float32
    )


def to_nodes(channels):
    return lax.all_to_all(
        channels.astype(jnp.bfloat16), ("blk", "sub"), split_axis=1, concat_axis=0, tiled=True
    )


def to_channels(values):
    return lax.all_to_all(
        values.astype(jnp.bfloat16), ("blk", "sub"), split_axis=0, concat_axis=1, tiled=True
    ).astype(jnp.float32)


def widened(rows):
    below = shifted(rows, "blk", 1)
    above = shifted(rows, "blk", -1)
    return lax.all_gather(jnp.concatenate([below, rows, above], 0), "sub", axis=0, tiled=True)


def combine_sums(wide_sums, per_device):
    mine = lax.psum_scatter(
        wide_sums.astype(jnp.bfloat16), "sub", scatter_dimension=0, tiled=True
    )
    from_above = shifted(mine[:per_device], "blk", -1)
    from_below = shifted(mine[2 * per_device :], "blk", 1)
    return (
        mine[per_device : 2 * per_device].astype(jnp.float32)
        + from_above.astype(jnp.float32)
        + from_below.astype(jnp.float32)
    )


TILE = 512
CHUNK = 512
LANES = 128
VMEM_BYTES = 60 * 2**20


def dot(left, right):
    return jnp.dot(left, right, preferred_element_type=jnp.float32)


def dot_left(left, right):
    return lax.dot_general(
        left, right, (((0,), (0,)), ((), ())), preferred_element_type=jnp.float32
    )


def split_low(values):
    high = values.astype(jnp.bfloat16)
    return high, (values - high.astype(jnp.float32)).astype(jnp.bfloat16)


def lay_rows(target, start, values):
    count, width = values.shape
    parts = width // LANES
    for j in range(parts):
        target[pl.ds(start * parts + j, count, stride=parts), :] = values[:, j * LANES : (j + 1) * LANES]


def read_rows(source, start, count, parts):
    return jnp.concatenate(
        [source[pl.ds(start * parts + j, count, stride=parts), :] for j in range(parts)], axis=1
    )


def load_table(wide, table, stage, sems):
    steps = wide.shape[0] // CHUNK

    def fetch(i, slot):
        return pltpu.make_async_copy(wide.at[pl.ds(i * CHUNK, CHUNK)], stage.at[slot], sems.at[slot])

    fetch(0, 0).start()

    def body(i, carry):
        slot = lax.rem(i, 2)

        @pl.when(i + 1 < steps)
        def _():
            fetch(i + 1, 1 - slot).start()

        fetch(i, slot).wait()

        def piece(k, carry):
            values = stage[slot, pl.ds(k * 64, 64), :].astype(jnp.float32)
            lay_rows(table, i * CHUNK + k * 64, values)
            return carry

        return lax.fori_loop(0, CHUNK // 64, piece, carry)

    lax.fori_loop(0, steps, body, 0)


def store_table(table, wide, stage, sems):
    steps = wide.shape[0] // CHUNK
    parts = wide.shape[1] // LANES

    def send(i, slot):
        return pltpu.make_async_copy(stage.at[slot], wide.at[pl.ds(i * CHUNK, CHUNK)], sems.at[slot])

    def body(i, carry):
        slot = lax.rem(i, 2)

        @pl.when(i >= 2)
        def _():
            send(i - 2, slot).wait()

        def piece(k, carry):
            values = read_rows(table, i * CHUNK + k * 64, 64, parts)
            stage[slot, pl.ds(k * 64, 64), :] = values.astype(jnp.bfloat16)
            return carry

        lax.fori_loop(0, CHUNK // 64, piece, 0)
        send(i, slot).start()
        return carry

    lax.fori_loop(0, steps, body, 0)
    for i in (steps - 2, steps - 1):
        send(i, i % 2).wait()


def clear(table):
    def body(i, carry):
        table[pl.ds(i * 512, 512), :] = jnp.zeros((512, LANES), table.dtype)
        return carry

    lax.fori_loop(0, table.shape[0] // 512, body, 0)


def gather_rows(index, base, table, rows, parts):
    count = rows.shape[0] // parts

    def body(i, carry):
        for u in range(16):
            slot = i * 16 + u
            place = index[base + slot]
            rows[pl.ds(pl.multiple_of(slot * parts, parts), parts), :] = table[
                pl.ds(pl.multiple_of(place * parts, parts), parts), :
            ]
        return carry

    lax.fori_loop(0, count // 16, body, 0)


def add_rows(index, base, rows, table, parts):
    count = rows.shape[0] // parts

    def body(i, carry):
        for u in range(0, 16, 2):
            slot = i * 16 + u
            one, two = index[base + slot], index[base + slot + 1]
            at_one = pl.ds(pl.multiple_of(one * parts, parts), parts)
            at_two = pl.ds(pl.multiple_of(two * parts, parts), parts)
            held_one, held_two = table[at_one, :], table[at_two, :]
            sum_one = held_one + rows[pl.ds(pl.multiple_of(slot * parts, parts), parts), :]
            held_two = jnp.where(one == two, sum_one, held_two)
            sum_two = held_two + rows[pl.ds(pl.multiple_of((slot + 1) * parts, parts), parts), :]
            table[at_one, :] = sum_one
            table[at_two, :] = sum_two
        return carry

    lax.fori_loop(0, count // 16, body, 0)


def row_normal(values):
    average = jnp.mean(values, -1, keepdims=True)
    centred = values - average
    variance = jnp.mean(centred * centred, -1, keepdims=True)
    scale = lax.rsqrt(variance + EPSILON)
    return centred * scale, scale


def forward_kernel(
    count, recv, send, edge, wide, nodes, w_one, b_one, w_two, b_two, gain, shift,
    result, first, second, received, sums,
    table, total, rows, stage, sems,
):
    step = pl.program_id(0)
    base = step * TILE
    width = nodes.shape[1]
    parts = width // LANES

    @pl.when(step == 0)
    def _():
        load_table(wide, table, stage, sems)
        clear(total)

    gather_rows(recv, base, table, rows, parts)
    from_recv = read_rows(rows, 0, TILE, parts).astype(jnp.bfloat16)
    received[...] = from_recv
    column = jnp.broadcast_to(send[0], (LANES, TILE)).T
    lane = lax.broadcasted_iota(jnp.int32, (TILE, LANES), 1)
    chosen = jnp.concatenate(
        [
            jnp.where(column == lane + j * LANES, 1.0, 0.0).astype(jnp.bfloat16)
            for j in range(nodes.shape[0] // LANES)
        ],
        axis=1,
    )
    from_send = dot(chosen, nodes[...]).astype(jnp.bfloat16)
    pre = (
        dot(edge[...], w_one[:width])
        + dot(from_send, w_one[width : 2 * width])
        + dot(from_recv, w_one[2 * width :])
        + b_one[...]
    )
    first[...] = pre
    act = (pre * jax.nn.sigmoid(pre)).astype(jnp.bfloat16)
    post = dot(act, w_two[...]) + b_two[...]
    second[...] = post
    normal, _ = row_normal(post)
    branch = normal * gain[...] + shift[...]
    live = base + lax.broadcasted_iota(jnp.int32, (TILE, 1), 0) < count[0]
    outcome = edge[...].astype(jnp.float32) + jnp.where(live, branch, 0.0)
    result[...] = outcome
    lay_rows(rows, 0, jnp.where(live, outcome, 0.0))
    add_rows(recv, base, rows, total, parts)

    @pl.when(step == pl.num_programs(0) - 1)
    def _():
        store_table(total, sums, stage, sems)


def edge_forward(count, recv, send, edge, wide, nodes, w_one, b_one, w_two, b_two, gain, shift):
    edges, width = edge.shape
    steps = edges // TILE
    parts = width // LANES
    hold = pl.BlockSpec(memory_space=pltpu.VMEM)
    scalar = pl.BlockSpec(memory_space=pltpu.SMEM)
    tile = pl.BlockSpec((TILE, width), lambda i: (i, 0))
    return pl.pallas_call(
        forward_kernel,
        grid=(steps,),
        in_specs=[
            scalar, scalar, pl.BlockSpec((1, 1, TILE), lambda i: (i, 0, 0)), tile,
            pl.BlockSpec(memory_space=pl.ANY), hold, hold, hold, hold, hold, hold, hold,
        ],
        out_specs=[tile, tile, tile, tile, pl.BlockSpec(memory_space=pl.ANY)],
        out_shape=[
            jax.ShapeDtypeStruct((edges, width), jnp.float32),
            jax.ShapeDtypeStruct((edges, width), jnp.float32),
            jax.ShapeDtypeStruct((edges, width), jnp.float32),
            jax.ShapeDtypeStruct((edges, width), jnp.bfloat16),
            jax.ShapeDtypeStruct(wide.shape, jnp.bfloat16),
        ],
        scratch_shapes=[
            pltpu.VMEM((wide.shape[0] * parts, LANES), jnp.float32),
            pltpu.VMEM((wide.shape[0] * parts, LANES), jnp.float32),
            pltpu.VMEM((TILE * parts, LANES), jnp.float32),
            pltpu.VMEM((2, CHUNK, width), jnp.bfloat16),
            pltpu.SemaphoreType.DMA((2,)),
        ],
        compiler_params=pltpu.CompilerParams(vmem_limit_bytes=VMEM_BYTES),
        name="edge_forward",
    )(count, recv, send.reshape(steps, 1, TILE), edge, wide, nodes, w_one, b_one, w_two, b_two, gain, shift)


def backward_kernel(
    count, recv, send, cotangent, edge, received, first, second, wide, nodes, w_one_t, w_two_t, gain,
    grad, sums, grad_one, grad_two, vectors, sender_grad,
    table, total, rows, stage, sems, by_sender,
):
    step = pl.program_id(0)
    base = step * TILE
    width = nodes.shape[1]
    parts = width // LANES

    @pl.when(step == 0)
    def _():
        load_table(wide, table, stage, sems)
        clear(total)
        grad_one[...] = jnp.zeros_like(grad_one)
        grad_two[...] = jnp.zeros_like(grad_two)
        vectors[...] = jnp.zeros_like(vectors)
        by_sender[...] = jnp.zeros_like(by_sender)

    gather_rows(recv, base, table, rows, parts)
    live = base + lax.broadcasted_iota(jnp.int32, (TILE, 1), 0) < count[0]
    upstream = cotangent[...].astype(jnp.float32) + jnp.where(live, read_rows(rows, 0, TILE, parts), 0.0)
    masked = jnp.where(live, upstream, 0.0)
    normal, scale = row_normal(second[...])
    vectors[2:3, :] += jnp.sum(masked * normal, 0, keepdims=True)
    vectors[3:4, :] += jnp.sum(masked, 0, keepdims=True)
    scaled = masked * gain[...]
    slope = jnp.mean(scaled * normal, -1, keepdims=True)
    grad_second = scale * (scaled - jnp.mean(scaled, -1, keepdims=True) - normal * slope)
    second_low = grad_second.astype(jnp.bfloat16)
    vectors[1:2, :] += jnp.sum(second_low.astype(jnp.float32), 0, keepdims=True)
    pre = first[...]
    logistic = jax.nn.sigmoid(pre)
    act = (pre * logistic).astype(jnp.bfloat16)
    grad_two[...] += dot_left(act, second_low)
    grad_first = dot(second_low, w_two_t[...]) * (logistic * (1.0 + pre * (1.0 - logistic)))
    first_low = grad_first.astype(jnp.bfloat16)
    first_wide = first_low.astype(jnp.float32)
    vectors[0:1, :] += jnp.sum(first_wide, 0, keepdims=True)
    grad_one[:width] += dot_left(edge[...], first_low)
    grad_one[2 * width :] += dot_left(received[...], first_low)
    node = lax.broadcasted_iota(jnp.int32, (nodes.shape[0], TILE), 0)
    chosen = jnp.where(node == send[0], 1.0, 0.0).astype(jnp.bfloat16)
    by_sender[...] += dot(chosen, first_low)
    grad[...] = upstream + dot(first_low, w_one_t[:, :width])
    lay_rows(rows, 0, first_wide)
    add_rows(recv, base, rows, total, parts)

    @pl.when(step == pl.num_programs(0) - 1)
    def _():
        high, rest = split_low(by_sender[...])
        grad_one[width : 2 * width] = dot_left(nodes[...], high) + dot_left(nodes[...], rest)
        middle = w_one_t[:, width : 2 * width]
        sender_grad[...] = dot(high, middle) + dot(rest, middle)
        store_table(total, sums, stage, sems)


def edge_backward(count, recv, send, cotangent, edge, received, first, second, wide, nodes, w_one_t, w_two_t, gain):
    edges, width = edge.shape
    steps = edges // TILE
    parts = width // LANES
    per_device = nodes.shape[0]
    hold = pl.BlockSpec(memory_space=pltpu.VMEM)
    scalar = pl.BlockSpec(memory_space=pltpu.SMEM)
    tile = pl.BlockSpec((TILE, width), lambda i: (i, 0))

    def whole(rows):
        return pl.BlockSpec((rows, width), lambda i: (0, 0))

    return pl.pallas_call(
        backward_kernel,
        grid=(steps,),
        in_specs=[
            scalar, scalar, pl.BlockSpec((1, 1, TILE), lambda i: (i, 0, 0)), tile, tile, tile, tile, tile,
            pl.BlockSpec(memory_space=pl.ANY), hold, hold, hold, hold,
        ],
        out_specs=[
            tile, pl.BlockSpec(memory_space=pl.ANY),
            whole(3 * width), whole(width), whole(8), whole(per_device),
        ],
        out_shape=[
            jax.ShapeDtypeStruct((edges, width), jnp.float32),
            jax.ShapeDtypeStruct(wide.shape, jnp.bfloat16),
            jax.ShapeDtypeStruct((3 * width, width), jnp.float32),
            jax.ShapeDtypeStruct((width, width), jnp.float32),
            jax.ShapeDtypeStruct((8, width), jnp.float32),
            jax.ShapeDtypeStruct((per_device, width), jnp.float32),
        ],
        scratch_shapes=[
            pltpu.VMEM((wide.shape[0] * parts, LANES), jnp.float32),
            pltpu.VMEM((wide.shape[0] * parts, LANES), jnp.float32),
            pltpu.VMEM((TILE * parts, LANES), jnp.float32),
            pltpu.VMEM((2, CHUNK, width), jnp.bfloat16),
            pltpu.SemaphoreType.DMA((2,)),
            pltpu.VMEM((per_device, width), jnp.float32),
        ],
        compiler_params=pltpu.CompilerParams(vmem_limit_bytes=VMEM_BYTES),
        name="edge_backward",
    )(count, recv, send.reshape(steps, 1, TILE), cotangent, edge, received, first, second, wide, nodes, w_one_t, w_two_t, gain)


def shards(
    node_input,
    edge_input,
    senders,
    receivers,
    edge_count,
    edge_w_one,
    edge_b_one,
    edge_w_two,
    edge_b_two,
    edge_gain,
    edge_shift,
    node_w_one,
    node_b_one,
    node_w_two,
    node_b_two,
    node_gain,
    node_shift,
    node_cotangent,
    edge_cotangent,
):
    groups = lax.axis_size("blk")
    sub_count = lax.axis_size("sub")
    block_index = lax.axis_index("blk")
    sub_index = lax.axis_index("sub")
    width = edge_input.shape[1]
    node_low = to_nodes(node_input).T
    node_upstream = to_nodes(node_cotangent).T.astype(jnp.float32)
    per_device = node_low.shape[0]
    per_group = per_device * sub_count
    my_start = (block_index * sub_count + sub_index) * per_device
    send_local = senders - my_start
    relative = (receivers // per_group - block_index + 1 + groups) % groups
    recv_sub = receivers % per_group // per_device
    recv_wide = (recv_sub * 3 + relative) * per_device + receivers % per_device
    wide_low = widened(node_low)
    edge_result, first_pre, second_pre, received, wide_sums = edge_forward(
        edge_count, recv_wide, send_local, edge_input, wide_low, node_low,
        edge_w_one, edge_b_one[None], edge_w_two, edge_b_two[None], edge_gain[None], edge_shift[None],
    )
    gathered = combine_sums(wide_sums, per_device)
    joined = jnp.concatenate([node_low, gathered.astype(jnp.bfloat16)], axis=1)
    third_pre = matmul(joined, node_w_one) + node_b_one
    third_act = jax.nn.silu(third_pre).astype(jnp.bfloat16)
    fourth_pre = matmul(third_act, node_w_two) + node_b_two
    node_branch, node_norm_back = jax.vjp(norm_apply, fourth_pre, node_gain, node_shift)
    grad_fourth, grad_node_gain, grad_node_shift = node_norm_back(node_upstream)
    fourth_low = grad_fourth.astype(jnp.bfloat16)
    grad_node_w_two = left_matmul(third_act, fourth_low)
    grad_node_b_two = jnp.sum(fourth_low.astype(jnp.float32), 0)
    grad_third = right_matmul(fourth_low, node_w_two) * silu_slope(third_pre)
    third_low = grad_third.astype(jnp.bfloat16)
    grad_node_w_one = left_matmul(joined, third_low)
    grad_node_b_one = jnp.sum(third_low.astype(jnp.float32), 0)
    grad_joined = right_matmul(third_low, node_w_one)
    grad_nodes = grad_joined[:, :width]
    grad_gathered = grad_joined[:, width:]
    wide_grad = widened(grad_gathered.astype(jnp.bfloat16))
    node_summed = lax.psum(
        (grad_node_w_one, grad_node_b_one, grad_node_w_two, grad_node_b_two, grad_node_gain, grad_node_shift),
        ("blk", "sub"),
    )
    node_out = node_input + to_channels(node_branch.T)
    edge_grad, receiver_wide, grad_edge_w_one, grad_edge_w_two, vectors, sender_grad = edge_backward(
        edge_count, recv_wide, send_local, edge_cotangent, edge_input, received, first_pre, second_pre,
        wide_grad, node_low, edge_w_one.T, edge_w_two.T, edge_gain[None],
    )
    grad_edge_b_one, grad_edge_b_two, grad_edge_gain, grad_edge_shift = (vectors[i] for i in range(4))
    high, rest = split_low(combine_sums(receiver_wide, per_device))
    receiver_weight = edge_w_one[2 * width :]
    receiver_grad = right_matmul(high, receiver_weight) + right_matmul(rest, receiver_weight)
    node_total = grad_nodes + sender_grad + receiver_grad
    summed = lax.psum(
        (
            grad_edge_w_one,
            grad_edge_b_one,
            grad_edge_w_two,
            grad_edge_b_two,
            grad_edge_gain,
            grad_edge_shift,
        ),
        ("blk", "sub"),
    )
    node_grad = node_cotangent + to_channels(node_total.T)
    return (
        node_out,
        edge_result,
        node_grad,
        edge_grad,
        summed[0],
        summed[1],
        summed[2],
        summed[3],
        summed[4],
        summed[5],
        node_summed[0],
        node_summed[1],
        node_summed[2],
        node_summed[3],
        node_summed[4],
        node_summed[5],
    )


def solution(mesh):
    placed = (
        P(("blk", "sub"), None),
        P(("blk", "sub"), None),
        P(("blk", "sub")),
        P(("blk", "sub")),
        P(("blk", "sub")),
        P(),
        P(),
        P(),
        P(),
        P(),
        P(),
        P(),
        P(),
        P(),
        P(),
        P(),
        P(),
        P(("blk", "sub"), None),
        P(("blk", "sub"), None),
    )
    return jax.shard_map(
        shards,
        mesh=mesh,
        in_specs=placed,
        out_specs=(
            P(("blk", "sub"), None),
            P(("blk", "sub"), None),
            P(("blk", "sub"), None),
            P(("blk", "sub"), None),
            P(),
            P(),
            P(),
            P(),
            P(),
            P(),
            P(),
            P(),
            P(),
            P(),
            P(),
            P(),
        ),
        check_vma=False,
    )
```

```python
import jax
import jax.numpy as jnp
from jax import lax
from jax.experimental import pallas as pl
from jax.experimental.pallas import tpu as pltpu
from jax.sharding import PartitionSpec as P

EPSILON = 1e-05


def norm_apply(values, gain, shift):
    average = jnp.mean(values, -1, keepdims=True)
    centred = values - average
    variance = jnp.mean(centred * centred, -1, keepdims=True)
    return centred * lax.rsqrt(variance + EPSILON) * gain + shift


def silu_slope(values):
    logistic = jax.nn.sigmoid(values)
    return logistic * (1.0 + values * (1.0 - logistic))


def matmul(left, right):
    return jnp.dot(left, right, preferred_element_type=jnp.float32)


def left_matmul(left, right):
    return lax.dot_general(
        left, right, (((0,), (0,)), ((), ())), preferred_element_type=jnp.float32
    )


def right_matmul(left, right):
    return lax.dot_general(
        left, right, (((1,), (1,)), ((), ())), preferred_element_type=jnp.float32
    )


def to_nodes(channels):
    return lax.all_to_all(
        channels.astype(jnp.bfloat16), ("blk", "sub"), split_axis=1, concat_axis=0, tiled=True
    )


def to_channels(values):
    return lax.all_to_all(
        values.astype(jnp.bfloat16), ("blk", "sub"), split_axis=0, concat_axis=1, tiled=True
    ).astype(jnp.float32)


TILE = 512
CHUNK = 512
LANES = 128
VMEM_BYTES = 60 * 2**20


def dot(left, right):
    return jnp.dot(left, right, preferred_element_type=jnp.float32)


def dot_left(left, right):
    return lax.dot_general(
        left, right, (((0,), (0,)), ((), ())), preferred_element_type=jnp.float32
    )


def split_low(values):
    high = values.astype(jnp.bfloat16)
    return high, (values - high.astype(jnp.float32)).astype(jnp.bfloat16)


def lay_rows(target, start, values):
    count, width = values.shape
    parts = width // LANES
    for j in range(parts):
        target[pl.ds(start * parts + j, count, stride=parts), :] = values[:, j * LANES : (j + 1) * LANES]


def read_rows(source, start, count, parts):
    return jnp.concatenate(
        [source[pl.ds(start * parts + j, count, stride=parts), :] for j in range(parts)], axis=1
    )


def load_table(wide, table, stage, sems):
    steps = wide.shape[0] // CHUNK

    def fetch(i, slot):
        return pltpu.make_async_copy(wide.at[pl.ds(i * CHUNK, CHUNK)], stage.at[slot], sems.at[slot])

    fetch(0, 0).start()

    def body(i, carry):
        slot = lax.rem(i, 2)

        @pl.when(i + 1 < steps)
        def _():
            fetch(i + 1, 1 - slot).start()

        fetch(i, slot).wait()

        def piece(k, carry):
            values = stage[slot, pl.ds(k * 64, 64), :].astype(jnp.float32)
            lay_rows(table, i * CHUNK + k * 64, values)
            return carry

        return lax.fori_loop(0, CHUNK // 64, piece, carry)

    lax.fori_loop(0, steps, body, 0)


def store_table(table, wide, stage, sems):
    steps = wide.shape[0] // CHUNK
    parts = wide.shape[1] // LANES

    def send(i, slot):
        return pltpu.make_async_copy(stage.at[slot], wide.at[pl.ds(i * CHUNK, CHUNK)], sems.at[slot])

    def body(i, carry):
        slot = lax.rem(i, 2)

        @pl.when(i >= 2)
        def _():
            send(i - 2, slot).wait()

        def piece(k, carry):
            values = read_rows(table, i * CHUNK + k * 64, 64, parts)
            stage[slot, pl.ds(k * 64, 64), :] = values.astype(jnp.bfloat16)
            return carry

        lax.fori_loop(0, CHUNK // 64, piece, 0)
        send(i, slot).start()
        return carry

    lax.fori_loop(0, steps, body, 0)
    for i in (steps - 2, steps - 1):
        send(i, i % 2).wait()


def clear(table):
    def body(i, carry):
        table[pl.ds(i * 512, 512), :] = jnp.zeros((512, LANES), table.dtype)
        return carry

    lax.fori_loop(0, table.shape[0] // 512, body, 0)


def gather_rows(index, base, table, rows, parts):
    count = rows.shape[0] // parts

    def body(i, carry):
        for u in range(16):
            slot = i * 16 + u
            place = index[base + slot]
            rows[pl.ds(pl.multiple_of(slot * parts, parts), parts), :] = table[
                pl.ds(pl.multiple_of(place * parts, parts), parts), :
            ]
        return carry

    lax.fori_loop(0, count // 16, body, 0)


def add_rows(index, base, rows, table, parts):
    count = rows.shape[0] // parts

    def body(i, carry):
        for u in range(0, 16, 2):
            slot = i * 16 + u
            one, two = index[base + slot], index[base + slot + 1]
            at_one = pl.ds(pl.multiple_of(one * parts, parts), parts)
            at_two = pl.ds(pl.multiple_of(two * parts, parts), parts)
            held_one, held_two = table[at_one, :], table[at_two, :]
            sum_one = held_one + rows[pl.ds(pl.multiple_of(slot * parts, parts), parts), :]
            held_two = jnp.where(one == two, sum_one, held_two)
            sum_two = held_two + rows[pl.ds(pl.multiple_of((slot + 1) * parts, parts), parts), :]
            table[at_one, :] = sum_one
            table[at_two, :] = sum_two
        return carry

    lax.fori_loop(0, count // 16, body, 0)


def row_normal(values):
    average = jnp.mean(values, -1, keepdims=True)
    centred = values - average
    variance = jnp.mean(centred * centred, -1, keepdims=True)
    scale = lax.rsqrt(variance + EPSILON)
    return centred * scale, scale


def forward_kernel(
    count, recv, send, edge, wide, nodes, w_one, b_one, w_two, b_two, gain, shift,
    result, first, second, received, sums,
    table, total, rows, stage, sems,
):
    step = pl.program_id(0)
    base = step * TILE
    width = nodes.shape[1]
    parts = width // LANES

    @pl.when(step == 0)
    def _():
        load_table(wide, table, stage, sems)
        clear(total)

    gather_rows(recv, base, table, rows, parts)
    from_recv = read_rows(rows, 0, TILE, parts).astype(jnp.bfloat16)
    received[...] = from_recv
    column = jnp.broadcast_to(send[0], (LANES, TILE)).T
    lane = lax.broadcasted_iota(jnp.int32, (TILE, LANES), 1)
    chosen = jnp.concatenate(
        [
            jnp.where(column == lane + j * LANES, 1.0, 0.0).astype(jnp.bfloat16)
            for j in range(nodes.shape[0] // LANES)
        ],
        axis=1,
    )
    from_send = dot(chosen, nodes[...]).astype(jnp.bfloat16)
    pre = (
        dot(edge[...], w_one[:width])
        + dot(from_send, w_one[width : 2 * width])
        + dot(from_recv, w_one[2 * width :])
        + b_one[...]
    )
    first[...] = pre
    act = (pre * jax.nn.sigmoid(pre)).astype(jnp.bfloat16)
    post = dot(act, w_two[...]) + b_two[...]
    second[...] = post
    normal, _ = row_normal(post)
    branch = normal * gain[...] + shift[...]
    live = base + lax.broadcasted_iota(jnp.int32, (TILE, 1), 0) < count[0]
    outcome = edge[...].astype(jnp.float32) + jnp.where(live, branch, 0.0)
    result[...] = outcome
    lay_rows(rows, 0, jnp.where(live, outcome, 0.0))
    add_rows(recv, base, rows, total, parts)

    @pl.when(step == pl.num_programs(0) - 1)
    def _():
        store_table(total, sums, stage, sems)


def edge_forward(count, recv, send, edge, wide, nodes, w_one, b_one, w_two, b_two, gain, shift):
    edges, width = edge.shape
    steps = edges // TILE
    parts = width // LANES
    hold = pl.BlockSpec(memory_space=pltpu.VMEM)
    scalar = pl.BlockSpec(memory_space=pltpu.SMEM)
    tile = pl.BlockSpec((TILE, width), lambda i: (i, 0))
    return pl.pallas_call(
        forward_kernel,
        grid=(steps,),
        in_specs=[
            scalar, scalar, pl.BlockSpec((1, 1, TILE), lambda i: (i, 0, 0)), tile,
            pl.BlockSpec(memory_space=pl.ANY), hold, hold, hold, hold, hold, hold, hold,
        ],
        out_specs=[tile, tile, tile, tile, pl.BlockSpec(memory_space=pl.ANY)],
        out_shape=[
            jax.ShapeDtypeStruct((edges, width), jnp.float32),
            jax.ShapeDtypeStruct((edges, width), jnp.float32),
            jax.ShapeDtypeStruct((edges, width), jnp.float32),
            jax.ShapeDtypeStruct((edges, width), jnp.bfloat16),
            jax.ShapeDtypeStruct(wide.shape, jnp.bfloat16),
        ],
        scratch_shapes=[
            pltpu.VMEM((wide.shape[0] * parts, LANES), jnp.float32),
            pltpu.VMEM((wide.shape[0] * parts, LANES), jnp.float32),
            pltpu.VMEM((TILE * parts, LANES), jnp.float32),
            pltpu.VMEM((2, CHUNK, width), jnp.bfloat16),
            pltpu.SemaphoreType.DMA((2,)),
        ],
        compiler_params=pltpu.CompilerParams(vmem_limit_bytes=VMEM_BYTES),
        name="edge_forward",
    )(count, recv, send.reshape(steps, 1, TILE), edge, wide, nodes, w_one, b_one, w_two, b_two, gain, shift)


def backward_kernel(
    count, recv, send, cotangent, edge, received, first, second, wide, nodes, w_one_t, w_two_t, gain,
    grad, sums, grad_one, grad_two, vectors, sender_grad,
    table, total, rows, stage, sems, by_sender,
):
    step = pl.program_id(0)
    base = step * TILE
    width = nodes.shape[1]
    parts = width // LANES

    @pl.when(step == 0)
    def _():
        load_table(wide, table, stage, sems)
        clear(total)
        grad_one[...] = jnp.zeros_like(grad_one)
        grad_two[...] = jnp.zeros_like(grad_two)
        vectors[...] = jnp.zeros_like(vectors)
        by_sender[...] = jnp.zeros_like(by_sender)

    gather_rows(recv, base, table, rows, parts)
    live = base + lax.broadcasted_iota(jnp.int32, (TILE, 1), 0) < count[0]
    upstream = cotangent[...].astype(jnp.float32) + jnp.where(live, read_rows(rows, 0, TILE, parts), 0.0)
    masked = jnp.where(live, upstream, 0.0)
    normal, scale = row_normal(second[...])
    vectors[2:3, :] += jnp.sum(masked * normal, 0, keepdims=True)
    vectors[3:4, :] += jnp.sum(masked, 0, keepdims=True)
    scaled = masked * gain[...]
    slope = jnp.mean(scaled * normal, -1, keepdims=True)
    grad_second = scale * (scaled - jnp.mean(scaled, -1, keepdims=True) - normal * slope)
    second_low = grad_second.astype(jnp.bfloat16)
    vectors[1:2, :] += jnp.sum(second_low.astype(jnp.float32), 0, keepdims=True)
    pre = first[...]
    logistic = jax.nn.sigmoid(pre)
    act = (pre * logistic).astype(jnp.bfloat16)
    grad_two[...] += dot_left(act, second_low)
    grad_first = dot(second_low, w_two_t[...]) * (logistic * (1.0 + pre * (1.0 - logistic)))
    first_low = grad_first.astype(jnp.bfloat16)
    first_wide = first_low.astype(jnp.float32)
    vectors[0:1, :] += jnp.sum(first_wide, 0, keepdims=True)
    grad_one[:width] += dot_left(edge[...], first_low)
    grad_one[2 * width :] += dot_left(received[...], first_low)
    node = lax.broadcasted_iota(jnp.int32, (nodes.shape[0], TILE), 0)
    chosen = jnp.where(node == send[0], 1.0, 0.0).astype(jnp.bfloat16)
    by_sender[...] += dot(chosen, first_low)
    grad[...] = upstream + dot(first_low, w_one_t[:, :width])
    lay_rows(rows, 0, first_wide)
    add_rows(recv, base, rows, total, parts)

    @pl.when(step == pl.num_programs(0) - 1)
    def _():
        high, rest = split_low(by_sender[...])
        grad_one[width : 2 * width] = dot_left(nodes[...], high) + dot_left(nodes[...], rest)
        middle = w_one_t[:, width : 2 * width]
        sender_grad[...] = dot(high, middle) + dot(rest, middle)
        store_table(total, sums, stage, sems)


def edge_backward(count, recv, send, cotangent, edge, received, first, second, wide, nodes, w_one_t, w_two_t, gain):
    edges, width = edge.shape
    steps = edges // TILE
    parts = width // LANES
    per_device = nodes.shape[0]
    hold = pl.BlockSpec(memory_space=pltpu.VMEM)
    scalar = pl.BlockSpec(memory_space=pltpu.SMEM)
    tile = pl.BlockSpec((TILE, width), lambda i: (i, 0))

    def whole(rows):
        return pl.BlockSpec((rows, width), lambda i: (0, 0))

    return pl.pallas_call(
        backward_kernel,
        grid=(steps,),
        in_specs=[
            scalar, scalar, pl.BlockSpec((1, 1, TILE), lambda i: (i, 0, 0)), tile, tile, tile, tile, tile,
            pl.BlockSpec(memory_space=pl.ANY), hold, hold, hold, hold,
        ],
        out_specs=[
            tile, pl.BlockSpec(memory_space=pl.ANY),
            whole(3 * width), whole(width), whole(8), whole(per_device),
        ],
        out_shape=[
            jax.ShapeDtypeStruct((edges, width), jnp.float32),
            jax.ShapeDtypeStruct(wide.shape, jnp.bfloat16),
            jax.ShapeDtypeStruct((3 * width, width), jnp.float32),
            jax.ShapeDtypeStruct((width, width), jnp.float32),
            jax.ShapeDtypeStruct((8, width), jnp.float32),
            jax.ShapeDtypeStruct((per_device, width), jnp.float32),
        ],
        scratch_shapes=[
            pltpu.VMEM((wide.shape[0] * parts, LANES), jnp.float32),
            pltpu.VMEM((wide.shape[0] * parts, LANES), jnp.float32),
            pltpu.VMEM((TILE * parts, LANES), jnp.float32),
            pltpu.VMEM((2, CHUNK, width), jnp.bfloat16),
            pltpu.SemaphoreType.DMA((2,)),
            pltpu.VMEM((per_device, width), jnp.float32),
        ],
        compiler_params=pltpu.CompilerParams(vmem_limit_bytes=VMEM_BYTES),
        name="edge_backward",
    )(count, recv, send.reshape(steps, 1, TILE), cotangent, edge, received, first, second, wide, nodes, w_one_t, w_two_t, gain)


MESH = pl.DeviceIdType.MESH
PIECES = 4


def places():
    groups = lax.axis_size("blk")
    group, sub = lax.axis_index("blk"), lax.axis_index("sub")
    odd = lax.rem(group, 2)
    return dict(
        group=group,
        sub=sub,
        sibling=sub + 1 - 2 * lax.rem(sub, 2),
        partner=lax.rem(sub + 2, 4),
        beside=group + 1 - 2 * odd,
        onward=lax.rem(group + 2 - 4 * odd + groups, groups),
        source=lax.rem(group - 2 + 4 * odd + groups, groups),
        near=2 - 2 * odd,
        far=2 * odd,
    )


def meet(senders, count):
    barrier = pltpu.get_barrier_semaphore()
    for device in senders:
        pl.semaphore_signal(barrier, inc=1, device_id=device, device_id_type=MESH)
    pl.semaphore_wait(barrier, count)


def spread_kernel(own, table, send_sems, recv_sems, keep_sem):
    at = places()
    group, sub, partner, near, far = at["group"], at["sub"], at["partner"], at["near"], at["far"]
    to_sibling = (group, at["sibling"])
    to_partner = (group, partner)
    to_beside = (at["beside"], sub)
    to_onward = (at["onward"], sub)
    size = own.shape[0] // PIECES
    meet((to_sibling, to_partner, to_beside, (at["source"], sub)), 4)

    def copy(kind, piece, source, slot, device):
        return pltpu.make_async_remote_copy(
            src_ref=source.at[pl.ds(piece * size, size)],
            dst_ref=table.at[slot[0], slot[1], pl.ds(piece * size, size)],
            send_sem=send_sems.at[kind, piece],
            recv_sem=recv_sems.at[kind, piece],
            device_id=device,
            device_id_type=MESH,
        )

    def move(kind, piece):
        if kind == 0:
            return copy(0, piece, own, (1, sub), to_partner)
        if kind == 1:
            return copy(1, piece, own, (far, sub), to_beside)
        if kind == 2:
            return copy(2, piece, own, (1, sub), to_sibling)
        slot, target, device = {
            3: ((1, partner), (far, partner), to_beside),
            4: ((1, partner), (1, partner), to_sibling),
            5: ((near, sub), (far, sub), to_onward),
            6: ((near, sub), (near, sub), to_sibling),
            7: ((near, partner), (far, partner), to_onward),
            8: ((near, partner), (near, partner), to_sibling),
            9: ((far, sub), (far, sub), to_sibling),
            10: ((far, partner), (far, partner), to_sibling),
        }[kind]
        return copy(kind, piece, table.at[slot[0], slot[1]], target, device)

    keep = pltpu.make_async_copy(own, table.at[1, sub], keep_sem)
    for piece in range(PIECES):
        for kind in (0, 1, 2):
            move(kind, piece).start()
    keep.start()

    def relay(arrived, kinds, piece):
        move(arrived, piece).wait_recv()
        for kind in kinds:
            move(kind, piece).start()

    for piece in range(PIECES):
        relay(0, (3, 4), piece)
        relay(1, (5, 6), piece)
    for piece in range(PIECES):
        relay(3, (7, 8), piece)
        relay(5, (9,), piece)
    for piece in range(PIECES):
        relay(7, (10,), piece)
    for kind in range(11):
        for piece in range(PIECES):
            if kind in (2, 4, 6, 8, 9, 10):
                move(kind, piece).wait_recv()
            move(kind, piece).wait_send()
    keep.wait()


def spread(own, collective):
    rows, width = own.shape
    return pl.pallas_call(
        spread_kernel,
        in_specs=[pl.BlockSpec(memory_space=pl.ANY)],
        out_specs=pl.BlockSpec(memory_space=pl.ANY),
        out_shape=jax.ShapeDtypeStruct((3, 4, rows, width), own.dtype),
        scratch_shapes=[
            pltpu.SemaphoreType.DMA((11, PIECES)),
            pltpu.SemaphoreType.DMA((11, PIECES)),
            pltpu.SemaphoreType.DMA,
        ],
        compiler_params=pltpu.CompilerParams(collective_id=collective, has_side_effects=True),
        name="spread_rows",
    )(own).reshape(12 * rows, width)


def collect_kernel(
    sums, out, mine, landed, far_out, far_in, near_out, near_in, pair_out, pair_in,
    keep_sems, give_sems, take_sems, send_sems, recv_sems,
):
    at = places()
    group, sub, partner, near, far = at["group"], at["sub"], at["partner"], at["near"], at["far"]
    sibling = at["sibling"]
    size = out.shape[0] // PIECES
    meet(((group, sibling), (group, partner), (at["beside"], sub), (at["onward"], sub)), 4)
    relations = (far, near, 1)

    def part(ref, piece):
        return ref.at[pl.ds(piece * size, size)]

    def keep(role, side, piece):
        return pltpu.make_async_copy(
            part(sums.at[relations[role], (sub, partner)[side]], piece),
            part(mine.at[role, side], piece),
            keep_sems.at[role, side, piece],
        )

    def give(role, side, piece):
        return pltpu.make_async_remote_copy(
            src_ref=part(sums.at[relations[role], (sibling, lax.rem(sibling + 2, 4))[side]], piece),
            dst_ref=part(landed.at[role, side], piece),
            send_sem=give_sems.at[role, side, piece],
            recv_sem=take_sems.at[role, side, piece],
            device_id=(group, sibling),
            device_id_type=MESH,
        )

    def hop(kind, piece):
        source, target, device = {
            0: (far_out.at[0], far_in.at[0], (at["source"], sub)),
            1: (far_out.at[1], far_in.at[1], (at["source"], sub)),
            2: (near_out.at[0], near_in.at[0], (at["beside"], sub)),
            3: (near_out.at[1], near_in.at[1], (at["beside"], sub)),
            4: (pair_out, pair_in, (group, partner)),
        }[kind]
        return pltpu.make_async_remote_copy(
            src_ref=part(source, piece),
            dst_ref=part(target, piece),
            send_sem=send_sems.at[kind, piece],
            recv_sem=recv_sems.at[kind, piece],
            device_id=device,
            device_id_type=MESH,
        )

    order = [(role, side, piece) for role in range(3) for side in (1, 0) for piece in range(PIECES)]
    for item in order:
        give(*item).start()
        keep(*item).start()

    def local(role, side, piece):
        keep(role, side, piece).wait()
        give(role, side, piece).wait_recv()
        rows = pl.ds(piece * size, size)
        return mine[role, side, rows, :].astype(jnp.float32) + landed[role, side, rows, :].astype(jnp.float32)

    def arrived(kind, ref, piece):
        hop(kind, piece).wait_recv()
        return ref[pl.ds(piece * size, size), :].astype(jnp.float32)

    for side in (1, 0):
        for piece in range(PIECES):
            far_out[side, pl.ds(piece * size, size), :] = local(0, side, piece).astype(jnp.bfloat16)
            hop(side, piece).start()
    for side in (1, 0):
        for piece in range(PIECES):
            value = local(1, side, piece) + arrived(side, far_in.at[side], piece)
            near_out[side, pl.ds(piece * size, size), :] = value.astype(jnp.bfloat16)
            hop(2 + side, piece).start()
    for piece in range(PIECES):
        value = local(2, 1, piece) + arrived(3, near_in.at[1], piece)
        pair_out[pl.ds(piece * size, size), :] = value.astype(jnp.bfloat16)
        hop(4, piece).start()
    for piece in range(PIECES):
        value = local(2, 0, piece) + arrived(2, near_in.at[0], piece) + arrived(4, pair_in, piece)
        out[pl.ds(piece * size, size), :] = value
    for item in order:
        give(*item).wait_send()
    for kind in range(5):
        for piece in range(PIECES):
            hop(kind, piece).wait_send()


def collect(sums, rows, collective):
    width = sums.shape[1]
    low = jnp.bfloat16
    return pl.pallas_call(
        collect_kernel,
        in_specs=[pl.BlockSpec(memory_space=pl.ANY)],
        out_specs=pl.BlockSpec(memory_space=pltpu.VMEM),
        out_shape=jax.ShapeDtypeStruct((rows, width), jnp.float32),
        scratch_shapes=[
            pltpu.VMEM((3, 2, rows, width), low),
            pltpu.VMEM((3, 2, rows, width), low),
            pltpu.VMEM((2, rows, width), low),
            pltpu.VMEM((2, rows, width), low),
            pltpu.VMEM((2, rows, width), low),
            pltpu.VMEM((2, rows, width), low),
            pltpu.VMEM((rows, width), low),
            pltpu.VMEM((rows, width), low),
            pltpu.SemaphoreType.DMA((3, 2, PIECES)),
            pltpu.SemaphoreType.DMA((3, 2, PIECES)),
            pltpu.SemaphoreType.DMA((3, 2, PIECES)),
            pltpu.SemaphoreType.DMA((5, PIECES)),
            pltpu.SemaphoreType.DMA((5, PIECES)),
        ],
        compiler_params=pltpu.CompilerParams(
            collective_id=collective, has_side_effects=True, vmem_limit_bytes=VMEM_BYTES
        ),
        name="collect_sums",
    )(sums.reshape(3, 4, rows, width))


def shards(
    node_input,
    edge_input,
    senders,
    receivers,
    edge_count,
    edge_w_one,
    edge_b_one,
    edge_w_two,
    edge_b_two,
    edge_gain,
    edge_shift,
    node_w_one,
    node_b_one,
    node_w_two,
    node_b_two,
    node_gain,
    node_shift,
    node_cotangent,
    edge_cotangent,
):
    groups = lax.axis_size("blk")
    sub_count = lax.axis_size("sub")
    block_index = lax.axis_index("blk")
    sub_index = lax.axis_index("sub")
    width = edge_input.shape[1]
    node_low = to_nodes(node_input).T
    node_upstream = to_nodes(node_cotangent).T.astype(jnp.float32)
    per_device = node_low.shape[0]
    per_group = per_device * sub_count
    my_start = (block_index * sub_count + sub_index) * per_device
    send_local = senders - my_start
    relative = (receivers // per_group - block_index + 1 + groups) % groups
    recv_wide = relative * per_group + receivers % per_group
    wide_low = spread(node_low, 0)
    edge_result, first_pre, second_pre, received, wide_sums = edge_forward(
        edge_count, recv_wide, send_local, edge_input, wide_low, node_low,
        edge_w_one, edge_b_one[None], edge_w_two, edge_b_two[None], edge_gain[None], edge_shift[None],
    )
    gathered = collect(wide_sums, per_device, 1)
    joined = jnp.concatenate([node_low, gathered.astype(jnp.bfloat16)], axis=1)
    third_pre = matmul(joined, node_w_one) + node_b_one
    third_act = jax.nn.silu(third_pre).astype(jnp.bfloat16)
    fourth_pre = matmul(third_act, node_w_two) + node_b_two
    node_branch, node_norm_back = jax.vjp(norm_apply, fourth_pre, node_gain, node_shift)
    grad_fourth, grad_node_gain, grad_node_shift = node_norm_back(node_upstream)
    fourth_low = grad_fourth.astype(jnp.bfloat16)
    grad_node_w_two = left_matmul(third_act, fourth_low)
    grad_node_b_two = jnp.sum(fourth_low.astype(jnp.float32), 0)
    grad_third = right_matmul(fourth_low, node_w_two) * silu_slope(third_pre)
    third_low = grad_third.astype(jnp.bfloat16)
    grad_node_w_one = left_matmul(joined, third_low)
    grad_node_b_one = jnp.sum(third_low.astype(jnp.float32), 0)
    grad_joined = right_matmul(third_low, node_w_one)
    grad_nodes = grad_joined[:, :width]
    grad_gathered = grad_joined[:, width:]
    wide_grad = spread(grad_gathered.astype(jnp.bfloat16), 2)
    node_grads = (
        grad_node_w_one, grad_node_b_one, grad_node_w_two, grad_node_b_two, grad_node_gain, grad_node_shift
    )
    wide_grad, node_grads = lax.optimization_barrier((wide_grad, node_grads))
    node_summed = lax.psum(node_grads, ("blk", "sub"))
    node_out = node_input + to_channels(node_branch.T)
    edge_grad, receiver_wide, grad_edge_w_one, grad_edge_w_two, vectors, sender_grad = edge_backward(
        edge_count, recv_wide, send_local, edge_cotangent, edge_input, received, first_pre, second_pre,
        wide_grad, node_low, edge_w_one.T, edge_w_two.T, edge_gain[None],
    )
    grad_edge_b_one, grad_edge_b_two, grad_edge_gain, grad_edge_shift = (vectors[i] for i in range(4))
    high, rest = split_low(collect(receiver_wide, per_device, 3))
    receiver_weight = edge_w_one[2 * width :]
    receiver_grad = right_matmul(high, receiver_weight) + right_matmul(rest, receiver_weight)
    node_total = grad_nodes + sender_grad + receiver_grad
    edge_grads = (
        grad_edge_w_one, grad_edge_b_one, grad_edge_w_two, grad_edge_b_two, grad_edge_gain, grad_edge_shift
    )
    edge_grads, node_summed = lax.optimization_barrier((edge_grads, node_summed))
    summed = lax.psum(edge_grads, ("blk", "sub"))
    node_grad = node_cotangent + to_channels(node_total.T)
    return (
        node_out,
        edge_result,
        node_grad,
        edge_grad,
        summed[0],
        summed[1],
        summed[2],
        summed[3],
        summed[4],
        summed[5],
        node_summed[0],
        node_summed[1],
        node_summed[2],
        node_summed[3],
        node_summed[4],
        node_summed[5],
    )


def solution(mesh):
    placed = (
        P(("blk", "sub"), None),
        P(("blk", "sub"), None),
        P(("blk", "sub")),
        P(("blk", "sub")),
        P(("blk", "sub")),
        P(),
        P(),
        P(),
        P(),
        P(),
        P(),
        P(),
        P(),
        P(),
        P(),
        P(),
        P(),
        P(("blk", "sub"), None),
        P(("blk", "sub"), None),
    )
    return jax.shard_map(
        shards,
        mesh=mesh,
        in_specs=placed,
        out_specs=(
            P(("blk", "sub"), None),
            P(("blk", "sub"), None),
            P(("blk", "sub"), None),
            P(("blk", "sub"), None),
            P(),
            P(),
            P(),
            P(),
            P(),
            P(),
            P(),
            P(),
            P(),
            P(),
            P(),
            P(),
        ),
        check_vma=False,
    )
```

```python
import jax
import jax.numpy as jnp
from jax import lax
from jax.experimental import pallas as pl
from jax.experimental.pallas import tpu as pltpu
from jax.sharding import PartitionSpec as P

EPSILON = 1e-05


def norm_apply(values, gain, shift):
    average = jnp.mean(values, -1, keepdims=True)
    centred = values - average
    variance = jnp.mean(centred * centred, -1, keepdims=True)
    return centred * lax.rsqrt(variance + EPSILON) * gain + shift


def silu_slope(values):
    logistic = jax.nn.sigmoid(values)
    return logistic * (1.0 + values * (1.0 - logistic))


def matmul(left, right):
    return jnp.dot(left, right, preferred_element_type=jnp.float32)


def left_matmul(left, right):
    return lax.dot_general(
        left, right, (((0,), (0,)), ((), ())), preferred_element_type=jnp.float32
    )


def right_matmul(left, right):
    return lax.dot_general(
        left, right, (((1,), (1,)), ((), ())), preferred_element_type=jnp.float32
    )


def to_nodes(channels):
    return lax.all_to_all(
        channels.astype(jnp.bfloat16), ("blk", "sub"), split_axis=1, concat_axis=0, tiled=True
    )


def to_channels(values):
    return lax.all_to_all(
        values.astype(jnp.bfloat16), ("blk", "sub"), split_axis=0, concat_axis=1, tiled=True
    ).astype(jnp.float32)


TILE = 512
CHUNK = 512
LANES = 128
VMEM_BYTES = 60 * 2**20


def dot(left, right):
    return jnp.dot(left, right, preferred_element_type=jnp.float32)


def dot_left(left, right):
    return lax.dot_general(
        left, right, (((0,), (0,)), ((), ())), preferred_element_type=jnp.float32
    )


def split_low(values):
    high = values.astype(jnp.bfloat16)
    return high, (values - high.astype(jnp.float32)).astype(jnp.bfloat16)


def lay_rows(target, start, values):
    count, width = values.shape
    parts = width // LANES
    for j in range(parts):
        target[pl.ds(start * parts + j, count, stride=parts), :] = values[:, j * LANES : (j + 1) * LANES]


def read_rows(source, start, count, parts):
    return jnp.concatenate(
        [source[pl.ds(start * parts + j, count, stride=parts), :] for j in range(parts)], axis=1
    )


def load_table(wide, table, stage, sems):
    steps = wide.shape[0] // CHUNK

    def fetch(i, slot):
        return pltpu.make_async_copy(wide.at[pl.ds(i * CHUNK, CHUNK)], stage.at[slot], sems.at[slot])

    fetch(0, 0).start()

    def body(i, carry):
        slot = lax.rem(i, 2)

        @pl.when(i + 1 < steps)
        def _():
            fetch(i + 1, 1 - slot).start()

        fetch(i, slot).wait()

        def piece(k, carry):
            values = stage[slot, pl.ds(k * 64, 64), :].astype(jnp.float32)
            lay_rows(table, i * CHUNK + k * 64, values)
            return carry

        return lax.fori_loop(0, CHUNK // 64, piece, carry)

    lax.fori_loop(0, steps, body, 0)


def store_table(table, wide, stage, sems):
    steps = wide.shape[0] // CHUNK
    parts = wide.shape[1] // LANES

    def send(i, slot):
        return pltpu.make_async_copy(stage.at[slot], wide.at[pl.ds(i * CHUNK, CHUNK)], sems.at[slot])

    def body(i, carry):
        slot = lax.rem(i, 2)

        @pl.when(i >= 2)
        def _():
            send(i - 2, slot).wait()

        def piece(k, carry):
            values = read_rows(table, i * CHUNK + k * 64, 64, parts)
            stage[slot, pl.ds(k * 64, 64), :] = values.astype(jnp.bfloat16)
            return carry

        lax.fori_loop(0, CHUNK // 64, piece, 0)
        send(i, slot).start()
        return carry

    lax.fori_loop(0, steps, body, 0)
    for i in (steps - 2, steps - 1):
        send(i, i % 2).wait()


def clear(table):
    def body(i, carry):
        table[pl.ds(i * 512, 512), :] = jnp.zeros((512, LANES), table.dtype)
        return carry

    lax.fori_loop(0, table.shape[0] // 512, body, 0)


def gather_rows(index, base, table, rows, parts):
    count = rows.shape[0] // parts

    def body(i, carry):
        for u in range(16):
            slot = i * 16 + u
            place = index[base + slot]
            rows[pl.ds(pl.multiple_of(slot * parts, parts), parts), :] = table[
                pl.ds(pl.multiple_of(place * parts, parts), parts), :
            ]
        return carry

    lax.fori_loop(0, count // 16, body, 0)


def add_rows(index, base, rows, table, parts):
    count = rows.shape[0] // parts

    def body(i, carry):
        for u in range(0, 16, 2):
            slot = i * 16 + u
            one, two = index[base + slot], index[base + slot + 1]
            at_one = pl.ds(pl.multiple_of(one * parts, parts), parts)
            at_two = pl.ds(pl.multiple_of(two * parts, parts), parts)
            held_one, held_two = table[at_one, :], table[at_two, :]
            sum_one = held_one + rows[pl.ds(pl.multiple_of(slot * parts, parts), parts), :]
            held_two = jnp.where(one == two, sum_one, held_two)
            sum_two = held_two + rows[pl.ds(pl.multiple_of((slot + 1) * parts, parts), parts), :]
            table[at_one, :] = sum_one
            table[at_two, :] = sum_two
        return carry

    lax.fori_loop(0, count // 16, body, 0)


def row_normal(values):
    average = jnp.mean(values, -1, keepdims=True)
    centred = values - average
    variance = jnp.mean(centred * centred, -1, keepdims=True)
    scale = lax.rsqrt(variance + EPSILON)
    return centred * scale, scale


def forward_kernel(
    count, recv, send, edge, wide, nodes, w_one, b_one, w_two, b_two, gain, shift,
    result, first, second, received, sums,
    table, total, rows, stage, sems,
):
    step = pl.program_id(0)
    base = step * TILE
    width = nodes.shape[1]
    parts = width // LANES

    @pl.when(step == 0)
    def _():
        load_table(wide, table, stage, sems)
        clear(total)

    gather_rows(recv, base, table, rows, parts)
    from_recv = read_rows(rows, 0, TILE, parts).astype(jnp.bfloat16)
    received[...] = from_recv
    column = jnp.broadcast_to(send[0], (LANES, TILE)).T
    lane = lax.broadcasted_iota(jnp.int32, (TILE, LANES), 1)
    chosen = jnp.concatenate(
        [
            jnp.where(column == lane + j * LANES, 1.0, 0.0).astype(jnp.bfloat16)
            for j in range(nodes.shape[0] // LANES)
        ],
        axis=1,
    )
    from_send = dot(chosen, nodes[...]).astype(jnp.bfloat16)
    pre = (
        dot(edge[...], w_one[:width])
        + dot(from_send, w_one[width : 2 * width])
        + dot(from_recv, w_one[2 * width :])
        + b_one[...]
    )
    first[...] = pre
    act = (pre * jax.nn.sigmoid(pre)).astype(jnp.bfloat16)
    post = dot(act, w_two[...]) + b_two[...]
    second[...] = post
    normal, _ = row_normal(post)
    branch = normal * gain[...] + shift[...]
    live = base + lax.broadcasted_iota(jnp.int32, (TILE, 1), 0) < count[0]
    outcome = edge[...].astype(jnp.float32) + jnp.where(live, branch, 0.0)
    result[...] = outcome
    lay_rows(rows, 0, jnp.where(live, outcome, 0.0))
    add_rows(recv, base, rows, total, parts)

    @pl.when(step == pl.num_programs(0) - 1)
    def _():
        store_table(total, sums, stage, sems)


def edge_forward(count, recv, send, edge, wide, nodes, w_one, b_one, w_two, b_two, gain, shift):
    edges, width = edge.shape
    steps = edges // TILE
    parts = width // LANES
    hold = pl.BlockSpec(memory_space=pltpu.VMEM)
    scalar = pl.BlockSpec(memory_space=pltpu.SMEM)
    tile = pl.BlockSpec((TILE, width), lambda i: (i, 0))
    return pl.pallas_call(
        forward_kernel,
        grid=(steps,),
        in_specs=[
            scalar, scalar, pl.BlockSpec((1, 1, TILE), lambda i: (i, 0, 0)), tile,
            pl.BlockSpec(memory_space=pl.ANY), hold, hold, hold, hold, hold, hold, hold,
        ],
        out_specs=[tile, tile, tile, tile, pl.BlockSpec(memory_space=pl.ANY)],
        out_shape=[
            jax.ShapeDtypeStruct((edges, width), jnp.float32),
            jax.ShapeDtypeStruct((edges, width), jnp.float32),
            jax.ShapeDtypeStruct((edges, width), jnp.float32),
            jax.ShapeDtypeStruct((edges, width), jnp.bfloat16),
            jax.ShapeDtypeStruct(wide.shape, jnp.bfloat16),
        ],
        scratch_shapes=[
            pltpu.VMEM((wide.shape[0] * parts, LANES), jnp.float32),
            pltpu.VMEM((wide.shape[0] * parts, LANES), jnp.float32),
            pltpu.VMEM((TILE * parts, LANES), jnp.float32),
            pltpu.VMEM((2, CHUNK, width), jnp.bfloat16),
            pltpu.SemaphoreType.DMA((2,)),
        ],
        compiler_params=pltpu.CompilerParams(vmem_limit_bytes=VMEM_BYTES),
        cost_estimate=pl.CostEstimate(
            flops=20 * edges * width * width, bytes_accessed=40 * edges * width, transcendentals=2 * edges * width
        ),
        name="edge_forward",
    )(count, recv, send.reshape(steps, 1, TILE), edge, wide, nodes, w_one, b_one, w_two, b_two, gain, shift)


def backward_kernel(
    count, recv, send, cotangent, edge, received, first, second, wide, nodes, w_one_t, w_two_t, gain,
    grad, sums, grads, vectors, sender_grad,
    table, total, rows, stage, sems, by_sender,
):
    step = pl.program_id(0)
    base = step * TILE
    width = nodes.shape[1]
    parts = width // LANES

    @pl.when(step == 0)
    def _():
        load_table(wide, table, stage, sems)
        clear(total)
        grads[...] = jnp.zeros_like(grads)
        vectors[...] = jnp.zeros_like(vectors)
        by_sender[...] = jnp.zeros_like(by_sender)

    gather_rows(recv, base, table, rows, parts)
    live = base + lax.broadcasted_iota(jnp.int32, (TILE, 1), 0) < count[0]
    upstream = cotangent[...].astype(jnp.float32) + jnp.where(live, read_rows(rows, 0, TILE, parts), 0.0)
    masked = jnp.where(live, upstream, 0.0)
    normal, scale = row_normal(second[...])
    vectors[2:3, :] += jnp.sum(masked * normal, 0, keepdims=True)
    vectors[3:4, :] += jnp.sum(masked, 0, keepdims=True)
    scaled = masked * gain[...]
    slope = jnp.mean(scaled * normal, -1, keepdims=True)
    grad_second = scale * (scaled - jnp.mean(scaled, -1, keepdims=True) - normal * slope)
    second_low = grad_second.astype(jnp.bfloat16)
    vectors[1:2, :] += jnp.sum(second_low.astype(jnp.float32), 0, keepdims=True)
    pre = first[...]
    logistic = jax.nn.sigmoid(pre)
    act = (pre * logistic).astype(jnp.bfloat16)
    grads[3 * width :] += dot_left(act, second_low)
    grad_first = dot(second_low, w_two_t[...]) * (logistic * (1.0 + pre * (1.0 - logistic)))
    first_low = grad_first.astype(jnp.bfloat16)
    first_wide = first_low.astype(jnp.float32)
    vectors[0:1, :] += jnp.sum(first_wide, 0, keepdims=True)
    grads[:width] += dot_left(edge[...], first_low)
    grads[2 * width : 3 * width] += dot_left(received[...], first_low)
    node = lax.broadcasted_iota(jnp.int32, (nodes.shape[0], TILE), 0)
    chosen = jnp.where(node == send[0], 1.0, 0.0).astype(jnp.bfloat16)
    by_sender[...] += dot(chosen, first_low)
    grad[...] = upstream + dot(first_low, w_one_t[:, :width])
    lay_rows(rows, 0, first_wide)
    add_rows(recv, base, rows, total, parts)

    @pl.when(step == pl.num_programs(0) - 1)
    def _():
        high, rest = split_low(by_sender[...])
        grads[width : 2 * width] = dot_left(nodes[...], high) + dot_left(nodes[...], rest)
        middle = w_one_t[:, width : 2 * width]
        sender_grad[...] = dot(high, middle) + dot(rest, middle)
        store_table(total, sums, stage, sems)


def edge_backward(count, recv, send, cotangent, edge, received, first, second, wide, nodes, w_one_t, w_two_t, gain):
    edges, width = edge.shape
    steps = edges // TILE
    parts = width // LANES
    per_device = nodes.shape[0]
    hold = pl.BlockSpec(memory_space=pltpu.VMEM)
    scalar = pl.BlockSpec(memory_space=pltpu.SMEM)
    tile = pl.BlockSpec((TILE, width), lambda i: (i, 0))

    def whole(rows):
        return pl.BlockSpec((rows, width), lambda i: (0, 0))

    return pl.pallas_call(
        backward_kernel,
        grid=(steps,),
        in_specs=[
            scalar, scalar, pl.BlockSpec((1, 1, TILE), lambda i: (i, 0, 0)), tile, tile, tile, tile, tile,
            pl.BlockSpec(memory_space=pl.ANY), hold, hold, hold, hold,
        ],
        out_specs=[
            tile, pl.BlockSpec(memory_space=pl.ANY),
            whole(4 * width), whole(8), whole(per_device),
        ],
        out_shape=[
            jax.ShapeDtypeStruct((edges, width), jnp.float32),
            jax.ShapeDtypeStruct(wide.shape, jnp.bfloat16),
            jax.ShapeDtypeStruct((4 * width, width), jnp.float32),
            jax.ShapeDtypeStruct((8, width), jnp.float32),
            jax.ShapeDtypeStruct((per_device, width), jnp.float32),
        ],
        scratch_shapes=[
            pltpu.VMEM((wide.shape[0] * parts, LANES), jnp.float32),
            pltpu.VMEM((wide.shape[0] * parts, LANES), jnp.float32),
            pltpu.VMEM((TILE * parts, LANES), jnp.float32),
            pltpu.VMEM((2, CHUNK, width), jnp.bfloat16),
            pltpu.SemaphoreType.DMA((2,)),
            pltpu.VMEM((per_device, width), jnp.float32),
        ],
        compiler_params=pltpu.CompilerParams(vmem_limit_bytes=VMEM_BYTES),
        cost_estimate=pl.CostEstimate(
            flops=24 * edges * width * width, bytes_accessed=40 * edges * width, transcendentals=2 * edges * width
        ),
        name="edge_backward",
    )(count, recv, send.reshape(steps, 1, TILE), cotangent, edge, received, first, second, wide, nodes, w_one_t, w_two_t, gain)


MESH = pl.DeviceIdType.MESH
PIECES = 4


def places():
    groups = lax.axis_size("blk")
    group, sub = lax.axis_index("blk"), lax.axis_index("sub")
    odd = lax.rem(group, 2)
    return dict(
        group=group,
        sub=sub,
        sibling=sub + 1 - 2 * lax.rem(sub, 2),
        partner=lax.rem(sub + 2, 4),
        beside=group + 1 - 2 * odd,
        onward=lax.rem(group + 2 - 4 * odd + groups, groups),
        source=lax.rem(group - 2 + 4 * odd + groups, groups),
        near=2 - 2 * odd,
        far=2 * odd,
    )


def meet(senders, count):
    barrier = pltpu.get_barrier_semaphore()
    for device in senders:
        pl.semaphore_signal(barrier, inc=1, device_id=device, device_id_type=MESH)
    pl.semaphore_wait(barrier, count)


def spread_kernel(own, table, send_sems, recv_sems, keep_sem):
    at = places()
    group, sub, partner, near, far = at["group"], at["sub"], at["partner"], at["near"], at["far"]
    to_sibling = (group, at["sibling"])
    to_partner = (group, partner)
    to_beside = (at["beside"], sub)
    to_onward = (at["onward"], sub)
    size = own.shape[0] // PIECES
    meet((to_sibling, to_partner, to_beside, (at["source"], sub)), 4)

    def copy(kind, piece, source, slot, device):
        return pltpu.make_async_remote_copy(
            src_ref=source.at[pl.ds(piece * size, size)],
            dst_ref=table.at[slot[0], slot[1], pl.ds(piece * size, size)],
            send_sem=send_sems.at[kind, piece],
            recv_sem=recv_sems.at[kind, piece],
            device_id=device,
            device_id_type=MESH,
        )

    def move(kind, piece):
        if kind == 0:
            return copy(0, piece, own, (1, sub), to_partner)
        if kind == 1:
            return copy(1, piece, own, (far, sub), to_beside)
        if kind == 2:
            return copy(2, piece, own, (1, sub), to_sibling)
        slot, target, device = {
            3: ((1, partner), (far, partner), to_beside),
            4: ((1, partner), (1, partner), to_sibling),
            5: ((near, sub), (far, sub), to_onward),
            6: ((near, sub), (near, sub), to_sibling),
            7: ((near, partner), (far, partner), to_onward),
            8: ((near, partner), (near, partner), to_sibling),
            9: ((far, sub), (far, sub), to_sibling),
            10: ((far, partner), (far, partner), to_sibling),
        }[kind]
        return copy(kind, piece, table.at[slot[0], slot[1]], target, device)

    keep = pltpu.make_async_copy(own, table.at[1, sub], keep_sem)
    for piece in range(PIECES):
        for kind in (0, 1, 2):
            move(kind, piece).start()
    keep.start()

    def relay(arrived, kinds, piece):
        move(arrived, piece).wait_recv()
        for kind in kinds:
            move(kind, piece).start()

    for piece in range(PIECES):
        relay(0, (3, 4), piece)
        relay(1, (5, 6), piece)
    for piece in range(PIECES):
        relay(3, (7, 8), piece)
        relay(5, (9,), piece)
    for piece in range(PIECES):
        relay(7, (10,), piece)
    for kind in range(11):
        for piece in range(PIECES):
            if kind in (2, 4, 6, 8, 9, 10):
                move(kind, piece).wait_recv()
            move(kind, piece).wait_send()
    keep.wait()


def spread(own, collective):
    rows, width = own.shape
    return pl.pallas_call(
        spread_kernel,
        in_specs=[pl.BlockSpec(memory_space=pl.ANY)],
        out_specs=pl.BlockSpec(memory_space=pl.ANY),
        out_shape=jax.ShapeDtypeStruct((3, 4, rows, width), own.dtype),
        scratch_shapes=[
            pltpu.SemaphoreType.DMA((11, PIECES)),
            pltpu.SemaphoreType.DMA((11, PIECES)),
            pltpu.SemaphoreType.DMA,
        ],
        compiler_params=pltpu.CompilerParams(collective_id=collective, has_side_effects=True),
        name="spread_rows",
    )(own).reshape(12 * rows, width)


def collect_kernel(
    sums, out, mine, landed, far_out, far_in, near_out, near_in, pair_out, pair_in,
    keep_sems, give_sems, take_sems, send_sems, recv_sems,
):
    at = places()
    group, sub, partner, near, far = at["group"], at["sub"], at["partner"], at["near"], at["far"]
    sibling = at["sibling"]
    size = out.shape[0] // PIECES
    meet(((group, sibling), (group, partner), (at["beside"], sub), (at["onward"], sub)), 4)
    relations = (far, near, 1)

    def part(ref, piece):
        return ref.at[pl.ds(piece * size, size)]

    def keep(role, side, piece):
        return pltpu.make_async_copy(
            part(sums.at[relations[role], (sub, partner)[side]], piece),
            part(mine.at[role, side], piece),
            keep_sems.at[role, side, piece],
        )

    def give(role, side, piece):
        return pltpu.make_async_remote_copy(
            src_ref=part(sums.at[relations[role], (sibling, lax.rem(sibling + 2, 4))[side]], piece),
            dst_ref=part(landed.at[role, side], piece),
            send_sem=give_sems.at[role, side, piece],
            recv_sem=take_sems.at[role, side, piece],
            device_id=(group, sibling),
            device_id_type=MESH,
        )

    def hop(kind, piece):
        source, target, device = {
            0: (far_out.at[0], far_in.at[0], (at["source"], sub)),
            1: (far_out.at[1], far_in.at[1], (at["source"], sub)),
            2: (near_out.at[0], near_in.at[0], (at["beside"], sub)),
            3: (near_out.at[1], near_in.at[1], (at["beside"], sub)),
            4: (pair_out, pair_in, (group, partner)),
        }[kind]
        return pltpu.make_async_remote_copy(
            src_ref=part(source, piece),
            dst_ref=part(target, piece),
            send_sem=send_sems.at[kind, piece],
            recv_sem=recv_sems.at[kind, piece],
            device_id=device,
            device_id_type=MESH,
        )

    order = [(role, side, piece) for role in range(3) for side in (1, 0) for piece in range(PIECES)]
    for item in order:
        give(*item).start()
        keep(*item).start()

    def local(role, side, piece):
        keep(role, side, piece).wait()
        give(role, side, piece).wait_recv()
        rows = pl.ds(piece * size, size)
        return mine[role, side, rows, :].astype(jnp.float32) + landed[role, side, rows, :].astype(jnp.float32)

    def arrived(kind, ref, piece):
        hop(kind, piece).wait_recv()
        return ref[pl.ds(piece * size, size), :].astype(jnp.float32)

    for side in (1, 0):
        for piece in range(PIECES):
            far_out[side, pl.ds(piece * size, size), :] = local(0, side, piece).astype(jnp.bfloat16)
            hop(side, piece).start()
    for side in (1, 0):
        for piece in range(PIECES):
            value = local(1, side, piece) + arrived(side, far_in.at[side], piece)
            near_out[side, pl.ds(piece * size, size), :] = value.astype(jnp.bfloat16)
            hop(2 + side, piece).start()
    for piece in range(PIECES):
        value = local(2, 1, piece) + arrived(3, near_in.at[1], piece)
        pair_out[pl.ds(piece * size, size), :] = value.astype(jnp.bfloat16)
        hop(4, piece).start()
    for piece in range(PIECES):
        value = local(2, 0, piece) + arrived(2, near_in.at[0], piece) + arrived(4, pair_in, piece)
        out[pl.ds(piece * size, size), :] = value
    for item in order:
        give(*item).wait_send()
    for kind in range(5):
        for piece in range(PIECES):
            hop(kind, piece).wait_send()


def collect(sums, rows, collective):
    width = sums.shape[1]
    low = jnp.bfloat16
    return pl.pallas_call(
        collect_kernel,
        in_specs=[pl.BlockSpec(memory_space=pl.ANY)],
        out_specs=pl.BlockSpec(memory_space=pltpu.VMEM),
        out_shape=jax.ShapeDtypeStruct((rows, width), jnp.float32),
        scratch_shapes=[
            pltpu.VMEM((3, 2, rows, width), low),
            pltpu.VMEM((3, 2, rows, width), low),
            pltpu.VMEM((2, rows, width), low),
            pltpu.VMEM((2, rows, width), low),
            pltpu.VMEM((2, rows, width), low),
            pltpu.VMEM((2, rows, width), low),
            pltpu.VMEM((rows, width), low),
            pltpu.VMEM((rows, width), low),
            pltpu.SemaphoreType.DMA((3, 2, PIECES)),
            pltpu.SemaphoreType.DMA((3, 2, PIECES)),
            pltpu.SemaphoreType.DMA((3, 2, PIECES)),
            pltpu.SemaphoreType.DMA((5, PIECES)),
            pltpu.SemaphoreType.DMA((5, PIECES)),
        ],
        compiler_params=pltpu.CompilerParams(
            collective_id=collective, has_side_effects=True, vmem_limit_bytes=VMEM_BYTES
        ),
        name="collect_sums",
    )(sums.reshape(3, 4, rows, width))


def finish_kernel(
    sums, grads, vectors, out, reduced, reduced_vectors,
    mine, landed, far_out, far_in, near_out, near_in, pair_out, pair_in,
    half, half_in, cross_out, cross_in, side_out, side_in, ring_out, ring_in, held, held_in,
    keep_sems, give_sems, take_sems, send_sems, recv_sems,
    load_sem, load_vector_sem, step_send, step_recv, ring_send, ring_recv, vector_send, vector_recv,
):
    at = places()
    group, sub, partner, near, far = at["group"], at["sub"], at["partner"], at["near"], at["far"]
    sibling = at["sibling"]
    groups = lax.axis_size("blk")
    along = groups // 2
    odd, spot = lax.rem(group, 2), group // 2
    core, chip = lax.rem(sub, 2), sub // 2
    size = out.shape[0] // PIECES
    low = jnp.bfloat16
    wide = jnp.float32
    to_sibling, to_partner, to_beside = (group, sibling), (group, partner), (at["beside"], sub)
    peers = [(2 * lax.rem(spot + k, along) + odd, sub) for k in range(1, along)]
    meet((to_sibling, to_partner, to_beside, *peers), 3 + len(peers))
    relations = (far, near, 1)

    rows = grads.shape[0]
    n_half, n_cross, n_side, n_ring = rows // 2, rows // 4, rows // 8, rows // 8 // along
    at_half = pl.multiple_of(core * n_half, n_half)
    at_cross = pl.multiple_of(at_half + chip * n_cross, n_cross)
    at_side = pl.multiple_of(at_cross + odd * n_side, n_side)
    at_ring = pl.multiple_of(at_side + spot * n_ring, n_ring)

    def remote(source, target, send, recv, device):
        return pltpu.make_async_remote_copy(
            src_ref=source, dst_ref=target, send_sem=send, recv_sem=recv,
            device_id=device, device_id_type=MESH,
        )

    def step(kind):
        if kind == 0:
            other = pl.ds(pl.multiple_of((1 - core) * n_half, n_half), n_half)
            source, target, device = grads.at[other], half_in, to_sibling
        elif kind == 1:
            source, target, device = cross_out, cross_in, to_partner
        elif kind == 2:
            source, target, device = side_out, side_in, to_beside
        else:
            start, count, device = {
                3: (at_side, n_side, to_beside),
                4: (at_cross, n_cross, to_partner),
                5: (at_half, n_half, to_sibling),
            }[kind]
            source = target = reduced.at[pl.ds(start, count)]
        return remote(source, target, step_send.at[kind], step_recv.at[kind], device)

    def ring(kind, k):
        if kind == 0:
            spot_to = lax.rem(spot + k, along)
            source = ring_out.at[pl.ds(pl.multiple_of(spot_to * n_ring, n_ring), n_ring)]
            target = ring_in.at[k - 1]
        else:
            source = target = reduced.at[pl.ds(at_ring, n_ring)]
        return remote(source, target, ring_send.at[kind, k - 1], ring_recv.at[kind, k - 1], peers[k - 1])

    def vector(kind):
        device = (to_sibling, to_partner, to_beside, *peers)[kind]
        return remote(
            held.at[min(kind, 3)], held_in.at[kind], vector_send.at[kind], vector_recv.at[kind], device
        )

    def pieces(count, body):
        block = min(count, 128)

        def run(i, carry):
            body(pl.multiple_of(i * block, block), block)
            return carry

        lax.fori_loop(0, count // block, run, 0)

    load = pltpu.make_async_copy(grads.at[pl.ds(at_half, n_half)], half, load_sem)
    load_vector = pltpu.make_async_copy(vectors, held.at[0], load_vector_sem)

    def part(ref, piece):
        return ref.at[pl.ds(piece * size, size)]

    def keep(role, side, piece):
        return pltpu.make_async_copy(
            part(sums.at[relations[role], (sub, partner)[side]], piece),
            part(mine.at[role, side], piece),
            keep_sems.at[role, side, piece],
        )

    def give(role, side, piece):
        return remote(
            part(sums.at[relations[role], (sibling, lax.rem(sibling + 2, 4))[side]], piece),
            part(landed.at[role, side], piece),
            give_sems.at[role, side, piece], take_sems.at[role, side, piece], to_sibling,
        )

    def hop(kind, piece):
        source, target, device = {
            0: (far_out.at[0], far_in.at[0], (at["source"], sub)),
            1: (far_out.at[1], far_in.at[1], (at["source"], sub)),
            2: (near_out.at[0], near_in.at[0], to_beside),
            3: (near_out.at[1], near_in.at[1], to_beside),
            4: (pair_out, pair_in, to_partner),
        }[kind]
        return remote(
            part(source, piece), part(target, piece), send_sems.at[kind, piece], recv_sems.at[kind, piece], device
        )

    order = [(role, side, piece) for role in range(3) for side in (1, 0) for piece in range(PIECES)]

    def local(role, side, piece):
        keep(role, side, piece).wait()
        give(role, side, piece).wait_recv()
        span = pl.ds(piece * size, size)
        return mine[role, side, span, :].astype(wide) + landed[role, side, span, :].astype(wide)

    def arrived(kind, ref, piece):
        hop(kind, piece).wait_recv()
        return ref[pl.ds(piece * size, size), :].astype(wide)

    def far_step(side, piece):
        far_out[side, pl.ds(piece * size, size), :] = local(0, side, piece).astype(low)
        hop(side, piece).start()

    def near_step(side, piece):
        value = local(1, side, piece) + arrived(side, far_in.at[side], piece)
        near_out[side, pl.ds(piece * size, size), :] = value.astype(low)
        hop(2 + side, piece).start()

    def pair_step(piece):
        value = local(2, 1, piece) + arrived(3, near_in.at[1], piece)
        pair_out[pl.ds(piece * size, size), :] = value.astype(low)
        hop(4, piece).start()

    def last_step(piece):
        value = local(2, 0, piece) + arrived(2, near_in.at[0], piece) + arrived(4, pair_in, piece)
        out[pl.ds(piece * size, size), :] = value

    def add_half():
        load.wait()
        step(0).wait_recv()
        other = (1 - chip) * n_cross

        def send_part(i, block):
            span = pl.ds(pl.multiple_of(other + i, block), block)
            cross_out[pl.ds(i, block), :] = (half[span, :] + half_in[span, :]).astype(low)

        pieces(n_cross, send_part)
        step(1).start()
        load_vector.wait()
        vector(0).start()

    def add_cross():
        mine_at, other = chip * n_cross, (1 - odd) * n_side
        step(1).wait_recv()

        def send_part(i, block):
            span = pl.ds(pl.multiple_of(other + i, block), block)
            here = pl.ds(pl.multiple_of(mine_at + other + i, block), block)
            side_out[pl.ds(i, block), :] = (half[here, :] + half_in[here, :] + cross_in[span, :].astype(wide)).astype(low)

        pieces(n_side, send_part)
        step(2).start()
        vector(0).wait_recv()
        held[1] = held[0] + held_in[0]
        vector(1).start()

    def add_side():
        from_side = odd * n_side
        step(2).wait_recv()

        def keep_part(i, block):
            span = pl.ds(pl.multiple_of(from_side + i, block), block)
            here = pl.ds(pl.multiple_of(chip * n_cross + from_side + i, block), block)
            value = half[here, :] + half_in[here, :] + cross_in[span, :].astype(wide) + side_in[pl.ds(i, block), :].astype(wide)
            half[here, :] = value
            ring_out[pl.ds(i, block), :] = value.astype(low)

        pieces(n_side, keep_part)
        for k in range(1, along):
            ring(0, k).start()
        vector(1).wait_recv()
        held[2] = held[1] + held_in[1]
        vector(2).start()

    def add_ring():
        here = pl.ds(pl.multiple_of(chip * n_cross + odd * n_side + spot * n_ring, n_ring), n_ring)
        value = half[here, :]
        for k in range(1, along):
            ring(0, k).wait_recv()
            value = value + ring_in[k - 1].astype(wide)
        reduced[pl.ds(at_ring, n_ring), :] = value.astype(low)
        for k in range(1, along):
            ring(1, k).start()
        vector(2).wait_recv()
        held[3] = held[2] + held_in[2]
        for k in range(1, along):
            vector(2 + k).start()

    def share_side():
        for k in range(1, along):
            ring(1, k).wait_recv()
        step(3).start()

    def share_cross():
        step(3).wait_recv()
        step(4).start()
        value = held[3]
        for k in range(1, along):
            vector(2 + k).wait_recv()
            value = value + held_in[2 + k]
        reduced_vectors[...] = value

    def share_half():
        step(4).wait_recv()
        step(5).start()

    for item in order[: 2 * PIECES]:
        give(*item).start()
        keep(*item).start()
    step(0).start()
    load.start()
    load_vector.start()
    for item in order[2 * PIECES :]:
        give(*item).start()
        keep(*item).start()
    for side in (1, 0):
        for piece in range(PIECES):
            far_step(side, piece)
    add_half()
    for piece in range(PIECES):
        near_step(1, piece)
    for piece in range(PIECES // 2):
        near_step(0, piece)
    add_cross()
    for piece in range(PIECES // 2, PIECES):
        near_step(0, piece)
    for piece in range(PIECES):
        pair_step(piece)
    add_side()
    for piece in range(PIECES):
        last_step(piece)
    add_ring()
    share_side()
    share_cross()
    share_half()
    step(5).wait_recv()
    for item in order:
        give(*item).wait_send()
    for kind in range(5):
        for piece in range(PIECES):
            hop(kind, piece).wait_send()
    for kind in range(6):
        step(kind).wait_send()
    for k in range(1, along):
        ring(0, k).wait_send()
        ring(1, k).wait_send()
    for kind in range(2 + along):
        vector(kind).wait_send()


def finish(sums, grads, vectors, rows, collective):
    width = sums.shape[1]
    low, wide = jnp.bfloat16, jnp.float32
    count = grads.shape[0]
    along = lax.axis_size("blk") // 2
    half = pltpu.VMEM((count // 2, width), wide)
    return pl.pallas_call(
        finish_kernel,
        in_specs=[pl.BlockSpec(memory_space=pl.ANY)] * 3,
        out_specs=[pl.BlockSpec(memory_space=pltpu.VMEM)] * 3,
        out_shape=[
            jax.ShapeDtypeStruct((rows, width), wide),
            jax.ShapeDtypeStruct(grads.shape, low),
            jax.ShapeDtypeStruct(vectors.shape, wide),
        ],
        scratch_shapes=[
            pltpu.VMEM((3, 2, rows, width), low),
            pltpu.VMEM((3, 2, rows, width), low),
            pltpu.VMEM((2, rows, width), low),
            pltpu.VMEM((2, rows, width), low),
            pltpu.VMEM((2, rows, width), low),
            pltpu.VMEM((2, rows, width), low),
            pltpu.VMEM((rows, width), low),
            pltpu.VMEM((rows, width), low),
            half,
            half,
            pltpu.VMEM((count // 4, width), low),
            pltpu.VMEM((count // 4, width), low),
            pltpu.VMEM((count // 8, width), low),
            pltpu.VMEM((count // 8, width), low),
            pltpu.VMEM((count // 8, width), low),
            pltpu.VMEM((along - 1, count // 8 // along, width), low),
            pltpu.VMEM((4, *vectors.shape), wide),
            pltpu.VMEM((2 + along, *vectors.shape), wide),
            pltpu.SemaphoreType.DMA((3, 2, PIECES)),
            pltpu.SemaphoreType.DMA((3, 2, PIECES)),
            pltpu.SemaphoreType.DMA((3, 2, PIECES)),
            pltpu.SemaphoreType.DMA((5, PIECES)),
            pltpu.SemaphoreType.DMA((5, PIECES)),
            pltpu.SemaphoreType.DMA,
            pltpu.SemaphoreType.DMA,
            pltpu.SemaphoreType.DMA((6,)),
            pltpu.SemaphoreType.DMA((6,)),
            pltpu.SemaphoreType.DMA((2, along - 1)),
            pltpu.SemaphoreType.DMA((2, along - 1)),
            pltpu.SemaphoreType.DMA((2 + along,)),
            pltpu.SemaphoreType.DMA((2 + along,)),
        ],
        compiler_params=pltpu.CompilerParams(
            collective_id=collective, has_side_effects=True, vmem_limit_bytes=VMEM_BYTES
        ),
        name="finish_sums",
    )(sums.reshape(3, 4, rows, width), grads, vectors)


def shards(
    node_input,
    edge_input,
    senders,
    receivers,
    edge_count,
    edge_w_one,
    edge_b_one,
    edge_w_two,
    edge_b_two,
    edge_gain,
    edge_shift,
    node_w_one,
    node_b_one,
    node_w_two,
    node_b_two,
    node_gain,
    node_shift,
    node_cotangent,
    edge_cotangent,
):
    groups = lax.axis_size("blk")
    sub_count = lax.axis_size("sub")
    block_index = lax.axis_index("blk")
    sub_index = lax.axis_index("sub")
    width = edge_input.shape[1]
    node_low = to_nodes(node_input).T
    node_upstream = to_nodes(node_cotangent).T.astype(jnp.float32)
    per_device = node_low.shape[0]
    per_group = per_device * sub_count
    my_start = (block_index * sub_count + sub_index) * per_device
    send_local = senders - my_start
    relative = (receivers // per_group - block_index + 1 + groups) % groups
    recv_wide = relative * per_group + receivers % per_group
    wide_low = spread(node_low, 0)
    edge_result, first_pre, second_pre, received, wide_sums = edge_forward(
        edge_count, recv_wide, send_local, edge_input, wide_low, node_low,
        edge_w_one, edge_b_one[None], edge_w_two, edge_b_two[None], edge_gain[None], edge_shift[None],
    )
    gathered = collect(wide_sums, per_device, 1)
    joined = jnp.concatenate([node_low, gathered.astype(jnp.bfloat16)], axis=1)
    third_pre = matmul(joined, node_w_one) + node_b_one
    third_act = jax.nn.silu(third_pre).astype(jnp.bfloat16)
    fourth_pre = matmul(third_act, node_w_two) + node_b_two
    node_branch, node_norm_back = jax.vjp(norm_apply, fourth_pre, node_gain, node_shift)
    grad_fourth, grad_node_gain, grad_node_shift = node_norm_back(node_upstream)
    fourth_low = grad_fourth.astype(jnp.bfloat16)
    grad_node_w_two = left_matmul(third_act, fourth_low)
    grad_node_b_two = jnp.sum(fourth_low.astype(jnp.float32), 0)
    grad_third = right_matmul(fourth_low, node_w_two) * silu_slope(third_pre)
    third_low = grad_third.astype(jnp.bfloat16)
    grad_node_w_one = left_matmul(joined, third_low)
    grad_node_b_one = jnp.sum(third_low.astype(jnp.float32), 0)
    grad_joined = right_matmul(third_low, node_w_one)
    grad_nodes = grad_joined[:, :width]
    grad_gathered = grad_joined[:, width:]
    wide_grad = spread(grad_gathered.astype(jnp.bfloat16), 2)
    node_grads = (grad_node_w_one, grad_node_w_two)
    wide_grad, node_grads = lax.optimization_barrier((wide_grad, node_grads))
    node_summed = lax.psum(node_grads, ("blk", "sub"))
    node_out = node_input + to_channels(node_branch.T)
    edge_grad, receiver_wide, edge_grads, vectors, sender_grad = edge_backward(
        edge_count, recv_wide, send_local, edge_cotangent, edge_input, received, first_pre, second_pre,
        wide_grad, node_low, edge_w_one.T, edge_w_two.T, edge_gain[None],
    )
    node_vectors = jnp.stack([grad_node_b_one, grad_node_b_two, grad_node_gain, grad_node_shift])
    receiver_sums, summed, vectors = finish(
        receiver_wide, edge_grads, jnp.concatenate([vectors[:4], node_vectors]), per_device, 3
    )
    summed = summed.astype(jnp.float32)
    high, rest = split_low(receiver_sums)
    receiver_weight = edge_w_one[2 * width :]
    receiver_grad = right_matmul(high, receiver_weight) + right_matmul(rest, receiver_weight)
    node_total = grad_nodes + sender_grad + receiver_grad
    node_grad = node_cotangent + to_channels(node_total.T)
    return (
        node_out,
        edge_result,
        node_grad,
        edge_grad,
        summed[: 3 * width],
        vectors[0],
        summed[3 * width :],
        vectors[1],
        vectors[2],
        vectors[3],
        node_summed[0],
        vectors[4],
        node_summed[1],
        vectors[5],
        vectors[6],
        vectors[7],
    )


def solution(mesh):
    placed = (
        P(("blk", "sub"), None),
        P(("blk", "sub"), None),
        P(("blk", "sub")),
        P(("blk", "sub")),
        P(("blk", "sub")),
        P(),
        P(),
        P(),
        P(),
        P(),
        P(),
        P(),
        P(),
        P(),
        P(),
        P(),
        P(),
        P(("blk", "sub"), None),
        P(("blk", "sub"), None),
    )
    return jax.shard_map(
        shards,
        mesh=mesh,
        in_specs=placed,
        out_specs=(
            P(("blk", "sub"), None),
            P(("blk", "sub"), None),
            P(("blk", "sub"), None),
            P(("blk", "sub"), None),
            P(),
            P(),
            P(),
            P(),
            P(),
            P(),
            P(),
            P(),
            P(),
            P(),
            P(),
            P(),
        ),
        check_vma=False,
    )
```

```python
import math
import jax
import jax.numpy as jnp
from jax import lax
from jax.experimental import pallas as pl
from jax.experimental.pallas import tpu as pltpu
from jax.sharding import PartitionSpec as P

EPSILON = 1e-05


def norm_apply(values, gain, shift):
    average = jnp.mean(values, -1, keepdims=True)
    centred = values - average
    variance = jnp.mean(centred * centred, -1, keepdims=True)
    return centred * lax.rsqrt(variance + EPSILON) * gain + shift


def silu_slope(values):
    logistic = jax.nn.sigmoid(values)
    return logistic * (1.0 + values * (1.0 - logistic))


def matmul(left, right):
    return jnp.dot(left, right, preferred_element_type=jnp.float32)


def left_matmul(left, right):
    return lax.dot_general(
        left, right, (((0,), (0,)), ((), ())), preferred_element_type=jnp.float32
    )


def right_matmul(left, right):
    return lax.dot_general(
        left, right, (((1,), (1,)), ((), ())), preferred_element_type=jnp.float32
    )


def to_nodes(channels):
    return lax.all_to_all(channels, ("blk", "sub"), split_axis=1, concat_axis=0, tiled=True)


def to_channels(values):
    return lax.all_to_all(
        values.astype(jnp.bfloat16), ("blk", "sub"), split_axis=0, concat_axis=1, tiled=True
    ).astype(jnp.float32)


TILE = 512
CHUNK = 512
LANES = 128
VMEM_BYTES = 60 * 2**20


def dot(left, right):
    return jnp.dot(left, right, preferred_element_type=jnp.float32)


def dot_left(left, right):
    return lax.dot_general(
        left, right, (((0,), (0,)), ((), ())), preferred_element_type=jnp.float32
    )


def split_low(values):
    high = values.astype(jnp.bfloat16)
    return high, (values - high.astype(jnp.float32)).astype(jnp.bfloat16)


def lay_rows(target, start, values):
    count, width = values.shape
    parts = width // LANES
    for j in range(parts):
        target[pl.ds(start * parts + j, count, stride=parts), :] = values[:, j * LANES : (j + 1) * LANES]


def read_rows(source, start, count, parts):
    return jnp.concatenate(
        [source[pl.ds(start * parts + j, count, stride=parts), :] for j in range(parts)], axis=1
    )


def load_table(wide, table, stage, sems):
    steps = wide.shape[0] // CHUNK

    def fetch(i, slot):
        return pltpu.make_async_copy(wide.at[pl.ds(i * CHUNK, CHUNK)], stage.at[slot], sems.at[slot])

    fetch(0, 0).start()

    def body(i, carry):
        slot = lax.rem(i, 2)

        @pl.when(i + 1 < steps)
        def _():
            fetch(i + 1, 1 - slot).start()

        fetch(i, slot).wait()

        def piece(k, carry):
            values = stage[slot, pl.ds(k * 64, 64), :].astype(jnp.float32)
            lay_rows(table, i * CHUNK + k * 64, values)
            return carry

        return lax.fori_loop(0, CHUNK // 64, piece, carry)

    lax.fori_loop(0, steps, body, 0)


def store_table(table, wide, stage, sems):
    steps = wide.shape[0] // CHUNK
    parts = wide.shape[1] // LANES

    def send(i, slot):
        return pltpu.make_async_copy(stage.at[slot], wide.at[pl.ds(i * CHUNK, CHUNK)], sems.at[slot])

    def body(i, carry):
        slot = lax.rem(i, 2)

        @pl.when(i >= 2)
        def _():
            send(i - 2, slot).wait()

        def piece(k, carry):
            values = read_rows(table, i * CHUNK + k * 64, 64, parts)
            stage[slot, pl.ds(k * 64, 64), :] = values.astype(jnp.bfloat16)
            return carry

        lax.fori_loop(0, CHUNK // 64, piece, 0)
        send(i, slot).start()
        return carry

    lax.fori_loop(0, steps, body, 0)
    for i in (steps - 2, steps - 1):
        send(i, i % 2).wait()


def clear(table):
    def body(i, carry):
        table[pl.ds(i * 512, 512), :] = jnp.zeros((512, LANES), table.dtype)
        return carry

    lax.fori_loop(0, table.shape[0] // 512, body, 0)


def gather_rows(index, base, table, rows, parts):
    count = rows.shape[0] // parts

    def body(i, carry):
        for u in range(16):
            slot = i * 16 + u
            place = index[base + slot]
            rows[pl.ds(pl.multiple_of(slot * parts, parts), parts), :] = table[
                pl.ds(pl.multiple_of(place * parts, parts), parts), :
            ]
        return carry

    lax.fori_loop(0, count // 16, body, 0)


def add_rows(index, base, rows, table, parts):
    count = rows.shape[0] // parts

    def body(i, carry):
        for u in range(0, 16, 2):
            slot = i * 16 + u
            one, two = index[base + slot], index[base + slot + 1]
            at_one = pl.ds(pl.multiple_of(one * parts, parts), parts)
            at_two = pl.ds(pl.multiple_of(two * parts, parts), parts)
            held_one, held_two = table[at_one, :], table[at_two, :]
            sum_one = held_one + rows[pl.ds(pl.multiple_of(slot * parts, parts), parts), :]
            held_two = jnp.where(one == two, sum_one, held_two)
            sum_two = held_two + rows[pl.ds(pl.multiple_of((slot + 1) * parts, parts), parts), :]
            table[at_one, :] = sum_one
            table[at_two, :] = sum_two
        return carry

    lax.fori_loop(0, count // 16, body, 0)


def row_normal(values):
    average = jnp.mean(values, -1, keepdims=True)
    centred = values - average
    variance = jnp.mean(centred * centred, -1, keepdims=True)
    scale = lax.rsqrt(variance + EPSILON)
    return centred * scale, scale


def forward_kernel(
    count, recv, send, edge, wide, nodes, w_one, b_one, w_two, b_two, gain, shift,
    result, first, second, received, sums,
    table, total, rows, stage, sems,
):
    step = pl.program_id(0)
    base = step * TILE
    width = nodes.shape[1]
    parts = width // LANES

    @pl.when(step == 0)
    def _():
        load_table(wide, table, stage, sems)
        clear(total)

    gather_rows(recv, base, table, rows, parts)
    from_recv = read_rows(rows, 0, TILE, parts).astype(jnp.bfloat16)
    received[...] = from_recv
    column = jnp.broadcast_to(send[0], (LANES, TILE)).T
    lane = lax.broadcasted_iota(jnp.int32, (TILE, LANES), 1)
    chosen = jnp.concatenate(
        [
            jnp.where(column == lane + j * LANES, 1.0, 0.0).astype(jnp.bfloat16)
            for j in range(nodes.shape[0] // LANES)
        ],
        axis=1,
    )
    from_send = dot(chosen, nodes[...]).astype(jnp.bfloat16)
    pre = (
        dot(edge[...], w_one[:width])
        + dot(from_send, w_one[width : 2 * width])
        + dot(from_recv, w_one[2 * width :])
        + b_one[...]
    )
    first[...] = pre
    act = (pre * jax.nn.sigmoid(pre)).astype(jnp.bfloat16)
    post = dot(act, w_two[...]) + b_two[...]
    second[...] = post
    normal, _ = row_normal(post)
    branch = normal * gain[...] + shift[...]
    live = base + lax.broadcasted_iota(jnp.int32, (TILE, 1), 0) < count[0]
    outcome = edge[...].astype(jnp.float32) + jnp.where(live, branch, 0.0)
    result[...] = outcome
    lay_rows(rows, 0, jnp.where(live, outcome, 0.0))
    add_rows(recv, base, rows, total, parts)

    @pl.when(step == pl.num_programs(0) - 1)
    def _():
        store_table(total, sums, stage, sems)


def edge_forward(count, recv, send, edge, wide, nodes, w_one, b_one, w_two, b_two, gain, shift):
    edges, width = edge.shape
    steps = edges // TILE
    parts = width // LANES
    hold = pl.BlockSpec(memory_space=pltpu.VMEM)
    scalar = pl.BlockSpec(memory_space=pltpu.SMEM)
    tile = pl.BlockSpec((TILE, width), lambda i: (i, 0))
    return pl.pallas_call(
        forward_kernel,
        grid=(steps,),
        in_specs=[
            scalar, scalar, pl.BlockSpec((1, 1, TILE), lambda i: (i, 0, 0)), tile,
            pl.BlockSpec(memory_space=pl.ANY), hold, hold, hold, hold, hold, hold, hold,
        ],
        out_specs=[tile, tile, tile, tile, pl.BlockSpec(memory_space=pl.ANY)],
        out_shape=[
            jax.ShapeDtypeStruct((edges, width), jnp.float32),
            jax.ShapeDtypeStruct((edges, width), jnp.float32),
            jax.ShapeDtypeStruct((edges, width), jnp.float32),
            jax.ShapeDtypeStruct((edges, width), jnp.bfloat16),
            jax.ShapeDtypeStruct(wide.shape, jnp.bfloat16),
        ],
        scratch_shapes=[
            pltpu.VMEM((wide.shape[0] * parts, LANES), jnp.float32),
            pltpu.VMEM((wide.shape[0] * parts, LANES), jnp.float32),
            pltpu.VMEM((TILE * parts, LANES), jnp.float32),
            pltpu.VMEM((2, CHUNK, width), jnp.bfloat16),
            pltpu.SemaphoreType.DMA((2,)),
        ],
        compiler_params=pltpu.CompilerParams(vmem_limit_bytes=VMEM_BYTES),
        cost_estimate=pl.CostEstimate(
            flops=20 * edges * width * width, bytes_accessed=40 * edges * width, transcendentals=2 * edges * width
        ),
        name="edge_forward",
    )(count, recv, send.reshape(steps, 1, TILE), edge, wide, nodes, w_one, b_one, w_two, b_two, gain, shift)


def backward_kernel(
    count, recv, send, cotangent, edge, received, first, second, wide, node_one, node_two, nodes, w_one_t, w_two_t, gain,
    grad, sums, all_grads, vectors, sender_grad,
    table, total, rows, stage, sems, by_sender, grads, pass_sems,
):
    step = pl.program_id(0)
    base = step * TILE
    width = nodes.shape[1]
    parts = width // LANES

    first_node = node_one.shape[0]
    passed = (
        pltpu.make_async_copy(node_one, all_grads.at[pl.ds(4 * width, first_node)], pass_sems.at[0]),
        pltpu.make_async_copy(
            node_two, all_grads.at[pl.ds(4 * width + first_node, node_two.shape[0])], pass_sems.at[1]
        ),
        pltpu.make_async_copy(grads, all_grads.at[pl.ds(0, 4 * width)], pass_sems.at[2]),
    )

    @pl.when(step == 0)
    def _():
        passed[0].start()
        passed[1].start()
        load_table(wide, table, stage, sems)
        clear(total)
        grads[...] = jnp.zeros_like(grads)
        vectors[...] = jnp.zeros_like(vectors)
        by_sender[...] = jnp.zeros_like(by_sender)

    gather_rows(recv, base, table, rows, parts)
    live = base + lax.broadcasted_iota(jnp.int32, (TILE, 1), 0) < count[0]
    upstream = cotangent[...].astype(jnp.float32) + jnp.where(live, read_rows(rows, 0, TILE, parts), 0.0)
    masked = jnp.where(live, upstream, 0.0)
    normal, scale = row_normal(second[...])
    vectors[2:3, :] += jnp.sum(masked * normal, 0, keepdims=True)
    vectors[3:4, :] += jnp.sum(masked, 0, keepdims=True)
    scaled = masked * gain[...]
    slope = jnp.mean(scaled * normal, -1, keepdims=True)
    grad_second = scale * (scaled - jnp.mean(scaled, -1, keepdims=True) - normal * slope)
    second_low = grad_second.astype(jnp.bfloat16)
    vectors[1:2, :] += jnp.sum(second_low.astype(jnp.float32), 0, keepdims=True)
    pre = first[...]
    logistic = jax.nn.sigmoid(pre)
    act = (pre * logistic).astype(jnp.bfloat16)
    grads[3 * width :] += dot_left(act, second_low)
    grad_first = dot(second_low, w_two_t[...]) * (logistic * (1.0 + pre * (1.0 - logistic)))
    first_low = grad_first.astype(jnp.bfloat16)
    first_wide = first_low.astype(jnp.float32)
    vectors[0:1, :] += jnp.sum(first_wide, 0, keepdims=True)
    grads[:width] += dot_left(edge[...], first_low)
    grads[2 * width : 3 * width] += dot_left(received[...], first_low)
    node = lax.broadcasted_iota(jnp.int32, (nodes.shape[0], TILE), 0)
    chosen = jnp.where(node == send[0], 1.0, 0.0).astype(jnp.bfloat16)
    by_sender[...] += dot(chosen, first_low)
    grad[...] = upstream + dot(first_low, w_one_t[:, :width])
    lay_rows(rows, 0, first_wide)
    add_rows(recv, base, rows, total, parts)

    @pl.when(step == pl.num_programs(0) - 1)
    def _():
        high, rest = split_low(by_sender[...])
        grads[width : 2 * width] = dot_left(nodes[...], high) + dot_left(nodes[...], rest)
        passed[2].start()
        middle = w_one_t[:, width : 2 * width]
        sender_grad[...] = dot(high, middle) + dot(rest, middle)
        store_table(total, sums, stage, sems)
        for copy in passed:
            copy.wait()


def edge_backward(
    count, recv, send, cotangent, edge, received, first, second, wide, node_one, node_two, nodes, w_one_t, w_two_t, gain
):
    edges, width = edge.shape
    steps = edges // TILE
    parts = width // LANES
    per_device = nodes.shape[0]
    hold = pl.BlockSpec(memory_space=pltpu.VMEM)
    scalar = pl.BlockSpec(memory_space=pltpu.SMEM)
    tile = pl.BlockSpec((TILE, width), lambda i: (i, 0))

    across = pl.BlockSpec(memory_space=pl.ANY)
    unit = 64 * lax.axis_size("blk")
    held = 4 * width + node_one.shape[0] + node_two.shape[0]
    padded = -(-held // unit) * unit

    def whole(rows):
        return pl.BlockSpec((rows, width), lambda i: (0, 0))

    return pl.pallas_call(
        backward_kernel,
        grid=(steps,),
        in_specs=[
            scalar, scalar, pl.BlockSpec((1, 1, TILE), lambda i: (i, 0, 0)), tile, tile, tile, tile, tile,
            across, across, across, hold, hold, hold, hold,
        ],
        out_specs=[
            tile, across, across, whole(8), whole(per_device),
        ],
        out_shape=[
            jax.ShapeDtypeStruct((edges, width), jnp.float32),
            jax.ShapeDtypeStruct(wide.shape, jnp.bfloat16),
            jax.ShapeDtypeStruct((padded, width), jnp.float32),
            jax.ShapeDtypeStruct((8, width), jnp.float32),
            jax.ShapeDtypeStruct((per_device, width), jnp.float32),
        ],
        scratch_shapes=[
            pltpu.VMEM((wide.shape[0] * parts, LANES), jnp.float32),
            pltpu.VMEM((wide.shape[0] * parts, LANES), jnp.float32),
            pltpu.VMEM((TILE * parts, LANES), jnp.float32),
            pltpu.VMEM((2, CHUNK, width), jnp.bfloat16),
            pltpu.SemaphoreType.DMA((2,)),
            pltpu.VMEM((per_device, width), jnp.float32),
            pltpu.VMEM((4 * width, width), jnp.float32),
            pltpu.SemaphoreType.DMA((3,)),
        ],
        compiler_params=pltpu.CompilerParams(vmem_limit_bytes=VMEM_BYTES),
        cost_estimate=pl.CostEstimate(
            flops=24 * edges * width * width, bytes_accessed=40 * edges * width, transcendentals=2 * edges * width
        ),
        name="edge_backward",
    )(count, recv, send.reshape(steps, 1, TILE), cotangent, edge, received, first, second, wide, node_one, node_two, nodes, w_one_t, w_two_t, gain)


MESH = pl.DeviceIdType.MESH
PIECES = 4


def places():
    groups = lax.axis_size("blk")
    group, sub = lax.axis_index("blk"), lax.axis_index("sub")
    odd = lax.rem(group, 2)
    return dict(
        group=group,
        sub=sub,
        sibling=sub + 1 - 2 * lax.rem(sub, 2),
        partner=lax.rem(sub + 2, 4),
        beside=group + 1 - 2 * odd,
        onward=lax.rem(group + 2 - 4 * odd + groups, groups),
        source=lax.rem(group - 2 + 4 * odd + groups, groups),
        near=2 - 2 * odd,
        far=2 * odd,
    )


def meet(senders, count):
    barrier = pltpu.get_barrier_semaphore()
    for device in senders:
        pl.semaphore_signal(barrier, inc=1, device_id=device, device_id_type=MESH)
    pl.semaphore_wait(barrier, count)


def spread_kernel(own, table, send_sems, recv_sems, keep_sem):
    at = places()
    group, sub, partner, near, far = at["group"], at["sub"], at["partner"], at["near"], at["far"]
    to_sibling = (group, at["sibling"])
    to_partner = (group, partner)
    to_beside = (at["beside"], sub)
    to_onward = (at["onward"], sub)
    size = own.shape[0] // PIECES
    meet((to_sibling, to_partner, to_beside, (at["source"], sub)), 4)

    def copy(kind, piece, source, slot, device):
        return pltpu.make_async_remote_copy(
            src_ref=source.at[pl.ds(piece * size, size)],
            dst_ref=table.at[slot[0], slot[1], pl.ds(piece * size, size)],
            send_sem=send_sems.at[kind, piece],
            recv_sem=recv_sems.at[kind, piece],
            device_id=device,
            device_id_type=MESH,
        )

    def move(kind, piece):
        if kind == 0:
            return copy(0, piece, own, (1, sub), to_partner)
        if kind == 1:
            return copy(1, piece, own, (far, sub), to_beside)
        if kind == 2:
            return copy(2, piece, own, (1, sub), to_sibling)
        slot, target, device = {
            3: ((1, partner), (far, partner), to_beside),
            4: ((1, partner), (1, partner), to_sibling),
            5: ((near, sub), (far, sub), to_onward),
            6: ((near, sub), (near, sub), to_sibling),
            7: ((near, partner), (far, partner), to_onward),
            8: ((near, partner), (near, partner), to_sibling),
            9: ((far, sub), (far, sub), to_sibling),
            10: ((far, partner), (far, partner), to_sibling),
        }[kind]
        return copy(kind, piece, table.at[slot[0], slot[1]], target, device)

    keep = pltpu.make_async_copy(own, table.at[1, sub], keep_sem)
    for piece in range(PIECES):
        for kind in (0, 1, 2):
            move(kind, piece).start()
    keep.start()

    def relay(arrived, kinds, piece):
        move(arrived, piece).wait_recv()
        for kind in kinds:
            move(kind, piece).start()

    for piece in range(PIECES):
        relay(0, (3, 4), piece)
        relay(1, (5, 6), piece)
    for piece in range(PIECES):
        relay(3, (7, 8), piece)
        relay(5, (9,), piece)
    for piece in range(PIECES):
        relay(7, (10,), piece)
    for kind in range(11):
        for piece in range(PIECES):
            if kind in (2, 4, 6, 8, 9, 10):
                move(kind, piece).wait_recv()
            move(kind, piece).wait_send()
    keep.wait()


def spread(own, collective):
    rows, width = own.shape
    return pl.pallas_call(
        spread_kernel,
        in_specs=[pl.BlockSpec(memory_space=pl.ANY)],
        out_specs=pl.BlockSpec(memory_space=pl.ANY),
        out_shape=jax.ShapeDtypeStruct((3, 4, rows, width), own.dtype),
        scratch_shapes=[
            pltpu.SemaphoreType.DMA((11, PIECES)),
            pltpu.SemaphoreType.DMA((11, PIECES)),
            pltpu.SemaphoreType.DMA,
        ],
        compiler_params=pltpu.CompilerParams(collective_id=collective, has_side_effects=True),
        name="spread_rows",
    )(own).reshape(12 * rows, width)


def collect_kernel(
    sums, out, mine, landed, far_out, far_in, near_out, near_in, pair_out, pair_in,
    keep_sems, give_sems, take_sems, send_sems, recv_sems,
):
    at = places()
    group, sub, partner, near, far = at["group"], at["sub"], at["partner"], at["near"], at["far"]
    sibling = at["sibling"]
    size = out.shape[0] // PIECES
    meet(((group, sibling), (group, partner), (at["beside"], sub), (at["onward"], sub)), 4)
    relations = (far, near, 1)

    def part(ref, piece):
        return ref.at[pl.ds(piece * size, size)]

    def keep(role, side, piece):
        return pltpu.make_async_copy(
            part(sums.at[relations[role], (sub, partner)[side]], piece),
            part(mine.at[role, side], piece),
            keep_sems.at[role, side, piece],
        )

    def give(role, side, piece):
        return pltpu.make_async_remote_copy(
            src_ref=part(sums.at[relations[role], (sibling, lax.rem(sibling + 2, 4))[side]], piece),
            dst_ref=part(landed.at[role, side], piece),
            send_sem=give_sems.at[role, side, piece],
            recv_sem=take_sems.at[role, side, piece],
            device_id=(group, sibling),
            device_id_type=MESH,
        )

    def hop(kind, piece):
        source, target, device = {
            0: (far_out.at[0], far_in.at[0], (at["source"], sub)),
            1: (far_out.at[1], far_in.at[1], (at["source"], sub)),
            2: (near_out.at[0], near_in.at[0], (at["beside"], sub)),
            3: (near_out.at[1], near_in.at[1], (at["beside"], sub)),
            4: (pair_out, pair_in, (group, partner)),
        }[kind]
        return pltpu.make_async_remote_copy(
            src_ref=part(source, piece),
            dst_ref=part(target, piece),
            send_sem=send_sems.at[kind, piece],
            recv_sem=recv_sems.at[kind, piece],
            device_id=device,
            device_id_type=MESH,
        )

    order = [(role, side, piece) for role in range(3) for side in (1, 0) for piece in range(PIECES)]
    for item in order:
        give(*item).start()
        keep(*item).start()

    def local(role, side, piece):
        keep(role, side, piece).wait()
        give(role, side, piece).wait_recv()
        rows = pl.ds(piece * size, size)
        return mine[role, side, rows, :].astype(jnp.float32) + landed[role, side, rows, :].astype(jnp.float32)

    def arrived(kind, ref, piece):
        hop(kind, piece).wait_recv()
        return ref[pl.ds(piece * size, size), :].astype(jnp.float32)

    for side in (1, 0):
        for piece in range(PIECES):
            far_out[side, pl.ds(piece * size, size), :] = local(0, side, piece).astype(jnp.bfloat16)
            hop(side, piece).start()
    for side in (1, 0):
        for piece in range(PIECES):
            value = local(1, side, piece) + arrived(side, far_in.at[side], piece)
            near_out[side, pl.ds(piece * size, size), :] = value.astype(jnp.bfloat16)
            hop(2 + side, piece).start()
    for piece in range(PIECES):
        value = local(2, 1, piece) + arrived(3, near_in.at[1], piece)
        pair_out[pl.ds(piece * size, size), :] = value.astype(jnp.bfloat16)
        hop(4, piece).start()
    for piece in range(PIECES):
        value = local(2, 0, piece) + arrived(2, near_in.at[0], piece) + arrived(4, pair_in, piece)
        out[pl.ds(piece * size, size), :] = value
    for item in order:
        give(*item).wait_send()
    for kind in range(5):
        for piece in range(PIECES):
            hop(kind, piece).wait_send()


def collect(sums, rows, collective):
    width = sums.shape[1]
    low = jnp.bfloat16
    return pl.pallas_call(
        collect_kernel,
        in_specs=[pl.BlockSpec(memory_space=pl.ANY)],
        out_specs=pl.BlockSpec(memory_space=pltpu.VMEM),
        out_shape=jax.ShapeDtypeStruct((rows, width), jnp.float32),
        scratch_shapes=[
            pltpu.VMEM((3, 2, rows, width), low),
            pltpu.VMEM((3, 2, rows, width), low),
            pltpu.VMEM((2, rows, width), low),
            pltpu.VMEM((2, rows, width), low),
            pltpu.VMEM((2, rows, width), low),
            pltpu.VMEM((2, rows, width), low),
            pltpu.VMEM((rows, width), low),
            pltpu.VMEM((rows, width), low),
            pltpu.SemaphoreType.DMA((3, 2, PIECES)),
            pltpu.SemaphoreType.DMA((3, 2, PIECES)),
            pltpu.SemaphoreType.DMA((3, 2, PIECES)),
            pltpu.SemaphoreType.DMA((5, PIECES)),
            pltpu.SemaphoreType.DMA((5, PIECES)),
        ],
        compiler_params=pltpu.CompilerParams(
            collective_id=collective, has_side_effects=True, vmem_limit_bytes=VMEM_BYTES
        ),
        name="collect_sums",
    )(sums.reshape(3, 4, rows, width))


def finish_kernel(
    sums, grads, vectors, out, reduced, reduced_vectors,
    mine, landed, far_out, far_in, near_out, near_in, pair_out, pair_in,
    half, half_in, cross_out, cross_in, side_out, side_in, ring_out, ring_in, held, held_in,
    keep_sems, give_sems, take_sems, send_sems, recv_sems,
    load_sem, load_vector_sem, step_send, step_recv, ring_send, ring_recv, vector_send, vector_recv,
):
    at = places()
    group, sub, partner, near, far = at["group"], at["sub"], at["partner"], at["near"], at["far"]
    sibling = at["sibling"]
    groups = lax.axis_size("blk")
    along = groups // 2
    odd, spot = lax.rem(group, 2), group // 2
    core, chip = lax.rem(sub, 2), sub // 2
    size = out.shape[0] // PIECES
    low = jnp.bfloat16
    wide = jnp.float32
    to_sibling, to_partner, to_beside = (group, sibling), (group, partner), (at["beside"], sub)
    peers = [(2 * lax.rem(spot + k, along) + odd, sub) for k in range(1, along)]
    meet((to_sibling, to_partner, to_beside, *peers), 3 + len(peers))
    relations = (far, near, 1)

    rows = grads.shape[0]
    n_half, n_cross, n_side, n_ring = rows // 2, rows // 4, rows // 8, rows // 8 // along
    at_half = pl.multiple_of(core * n_half, n_half)
    at_cross = pl.multiple_of(at_half + chip * n_cross, n_cross)
    at_side = pl.multiple_of(at_cross + odd * n_side, n_side)
    at_ring = pl.multiple_of(at_side + spot * n_ring, n_ring)

    def remote(source, target, send, recv, device):
        return pltpu.make_async_remote_copy(
            src_ref=source, dst_ref=target, send_sem=send, recv_sem=recv,
            device_id=device, device_id_type=MESH,
        )

    def step(kind):
        if kind == 0:
            other = pl.ds(pl.multiple_of((1 - core) * n_half, n_half), n_half)
            source, target, device = grads.at[other], half_in, to_sibling
        elif kind == 1:
            source, target, device = cross_out, cross_in, to_partner
        elif kind == 2:
            source, target, device = side_out, side_in, to_beside
        else:
            start, count, device = {
                3: (at_side, n_side, to_beside),
                4: (at_cross, n_cross, to_partner),
                5: (at_half, n_half, to_sibling),
            }[kind]
            source = target = reduced.at[pl.ds(start, count)]
        return remote(source, target, step_send.at[kind], step_recv.at[kind], device)

    def ring(kind, k):
        if kind == 0:
            spot_to = lax.rem(spot + k, along)
            source = ring_out.at[pl.ds(pl.multiple_of(spot_to * n_ring, n_ring), n_ring)]
            target = ring_in.at[k - 1]
        else:
            source = target = reduced.at[pl.ds(at_ring, n_ring)]
        return remote(source, target, ring_send.at[kind, k - 1], ring_recv.at[kind, k - 1], peers[k - 1])

    def vector(kind):
        device = (to_sibling, to_partner, to_beside, *peers)[kind]
        return remote(
            held.at[min(kind, 3)], held_in.at[kind], vector_send.at[kind], vector_recv.at[kind], device
        )

    def pieces(count, body):
        block = math.gcd(count, 128)

        def run(i, carry):
            body(pl.multiple_of(i * block, block), block)
            return carry

        lax.fori_loop(0, count // block, run, 0)

    load = pltpu.make_async_copy(grads.at[pl.ds(at_half, n_half)], half, load_sem)
    load_vector = pltpu.make_async_copy(vectors, held.at[0], load_vector_sem)

    def part(ref, piece):
        return ref.at[pl.ds(piece * size, size)]

    def keep(role, side, piece):
        return pltpu.make_async_copy(
            part(sums.at[relations[role], (sub, partner)[side]], piece),
            part(mine.at[role, side], piece),
            keep_sems.at[role, side, piece],
        )

    def give(role, side, piece):
        return remote(
            part(sums.at[relations[role], (sibling, lax.rem(sibling + 2, 4))[side]], piece),
            part(landed.at[role, side], piece),
            give_sems.at[role, side, piece], take_sems.at[role, side, piece], to_sibling,
        )

    def hop(kind, piece):
        source, target, device = {
            0: (far_out.at[0], far_in.at[0], (at["source"], sub)),
            1: (far_out.at[1], far_in.at[1], (at["source"], sub)),
            2: (near_out.at[0], near_in.at[0], to_beside),
            3: (near_out.at[1], near_in.at[1], to_beside),
            4: (pair_out, pair_in, to_partner),
        }[kind]
        return remote(
            part(source, piece), part(target, piece), send_sems.at[kind, piece], recv_sems.at[kind, piece], device
        )

    order = [(role, side, piece) for role in range(3) for side in (1, 0) for piece in range(PIECES)]

    def local(role, side, piece):
        keep(role, side, piece).wait()
        give(role, side, piece).wait_recv()
        span = pl.ds(piece * size, size)
        return mine[role, side, span, :].astype(wide) + landed[role, side, span, :].astype(wide)

    def arrived(kind, ref, piece):
        hop(kind, piece).wait_recv()
        return ref[pl.ds(piece * size, size), :].astype(wide)

    def far_step(side, piece):
        far_out[side, pl.ds(piece * size, size), :] = local(0, side, piece).astype(low)
        hop(side, piece).start()

    def near_step(side, piece):
        value = local(1, side, piece) + arrived(side, far_in.at[side], piece)
        near_out[side, pl.ds(piece * size, size), :] = value.astype(low)
        hop(2 + side, piece).start()

    def pair_step(piece):
        value = local(2, 1, piece) + arrived(3, near_in.at[1], piece)
        pair_out[pl.ds(piece * size, size), :] = value.astype(low)
        hop(4, piece).start()

    def last_step(piece):
        value = local(2, 0, piece) + arrived(2, near_in.at[0], piece) + arrived(4, pair_in, piece)
        out[pl.ds(piece * size, size), :] = value

    def add_half():
        load.wait()
        step(0).wait_recv()
        other = (1 - chip) * n_cross

        def send_part(i, block):
            span = pl.ds(pl.multiple_of(other + i, block), block)
            cross_out[pl.ds(i, block), :] = (half[span, :] + half_in[span, :]).astype(low)

        pieces(n_cross, send_part)
        step(1).start()
        load_vector.wait()
        vector(0).start()

    def add_cross():
        mine_at, other = chip * n_cross, (1 - odd) * n_side
        step(1).wait_recv()

        def send_part(i, block):
            span = pl.ds(pl.multiple_of(other + i, block), block)
            here = pl.ds(pl.multiple_of(mine_at + other + i, block), block)
            side_out[pl.ds(i, block), :] = (half[here, :] + half_in[here, :] + cross_in[span, :].astype(wide)).astype(low)

        pieces(n_side, send_part)
        step(2).start()
        vector(0).wait_recv()
        held[1] = held[0] + held_in[0]
        vector(1).start()

    def add_side():
        from_side = odd * n_side
        step(2).wait_recv()

        def keep_part(i, block):
            span = pl.ds(pl.multiple_of(from_side + i, block), block)
            here = pl.ds(pl.multiple_of(chip * n_cross + from_side + i, block), block)
            value = half[here, :] + half_in[here, :] + cross_in[span, :].astype(wide) + side_in[pl.ds(i, block), :].astype(wide)
            half[here, :] = value
            ring_out[pl.ds(i, block), :] = value.astype(low)

        pieces(n_side, keep_part)
        for k in range(1, along):
            ring(0, k).start()
        vector(1).wait_recv()
        held[2] = held[1] + held_in[1]
        vector(2).start()

    def add_ring():
        here = pl.ds(pl.multiple_of(chip * n_cross + odd * n_side + spot * n_ring, n_ring), n_ring)
        value = half[here, :]
        for k in range(1, along):
            ring(0, k).wait_recv()
            value = value + ring_in[k - 1].astype(wide)
        reduced[pl.ds(at_ring, n_ring), :] = value.astype(low)
        for k in range(1, along):
            ring(1, k).start()
        vector(2).wait_recv()
        held[3] = held[2] + held_in[2]
        for k in range(1, along):
            vector(2 + k).start()

    def share_side():
        for k in range(1, along):
            ring(1, k).wait_recv()
        step(3).start()

    def share_cross():
        step(3).wait_recv()
        step(4).start()
        value = held[3]
        for k in range(1, along):
            vector(2 + k).wait_recv()
            value = value + held_in[2 + k]
        reduced_vectors[...] = value

    def share_half():
        step(4).wait_recv()
        step(5).start()

    for item in order[: 2 * PIECES]:
        give(*item).start()
        keep(*item).start()
    step(0).start()
    load.start()
    load_vector.start()
    for item in order[2 * PIECES :]:
        give(*item).start()
        keep(*item).start()
    for side in (1, 0):
        for piece in range(PIECES):
            far_step(side, piece)
    add_half()
    for piece in range(PIECES):
        near_step(1, piece)
    for piece in range(PIECES // 2):
        near_step(0, piece)
    add_cross()
    for piece in range(PIECES // 2, PIECES):
        near_step(0, piece)
    for piece in range(PIECES):
        pair_step(piece)
    add_side()
    for piece in range(PIECES):
        last_step(piece)
    add_ring()
    share_side()
    share_cross()
    share_half()
    step(5).wait_recv()
    for item in order:
        give(*item).wait_send()
    for kind in range(5):
        for piece in range(PIECES):
            hop(kind, piece).wait_send()
    for kind in range(6):
        step(kind).wait_send()
    for k in range(1, along):
        ring(0, k).wait_send()
        ring(1, k).wait_send()
    for kind in range(2 + along):
        vector(kind).wait_send()


def finish(sums, grads, vectors, rows, collective):
    width = sums.shape[1]
    low, wide = jnp.bfloat16, jnp.float32
    count = grads.shape[0]
    along = lax.axis_size("blk") // 2
    half = pltpu.VMEM((count // 2, width), wide)
    return pl.pallas_call(
        finish_kernel,
        in_specs=[pl.BlockSpec(memory_space=pl.ANY)] * 3,
        out_specs=[pl.BlockSpec(memory_space=pltpu.VMEM)] * 3,
        out_shape=[
            jax.ShapeDtypeStruct((rows, width), wide),
            jax.ShapeDtypeStruct(grads.shape, low),
            jax.ShapeDtypeStruct(vectors.shape, wide),
        ],
        scratch_shapes=[
            pltpu.VMEM((3, 2, rows, width), low),
            pltpu.VMEM((3, 2, rows, width), low),
            pltpu.VMEM((2, rows, width), low),
            pltpu.VMEM((2, rows, width), low),
            pltpu.VMEM((2, rows, width), low),
            pltpu.VMEM((2, rows, width), low),
            pltpu.VMEM((rows, width), low),
            pltpu.VMEM((rows, width), low),
            half,
            half,
            pltpu.VMEM((count // 4, width), low),
            pltpu.VMEM((count // 4, width), low),
            pltpu.VMEM((count // 8, width), low),
            pltpu.VMEM((count // 8, width), low),
            pltpu.VMEM((count // 8, width), low),
            pltpu.VMEM((along - 1, count // 8 // along, width), low),
            pltpu.VMEM((4, *vectors.shape), wide),
            pltpu.VMEM((2 + along, *vectors.shape), wide),
            pltpu.SemaphoreType.DMA((3, 2, PIECES)),
            pltpu.SemaphoreType.DMA((3, 2, PIECES)),
            pltpu.SemaphoreType.DMA((3, 2, PIECES)),
            pltpu.SemaphoreType.DMA((5, PIECES)),
            pltpu.SemaphoreType.DMA((5, PIECES)),
            pltpu.SemaphoreType.DMA,
            pltpu.SemaphoreType.DMA,
            pltpu.SemaphoreType.DMA((6,)),
            pltpu.SemaphoreType.DMA((6,)),
            pltpu.SemaphoreType.DMA((2, along - 1)),
            pltpu.SemaphoreType.DMA((2, along - 1)),
            pltpu.SemaphoreType.DMA((2 + along,)),
            pltpu.SemaphoreType.DMA((2 + along,)),
        ],
        compiler_params=pltpu.CompilerParams(
            collective_id=collective, has_side_effects=True, vmem_limit_bytes=VMEM_BYTES
        ),
        name="finish_sums",
    )(sums.reshape(3, 4, rows, width), grads, vectors)


def shards(
    node_input,
    edge_input,
    senders,
    receivers,
    edge_count,
    edge_w_one,
    edge_b_one,
    edge_w_two,
    edge_b_two,
    edge_gain,
    edge_shift,
    node_w_one,
    node_b_one,
    node_w_two,
    node_b_two,
    node_gain,
    node_shift,
    node_cotangent,
    edge_cotangent,
):
    groups = lax.axis_size("blk")
    sub_count = lax.axis_size("sub")
    block_index = lax.axis_index("blk")
    sub_index = lax.axis_index("sub")
    width = edge_input.shape[1]
    node_low = to_nodes(node_input.astype(jnp.bfloat16)).T
    node_upstream = to_nodes(node_cotangent).T
    per_device = node_low.shape[0]
    per_group = per_device * sub_count
    my_start = (block_index * sub_count + sub_index) * per_device
    send_local = senders - my_start
    relative = (receivers // per_group - block_index + 1 + groups) % groups
    recv_wide = relative * per_group + receivers % per_group
    wide_low = spread(node_low, 0)
    edge_result, first_pre, second_pre, received, wide_sums = edge_forward(
        edge_count, recv_wide, send_local, edge_input, wide_low, node_low,
        edge_w_one, edge_b_one[None], edge_w_two, edge_b_two[None], edge_gain[None], edge_shift[None],
    )
    gathered = collect(wide_sums, per_device, 1)
    joined = jnp.concatenate([node_low, gathered.astype(jnp.bfloat16)], axis=1)
    third_pre = matmul(joined, node_w_one) + node_b_one
    third_act = jax.nn.silu(third_pre).astype(jnp.bfloat16)
    fourth_pre = matmul(third_act, node_w_two) + node_b_two
    node_branch, node_norm_back = jax.vjp(norm_apply, fourth_pre, node_gain, node_shift)
    grad_fourth, grad_node_gain, grad_node_shift = node_norm_back(node_upstream)
    fourth_low = grad_fourth.astype(jnp.bfloat16)
    grad_node_w_two = left_matmul(third_act, fourth_low)
    grad_node_b_two = jnp.sum(fourth_low.astype(jnp.float32), 0)
    grad_third = right_matmul(fourth_low, node_w_two) * silu_slope(third_pre)
    third_low = grad_third.astype(jnp.bfloat16)
    grad_node_w_one = left_matmul(joined, third_low)
    grad_node_b_one = jnp.sum(third_low.astype(jnp.float32), 0)
    grad_joined = right_matmul(third_low, node_w_one)
    grad_nodes = grad_joined[:, :width]
    grad_gathered = grad_joined[:, width:]
    wide_grad = spread(grad_gathered.astype(jnp.bfloat16), 2)
    node_out = node_input + to_channels(node_branch.T)
    edge_grad, receiver_wide, grads, vectors, sender_grad = edge_backward(
        edge_count, recv_wide, send_local, edge_cotangent, edge_input, received, first_pre, second_pre,
        wide_grad, grad_node_w_one, grad_node_w_two, node_low, edge_w_one.T, edge_w_two.T, edge_gain[None],
    )
    node_vectors = jnp.stack([grad_node_b_one, grad_node_b_two, grad_node_gain, grad_node_shift])
    receiver_sums, summed, vectors = finish(
        receiver_wide, grads, jnp.concatenate([vectors[:4], node_vectors]), per_device, 3
    )
    summed = summed.astype(jnp.float32)
    high, rest = split_low(receiver_sums)
    receiver_weight = edge_w_one[2 * width :]
    receiver_grad = right_matmul(high, receiver_weight) + right_matmul(rest, receiver_weight)
    node_total = grad_nodes + sender_grad + receiver_grad
    node_grad = node_cotangent + to_channels(node_total.T)
    return (
        node_out,
        edge_result,
        node_grad,
        edge_grad,
        summed[: 3 * width],
        vectors[0],
        summed[3 * width : 4 * width],
        vectors[1],
        vectors[2],
        vectors[3],
        summed[4 * width : 6 * width],
        vectors[4],
        summed[6 * width : 7 * width],
        vectors[5],
        vectors[6],
        vectors[7],
    )


def solution(mesh):
    placed = (
        P(("blk", "sub"), None),
        P(("blk", "sub"), None),
        P(("blk", "sub")),
        P(("blk", "sub")),
        P(("blk", "sub")),
        P(),
        P(),
        P(),
        P(),
        P(),
        P(),
        P(),
        P(),
        P(),
        P(),
        P(),
        P(),
        P(("blk", "sub"), None),
        P(("blk", "sub"), None),
    )
    return jax.shard_map(
        shards,
        mesh=mesh,
        in_specs=placed,
        out_specs=(
            P(("blk", "sub"), None),
            P(("blk", "sub"), None),
            P(("blk", "sub"), None),
            P(("blk", "sub"), None),
            P(),
            P(),
            P(),
            P(),
            P(),
            P(),
            P(),
            P(),
            P(),
            P(),
            P(),
            P(),
        ),
        check_vma=False,
    )
```

```python
import functools
import math

import jax
import jax.numpy as jnp
from jax import lax
from jax.experimental import pallas as pl
from jax.experimental.pallas import tpu as pltpu
from jax.sharding import PartitionSpec as P

EPSILON = 1e-05


def norm_apply(values, gain, shift):
    average = jnp.mean(values, -1, keepdims=True)
    centred = values - average
    variance = jnp.mean(centred * centred, -1, keepdims=True)
    return centred * lax.rsqrt(variance + EPSILON) * gain + shift


def silu_slope(values):
    logistic = jax.nn.sigmoid(values)
    return logistic * (1.0 + values * (1.0 - logistic))


def matmul(left, right):
    return jnp.dot(left, right, preferred_element_type=jnp.float32)


def left_matmul(left, right):
    return lax.dot_general(
        left, right, (((0,), (0,)), ((), ())), preferred_element_type=jnp.float32
    )


def right_matmul(left, right):
    return lax.dot_general(
        left, right, (((1,), (1,)), ((), ())), preferred_element_type=jnp.float32
    )


def to_nodes(channels):
    return lax.all_to_all(channels, ("blk", "sub"), split_axis=1, concat_axis=0, tiled=True)


def to_channels(values):
    return lax.all_to_all(
        values.astype(jnp.bfloat16), ("blk", "sub"), split_axis=0, concat_axis=1, tiled=True
    ).astype(jnp.float32)


TILE = 512
CHUNK = 512
LANES = 128
VMEM_BYTES = 60 * 2**20


def dot(left, right):
    return jnp.dot(left, right, preferred_element_type=jnp.float32)


def dot_left(left, right):
    return lax.dot_general(
        left, right, (((0,), (0,)), ((), ())), preferred_element_type=jnp.float32
    )


def split_low(values):
    high = values.astype(jnp.bfloat16)
    return high, (values - high.astype(jnp.float32)).astype(jnp.bfloat16)


def lay_rows(target, start, values):
    count, width = values.shape
    parts = width // LANES
    for j in range(parts):
        target[pl.ds(start * parts + j, count, stride=parts), :] = values[:, j * LANES : (j + 1) * LANES]


def read_rows(source, start, count, parts):
    return jnp.concatenate(
        [source[pl.ds(start * parts + j, count, stride=parts), :] for j in range(parts)], axis=1
    )


def load_table(wide, table, stage, sems):
    steps = wide.shape[0] // CHUNK

    def fetch(i, slot):
        return pltpu.make_async_copy(wide.at[pl.ds(i * CHUNK, CHUNK)], stage.at[slot], sems.at[slot])

    fetch(0, 0).start()

    def body(i, carry):
        slot = lax.rem(i, 2)

        @pl.when(i + 1 < steps)
        def _():
            fetch(i + 1, 1 - slot).start()

        fetch(i, slot).wait()

        def piece(k, carry):
            values = stage[slot, pl.ds(k * 64, 64), :].astype(jnp.float32)
            lay_rows(table, i * CHUNK + k * 64, values)
            return carry

        return lax.fori_loop(0, CHUNK // 64, piece, carry)

    lax.fori_loop(0, steps, body, 0)


def store_table(table, wide, stage, sems):
    steps = wide.shape[0] // CHUNK
    parts = wide.shape[1] // LANES

    def send(i, slot):
        return pltpu.make_async_copy(stage.at[slot], wide.at[pl.ds(i * CHUNK, CHUNK)], sems.at[slot])

    def body(i, carry):
        slot = lax.rem(i, 2)

        @pl.when(i >= 2)
        def _():
            send(i - 2, slot).wait()

        def piece(k, carry):
            values = read_rows(table, i * CHUNK + k * 64, 64, parts)
            stage[slot, pl.ds(k * 64, 64), :] = values.astype(jnp.bfloat16)
            return carry

        lax.fori_loop(0, CHUNK // 64, piece, 0)
        send(i, slot).start()
        return carry

    lax.fori_loop(0, steps, body, 0)
    for i in (steps - 2, steps - 1):
        send(i, i % 2).wait()


def clear(table):
    def body(i, carry):
        table[pl.ds(i * 512, 512), :] = jnp.zeros((512, LANES), table.dtype)
        return carry

    lax.fori_loop(0, table.shape[0] // 512, body, 0)


def gather_rows(index, base, table, rows, parts):
    count = rows.shape[0] // parts

    def body(i, carry):
        for u in range(16):
            slot = i * 16 + u
            place = index[base + slot]
            rows[pl.ds(pl.multiple_of(slot * parts, parts), parts), :] = table[
                pl.ds(pl.multiple_of(place * parts, parts), parts), :
            ]
        return carry

    lax.fori_loop(0, count // 16, body, 0)


def add_rows(index, base, rows, table, parts):
    count = rows.shape[0] // parts

    def body(i, carry):
        for u in range(0, 16, 2):
            slot = i * 16 + u
            one, two = index[base + slot], index[base + slot + 1]
            at_one = pl.ds(pl.multiple_of(one * parts, parts), parts)
            at_two = pl.ds(pl.multiple_of(two * parts, parts), parts)
            held_one, held_two = table[at_one, :], table[at_two, :]
            sum_one = held_one + rows[pl.ds(pl.multiple_of(slot * parts, parts), parts), :]
            held_two = jnp.where(one == two, sum_one, held_two)
            sum_two = held_two + rows[pl.ds(pl.multiple_of((slot + 1) * parts, parts), parts), :]
            table[at_one, :] = sum_one
            table[at_two, :] = sum_two
        return carry

    lax.fori_loop(0, count // 16, body, 0)


def row_normal(values):
    average = jnp.mean(values, -1, keepdims=True)
    centred = values - average
    variance = jnp.mean(centred * centred, -1, keepdims=True)
    scale = lax.rsqrt(variance + EPSILON)
    return centred * scale, scale


def forward_kernel(
    count, recv, send, edge, wide, nodes, w_one, b_one, w_two, b_two, gain, shift,
    result, first, second, received, sums,
    table, total, rows, stage, sems,
):
    step = pl.program_id(0)
    base = step * TILE
    width = nodes.shape[1]
    parts = width // LANES

    @pl.when(step == 0)
    def _():
        load_table(wide, table, stage, sems)
        clear(total)

    gather_rows(recv, base, table, rows, parts)
    from_recv = read_rows(rows, 0, TILE, parts).astype(jnp.bfloat16)
    received[...] = from_recv
    column = jnp.broadcast_to(send[0], (LANES, TILE)).T
    lane = lax.broadcasted_iota(jnp.int32, (TILE, LANES), 1)
    chosen = jnp.concatenate(
        [
            jnp.where(column == lane + j * LANES, 1.0, 0.0).astype(jnp.bfloat16)
            for j in range(nodes.shape[0] // LANES)
        ],
        axis=1,
    )
    from_send = dot(chosen, nodes[...]).astype(jnp.bfloat16)
    pre = (
        dot(edge[...], w_one[:width])
        + dot(from_send, w_one[width : 2 * width])
        + dot(from_recv, w_one[2 * width :])
        + b_one[...]
    )
    first[...] = pre
    act = (pre * jax.nn.sigmoid(pre)).astype(jnp.bfloat16)
    post = dot(act, w_two[...]) + b_two[...]
    second[...] = post
    normal, _ = row_normal(post)
    branch = normal * gain[...] + shift[...]
    live = base + lax.broadcasted_iota(jnp.int32, (TILE, 1), 0) < count[0]
    outcome = edge[...].astype(jnp.float32) + jnp.where(live, branch, 0.0)
    result[...] = outcome
    lay_rows(rows, 0, jnp.where(live, outcome, 0.0))
    add_rows(recv, base, rows, total, parts)

    @pl.when(step == pl.num_programs(0) - 1)
    def _():
        store_table(total, sums, stage, sems)


def edge_forward(count, recv, send, edge, wide, nodes, w_one, b_one, w_two, b_two, gain, shift):
    edges, width = edge.shape
    steps = edges // TILE
    parts = width // LANES
    hold = pl.BlockSpec(memory_space=pltpu.VMEM)
    scalar = pl.BlockSpec(memory_space=pltpu.SMEM)
    tile = pl.BlockSpec((TILE, width), lambda i: (i, 0))
    return pl.pallas_call(
        forward_kernel,
        grid=(steps,),
        in_specs=[
            scalar, scalar, pl.BlockSpec((1, 1, TILE), lambda i: (i, 0, 0)), tile,
            pl.BlockSpec(memory_space=pl.ANY), hold, hold, hold, hold, hold, hold, hold,
        ],
        out_specs=[tile, tile, tile, tile, pl.BlockSpec(memory_space=pl.ANY)],
        out_shape=[
            jax.ShapeDtypeStruct((edges, width), jnp.float32),
            jax.ShapeDtypeStruct((edges, width), jnp.float32),
            jax.ShapeDtypeStruct((edges, width), jnp.float32),
            jax.ShapeDtypeStruct((edges, width), jnp.bfloat16),
            jax.ShapeDtypeStruct(wide.shape, jnp.bfloat16),
        ],
        scratch_shapes=[
            pltpu.VMEM((wide.shape[0] * parts, LANES), jnp.float32),
            pltpu.VMEM((wide.shape[0] * parts, LANES), jnp.float32),
            pltpu.VMEM((TILE * parts, LANES), jnp.float32),
            pltpu.VMEM((2, CHUNK, width), jnp.bfloat16),
            pltpu.SemaphoreType.DMA((2,)),
        ],
        compiler_params=pltpu.CompilerParams(vmem_limit_bytes=VMEM_BYTES),
        cost_estimate=pl.CostEstimate(
            flops=20 * edges * width * width, bytes_accessed=40 * edges * width, transcendentals=2 * edges * width
        ),
        name="edge_forward",
    )(count, recv, send.reshape(steps, 1, TILE), edge, wide, nodes, w_one, b_one, w_two, b_two, gain, shift)


def backward_kernel(
    count, recv, send, cotangent, edge, received, first, second, wide, node_one, node_two, node_part, nodes, w_one_t, w_two_t, gain,
    grad, sums, all_grads, vectors, sender_grad,
    table, total, rows, stage, sems, by_sender, grads, pass_sems,
):
    step = pl.program_id(0)
    base = step * TILE
    width = nodes.shape[1]
    parts = width // LANES

    first_node = node_one.shape[0]
    passed = (
        pltpu.make_async_copy(node_one, grads.at[pl.ds(4 * width, first_node)], pass_sems.at[0]),
        pltpu.make_async_copy(node_two, grads.at[pl.ds(4 * width + first_node, node_two.shape[0])], pass_sems.at[1]),
        pltpu.make_async_copy(grads, all_grads, pass_sems.at[2]),
    )

    @pl.when(step == 0)
    def _():
        passed[0].start()
        passed[1].start()
        load_table(wide, table, stage, sems)
        clear(total)
        grads[: 4 * width] = jnp.zeros((4 * width, width), grads.dtype)
        vectors[...] = jnp.zeros_like(vectors)
        by_sender[...] = jnp.zeros_like(by_sender)

    gather_rows(recv, base, table, rows, parts)
    live = base + lax.broadcasted_iota(jnp.int32, (TILE, 1), 0) < count[0]
    upstream = cotangent[...].astype(jnp.float32) + jnp.where(live, read_rows(rows, 0, TILE, parts), 0.0)
    masked = jnp.where(live, upstream, 0.0)
    normal, scale = row_normal(second[...])
    vectors[2:3, :] += jnp.sum(masked * normal, 0, keepdims=True)
    vectors[3:4, :] += jnp.sum(masked, 0, keepdims=True)
    scaled = masked * gain[...]
    slope = jnp.mean(scaled * normal, -1, keepdims=True)
    grad_second = scale * (scaled - jnp.mean(scaled, -1, keepdims=True) - normal * slope)
    second_low = grad_second.astype(jnp.bfloat16)
    vectors[1:2, :] += jnp.sum(second_low.astype(jnp.float32), 0, keepdims=True)
    pre = first[...]
    logistic = jax.nn.sigmoid(pre)
    act = (pre * logistic).astype(jnp.bfloat16)
    grads[3 * width : 4 * width] += dot_left(act, second_low)
    grad_first = dot(second_low, w_two_t[...]) * (logistic * (1.0 + pre * (1.0 - logistic)))
    first_low = grad_first.astype(jnp.bfloat16)
    first_wide = first_low.astype(jnp.float32)
    vectors[0:1, :] += jnp.sum(first_wide, 0, keepdims=True)
    grads[:width] += dot_left(edge[...], first_low)
    grads[2 * width : 3 * width] += dot_left(received[...], first_low)
    node = lax.broadcasted_iota(jnp.int32, (nodes.shape[0], TILE), 0)
    chosen = jnp.where(node == send[0], 1.0, 0.0).astype(jnp.bfloat16)
    by_sender[...] += dot(chosen, first_low)
    grad[...] = upstream + dot(first_low, w_one_t[:, :width])
    lay_rows(rows, 0, first_wide)
    add_rows(recv, base, rows, total, parts)

    @pl.when(step == pl.num_programs(0) - 1)
    def _():
        high, rest = split_low(by_sender[...])
        grads[width : 2 * width] = dot_left(nodes[...], high) + dot_left(nodes[...], rest)
        passed[0].wait()
        passed[1].wait()
        passed[2].start()
        middle = w_one_t[:, width : 2 * width]
        sender_grad[...] = node_part[...] + dot(high, middle) + dot(rest, middle)
        store_table(total, sums, stage, sems)
        passed[2].wait()


def edge_backward(
    count, recv, send, cotangent, edge, received, first, second, wide, node_one, node_two, node_part, nodes,
    w_one_t, w_two_t, gain,
):
    edges, width = edge.shape
    steps = edges // TILE
    parts = width // LANES
    per_device = nodes.shape[0]
    hold = pl.BlockSpec(memory_space=pltpu.VMEM)
    scalar = pl.BlockSpec(memory_space=pltpu.SMEM)
    tile = pl.BlockSpec((TILE, width), lambda i: (i, 0))

    across = pl.BlockSpec(memory_space=pl.ANY)
    unit = 64 * lax.axis_size("blk")
    held = 4 * width + node_one.shape[0] + node_two.shape[0]
    padded = -(-held // unit) * unit

    def whole(rows):
        return pl.BlockSpec((rows, width), lambda i: (0, 0))

    return pl.pallas_call(
        backward_kernel,
        grid=(steps,),
        in_specs=[
            scalar, scalar, pl.BlockSpec((1, 1, TILE), lambda i: (i, 0, 0)), tile, tile, tile, tile, tile,
            across, across, across, hold, hold, hold, hold, hold,
        ],
        out_specs=[
            tile, across, across, whole(8), whole(per_device),
        ],
        out_shape=[
            jax.ShapeDtypeStruct((edges, width), jnp.float32),
            jax.ShapeDtypeStruct(wide.shape, jnp.bfloat16),
            jax.ShapeDtypeStruct((padded, width), jnp.float32),
            jax.ShapeDtypeStruct((8, width), jnp.float32),
            jax.ShapeDtypeStruct((per_device, width), jnp.float32),
        ],
        scratch_shapes=[
            pltpu.VMEM((wide.shape[0] * parts, LANES), jnp.float32),
            pltpu.VMEM((wide.shape[0] * parts, LANES), jnp.float32),
            pltpu.VMEM((TILE * parts, LANES), jnp.float32),
            pltpu.VMEM((2, CHUNK, width), jnp.bfloat16),
            pltpu.SemaphoreType.DMA((2,)),
            pltpu.VMEM((per_device, width), jnp.float32),
            pltpu.VMEM((padded, width), jnp.float32),
            pltpu.SemaphoreType.DMA((3,)),
        ],
        compiler_params=pltpu.CompilerParams(vmem_limit_bytes=VMEM_BYTES),
        cost_estimate=pl.CostEstimate(
            flops=24 * edges * width * width, bytes_accessed=40 * edges * width, transcendentals=2 * edges * width
        ),
        name="edge_backward",
    )(
        count, recv, send.reshape(steps, 1, TILE), cotangent, edge, received, first, second, wide, node_one, node_two,
        node_part, nodes, w_one_t, w_two_t, gain,
    )


MESH = pl.DeviceIdType.MESH
PIECES = 4
LOW = jnp.bfloat16
WIDE = jnp.float32


def places():
    groups = lax.axis_size("blk")
    group, sub = lax.axis_index("blk"), lax.axis_index("sub")
    odd = lax.rem(group, 2)
    along = groups // 2
    spot = group // 2
    beside = group + 1 - 2 * odd
    return dict(
        group=group,
        sub=sub,
        core=lax.rem(sub, 2),
        chip=sub // 2,
        odd=odd,
        spot=spot,
        along=along,
        sibling=sub + 1 - 2 * lax.rem(sub, 2),
        partner=lax.rem(sub + 2, 4),
        to_sibling=(group, sub + 1 - 2 * lax.rem(sub, 2)),
        to_partner=(group, lax.rem(sub + 2, 4)),
        to_beside=(beside, sub),
        to_onward=(lax.rem(group + 2 - 4 * odd + groups, groups), sub),
        to_source=(lax.rem(group - 2 + 4 * odd + groups, groups), sub),
        peers=[(2 * lax.rem(spot + k, along) + odd, sub) for k in range(1, along)],
        near=2 - 2 * odd,
        far=2 * odd,
    )


def meet(senders):
    barrier = pltpu.get_barrier_semaphore()
    for device in senders:
        pl.semaphore_signal(barrier, inc=1, device_id=device, device_id_type=MESH)
    pl.semaphore_wait(barrier, len(senders))


def meet_all():
    barrier = pltpu.get_barrier_semaphore()
    subs = lax.axis_size("sub")
    devices = lax.axis_size("blk") * subs
    here = lax.axis_index("blk") * subs + lax.axis_index("sub")

    def greet(k, carry):
        there = lax.rem(here + k, devices)
        pl.semaphore_signal(barrier, inc=1, device_id=(there // subs, lax.rem(there, subs)), device_id_type=MESH)
        return carry

    lax.fori_loop(1, devices, greet, 0)
    pl.semaphore_wait(barrier, devices - 1)


def remote(source, target, send, recv, device):
    return pltpu.make_async_remote_copy(
        src_ref=source, dst_ref=target, send_sem=send, recv_sem=recv, device_id=device, device_id_type=MESH
    )


def in_pieces(count, body):
    block = math.gcd(count, 128)

    def run(i, carry):
        body(pl.multiple_of(i * block, block), block)
        return carry

    lax.fori_loop(0, count // block, run, 0)


def reducer_scratch(rows, width, along):
    return [
        pltpu.VMEM((rows // 2, width), WIDE),
        pltpu.VMEM((rows // 2, width), WIDE),
        pltpu.VMEM((rows // 4, width), LOW),
        pltpu.VMEM((rows // 4, width), LOW),
        pltpu.VMEM((rows // 8, width), LOW),
        pltpu.VMEM((rows // 8, width), LOW),
        pltpu.VMEM((rows // 8, width), LOW),
        pltpu.VMEM((along - 1, rows // 8 // along, width), LOW),
        pltpu.SemaphoreType.DMA,
        pltpu.SemaphoreType.DMA((6,)),
        pltpu.SemaphoreType.DMA((6,)),
        pltpu.SemaphoreType.DMA((2, along - 1)),
        pltpu.SemaphoreType.DMA((2, along - 1)),
    ]


def reducer(at, grads, reduced, first, rows, swap, refs):
    (
        half, half_in, cross_out, cross_in, side_out, side_in, ring_out, ring_in,
        load_sem, step_send, step_recv, ring_send, ring_recv,
    ) = refs
    along, peers = at["along"], at["peers"]
    turns = [(at["chip"], at["to_partner"]), (at["odd"], at["to_beside"])]
    (bit_one, device_one), (bit_two, device_two) = turns[::-1] if swap else turns
    core, spot = at["core"], at["spot"]
    n_half, n_cross, n_side, n_ring = rows // 2, rows // 4, rows // 8, rows // 8 // along
    at_half = first + core * n_half
    at_cross = at_half + bit_one * n_cross
    at_side = at_cross + bit_two * n_side
    at_ring = at_side + spot * n_ring

    def span(start, count):
        return pl.ds(pl.multiple_of(start, 16), count)

    def step(kind):
        if kind == 0:
            source, target, device = grads.at[span(first + (1 - core) * n_half, n_half)], half_in, at["to_sibling"]
        elif kind == 1:
            source, target, device = cross_out, cross_in, device_one
        elif kind == 2:
            source, target, device = side_out, side_in, device_two
        else:
            start, count, device = {
                3: (at_side, n_side, device_two),
                4: (at_cross, n_cross, device_one),
                5: (at_half, n_half, at["to_sibling"]),
            }[kind]
            source = target = reduced.at[span(start, count)]
        return remote(source, target, step_send.at[kind], step_recv.at[kind], device)

    def ring(kind, k):
        if kind == 0:
            source = ring_out.at[span(lax.rem(spot + k, along) * n_ring, n_ring)]
            target = ring_in.at[k - 1]
        else:
            source = target = reduced.at[span(at_ring, n_ring)]
        return remote(source, target, ring_send.at[kind, k - 1], ring_recv.at[kind, k - 1], peers[k - 1])

    load = pltpu.make_async_copy(grads.at[span(at_half, n_half)], half, load_sem)

    def start():
        step(0).start()
        load.start()

    def add_half():
        load.wait()
        step(0).wait_recv()
        other = (1 - bit_one) * n_cross

        def part(i, block):
            here = pl.ds(pl.multiple_of(other + i, block), block)
            cross_out[pl.ds(i, block), :] = (half[here, :] + half_in[here, :]).astype(LOW)

        in_pieces(n_cross, part)
        step(1).start()

    def add_cross():
        mine, other = bit_one * n_cross, (1 - bit_two) * n_side
        step(1).wait_recv()

        def part(i, block):
            there = pl.ds(pl.multiple_of(other + i, block), block)
            here = pl.ds(pl.multiple_of(mine + other + i, block), block)
            side_out[pl.ds(i, block), :] = (half[here, :] + half_in[here, :] + cross_in[there, :].astype(WIDE)).astype(LOW)

        in_pieces(n_side, part)
        step(2).start()

    def add_side():
        mine, kept = bit_one * n_cross, bit_two * n_side
        step(2).wait_recv()

        def part(i, block):
            there = pl.ds(pl.multiple_of(kept + i, block), block)
            here = pl.ds(pl.multiple_of(mine + kept + i, block), block)
            flat = pl.ds(i, block)
            value = half[here, :] + half_in[here, :] + cross_in[there, :].astype(WIDE) + side_in[flat, :].astype(WIDE)
            half[here, :] = value
            ring_out[flat, :] = value.astype(LOW)

        in_pieces(n_side, part)
        for k in range(1, along):
            ring(0, k).start()

    def add_ring():
        value = half[span(bit_one * n_cross + bit_two * n_side + spot * n_ring, n_ring), :]
        for k in range(1, along):
            ring(0, k).wait_recv()
            value = value + ring_in[k - 1].astype(WIDE)
        reduced[span(at_ring, n_ring), :] = value.astype(LOW)
        for k in range(1, along):
            ring(1, k).start()

    def share_side():
        for k in range(1, along):
            ring(1, k).wait_recv()
        step(3).start()

    def share_cross():
        step(3).wait_recv()
        step(4).start()

    def share_half():
        step(4).wait_recv()
        step(5).start()

    def last():
        step(5).wait_recv()

    def drain():
        for kind in range(6):
            step(kind).wait_send()
        for k in range(1, along):
            ring(0, k).wait_send()
            ring(1, k).wait_send()

    return [start, add_half, add_cross, add_side, add_ring, share_side, share_cross, share_half, last, drain]


def vector_scratch(shape, along):
    return [
        pltpu.VMEM((4, *shape), WIDE),
        pltpu.VMEM((2 + along, *shape), WIDE),
        pltpu.SemaphoreType.DMA((2 + along,)),
        pltpu.SemaphoreType.DMA((2 + along,)),
    ]


def vector_reducer(at, vectors, reduced, refs):
    held, held_in, send_sems, recv_sems = refs
    along = at["along"]
    devices = (at["to_sibling"], at["to_partner"], at["to_beside"], *at["peers"])

    def move(kind):
        return remote(held.at[min(kind, 3)], held_in.at[kind], send_sems.at[kind], recv_sems.at[kind], devices[kind])

    def start():
        held[0] = vectors[...]
        move(0).start()

    def turn(kind):
        def run():
            move(kind).wait_recv()
            held[kind + 1] = held[kind] + held_in[kind]
            for k in range(kind + 1, kind + 2 if kind < 2 else 2 + along):
                move(k).start()

        return run

    def last():
        value = held[3]
        for k in range(3, 2 + along):
            move(k).wait_recv()
            value = value + held_in[k]
        reduced[...] = value
        for k in range(2 + along):
            move(k).wait_send()

    return [start, turn(0), turn(1), turn(2), last]


def both(streams):
    return [lambda steps=steps: [step() for step in steps] for steps in zip(*streams)]


def spread_moves(at, own, table, keep_sem, send_sems, recv_sems):
    sub, partner, near, far = at["sub"], at["partner"], at["near"], at["far"]
    to_sibling, to_partner, to_beside, to_onward = (
        at["to_sibling"], at["to_partner"], at["to_beside"], at["to_onward"]
    )
    size = own.shape[0] // PIECES

    def move(kind, piece):
        source, slot, device = {
            0: (None, (1, sub), to_partner),
            1: (None, (far, sub), to_beside),
            2: (None, (1, sub), to_sibling),
            3: ((1, partner), (far, partner), to_beside),
            4: ((1, partner), (1, partner), to_sibling),
            5: ((near, sub), (far, sub), to_onward),
            6: ((near, sub), (near, sub), to_sibling),
            7: ((near, partner), (far, partner), to_onward),
            8: ((near, partner), (near, partner), to_sibling),
            9: ((far, sub), (far, sub), to_sibling),
            10: ((far, partner), (far, partner), to_sibling),
        }[kind]
        source = own if source is None else table.at[source[0], source[1]]
        rows = pl.ds(piece * size, size)
        return remote(
            source.at[rows], table.at[slot[0], slot[1], rows],
            send_sems.at[kind, piece], recv_sems.at[kind, piece], device,
        )

    keep = pltpu.make_async_copy(own, table.at[1, sub], keep_sem)

    def start():
        for piece in range(PIECES):
            for kind in (0, 1, 2):
                move(kind, piece).start()
        keep.start()

    def relay(arrived, kinds, piece):
        move(arrived, piece).wait_recv()
        for kind in kinds:
            move(kind, piece).start()

    def one(piece):
        relay(0, (3, 4), piece)
        relay(1, (5, 6), piece)

    def two(piece):
        relay(3, (7, 8), piece)
        relay(5, (9,), piece)

    def three(piece):
        relay(7, (10,), piece)

    def drain():
        for kind in range(11):
            for piece in range(PIECES):
                if kind in (2, 4, 6, 8, 9, 10):
                    move(kind, piece).wait_recv()
                move(kind, piece).wait_send()
        keep.wait()

    return start, one, two, three, drain


def spread_scratch():
    return [
        pltpu.SemaphoreType.DMA,
        pltpu.SemaphoreType.DMA((11, PIECES)),
        pltpu.SemaphoreType.DMA((11, PIECES)),
    ]


def spread_kernel(own, table, *refs):
    at = places()
    meet((at["to_sibling"], at["to_partner"], at["to_beside"], at["to_source"]))
    start, one, two, three, drain = spread_moves(at, own, table, *refs)
    start()
    for stage in (one, two, three):
        for piece in range(PIECES):
            stage(piece)
    drain()


def spread(own, collective):
    rows, width = own.shape
    return pl.pallas_call(
        spread_kernel,
        in_specs=[pl.BlockSpec(memory_space=pltpu.VMEM)],
        out_specs=pl.BlockSpec(memory_space=pl.ANY),
        out_shape=jax.ShapeDtypeStruct((3, 4, rows, width), own.dtype),
        scratch_shapes=spread_scratch(),
        compiler_params=pltpu.CompilerParams(collective_id=collective, has_side_effects=True),
        name="spread_rows",
    )(own).reshape(12 * rows, width)


def collect_scratch(rows, width):
    return [
        pltpu.VMEM((3, 2, rows, width), LOW),
        pltpu.VMEM((3, 2, rows, width), LOW),
        pltpu.VMEM((2, rows, width), LOW),
        pltpu.VMEM((2, rows, width), LOW),
        pltpu.VMEM((2, rows, width), LOW),
        pltpu.VMEM((2, rows, width), LOW),
        pltpu.VMEM((rows, width), LOW),
        pltpu.VMEM((rows, width), LOW),
        pltpu.SemaphoreType.DMA((3, 2, PIECES)),
        pltpu.SemaphoreType.DMA((3, 2, PIECES)),
        pltpu.SemaphoreType.DMA((3, 2, PIECES)),
        pltpu.SemaphoreType.DMA((5, PIECES)),
        pltpu.SemaphoreType.DMA((5, PIECES)),
    ]


def collect_moves(at, sums, out, refs):
    (
        mine, landed, far_out, far_in, near_out, near_in, pair_out, pair_in,
        keep_sems, give_sems, take_sems, send_sems, recv_sems,
    ) = refs
    sub, partner, sibling = at["sub"], at["partner"], at["sibling"]
    relations = (at["far"], at["near"], 1)
    size = out.shape[0] // PIECES

    def part(ref, piece):
        return ref.at[pl.ds(piece * size, size)]

    def keep(role, side, piece):
        return pltpu.make_async_copy(
            part(sums.at[relations[role], (sub, partner)[side]], piece),
            part(mine.at[role, side], piece),
            keep_sems.at[role, side, piece],
        )

    def give(role, side, piece):
        return remote(
            part(sums.at[relations[role], (sibling, lax.rem(sibling + 2, 4))[side]], piece),
            part(landed.at[role, side], piece),
            give_sems.at[role, side, piece], take_sems.at[role, side, piece], at["to_sibling"],
        )

    def hop(kind, piece):
        source, target, device = {
            0: (far_out.at[0], far_in.at[0], at["to_source"]),
            1: (far_out.at[1], far_in.at[1], at["to_source"]),
            2: (near_out.at[0], near_in.at[0], at["to_beside"]),
            3: (near_out.at[1], near_in.at[1], at["to_beside"]),
            4: (pair_out, pair_in, at["to_partner"]),
        }[kind]
        return remote(
            part(source, piece), part(target, piece), send_sems.at[kind, piece], recv_sems.at[kind, piece], device
        )

    order = [(role, side, piece) for role in range(3) for side in (1, 0) for piece in range(PIECES)]

    def local(role, side, piece):
        keep(role, side, piece).wait()
        give(role, side, piece).wait_recv()
        rows = pl.ds(piece * size, size)
        return mine[role, side, rows, :].astype(WIDE) + landed[role, side, rows, :].astype(WIDE)

    def arrived(kind, ref, piece):
        hop(kind, piece).wait_recv()
        return ref[pl.ds(piece * size, size), :].astype(WIDE)

    def start(role):
        for item in order:
            if item[0] == role:
                give(*item).start()
                keep(*item).start()

    def far_step(side, piece):
        far_out[side, pl.ds(piece * size, size), :] = local(0, side, piece).astype(LOW)
        hop(side, piece).start()

    def near_step(side, piece):
        value = local(1, side, piece) + arrived(side, far_in.at[side], piece)
        near_out[side, pl.ds(piece * size, size), :] = value.astype(LOW)
        hop(2 + side, piece).start()

    def pair_step(piece):
        value = local(2, 1, piece) + arrived(3, near_in.at[1], piece)
        pair_out[pl.ds(piece * size, size), :] = value.astype(LOW)
        hop(4, piece).start()

    def last_step(piece):
        value = local(2, 0, piece) + arrived(2, near_in.at[0], piece) + arrived(4, pair_in, piece)
        out[pl.ds(piece * size, size), :] = value

    def drain():
        for item in order:
            give(*item).wait_send()
        for kind in range(5):
            for piece in range(PIECES):
                hop(kind, piece).wait_send()

    return start, far_step, near_step, pair_step, last_step, drain


def collect_kernel(sums, out, *refs):
    at = places()
    meet((at["to_sibling"], at["to_partner"], at["to_beside"], at["to_onward"]))
    start, far_step, near_step, pair_step, last_step, drain = collect_moves(at, sums, out, refs)
    for role in range(3):
        start(role)
    for step in (far_step, near_step):
        for side in (1, 0):
            for piece in range(PIECES):
                step(side, piece)
    for piece in range(PIECES):
        pair_step(piece)
    for piece in range(PIECES):
        last_step(piece)
    drain()


def collect(sums, rows, collective):
    width = sums.shape[1]
    return pl.pallas_call(
        collect_kernel,
        in_specs=[pl.BlockSpec(memory_space=pl.ANY)],
        out_specs=pl.BlockSpec(memory_space=pltpu.VMEM),
        out_shape=jax.ShapeDtypeStruct((rows, width), WIDE),
        scratch_shapes=collect_scratch(rows, width),
        compiler_params=pltpu.CompilerParams(
            collective_id=collective, has_side_effects=True, vmem_limit_bytes=VMEM_BYTES
        ),
        name="collect_sums",
    )(sums.reshape(3, 4, rows, width))


def exchange_scratch(rows, width, devices):
    slab = width // devices * (rows // LANES)
    return [
        pltpu.VMEM((devices * slab, LANES), WIDE),
        pltpu.VMEM((devices * slab, LANES), LOW),
        pltpu.VMEM((devices, slab, LANES), LOW),
        pltpu.VMEM((slab, LANES), WIDE),
        pltpu.SemaphoreType.DMA((devices - 1,)),
        pltpu.SemaphoreType.DMA((devices - 1,)),
    ]


def exchange_moves(residual, out, refs):
    flat, packed, landed, opened, send_sems, recv_sems = refs
    subs = lax.axis_size("sub")
    devices = lax.axis_size("blk") * subs
    here = lax.axis_index("blk") * subs + lax.axis_index("sub")
    slab = landed.shape[1]
    channels = out.shape[0]
    parts = slab // channels
    nodes = parts * LANES

    def move(k):
        there = lax.rem(here + k, devices)
        return remote(
            packed.at[pl.ds(pl.multiple_of(there * slab, slab), slab)], landed.at[here],
            send_sems.at[k - 1], recv_sems.at[k - 1], (there // subs, lax.rem(there, subs)),
        )

    def start(values):
        lay_rows(flat, 0, values.T)

        def cast(i, block):
            packed[pl.ds(i, block), :] = flat[pl.ds(i, block), :].astype(LOW)

        in_pieces(flat.shape[0], cast)

        def send(k, carry):
            move(k).start()
            return carry

        lax.fori_loop(1, devices, send, 0)

    def open_slab(source, device):
        opened[...] = source.astype(WIDE)
        for j in range(parts):
            columns = pl.ds(pl.multiple_of(device * nodes + j * LANES, LANES), LANES)
            out[:, columns] = residual[:, columns] + opened[pl.ds(j, channels, stride=parts), :]

    def last():
        open_slab(packed[pl.ds(pl.multiple_of(here * slab, slab), slab), :], here)

        def take(k, carry):
            move(k).wait_recv()
            device = lax.rem(here - k + devices, devices)
            open_slab(landed[device], device)
            return carry

        lax.fori_loop(1, devices, take, 0)

        def sent(k, carry):
            move(k).wait_send()
            return carry

        lax.fori_loop(1, devices, sent, 0)

    return start, last


def finish_kernel(
    cut, sums, grads, vectors, node_part, weight, residual, node_grad, reduced, reduced_vectors, total, *refs
):
    at = places()
    meet_all()
    sizes = len(reducer_scratch(64, 128, 2))
    count = len(collect_scratch(64, 128))
    start, far_step, near_step, pair_step, last_step, drain = collect_moves(at, sums, total, refs[:count])
    refs = refs[count:]
    steps = both([
        reducer(at, grads, reduced, 0, cut, False, refs[:sizes]),
        reducer(at, grads, reduced, cut, grads.shape[0] - cut, True, refs[sizes : 2 * sizes]),
    ])
    refs = refs[2 * sizes :]
    vector_steps = vector_reducer(at, vectors, reduced_vectors, refs[:4])
    exchange, receive = exchange_moves(residual, node_grad, refs[4:])
    start(0)
    steps[0]()
    vector_steps[0]()
    start(1)
    start(2)
    for side in (1, 0):
        for piece in range(PIECES):
            far_step(side, piece)
    steps[1]()
    vector_steps[1]()
    for piece in range(PIECES):
        near_step(1, piece)
    steps[2]()
    vector_steps[2]()
    for piece in range(PIECES):
        near_step(0, piece)
    for piece in range(PIECES):
        pair_step(piece)
    steps[3]()
    vector_steps[3]()
    for piece in range(PIECES):
        last_step(piece)
    steps[4]()
    high, rest = split_low(total[...])
    exchange(node_part[...] + dot(high, weight[...]) + dot(rest, weight[...]))
    for step in steps[5:8]:
        step()
    receive()
    steps[8]()
    vector_steps[4]()
    drain()
    steps[9]()


def finish(sums, grads, vectors, node_part, weight, residual, cut, collective):
    rows, width = node_part.shape
    along = lax.axis_size("blk") // 2
    devices = lax.axis_size("blk") * lax.axis_size("sub")
    hold = pl.BlockSpec(memory_space=pltpu.VMEM)
    across = pl.BlockSpec(memory_space=pl.ANY)
    return pl.pallas_call(
        functools.partial(finish_kernel, cut),
        in_specs=[across, across, hold, hold, hold, hold],
        out_specs=[hold] * 3,
        out_shape=[
            jax.ShapeDtypeStruct(residual.shape, WIDE),
            jax.ShapeDtypeStruct(grads.shape, LOW),
            jax.ShapeDtypeStruct(vectors.shape, WIDE),
        ],
        scratch_shapes=[
            pltpu.VMEM((rows, width), WIDE),
            *collect_scratch(rows, width),
            *reducer_scratch(cut, width, along),
            *reducer_scratch(grads.shape[0] - cut, width, along),
            *vector_scratch(vectors.shape, along),
            *exchange_scratch(rows, width, devices),
        ],
        compiler_params=pltpu.CompilerParams(
            collective_id=collective, has_side_effects=True, vmem_limit_bytes=VMEM_BYTES
        ),
        name="finish_sums",
    )(sums.reshape(3, 4, rows, width), grads, vectors, node_part, weight, residual)


def shards(
    node_input,
    edge_input,
    senders,
    receivers,
    edge_count,
    edge_w_one,
    edge_b_one,
    edge_w_two,
    edge_b_two,
    edge_gain,
    edge_shift,
    node_w_one,
    node_b_one,
    node_w_two,
    node_b_two,
    node_gain,
    node_shift,
    node_cotangent,
    edge_cotangent,
):
    groups = lax.axis_size("blk")
    sub_count = lax.axis_size("sub")
    block_index = lax.axis_index("blk")
    sub_index = lax.axis_index("sub")
    width = edge_input.shape[1]
    node_low = to_nodes(node_input.astype(jnp.bfloat16)).T
    node_upstream = to_nodes(node_cotangent).T
    per_device = node_low.shape[0]
    per_group = per_device * sub_count
    my_start = (block_index * sub_count + sub_index) * per_device
    send_local = senders - my_start
    relative = (receivers // per_group - block_index + 1 + groups) % groups
    recv_wide = relative * per_group + receivers % per_group
    wide_low = spread(node_low, 0)
    edge_result, first_pre, second_pre, received, wide_sums = edge_forward(
        edge_count, recv_wide, send_local, edge_input, wide_low, node_low,
        edge_w_one, edge_b_one[None], edge_w_two, edge_b_two[None], edge_gain[None], edge_shift[None],
    )
    gathered = collect(wide_sums, per_device, 1)
    joined = jnp.concatenate([node_low, gathered.astype(jnp.bfloat16)], axis=1)
    third_pre = matmul(joined, node_w_one) + node_b_one
    third_act = jax.nn.silu(third_pre).astype(jnp.bfloat16)
    fourth_pre = matmul(third_act, node_w_two) + node_b_two
    node_branch, node_norm_back = jax.vjp(norm_apply, fourth_pre, node_gain, node_shift)
    grad_fourth, grad_node_gain, grad_node_shift = node_norm_back(node_upstream)
    fourth_low = grad_fourth.astype(jnp.bfloat16)
    grad_node_w_two = left_matmul(third_act, fourth_low)
    grad_node_b_two = jnp.sum(fourth_low.astype(jnp.float32), 0)
    grad_third = right_matmul(fourth_low, node_w_two) * silu_slope(third_pre)
    third_low = grad_third.astype(jnp.bfloat16)
    grad_node_w_one = left_matmul(joined, third_low)
    grad_node_b_one = jnp.sum(third_low.astype(jnp.float32), 0)
    grad_joined = right_matmul(third_low, node_w_one)
    grad_gathered = grad_joined[:, width:]
    wide_grad = spread(grad_gathered.astype(jnp.bfloat16), 2)
    node_out = node_input + to_channels(node_branch.T)
    w_one_t = edge_w_one.T
    edge_grad, receiver_wide, grads, vectors, node_part = edge_backward(
        edge_count, recv_wide, send_local, edge_cotangent, edge_input, received, first_pre, second_pre,
        wide_grad, grad_node_w_one, grad_node_w_two, grad_joined[:, :width], node_low, w_one_t, edge_w_two.T,
        edge_gain[None],
    )
    node_vectors = jnp.stack([grad_node_b_one, grad_node_b_two, grad_node_gain, grad_node_shift])
    node_grad, summed, vectors = finish(
        receiver_wide, grads, jnp.concatenate([vectors[:4], node_vectors]), node_part, w_one_t[:, 2 * width :],
        node_cotangent, 4 * width, 3,
    )
    summed = summed.astype(jnp.float32)
    return (
        node_out,
        edge_result,
        node_grad,
        edge_grad,
        summed[: 3 * width],
        vectors[0],
        summed[3 * width : 4 * width],
        vectors[1],
        vectors[2],
        vectors[3],
        summed[4 * width : 6 * width],
        vectors[4],
        summed[6 * width : 7 * width],
        vectors[5],
        vectors[6],
        vectors[7],
    )


def solution(mesh):
    placed = (
        P(("blk", "sub"), None),
        P(("blk", "sub"), None),
        P(("blk", "sub")),
        P(("blk", "sub")),
        P(("blk", "sub")),
        P(),
        P(),
        P(),
        P(),
        P(),
        P(),
        P(),
        P(),
        P(),
        P(),
        P(),
        P(),
        P(("blk", "sub"), None),
        P(("blk", "sub"), None),
    )
    return jax.shard_map(
        shards,
        mesh=mesh,
        in_specs=placed,
        out_specs=(
            P(("blk", "sub"), None),
            P(("blk", "sub"), None),
            P(("blk", "sub"), None),
            P(("blk", "sub"), None),
            P(),
            P(),
            P(),
            P(),
            P(),
            P(),
            P(),
            P(),
            P(),
            P(),
            P(),
            P(),
        ),
        check_vma=False,
    )
```

```python
import functools
import math

import jax
import jax.numpy as jnp
from jax import lax
from jax.experimental import pallas as pl
from jax.experimental.pallas import tpu as pltpu
from jax.sharding import PartitionSpec as P

EPSILON = 1e-05


def norm_apply(values, gain, shift):
    average = jnp.mean(values, -1, keepdims=True)
    centred = values - average
    variance = jnp.mean(centred * centred, -1, keepdims=True)
    return centred * lax.rsqrt(variance + EPSILON) * gain + shift


def silu_slope(values):
    logistic = jax.nn.sigmoid(values)
    return logistic * (1.0 + values * (1.0 - logistic))


def matmul(left, right):
    return jnp.dot(left, right, preferred_element_type=jnp.float32)


def left_matmul(left, right):
    return lax.dot_general(
        left, right, (((0,), (0,)), ((), ())), preferred_element_type=jnp.float32
    )


def right_matmul(left, right):
    return lax.dot_general(
        left, right, (((1,), (1,)), ((), ())), preferred_element_type=jnp.float32
    )


def to_nodes(channels):
    return lax.all_to_all(channels, ("blk", "sub"), split_axis=1, concat_axis=0, tiled=True)


def to_channels(values):
    return lax.all_to_all(
        values.astype(jnp.bfloat16), ("blk", "sub"), split_axis=0, concat_axis=1, tiled=True
    ).astype(jnp.float32)


TILE = 512
CHUNK = 512
LANES = 128
VMEM_BYTES = 60 * 2**20


def dot(left, right):
    return jnp.dot(left, right, preferred_element_type=jnp.float32)


def dot_left(left, right):
    return lax.dot_general(
        left, right, (((0,), (0,)), ((), ())), preferred_element_type=jnp.float32
    )


def split_low(values):
    high = values.astype(jnp.bfloat16)
    return high, (values - high.astype(jnp.float32)).astype(jnp.bfloat16)


def lay_rows(target, start, values):
    count, width = values.shape
    parts = width // LANES
    for j in range(parts):
        target[pl.ds(start * parts + j, count, stride=parts), :] = values[:, j * LANES : (j + 1) * LANES]


def read_rows(source, start, count, parts):
    return jnp.concatenate(
        [source[pl.ds(start * parts + j, count, stride=parts), :] for j in range(parts)], axis=1
    )


def load_table(wide, table, stage, sems):
    steps = wide.shape[0] // CHUNK

    def fetch(i, slot):
        return pltpu.make_async_copy(wide.at[pl.ds(i * CHUNK, CHUNK)], stage.at[slot], sems.at[slot])

    fetch(0, 0).start()

    def body(i, carry):
        slot = lax.rem(i, 2)

        @pl.when(i + 1 < steps)
        def _():
            fetch(i + 1, 1 - slot).start()

        fetch(i, slot).wait()

        def piece(k, carry):
            values = stage[slot, pl.ds(k * 64, 64), :].astype(jnp.float32)
            lay_rows(table, i * CHUNK + k * 64, values)
            return carry

        return lax.fori_loop(0, CHUNK // 64, piece, carry)

    lax.fori_loop(0, steps, body, 0)


def store_table(table, wide, stage, sems):
    steps = wide.shape[0] // CHUNK
    parts = wide.shape[1] // LANES

    def send(i, slot):
        return pltpu.make_async_copy(stage.at[slot], wide.at[pl.ds(i * CHUNK, CHUNK)], sems.at[slot])

    def body(i, carry):
        slot = lax.rem(i, 2)

        @pl.when(i >= 2)
        def _():
            send(i - 2, slot).wait()

        def piece(k, carry):
            values = read_rows(table, i * CHUNK + k * 64, 64, parts)
            stage[slot, pl.ds(k * 64, 64), :] = values.astype(jnp.bfloat16)
            return carry

        lax.fori_loop(0, CHUNK // 64, piece, 0)
        send(i, slot).start()
        return carry

    lax.fori_loop(0, steps, body, 0)
    for i in (steps - 2, steps - 1):
        send(i, i % 2).wait()


def clear(table):
    def body(i, carry):
        table[pl.ds(i * 512, 512), :] = jnp.zeros((512, LANES), table.dtype)
        return carry

    lax.fori_loop(0, table.shape[0] // 512, body, 0)


def gather_rows(index, base, table, rows, parts):
    count = rows.shape[0] // parts

    def body(i, carry):
        for u in range(16):
            slot = i * 16 + u
            place = index[base + slot]
            rows[pl.ds(pl.multiple_of(slot * parts, parts), parts), :] = table[
                pl.ds(pl.multiple_of(place * parts, parts), parts), :
            ]
        return carry

    lax.fori_loop(0, count // 16, body, 0)


def add_rows(index, base, rows, table, parts):
    count = rows.shape[0] // parts

    def body(i, carry):
        for u in range(0, 16, 2):
            slot = i * 16 + u
            one, two = index[base + slot], index[base + slot + 1]
            at_one = pl.ds(pl.multiple_of(one * parts, parts), parts)
            at_two = pl.ds(pl.multiple_of(two * parts, parts), parts)
            held_one, held_two = table[at_one, :], table[at_two, :]
            sum_one = held_one + rows[pl.ds(pl.multiple_of(slot * parts, parts), parts), :]
            held_two = jnp.where(one == two, sum_one, held_two)
            sum_two = held_two + rows[pl.ds(pl.multiple_of((slot + 1) * parts, parts), parts), :]
            table[at_one, :] = sum_one
            table[at_two, :] = sum_two
        return carry

    lax.fori_loop(0, count // 16, body, 0)


def row_normal(values):
    average = jnp.mean(values, -1, keepdims=True)
    centred = values - average
    variance = jnp.mean(centred * centred, -1, keepdims=True)
    scale = lax.rsqrt(variance + EPSILON)
    return centred * scale, scale


def forward_kernel(
    count, recv, send, edge, wide, nodes, w_one, b_one, w_two, b_two, gain, shift,
    result, first, second, received, sums,
    table, total, rows, stage, sems,
):
    step = pl.program_id(0)
    base = step * TILE
    width = nodes.shape[1]
    parts = width // LANES

    @pl.when(step == 0)
    def _():
        load_table(wide, table, stage, sems)
        clear(total)

    gather_rows(recv, base, table, rows, parts)
    from_recv = read_rows(rows, 0, TILE, parts).astype(jnp.bfloat16)
    received[...] = from_recv
    column = jnp.broadcast_to(send[0], (LANES, TILE)).T
    lane = lax.broadcasted_iota(jnp.int32, (TILE, LANES), 1)
    chosen = jnp.concatenate(
        [
            jnp.where(column == lane + j * LANES, 1.0, 0.0).astype(jnp.bfloat16)
            for j in range(nodes.shape[0] // LANES)
        ],
        axis=1,
    )
    from_send = dot(chosen, nodes[...]).astype(jnp.bfloat16)
    pre = (
        dot(edge[...], w_one[:width])
        + dot(from_send, w_one[width : 2 * width])
        + dot(from_recv, w_one[2 * width :])
        + b_one[...]
    )
    first[...] = pre
    act = (pre * jax.nn.sigmoid(pre)).astype(jnp.bfloat16)
    post = dot(act, w_two[...]) + b_two[...]
    second[...] = post
    normal, _ = row_normal(post)
    branch = normal * gain[...] + shift[...]
    live = base + lax.broadcasted_iota(jnp.int32, (TILE, 1), 0) < count[0]
    outcome = edge[...].astype(jnp.float32) + jnp.where(live, branch, 0.0)
    result[...] = outcome
    lay_rows(rows, 0, jnp.where(live, outcome, 0.0))
    add_rows(recv, base, rows, total, parts)

    @pl.when(step == pl.num_programs(0) - 1)
    def _():
        store_table(total, sums, stage, sems)


def edge_forward(count, recv, send, edge, wide, nodes, w_one, b_one, w_two, b_two, gain, shift):
    edges, width = edge.shape
    steps = edges // TILE
    parts = width // LANES
    hold = pl.BlockSpec(memory_space=pltpu.VMEM)
    scalar = pl.BlockSpec(memory_space=pltpu.SMEM)
    tile = pl.BlockSpec((TILE, width), lambda i: (i, 0))
    return pl.pallas_call(
        forward_kernel,
        grid=(steps,),
        in_specs=[
            scalar, scalar, pl.BlockSpec((1, 1, TILE), lambda i: (i, 0, 0)), tile,
            pl.BlockSpec(memory_space=pl.ANY), hold, hold, hold, hold, hold, hold, hold,
        ],
        out_specs=[tile, tile, tile, tile, pl.BlockSpec(memory_space=pl.ANY)],
        out_shape=[
            jax.ShapeDtypeStruct((edges, width), jnp.float32),
            jax.ShapeDtypeStruct((edges, width), jnp.float32),
            jax.ShapeDtypeStruct((edges, width), jnp.float32),
            jax.ShapeDtypeStruct((edges, width), jnp.bfloat16),
            jax.ShapeDtypeStruct(wide.shape, jnp.bfloat16),
        ],
        scratch_shapes=[
            pltpu.VMEM((wide.shape[0] * parts, LANES), jnp.float32),
            pltpu.VMEM((wide.shape[0] * parts, LANES), jnp.float32),
            pltpu.VMEM((TILE * parts, LANES), jnp.float32),
            pltpu.VMEM((2, CHUNK, width), jnp.bfloat16),
            pltpu.SemaphoreType.DMA((2,)),
        ],
        compiler_params=pltpu.CompilerParams(vmem_limit_bytes=VMEM_BYTES),
        cost_estimate=pl.CostEstimate(
            flops=20 * edges * width * width, bytes_accessed=40 * edges * width, transcendentals=2 * edges * width
        ),
        name="edge_forward",
    )(count, recv, send.reshape(steps, 1, TILE), edge, wide, nodes, w_one, b_one, w_two, b_two, gain, shift)


def backward_kernel(
    count, recv, send, cotangent, edge, received, first, second, wide, node_one, node_two, node_part, nodes, w_one_t, w_two_t, gain,
    grad, sums, all_grads, vectors, sender_grad,
    table, total, rows, stage, sems, by_sender, grads, pass_sems,
):
    step = pl.program_id(0)
    base = step * TILE
    width = nodes.shape[1]
    parts = width // LANES

    first_node = node_one.shape[0]
    passed = (
        pltpu.make_async_copy(node_one, grads.at[pl.ds(4 * width, first_node)], pass_sems.at[0]),
        pltpu.make_async_copy(node_two, grads.at[pl.ds(4 * width + first_node, node_two.shape[0])], pass_sems.at[1]),
        pltpu.make_async_copy(grads, all_grads, pass_sems.at[2]),
    )

    @pl.when(step == 0)
    def _():
        passed[0].start()
        passed[1].start()
        load_table(wide, table, stage, sems)
        clear(total)
        grads[: 4 * width] = jnp.zeros((4 * width, width), grads.dtype)
        vectors[...] = jnp.zeros_like(vectors)
        by_sender[...] = jnp.zeros_like(by_sender)

    gather_rows(recv, base, table, rows, parts)
    live = base + lax.broadcasted_iota(jnp.int32, (TILE, 1), 0) < count[0]
    upstream = cotangent[...].astype(jnp.float32) + jnp.where(live, read_rows(rows, 0, TILE, parts), 0.0)
    masked = jnp.where(live, upstream, 0.0)
    normal, scale = row_normal(second[...])
    vectors[2:3, :] += jnp.sum(masked * normal, 0, keepdims=True)
    vectors[3:4, :] += jnp.sum(masked, 0, keepdims=True)
    scaled = masked * gain[...]
    slope = jnp.mean(scaled * normal, -1, keepdims=True)
    grad_second = scale * (scaled - jnp.mean(scaled, -1, keepdims=True) - normal * slope)
    second_low = grad_second.astype(jnp.bfloat16)
    vectors[1:2, :] += jnp.sum(second_low.astype(jnp.float32), 0, keepdims=True)
    pre = first[...]
    logistic = jax.nn.sigmoid(pre)
    act = (pre * logistic).astype(jnp.bfloat16)
    grads[3 * width : 4 * width] += dot_left(act, second_low)
    grad_first = dot(second_low, w_two_t[...]) * (logistic * (1.0 + pre * (1.0 - logistic)))
    first_low = grad_first.astype(jnp.bfloat16)
    first_wide = first_low.astype(jnp.float32)
    vectors[0:1, :] += jnp.sum(first_wide, 0, keepdims=True)
    grads[:width] += dot_left(edge[...], first_low)
    grads[2 * width : 3 * width] += dot_left(received[...], first_low)
    node = lax.broadcasted_iota(jnp.int32, (nodes.shape[0], TILE), 0)
    chosen = jnp.where(node == send[0], 1.0, 0.0).astype(jnp.bfloat16)
    by_sender[...] += dot(chosen, first_low)
    grad[...] = upstream + dot(first_low, w_one_t[:, :width])
    lay_rows(rows, 0, first_wide)
    add_rows(recv, base, rows, total, parts)

    @pl.when(step == pl.num_programs(0) - 1)
    def _():
        high, rest = split_low(by_sender[...])
        grads[width : 2 * width] = dot_left(nodes[...], high) + dot_left(nodes[...], rest)
        passed[0].wait()
        passed[1].wait()
        passed[2].start()
        middle = w_one_t[:, width : 2 * width]
        sender_grad[...] = node_part[...] + dot(high, middle) + dot(rest, middle)
        store_table(total, sums, stage, sems)
        passed[2].wait()


def edge_backward(
    count, recv, send, cotangent, edge, received, first, second, wide, node_one, node_two, node_part, nodes,
    w_one_t, w_two_t, gain,
):
    edges, width = edge.shape
    steps = edges // TILE
    parts = width // LANES
    per_device = nodes.shape[0]
    hold = pl.BlockSpec(memory_space=pltpu.VMEM)
    scalar = pl.BlockSpec(memory_space=pltpu.SMEM)
    tile = pl.BlockSpec((TILE, width), lambda i: (i, 0))

    across = pl.BlockSpec(memory_space=pl.ANY)
    unit = 64 * lax.axis_size("blk")
    held = 4 * width + node_one.shape[0] + node_two.shape[0]
    padded = -(-held // unit) * unit

    def whole(rows):
        return pl.BlockSpec((rows, width), lambda i: (0, 0))

    return pl.pallas_call(
        backward_kernel,
        grid=(steps,),
        in_specs=[
            scalar, scalar, pl.BlockSpec((1, 1, TILE), lambda i: (i, 0, 0)), tile, tile, tile, tile, tile,
            across, across, across, hold, hold, hold, hold, hold,
        ],
        out_specs=[
            tile, across, across, whole(8), whole(per_device),
        ],
        out_shape=[
            jax.ShapeDtypeStruct((edges, width), jnp.float32),
            jax.ShapeDtypeStruct(wide.shape, jnp.bfloat16),
            jax.ShapeDtypeStruct((padded, width), jnp.float32),
            jax.ShapeDtypeStruct((8, width), jnp.float32),
            jax.ShapeDtypeStruct((per_device, width), jnp.float32),
        ],
        scratch_shapes=[
            pltpu.VMEM((wide.shape[0] * parts, LANES), jnp.float32),
            pltpu.VMEM((wide.shape[0] * parts, LANES), jnp.float32),
            pltpu.VMEM((TILE * parts, LANES), jnp.float32),
            pltpu.VMEM((2, CHUNK, width), jnp.bfloat16),
            pltpu.SemaphoreType.DMA((2,)),
            pltpu.VMEM((per_device, width), jnp.float32),
            pltpu.VMEM((padded, width), jnp.float32),
            pltpu.SemaphoreType.DMA((3,)),
        ],
        compiler_params=pltpu.CompilerParams(vmem_limit_bytes=VMEM_BYTES),
        cost_estimate=pl.CostEstimate(
            flops=24 * edges * width * width, bytes_accessed=40 * edges * width, transcendentals=2 * edges * width
        ),
        name="edge_backward",
    )(
        count, recv, send.reshape(steps, 1, TILE), cotangent, edge, received, first, second, wide, node_one, node_two,
        node_part, nodes, w_one_t, w_two_t, gain,
    )


MESH = pl.DeviceIdType.MESH
PIECES = 4
LOW = jnp.bfloat16
WIDE = jnp.float32


def places():
    groups = lax.axis_size("blk")
    group, sub = lax.axis_index("blk"), lax.axis_index("sub")
    odd = lax.rem(group, 2)
    along = groups // 2
    spot = group // 2
    beside = group + 1 - 2 * odd
    return dict(
        group=group,
        sub=sub,
        core=lax.rem(sub, 2),
        chip=sub // 2,
        odd=odd,
        spot=spot,
        along=along,
        sibling=sub + 1 - 2 * lax.rem(sub, 2),
        partner=lax.rem(sub + 2, 4),
        to_sibling=(group, sub + 1 - 2 * lax.rem(sub, 2)),
        to_partner=(group, lax.rem(sub + 2, 4)),
        to_beside=(beside, sub),
        to_onward=(lax.rem(group + 2 - 4 * odd + groups, groups), sub),
        to_source=(lax.rem(group - 2 + 4 * odd + groups, groups), sub),
        peers=[(2 * lax.rem(spot + k, along) + odd, sub) for k in range(1, along)],
        near=2 - 2 * odd,
        far=2 * odd,
    )


def meet(senders):
    barrier = pltpu.get_barrier_semaphore()
    for device in senders:
        pl.semaphore_signal(barrier, inc=1, device_id=device, device_id_type=MESH)
    pl.semaphore_wait(barrier, len(senders))


def meet_all():
    barrier = pltpu.get_barrier_semaphore()
    subs = lax.axis_size("sub")
    devices = lax.axis_size("blk") * subs
    here = lax.axis_index("blk") * subs + lax.axis_index("sub")

    def greet(k, carry):
        there = lax.rem(here + k, devices)
        pl.semaphore_signal(barrier, inc=1, device_id=(there // subs, lax.rem(there, subs)), device_id_type=MESH)
        return carry

    lax.fori_loop(1, devices, greet, 0)
    pl.semaphore_wait(barrier, devices - 1)


def remote(source, target, send, recv, device):
    return pltpu.make_async_remote_copy(
        src_ref=source, dst_ref=target, send_sem=send, recv_sem=recv, device_id=device, device_id_type=MESH
    )


def in_pieces(count, body):
    block = math.gcd(count, 128)

    def run(i, carry):
        body(pl.multiple_of(i * block, block), block)
        return carry

    lax.fori_loop(0, count // block, run, 0)


def reducer_scratch(rows, width, along):
    return [
        pltpu.VMEM((rows // 2, width), WIDE),
        pltpu.VMEM((rows // 2, width), WIDE),
        pltpu.VMEM((rows // 4, width), LOW),
        pltpu.VMEM((rows // 4, width), LOW),
        pltpu.VMEM((rows // 8, width), LOW),
        pltpu.VMEM((rows // 8, width), LOW),
        pltpu.VMEM((rows // 8, width), LOW),
        pltpu.VMEM((along - 1, rows // 8 // along, width), LOW),
        pltpu.SemaphoreType.DMA,
        pltpu.SemaphoreType.DMA((6,)),
        pltpu.SemaphoreType.DMA((6,)),
        pltpu.SemaphoreType.DMA((2, along - 1)),
        pltpu.SemaphoreType.DMA((2, along - 1)),
    ]


def reducer(at, grads, reduced, first, rows, swap, refs):
    (
        half, half_in, cross_out, cross_in, side_out, side_in, ring_out, ring_in,
        load_sem, step_send, step_recv, ring_send, ring_recv,
    ) = refs
    along, peers = at["along"], at["peers"]
    turns = [(at["chip"], at["to_partner"]), (at["odd"], at["to_beside"])]
    (bit_one, device_one), (bit_two, device_two) = turns[::-1] if swap else turns
    core, spot = at["core"], at["spot"]
    n_half, n_cross, n_side, n_ring = rows // 2, rows // 4, rows // 8, rows // 8 // along
    at_half = first + core * n_half
    at_cross = at_half + bit_one * n_cross
    at_side = at_cross + bit_two * n_side
    at_ring = at_side + spot * n_ring

    def span(start, count):
        return pl.ds(pl.multiple_of(start, 16), count)

    def step(kind):
        if kind == 0:
            source, target, device = grads.at[span(first + (1 - core) * n_half, n_half)], half_in, at["to_sibling"]
        elif kind == 1:
            source, target, device = cross_out, cross_in, device_one
        elif kind == 2:
            source, target, device = side_out, side_in, device_two
        else:
            start, count, device = {
                3: (at_side, n_side, device_two),
                4: (at_cross, n_cross, device_one),
                5: (at_half, n_half, at["to_sibling"]),
            }[kind]
            source = target = reduced.at[span(start, count)]
        return remote(source, target, step_send.at[kind], step_recv.at[kind], device)

    def ring(kind, k):
        if kind == 0:
            source = ring_out.at[span(lax.rem(spot + k, along) * n_ring, n_ring)]
            target = ring_in.at[k - 1]
        else:
            source = target = reduced.at[span(at_ring, n_ring)]
        return remote(source, target, ring_send.at[kind, k - 1], ring_recv.at[kind, k - 1], peers[k - 1])

    load = pltpu.make_async_copy(grads.at[span(at_half, n_half)], half, load_sem)

    def start():
        step(0).start()
        load.start()

    def add_half():
        load.wait()
        step(0).wait_recv()
        other = (1 - bit_one) * n_cross

        def part(i, block):
            here = pl.ds(pl.multiple_of(other + i, block), block)
            cross_out[pl.ds(i, block), :] = (half[here, :] + half_in[here, :]).astype(LOW)

        in_pieces(n_cross, part)
        step(1).start()

    def add_cross():
        mine, other = bit_one * n_cross, (1 - bit_two) * n_side
        step(1).wait_recv()

        def part(i, block):
            there = pl.ds(pl.multiple_of(other + i, block), block)
            here = pl.ds(pl.multiple_of(mine + other + i, block), block)
            side_out[pl.ds(i, block), :] = (half[here, :] + half_in[here, :] + cross_in[there, :].astype(WIDE)).astype(LOW)

        in_pieces(n_side, part)
        step(2).start()

    def add_side():
        mine, kept = bit_one * n_cross, bit_two * n_side
        step(2).wait_recv()

        def part(i, block):
            there = pl.ds(pl.multiple_of(kept + i, block), block)
            here = pl.ds(pl.multiple_of(mine + kept + i, block), block)
            flat = pl.ds(i, block)
            value = half[here, :] + half_in[here, :] + cross_in[there, :].astype(WIDE) + side_in[flat, :].astype(WIDE)
            half[here, :] = value
            ring_out[flat, :] = value.astype(LOW)

        in_pieces(n_side, part)
        for k in range(1, along):
            ring(0, k).start()

    def add_ring():
        value = half[span(bit_one * n_cross + bit_two * n_side + spot * n_ring, n_ring), :]
        for k in range(1, along):
            ring(0, k).wait_recv()
            value = value + ring_in[k - 1].astype(WIDE)
        reduced[span(at_ring, n_ring), :] = value.astype(LOW)
        for k in range(1, along):
            ring(1, k).start()

    def share_side():
        for k in range(1, along):
            ring(1, k).wait_recv()
        step(3).start()

    def share_cross():
        step(3).wait_recv()
        step(4).start()

    def share_half():
        step(4).wait_recv()
        step(5).start()

    def last():
        step(5).wait_recv()

    def drain():
        for kind in range(6):
            step(kind).wait_send()
        for k in range(1, along):
            ring(0, k).wait_send()
            ring(1, k).wait_send()

    return [start, add_half, add_cross, add_side, add_ring, share_side, share_cross, share_half, last, drain]


def vector_scratch(shape, along):
    return [
        pltpu.VMEM((4, *shape), WIDE),
        pltpu.VMEM((2 + along, *shape), WIDE),
        pltpu.SemaphoreType.DMA((2 + along,)),
        pltpu.SemaphoreType.DMA((2 + along,)),
    ]


def vector_reducer(at, vectors, reduced, refs):
    held, held_in, send_sems, recv_sems = refs
    along = at["along"]
    devices = (at["to_sibling"], at["to_partner"], at["to_beside"], *at["peers"])

    def move(kind):
        return remote(held.at[min(kind, 3)], held_in.at[kind], send_sems.at[kind], recv_sems.at[kind], devices[kind])

    def start():
        held[0] = vectors[...]
        move(0).start()

    def turn(kind):
        def run():
            move(kind).wait_recv()
            held[kind + 1] = held[kind] + held_in[kind]
            for k in range(kind + 1, kind + 2 if kind < 2 else 2 + along):
                move(k).start()

        return run

    def last():
        value = held[3]
        for k in range(3, 2 + along):
            move(k).wait_recv()
            value = value + held_in[k]
        reduced[...] = value
        for k in range(2 + along):
            move(k).wait_send()

    return [start, turn(0), turn(1), turn(2), last]


def both(streams):
    return [lambda steps=steps: [step() for step in steps] for steps in zip(*streams)]


def spread_moves(at, own, table, keep_sem, send_sems, recv_sems):
    sub, partner, near, far = at["sub"], at["partner"], at["near"], at["far"]
    to_sibling, to_partner, to_beside, to_onward = (
        at["to_sibling"], at["to_partner"], at["to_beside"], at["to_onward"]
    )
    size = own.shape[0] // PIECES

    def move(kind, piece):
        source, slot, device = {
            0: (None, (1, sub), to_partner),
            1: (None, (far, sub), to_beside),
            2: (None, (1, sub), to_sibling),
            3: ((1, partner), (far, partner), to_beside),
            4: ((1, partner), (1, partner), to_sibling),
            5: ((near, sub), (far, sub), to_onward),
            6: ((near, sub), (near, sub), to_sibling),
            7: ((near, partner), (far, partner), to_onward),
            8: ((near, partner), (near, partner), to_sibling),
            9: ((far, sub), (far, sub), to_sibling),
            10: ((far, partner), (far, partner), to_sibling),
        }[kind]
        source = own if source is None else table.at[source[0], source[1]]
        rows = pl.ds(piece * size, size)
        return remote(
            source.at[rows], table.at[slot[0], slot[1], rows],
            send_sems.at[kind, piece], recv_sems.at[kind, piece], device,
        )

    keep = pltpu.make_async_copy(own, table.at[1, sub], keep_sem)

    def start():
        for piece in range(PIECES):
            for kind in (0, 1, 2):
                move(kind, piece).start()
        keep.start()

    def relay(arrived, kinds, piece):
        move(arrived, piece).wait_recv()
        for kind in kinds:
            move(kind, piece).start()

    def one(piece):
        relay(0, (3, 4), piece)
        relay(1, (5, 6), piece)

    def two(piece):
        relay(3, (7, 8), piece)
        relay(5, (9,), piece)

    def three(piece):
        relay(7, (10,), piece)

    def drain():
        for kind in range(11):
            for piece in range(PIECES):
                if kind in (2, 4, 6, 8, 9, 10):
                    move(kind, piece).wait_recv()
                move(kind, piece).wait_send()
        keep.wait()

    return start, one, two, three, drain


def spread_scratch():
    return [
        pltpu.SemaphoreType.DMA,
        pltpu.SemaphoreType.DMA((11, PIECES)),
        pltpu.SemaphoreType.DMA((11, PIECES)),
    ]


def spread_kernel(own, table, *refs):
    at = places()
    meet((at["to_sibling"], at["to_partner"], at["to_beside"], at["to_source"]))
    start, one, two, three, drain = spread_moves(at, own, table, *refs)
    start()
    for stage in (one, two, three):
        for piece in range(PIECES):
            stage(piece)
    drain()


def spread(own, collective):
    rows, width = own.shape
    return pl.pallas_call(
        spread_kernel,
        in_specs=[pl.BlockSpec(memory_space=pltpu.VMEM)],
        out_specs=pl.BlockSpec(memory_space=pl.ANY),
        out_shape=jax.ShapeDtypeStruct((3, 4, rows, width), own.dtype),
        scratch_shapes=spread_scratch(),
        compiler_params=pltpu.CompilerParams(collective_id=collective, has_side_effects=True),
        name="spread_rows",
    )(own).reshape(12 * rows, width)


def collect_scratch(rows, width):
    return [
        pltpu.VMEM((3, 2, rows, width), LOW),
        pltpu.VMEM((3, 2, rows, width), LOW),
        pltpu.VMEM((2, rows, width), LOW),
        pltpu.VMEM((2, rows, width), LOW),
        pltpu.VMEM((2, rows, width), LOW),
        pltpu.VMEM((2, rows, width), LOW),
        pltpu.VMEM((rows, width), LOW),
        pltpu.VMEM((rows, width), LOW),
        pltpu.SemaphoreType.DMA((3, 2, PIECES)),
        pltpu.SemaphoreType.DMA((3, 2, PIECES)),
        pltpu.SemaphoreType.DMA((3, 2, PIECES)),
        pltpu.SemaphoreType.DMA((5, PIECES)),
        pltpu.SemaphoreType.DMA((5, PIECES)),
    ]


def collect_moves(at, sums, out, refs):
    (
        mine, landed, far_out, far_in, near_out, near_in, pair_out, pair_in,
        keep_sems, give_sems, take_sems, send_sems, recv_sems,
    ) = refs
    sub, partner, sibling = at["sub"], at["partner"], at["sibling"]
    relations = (at["far"], at["near"], 1)
    size = out.shape[0] // PIECES

    def part(ref, piece):
        return ref.at[pl.ds(piece * size, size)]

    def keep(role, side, piece):
        return pltpu.make_async_copy(
            part(sums.at[relations[role], (sub, partner)[side]], piece),
            part(mine.at[role, side], piece),
            keep_sems.at[role, side, piece],
        )

    def give(role, side, piece):
        return remote(
            part(sums.at[relations[role], (sibling, lax.rem(sibling + 2, 4))[side]], piece),
            part(landed.at[role, side], piece),
            give_sems.at[role, side, piece], take_sems.at[role, side, piece], at["to_sibling"],
        )

    def hop(kind, piece):
        source, target, device = {
            0: (far_out.at[0], far_in.at[0], at["to_source"]),
            1: (far_out.at[1], far_in.at[1], at["to_source"]),
            2: (near_out.at[0], near_in.at[0], at["to_beside"]),
            3: (near_out.at[1], near_in.at[1], at["to_beside"]),
            4: (pair_out, pair_in, at["to_partner"]),
        }[kind]
        return remote(
            part(source, piece), part(target, piece), send_sems.at[kind, piece], recv_sems.at[kind, piece], device
        )

    order = [(role, side, piece) for role in range(3) for side in (1, 0) for piece in range(PIECES)]

    def local(role, side, piece):
        keep(role, side, piece).wait()
        give(role, side, piece).wait_recv()
        rows = pl.ds(piece * size, size)
        return mine[role, side, rows, :].astype(WIDE) + landed[role, side, rows, :].astype(WIDE)

    def arrived(kind, ref, piece):
        hop(kind, piece).wait_recv()
        return ref[pl.ds(piece * size, size), :].astype(WIDE)

    def start(role):
        for item in order:
            if item[0] == role:
                give(*item).start()
                keep(*item).start()

    def far_step(side, piece):
        far_out[side, pl.ds(piece * size, size), :] = local(0, side, piece).astype(LOW)
        hop(side, piece).start()

    def near_step(side, piece):
        value = local(1, side, piece) + arrived(side, far_in.at[side], piece)
        near_out[side, pl.ds(piece * size, size), :] = value.astype(LOW)
        hop(2 + side, piece).start()

    def pair_step(piece):
        value = local(2, 1, piece) + arrived(3, near_in.at[1], piece)
        pair_out[pl.ds(piece * size, size), :] = value.astype(LOW)
        hop(4, piece).start()

    def last_step(piece):
        value = local(2, 0, piece) + arrived(2, near_in.at[0], piece) + arrived(4, pair_in, piece)
        out[pl.ds(piece * size, size), :] = value

    def drain():
        for item in order:
            give(*item).wait_send()
        for kind in range(5):
            for piece in range(PIECES):
                hop(kind, piece).wait_send()

    return start, far_step, near_step, pair_step, last_step, drain


def collect_kernel(sums, out, *refs):
    at = places()
    meet((at["to_sibling"], at["to_partner"], at["to_beside"], at["to_onward"]))
    start, far_step, near_step, pair_step, last_step, drain = collect_moves(at, sums, out, refs)
    for role in range(3):
        start(role)
    for step in (far_step, near_step):
        for side in (1, 0):
            for piece in range(PIECES):
                step(side, piece)
    for piece in range(PIECES):
        pair_step(piece)
    for piece in range(PIECES):
        last_step(piece)
    drain()


def collect(sums, rows, collective):
    width = sums.shape[1]
    return pl.pallas_call(
        collect_kernel,
        in_specs=[pl.BlockSpec(memory_space=pl.ANY)],
        out_specs=pl.BlockSpec(memory_space=pltpu.VMEM),
        out_shape=jax.ShapeDtypeStruct((rows, width), WIDE),
        scratch_shapes=collect_scratch(rows, width),
        compiler_params=pltpu.CompilerParams(
            collective_id=collective, has_side_effects=True, vmem_limit_bytes=VMEM_BYTES
        ),
        name="collect_sums",
    )(sums.reshape(3, 4, rows, width))


def exchange_scratch(rows, width, devices):
    slab = width // devices * (rows // LANES)
    return [
        pltpu.VMEM((devices * slab, LANES), WIDE),
        pltpu.VMEM((devices * slab, LANES), LOW),
        pltpu.VMEM((devices, slab, LANES), LOW),
        pltpu.VMEM((slab, LANES), WIDE),
        pltpu.SemaphoreType.DMA((devices - 1,)),
        pltpu.SemaphoreType.DMA((devices - 1,)),
    ]


def exchange_moves(residual, out, refs):
    flat, packed, landed, opened, send_sems, recv_sems = refs
    subs = lax.axis_size("sub")
    devices = lax.axis_size("blk") * subs
    here = lax.axis_index("blk") * subs + lax.axis_index("sub")
    slab = landed.shape[1]
    channels = out.shape[0]
    parts = slab // channels
    nodes = parts * LANES

    def move(k):
        there = lax.rem(here + k, devices)
        return remote(
            packed.at[pl.ds(pl.multiple_of(there * slab, slab), slab)], landed.at[here],
            send_sems.at[k - 1], recv_sems.at[k - 1], (there // subs, lax.rem(there, subs)),
        )

    def start(values):
        lay_rows(flat, 0, values.T)

        def cast(i, block):
            packed[pl.ds(i, block), :] = flat[pl.ds(i, block), :].astype(LOW)

        in_pieces(flat.shape[0], cast)

        def send(k, carry):
            move(k).start()
            return carry

        lax.fori_loop(1, devices, send, 0)

    def open_slab(source, device):
        opened[...] = source.astype(WIDE)
        for j in range(parts):
            columns = pl.ds(pl.multiple_of(device * nodes + j * LANES, LANES), LANES)
            out[:, columns] = residual[:, columns] + opened[pl.ds(j, channels, stride=parts), :]

    def last():
        open_slab(packed[pl.ds(pl.multiple_of(here * slab, slab), slab), :], here)

        def take(k, carry):
            move(k).wait_recv()
            device = lax.rem(here - k + devices, devices)
            open_slab(landed[device], device)
            return carry

        lax.fori_loop(1, devices, take, 0)

        def sent(k, carry):
            move(k).wait_send()
            return carry

        lax.fori_loop(1, devices, sent, 0)

    return start, last


def finish_kernel(
    cut, sums, grads, vectors, node_part, weight, residual, node_grad, reduced, reduced_vectors, total, *refs
):
    at = places()
    meet_all()
    sizes = len(reducer_scratch(64, 128, 2))
    count = len(collect_scratch(64, 128))
    start, far_step, near_step, pair_step, last_step, drain = collect_moves(at, sums, total, refs[:count])
    refs = refs[count:]
    steps = both([
        reducer(at, grads, reduced, 0, cut, False, refs[:sizes]),
        reducer(at, grads, reduced, cut, grads.shape[0] - cut, True, refs[sizes : 2 * sizes]),
    ])
    refs = refs[2 * sizes :]
    vector_steps = vector_reducer(at, vectors, reduced_vectors, refs[:4])
    exchange, receive = exchange_moves(residual, node_grad, refs[4:])
    start(0)
    steps[0]()
    vector_steps[0]()
    start(1)
    start(2)
    for side in (1, 0):
        for piece in range(PIECES):
            far_step(side, piece)
    steps[1]()
    vector_steps[1]()
    for piece in range(PIECES):
        near_step(1, piece)
    steps[2]()
    vector_steps[2]()
    for piece in range(PIECES):
        near_step(0, piece)
    for piece in range(PIECES):
        pair_step(piece)
    steps[3]()
    vector_steps[3]()
    for piece in range(PIECES):
        last_step(piece)
    steps[4]()
    high, rest = split_low(total[...])
    exchange(node_part[...] + dot(high, weight[...]) + dot(rest, weight[...]))
    for step in steps[5:8]:
        step()
    receive()
    steps[8]()
    vector_steps[4]()
    drain()
    steps[9]()


def finish(sums, grads, vectors, node_part, weight, residual, cut, collective):
    rows, width = node_part.shape
    along = lax.axis_size("blk") // 2
    devices = lax.axis_size("blk") * lax.axis_size("sub")
    hold = pl.BlockSpec(memory_space=pltpu.VMEM)
    across = pl.BlockSpec(memory_space=pl.ANY)
    return pl.pallas_call(
        functools.partial(finish_kernel, cut),
        in_specs=[across, across, hold, hold, hold, hold],
        out_specs=[hold] * 3,
        out_shape=[
            jax.ShapeDtypeStruct(residual.shape, WIDE),
            jax.ShapeDtypeStruct(grads.shape, LOW),
            jax.ShapeDtypeStruct(vectors.shape, WIDE),
        ],
        scratch_shapes=[
            pltpu.VMEM((rows, width), WIDE),
            *collect_scratch(rows, width),
            *reducer_scratch(cut, width, along),
            *reducer_scratch(grads.shape[0] - cut, width, along),
            *vector_scratch(vectors.shape, along),
            *exchange_scratch(rows, width, devices),
        ],
        compiler_params=pltpu.CompilerParams(
            collective_id=collective, has_side_effects=True, vmem_limit_bytes=VMEM_BYTES
        ),
        name="finish_sums",
    )(sums.reshape(3, 4, rows, width), grads, vectors, node_part, weight, residual)


def scatter_scratch(channels, nodes, devices):
    slab = channels * (nodes // LANES)
    return [
        pltpu.VMEM((devices * slab, LANES), WIDE),
        pltpu.VMEM((devices * slab, LANES), LOW),
        pltpu.VMEM((devices, slab, LANES), LOW),
        pltpu.VMEM((slab, LANES), WIDE),
        pltpu.VMEM((nodes // LANES * devices * channels, LANES), WIDE),
        pltpu.SemaphoreType.DMA((devices - 1,)),
        pltpu.SemaphoreType.DMA((devices - 1,)),
    ]


def scatter_moves(shard, refs):
    flat, packed, landed, opened, square, send_sems, recv_sems = refs
    subs = lax.axis_size("sub")
    devices = lax.axis_size("blk") * subs
    here = lax.axis_index("blk") * subs + lax.axis_index("sub")
    slab = landed.shape[1]
    channels = shard.shape[0]
    parts = slab // channels
    nodes = parts * LANES

    def move(k):
        there = lax.rem(here + k, devices)
        return remote(
            packed.at[pl.ds(pl.multiple_of(there * slab, slab), slab)], landed.at[here],
            send_sems.at[k - 1], recv_sems.at[k - 1], (there // subs, lax.rem(there, subs)),
        )

    def start():
        def pack(k, carry):
            device = lax.rem(here + k, devices)
            rows = pl.ds(pl.multiple_of(device * slab, slab), slab)
            for j in range(parts):
                columns = pl.ds(pl.multiple_of(device * nodes + j * LANES, LANES), LANES)
                flat[pl.ds(device * slab + j, channels, stride=parts), :] = shard[:, columns]
            packed[rows, :] = flat[rows, :].astype(LOW)
            return carry

        def send(k, carry):
            pack(k, carry)
            move(k).start()
            return carry

        lax.fori_loop(1, devices, send, 0)
        pack(0, 0)

    def open_slab(source, device):
        opened[...] = source.astype(WIDE)
        for j in range(parts):
            rows = pl.ds(pl.multiple_of((j * devices + device) * channels, channels), channels)
            square[rows, :] = opened[pl.ds(j, channels, stride=parts), :]

    def last(rows):
        open_slab(packed[pl.ds(pl.multiple_of(here * slab, slab), slab), :], here)

        def take(k, carry):
            move(k).wait_recv()
            device = lax.rem(here - k + devices, devices)
            open_slab(landed[device], device)
            return carry

        lax.fori_loop(1, devices, take, 0)
        width = devices * channels
        for j in range(parts):
            rows[j * LANES : (j + 1) * LANES, :] = square[j * width : (j + 1) * width, :].T.astype(LOW)

    def drain():
        def sent(k, carry):
            move(k).wait_send()
            return carry

        lax.fori_loop(1, devices, sent, 0)

    return start, last, drain


def begin_kernel(shard, later, own, table, later_out, held, held_sem, *refs):
    at = places()
    fetch = pltpu.make_async_copy(later, held, held_sem)
    fetch.start()
    meet_all()
    start, last, drain = scatter_moves(shard, refs[3:])
    start()
    last(own)
    begin, one, two, three, end = spread_moves(at, own, table, *refs[:3])
    begin()
    fetch.wait()
    give = pltpu.make_async_copy(held, later_out, held_sem)
    give.start()
    drain()
    for stage in (one, two, three):
        for piece in range(PIECES):
            stage(piece)
    give.wait()
    end()


def begin(shard, later, rows, collective):
    channels, nodes = shard.shape
    devices = lax.axis_size("blk") * lax.axis_size("sub")
    width = channels * devices
    hold = pl.BlockSpec(memory_space=pltpu.VMEM)
    across = pl.BlockSpec(memory_space=pl.ANY)
    own, table, later = pl.pallas_call(
        begin_kernel,
        in_specs=[hold, across],
        out_specs=[hold, across, across],
        out_shape=[
            jax.ShapeDtypeStruct((rows, width), LOW),
            jax.ShapeDtypeStruct((3, 4, rows, width), LOW),
            jax.ShapeDtypeStruct(later.shape, later.dtype),
        ],
        scratch_shapes=[
            pltpu.VMEM(later.shape, later.dtype),
            pltpu.SemaphoreType.DMA,
            *spread_scratch(),
            *scatter_scratch(channels, rows, devices),
        ],
        compiler_params=pltpu.CompilerParams(
            collective_id=collective, has_side_effects=True, vmem_limit_bytes=VMEM_BYTES
        ),
        name="begin_rows",
    )(shard, later)
    return own, table.reshape(12 * rows, width), later


def shards(
    node_input,
    edge_input,
    senders,
    receivers,
    edge_count,
    edge_w_one,
    edge_b_one,
    edge_w_two,
    edge_b_two,
    edge_gain,
    edge_shift,
    node_w_one,
    node_b_one,
    node_w_two,
    node_b_two,
    node_gain,
    node_shift,
    node_cotangent,
    edge_cotangent,
):
    groups = lax.axis_size("blk")
    sub_count = lax.axis_size("sub")
    block_index = lax.axis_index("blk")
    sub_index = lax.axis_index("sub")
    width = edge_input.shape[1]
    per_device = node_input.shape[1] // (groups * sub_count)
    node_low, wide_low, cotangent_later = begin(node_input, node_cotangent, per_device, 0)
    node_upstream = to_nodes(cotangent_later).T
    per_group = per_device * sub_count
    my_start = (block_index * sub_count + sub_index) * per_device
    send_local = senders - my_start
    relative = (receivers // per_group - block_index + 1 + groups) % groups
    recv_wide = relative * per_group + receivers % per_group
    edge_result, first_pre, second_pre, received, wide_sums = edge_forward(
        edge_count, recv_wide, send_local, edge_input, wide_low, node_low,
        edge_w_one, edge_b_one[None], edge_w_two, edge_b_two[None], edge_gain[None], edge_shift[None],
    )
    gathered = collect(wide_sums, per_device, 1)
    joined = jnp.concatenate([node_low, gathered.astype(jnp.bfloat16)], axis=1)
    third_pre = matmul(joined, node_w_one) + node_b_one
    third_act = jax.nn.silu(third_pre).astype(jnp.bfloat16)
    fourth_pre = matmul(third_act, node_w_two) + node_b_two
    node_branch, node_norm_back = jax.vjp(norm_apply, fourth_pre, node_gain, node_shift)
    grad_fourth, grad_node_gain, grad_node_shift = node_norm_back(node_upstream)
    fourth_low = grad_fourth.astype(jnp.bfloat16)
    grad_node_w_two = left_matmul(third_act, fourth_low)
    grad_node_b_two = jnp.sum(fourth_low.astype(jnp.float32), 0)
    grad_third = right_matmul(fourth_low, node_w_two) * silu_slope(third_pre)
    third_low = grad_third.astype(jnp.bfloat16)
    grad_node_w_one = left_matmul(joined, third_low)
    grad_node_b_one = jnp.sum(third_low.astype(jnp.float32), 0)
    grad_joined = right_matmul(third_low, node_w_one)
    grad_gathered = grad_joined[:, width:]
    wide_grad = spread(grad_gathered.astype(jnp.bfloat16), 2)
    node_out = node_input + to_channels(node_branch.T)
    w_one_t = edge_w_one.T
    edge_grad, receiver_wide, grads, vectors, node_part = edge_backward(
        edge_count, recv_wide, send_local, edge_cotangent, edge_input, received, first_pre, second_pre,
        wide_grad, grad_node_w_one, grad_node_w_two, grad_joined[:, :width], node_low, w_one_t, edge_w_two.T,
        edge_gain[None],
    )
    node_vectors = jnp.stack([grad_node_b_one, grad_node_b_two, grad_node_gain, grad_node_shift])
    node_grad, summed, vectors = finish(
        receiver_wide, grads, jnp.concatenate([vectors[:4], node_vectors]), node_part, w_one_t[:, 2 * width :],
        node_cotangent, 4 * width, 3,
    )
    summed = summed.astype(jnp.float32)
    return (
        node_out,
        edge_result,
        node_grad,
        edge_grad,
        summed[: 3 * width],
        vectors[0],
        summed[3 * width : 4 * width],
        vectors[1],
        vectors[2],
        vectors[3],
        summed[4 * width : 6 * width],
        vectors[4],
        summed[6 * width : 7 * width],
        vectors[5],
        vectors[6],
        vectors[7],
    )


def solution(mesh):
    placed = (
        P(("blk", "sub"), None),
        P(("blk", "sub"), None),
        P(("blk", "sub")),
        P(("blk", "sub")),
        P(("blk", "sub")),
        P(),
        P(),
        P(),
        P(),
        P(),
        P(),
        P(),
        P(),
        P(),
        P(),
        P(),
        P(),
        P(("blk", "sub"), None),
        P(("blk", "sub"), None),
    )
    return jax.shard_map(
        shards,
        mesh=mesh,
        in_specs=placed,
        out_specs=(
            P(("blk", "sub"), None),
            P(("blk", "sub"), None),
            P(("blk", "sub"), None),
            P(("blk", "sub"), None),
            P(),
            P(),
            P(),
            P(),
            P(),
            P(),
            P(),
            P(),
            P(),
            P(),
            P(),
            P(),
        ),
        check_vma=False,
    )
```

```python
import functools
import math

import jax
import jax.numpy as jnp
from jax import lax
from jax.experimental import pallas as pl
from jax.experimental.pallas import tpu as pltpu
from jax.sharding import PartitionSpec as P

EPSILON = 1e-05


def norm_apply(values, gain, shift):
    average = jnp.mean(values, -1, keepdims=True)
    centred = values - average
    variance = jnp.mean(centred * centred, -1, keepdims=True)
    return centred * lax.rsqrt(variance + EPSILON) * gain + shift


def silu_slope(values):
    logistic = jax.nn.sigmoid(values)
    return logistic * (1.0 + values * (1.0 - logistic))


def matmul(left, right):
    return jnp.dot(left, right, preferred_element_type=jnp.float32)


def left_matmul(left, right):
    return lax.dot_general(
        left, right, (((0,), (0,)), ((), ())), preferred_element_type=jnp.float32
    )


def right_matmul(left, right):
    return lax.dot_general(
        left, right, (((1,), (1,)), ((), ())), preferred_element_type=jnp.float32
    )


def to_nodes(channels):
    return lax.all_to_all(channels, ("blk", "sub"), split_axis=1, concat_axis=0, tiled=True)


def to_channels(values):
    return lax.all_to_all(
        values.astype(jnp.bfloat16), ("blk", "sub"), split_axis=0, concat_axis=1, tiled=True
    ).astype(jnp.float32)


TILE = 512
CHUNK = 512
LANES = 128
VMEM_BYTES = 60 * 2**20


def dot(left, right):
    return jnp.dot(left, right, preferred_element_type=jnp.float32)


def dot_left(left, right):
    return lax.dot_general(
        left, right, (((0,), (0,)), ((), ())), preferred_element_type=jnp.float32
    )


def dot_right(left, right):
    return lax.dot_general(
        left, right, (((1,), (1,)), ((), ())), preferred_element_type=jnp.float32
    )


def split_low(values):
    high = values.astype(jnp.bfloat16)
    return high, (values - high.astype(jnp.float32)).astype(jnp.bfloat16)


def lay_rows(target, start, values):
    count, width = values.shape
    parts = width // LANES
    for j in range(parts):
        target[pl.ds(start * parts + j, count, stride=parts), :] = values[:, j * LANES : (j + 1) * LANES]


def read_rows(source, start, count, parts):
    return jnp.concatenate(
        [source[pl.ds(start * parts + j, count, stride=parts), :] for j in range(parts)], axis=1
    )


def load_table(wide, table, stage, sems):
    steps = wide.shape[0] // CHUNK

    def fetch(i, slot):
        return pltpu.make_async_copy(wide.at[pl.ds(i * CHUNK, CHUNK)], stage.at[slot], sems.at[slot])

    fetch(0, 0).start()

    def body(i, carry):
        slot = lax.rem(i, 2)

        @pl.when(i + 1 < steps)
        def _():
            fetch(i + 1, 1 - slot).start()

        fetch(i, slot).wait()

        def piece(k, carry):
            values = stage[slot, pl.ds(k * 64, 64), :].astype(jnp.float32)
            lay_rows(table, i * CHUNK + k * 64, values)
            return carry

        return lax.fori_loop(0, CHUNK // 64, piece, carry)

    lax.fori_loop(0, steps, body, 0)


def gather_rows(index, base, table, rows, parts):
    count = rows.shape[0] // parts

    def body(i, carry):
        for u in range(16):
            slot = i * 16 + u
            place = index[base + slot]
            rows[pl.ds(pl.multiple_of(slot * parts, parts), parts), :] = table[
                pl.ds(pl.multiple_of(place * parts, parts), parts), :
            ]
        return carry

    lax.fori_loop(0, count // 16, body, 0)


def row_normal(values):
    average = jnp.mean(values, -1, keepdims=True)
    centred = values - average
    variance = jnp.mean(centred * centred, -1, keepdims=True)
    scale = lax.rsqrt(variance + EPSILON)
    return centred * scale, scale


def forward_kernel(
    count, recv, send, edge, wide, nodes, w_one, b_one, w_two, b_two, gain, shift,
    result, first, second, received, message,
    table, rows, stage, sems,
):
    step = pl.program_id(0)
    base = step * TILE
    width = nodes.shape[1]
    parts = width // LANES

    @pl.when(step == 0)
    def _():
        load_table(wide, table, stage, sems)

    gather_rows(recv, base, table, rows, parts)
    from_recv = read_rows(rows, 0, TILE, parts).astype(jnp.bfloat16)
    received[...] = from_recv
    lane = lax.broadcasted_iota(jnp.int32, (LANES, LANES), 1)
    chosen = []
    for i in range(TILE // LANES):
        column = jnp.broadcast_to(send[pl.ds(step * (TILE // LANES) + i, 1), :], (LANES, LANES)).T
        chosen.append(
            jnp.concatenate(
                [
                    jnp.where(column == lane + j * LANES, 1.0, 0.0).astype(jnp.bfloat16)
                    for j in range(nodes.shape[0] // LANES)
                ],
                axis=1,
            )
        )
    chosen = jnp.concatenate(chosen, axis=0)
    from_send = dot(chosen, nodes[...]).astype(jnp.bfloat16)
    pre = (
        dot(edge[...], w_one[:width])
        + dot(from_send, w_one[width : 2 * width])
        + dot(from_recv, w_one[2 * width :])
        + b_one[...]
    )
    first[...] = pre
    act = (pre * jax.nn.sigmoid(pre)).astype(jnp.bfloat16)
    post = dot(act, w_two[...]) + b_two[...]
    second[...] = post
    normal, _ = row_normal(post)
    branch = normal * gain[...] + shift[...]
    live = base + lax.broadcasted_iota(jnp.int32, (TILE, 1), 0) < count[0]
    outcome = edge[...].astype(jnp.float32) + jnp.where(live, branch, 0.0)
    result[...] = outcome
    message[...] = jnp.where(live, outcome, 0.0).astype(jnp.bfloat16)


def edge_forward(count, recv, send, edge, wide, nodes, w_one, b_one, w_two, b_two, gain, shift):
    edges, width = edge.shape
    steps = edges // TILE
    parts = width // LANES
    hold = pl.BlockSpec(memory_space=pltpu.VMEM)
    scalar = pl.BlockSpec(memory_space=pltpu.SMEM)
    tile = pl.BlockSpec((TILE, width), lambda i: (i, 0))
    return pl.pallas_call(
        forward_kernel,
        grid=(steps,),
        in_specs=[
            scalar, scalar, hold, tile,
            pl.BlockSpec(memory_space=pl.ANY), hold, hold, hold, hold, hold, hold, hold,
        ],
        out_specs=[tile] * 5,
        out_shape=[
            jax.ShapeDtypeStruct((edges, width), jnp.float32),
            jax.ShapeDtypeStruct((edges, width), jnp.float32),
            jax.ShapeDtypeStruct((edges, width), jnp.float32),
            jax.ShapeDtypeStruct((edges, width), jnp.bfloat16),
            jax.ShapeDtypeStruct((edges, width), jnp.bfloat16),
        ],
        scratch_shapes=[
            pltpu.VMEM((wide.shape[0] * parts, LANES), jnp.float32),
            pltpu.VMEM((TILE * parts, LANES), jnp.float32),
            pltpu.VMEM((2, CHUNK, width), jnp.bfloat16),
            pltpu.SemaphoreType.DMA((2,)),
        ],
        compiler_params=pltpu.CompilerParams(vmem_limit_bytes=VMEM_BYTES),
        cost_estimate=pl.CostEstimate(
            flops=20 * edges * width * width, bytes_accessed=40 * edges * width, transcendentals=2 * edges * width
        ),
        name="edge_forward",
    )(count, recv, send, edge, wide, nodes, w_one, b_one, w_two, b_two, gain, shift)


def backward_kernel(
    count, recv, send, cotangent, edge, received, first, second, wide, node_one, node_two, node_part, nodes, w_one, w_two, gain,
    grad, message, all_grads, vectors, sender_grad,
    table, rows, stage, sems, by_sender, grads, pass_sems,
):
    step = pl.program_id(0)
    base = step * TILE
    width = nodes.shape[1]
    parts = width // LANES

    first_node = node_one.shape[0]
    passed = (
        pltpu.make_async_copy(node_one, grads.at[pl.ds(4 * width, first_node)], pass_sems.at[0]),
        pltpu.make_async_copy(node_two, grads.at[pl.ds(4 * width + first_node, node_two.shape[0])], pass_sems.at[1]),
        pltpu.make_async_copy(grads, all_grads, pass_sems.at[2]),
    )

    @pl.when(step == 0)
    def _():
        passed[0].start()
        passed[1].start()
        load_table(wide, table, stage, sems)
        grads[: 4 * width] = jnp.zeros((4 * width, width), grads.dtype)
        vectors[...] = jnp.zeros_like(vectors)
        by_sender[...] = jnp.zeros_like(by_sender)

    gather_rows(recv, base, table, rows, parts)
    live = base + lax.broadcasted_iota(jnp.int32, (TILE, 1), 0) < count[0]
    upstream = cotangent[...].astype(jnp.float32) + jnp.where(live, read_rows(rows, 0, TILE, parts), 0.0)
    masked = jnp.where(live, upstream, 0.0)
    normal, scale = row_normal(second[...])
    vectors[2:3, :] += jnp.sum(masked * normal, 0, keepdims=True)
    vectors[3:4, :] += jnp.sum(masked, 0, keepdims=True)
    scaled = masked * gain[...]
    slope = jnp.mean(scaled * normal, -1, keepdims=True)
    grad_second = scale * (scaled - jnp.mean(scaled, -1, keepdims=True) - normal * slope)
    second_low = grad_second.astype(jnp.bfloat16)
    vectors[1:2, :] += jnp.sum(second_low.astype(jnp.float32), 0, keepdims=True)
    pre = first[...]
    logistic = jax.nn.sigmoid(pre)
    act = (pre * logistic).astype(jnp.bfloat16)
    grads[3 * width : 4 * width] += dot_left(act, second_low)
    grad_first = dot_right(second_low, w_two[...]) * (logistic * (1.0 + pre * (1.0 - logistic)))
    first_low = grad_first.astype(jnp.bfloat16)
    message[...] = first_low
    vectors[0:1, :] += jnp.sum(first_low.astype(jnp.float32), 0, keepdims=True)
    grads[:width] += dot_left(edge[...], first_low)
    grads[2 * width : 3 * width] += dot_left(received[...], first_low)
    node = lax.broadcasted_iota(jnp.int32, (nodes.shape[0], LANES), 0)
    chosen = jnp.concatenate(
        [
            jnp.where(node == send[pl.ds(step * (TILE // LANES) + i, 1), :], 1.0, 0.0).astype(jnp.bfloat16)
            for i in range(TILE // LANES)
        ],
        axis=1,
    )
    by_sender[...] += dot(chosen, first_low)
    grad[...] = upstream + dot_right(first_low, w_one[:width])

    @pl.when(step == pl.num_programs(0) - 1)
    def _():
        high, rest = split_low(by_sender[...])
        grads[width : 2 * width] = dot_left(nodes[...], high) + dot_left(nodes[...], rest)
        passed[0].wait()
        passed[1].wait()
        passed[2].start()
        middle = w_one[width : 2 * width]
        sender_grad[...] = node_part[...] + dot_right(high, middle) + dot_right(rest, middle)
        passed[2].wait()


def edge_backward(
    count, recv, send, cotangent, edge, received, first, second, wide, node_one, node_two, node_part, nodes,
    w_one, w_two, gain,
):
    edges, width = edge.shape
    steps = edges // TILE
    parts = width // LANES
    per_device = nodes.shape[0]
    hold = pl.BlockSpec(memory_space=pltpu.VMEM)
    scalar = pl.BlockSpec(memory_space=pltpu.SMEM)
    tile = pl.BlockSpec((TILE, width), lambda i: (i, 0))

    across = pl.BlockSpec(memory_space=pl.ANY)
    unit = 64 * lax.axis_size("blk")
    held = 4 * width + node_one.shape[0] + node_two.shape[0]
    padded = -(-held // unit) * unit

    def whole(rows):
        return pl.BlockSpec((rows, width), lambda i: (0, 0))

    return pl.pallas_call(
        backward_kernel,
        grid=(steps,),
        in_specs=[
            scalar, scalar, hold, tile, tile, tile, tile, tile,
            across, across, across, hold, hold, hold, hold, hold,
        ],
        out_specs=[
            tile, tile, across, whole(8), whole(per_device),
        ],
        out_shape=[
            jax.ShapeDtypeStruct((edges, width), jnp.float32),
            jax.ShapeDtypeStruct((edges, width), jnp.bfloat16),
            jax.ShapeDtypeStruct((padded, width), jnp.float32),
            jax.ShapeDtypeStruct((8, width), jnp.float32),
            jax.ShapeDtypeStruct((per_device, width), jnp.float32),
        ],
        scratch_shapes=[
            pltpu.VMEM((wide.shape[0] * parts, LANES), jnp.float32),
            pltpu.VMEM((TILE * parts, LANES), jnp.float32),
            pltpu.VMEM((2, CHUNK, width), jnp.bfloat16),
            pltpu.SemaphoreType.DMA((2,)),
            pltpu.VMEM((per_device, width), jnp.float32),
            pltpu.VMEM((padded, width), jnp.float32),
            pltpu.SemaphoreType.DMA((3,)),
        ],
        compiler_params=pltpu.CompilerParams(vmem_limit_bytes=VMEM_BYTES),
        cost_estimate=pl.CostEstimate(
            flops=24 * edges * width * width, bytes_accessed=40 * edges * width, transcendentals=2 * edges * width
        ),
        name="edge_backward",
    )(
        count, recv, send, cotangent, edge, received, first, second, wide, node_one, node_two,
        node_part, nodes, w_one, w_two, gain,
    )


MESH = pl.DeviceIdType.MESH
PIECES = 4
LOW = jnp.bfloat16
WIDE = jnp.float32


def places():
    groups = lax.axis_size("blk")
    group, sub = lax.axis_index("blk"), lax.axis_index("sub")
    odd = lax.rem(group, 2)
    along = groups // 2
    spot = group // 2
    beside = group + 1 - 2 * odd
    return dict(
        group=group,
        sub=sub,
        core=lax.rem(sub, 2),
        chip=sub // 2,
        odd=odd,
        spot=spot,
        along=along,
        sibling=sub + 1 - 2 * lax.rem(sub, 2),
        partner=lax.rem(sub + 2, 4),
        to_sibling=(group, sub + 1 - 2 * lax.rem(sub, 2)),
        to_partner=(group, lax.rem(sub + 2, 4)),
        to_beside=(beside, sub),
        to_onward=(lax.rem(group + 2 - 4 * odd + groups, groups), sub),
        to_source=(lax.rem(group - 2 + 4 * odd + groups, groups), sub),
        peers=[(2 * lax.rem(spot + k, along) + odd, sub) for k in range(1, along)],
        near=2 - 2 * odd,
        far=2 * odd,
    )


def meet(senders):
    barrier = pltpu.get_barrier_semaphore()
    for device in senders:
        pl.semaphore_signal(barrier, inc=1, device_id=device, device_id_type=MESH)
    pl.semaphore_wait(barrier, len(senders))


def meet_all():
    barrier = pltpu.get_barrier_semaphore()
    subs = lax.axis_size("sub")
    devices = lax.axis_size("blk") * subs
    here = lax.axis_index("blk") * subs + lax.axis_index("sub")

    def greet(k, carry):
        there = lax.rem(here + k, devices)
        pl.semaphore_signal(barrier, inc=1, device_id=(there // subs, lax.rem(there, subs)), device_id_type=MESH)
        return carry

    lax.fori_loop(1, devices, greet, 0)
    pl.semaphore_wait(barrier, devices - 1)


def remote(source, target, send, recv, device):
    return pltpu.make_async_remote_copy(
        src_ref=source, dst_ref=target, send_sem=send, recv_sem=recv, device_id=device, device_id_type=MESH
    )


def in_pieces(count, body):
    block = math.gcd(count, 128)

    def run(i, carry):
        body(pl.multiple_of(i * block, block), block)
        return carry

    lax.fori_loop(0, count // block, run, 0)


def reducer_scratch(rows, width, along):
    return [
        pltpu.VMEM((rows // 2, width), WIDE),
        pltpu.VMEM((rows // 2, width), WIDE),
        pltpu.VMEM((rows // 4, width), LOW),
        pltpu.VMEM((rows // 4, width), LOW),
        pltpu.VMEM((rows // 8, width), LOW),
        pltpu.VMEM((rows // 8, width), LOW),
        pltpu.VMEM((rows // 8, width), LOW),
        pltpu.VMEM((along - 1, rows // 8 // along, width), LOW),
        pltpu.SemaphoreType.DMA,
        pltpu.SemaphoreType.DMA((6,)),
        pltpu.SemaphoreType.DMA((6,)),
        pltpu.SemaphoreType.DMA((2, along - 1)),
        pltpu.SemaphoreType.DMA((2, along - 1)),
    ]


def reducer(at, grads, reduced, first, rows, swap, refs):
    (
        half, half_in, cross_out, cross_in, side_out, side_in, ring_out, ring_in,
        load_sem, step_send, step_recv, ring_send, ring_recv,
    ) = refs
    along, peers = at["along"], at["peers"]
    turns = [(at["chip"], at["to_partner"]), (at["odd"], at["to_beside"])]
    (bit_one, device_one), (bit_two, device_two) = turns[::-1] if swap else turns
    core, spot = at["core"], at["spot"]
    n_half, n_cross, n_side, n_ring = rows // 2, rows // 4, rows // 8, rows // 8 // along
    at_half = first + core * n_half
    at_cross = at_half + bit_one * n_cross
    at_side = at_cross + bit_two * n_side
    at_ring = at_side + spot * n_ring

    def span(start, count):
        return pl.ds(pl.multiple_of(start, 16), count)

    def step(kind):
        if kind == 0:
            source, target, device = grads.at[span(first + (1 - core) * n_half, n_half)], half_in, at["to_sibling"]
        elif kind == 1:
            source, target, device = cross_out, cross_in, device_one
        elif kind == 2:
            source, target, device = side_out, side_in, device_two
        else:
            start, count, device = {
                3: (at_side, n_side, device_two),
                4: (at_cross, n_cross, device_one),
                5: (at_half, n_half, at["to_sibling"]),
            }[kind]
            source = target = reduced.at[span(start, count)]
        return remote(source, target, step_send.at[kind], step_recv.at[kind], device)

    def ring(kind, k):
        if kind == 0:
            source = ring_out.at[span(lax.rem(spot + k, along) * n_ring, n_ring)]
            target = ring_in.at[k - 1]
        else:
            source = target = reduced.at[span(at_ring, n_ring)]
        return remote(source, target, ring_send.at[kind, k - 1], ring_recv.at[kind, k - 1], peers[k - 1])

    load = pltpu.make_async_copy(grads.at[span(at_half, n_half)], half, load_sem)

    def start():
        step(0).start()
        load.start()

    def add_half():
        load.wait()
        step(0).wait_recv()
        other = (1 - bit_one) * n_cross

        def part(i, block):
            here = pl.ds(pl.multiple_of(other + i, block), block)
            cross_out[pl.ds(i, block), :] = (half[here, :] + half_in[here, :]).astype(LOW)

        in_pieces(n_cross, part)
        step(1).start()

    def add_cross():
        mine, other = bit_one * n_cross, (1 - bit_two) * n_side
        step(1).wait_recv()

        def part(i, block):
            there = pl.ds(pl.multiple_of(other + i, block), block)
            here = pl.ds(pl.multiple_of(mine + other + i, block), block)
            side_out[pl.ds(i, block), :] = (half[here, :] + half_in[here, :] + cross_in[there, :].astype(WIDE)).astype(LOW)

        in_pieces(n_side, part)
        step(2).start()

    def add_side():
        mine, kept = bit_one * n_cross, bit_two * n_side
        step(2).wait_recv()

        def part(i, block):
            there = pl.ds(pl.multiple_of(kept + i, block), block)
            here = pl.ds(pl.multiple_of(mine + kept + i, block), block)
            flat = pl.ds(i, block)
            value = half[here, :] + half_in[here, :] + cross_in[there, :].astype(WIDE) + side_in[flat, :].astype(WIDE)
            half[here, :] = value
            ring_out[flat, :] = value.astype(LOW)

        in_pieces(n_side, part)
        for k in range(1, along):
            ring(0, k).start()

    def add_ring():
        value = half[span(bit_one * n_cross + bit_two * n_side + spot * n_ring, n_ring), :]
        for k in range(1, along):
            ring(0, k).wait_recv()
            value = value + ring_in[k - 1].astype(WIDE)
        reduced[span(at_ring, n_ring), :] = value.astype(LOW)
        for k in range(1, along):
            ring(1, k).start()

    def share_side():
        for k in range(1, along):
            ring(1, k).wait_recv()
        step(3).start()

    def share_cross():
        step(3).wait_recv()
        step(4).start()

    def share_half():
        step(4).wait_recv()
        step(5).start()

    def last():
        step(5).wait_recv()

    def drain():
        for kind in range(6):
            step(kind).wait_send()
        for k in range(1, along):
            ring(0, k).wait_send()
            ring(1, k).wait_send()

    return [start, add_half, add_cross, add_side, add_ring, share_side, share_cross, share_half, last, drain]


def vector_scratch(shape, along):
    return [
        pltpu.VMEM((4, *shape), WIDE),
        pltpu.VMEM((2 + along, *shape), WIDE),
        pltpu.SemaphoreType.DMA((2 + along,)),
        pltpu.SemaphoreType.DMA((2 + along,)),
    ]


def vector_reducer(at, vectors, reduced, refs):
    held, held_in, send_sems, recv_sems = refs
    along = at["along"]
    devices = (at["to_sibling"], at["to_partner"], at["to_beside"], *at["peers"])

    def move(kind):
        return remote(held.at[min(kind, 3)], held_in.at[kind], send_sems.at[kind], recv_sems.at[kind], devices[kind])

    def start():
        held[0] = vectors[...]
        move(0).start()

    def turn(kind):
        def run():
            move(kind).wait_recv()
            held[kind + 1] = held[kind] + held_in[kind]
            for k in range(kind + 1, kind + 2 if kind < 2 else 2 + along):
                move(k).start()

        return run

    def last():
        value = held[3]
        for k in range(3, 2 + along):
            move(k).wait_recv()
            value = value + held_in[k]
        reduced[...] = value
        for k in range(2 + along):
            move(k).wait_send()

    return [start, turn(0), turn(1), turn(2), last]


def both(streams):
    return [lambda steps=steps: [step() for step in steps] for steps in zip(*streams)]


def spread_moves(at, own, table, keep_sem, send_sems, recv_sems):
    sub, partner, near, far = at["sub"], at["partner"], at["near"], at["far"]
    to_sibling, to_partner, to_beside, to_onward = (
        at["to_sibling"], at["to_partner"], at["to_beside"], at["to_onward"]
    )
    size = own.shape[0] // PIECES

    def move(kind, piece):
        source, slot, device = {
            0: (None, (1, sub), to_partner),
            1: (None, (far, sub), to_beside),
            2: (None, (1, sub), to_sibling),
            3: ((1, partner), (far, partner), to_beside),
            4: ((1, partner), (1, partner), to_sibling),
            5: ((near, sub), (far, sub), to_onward),
            6: ((near, sub), (near, sub), to_sibling),
            7: ((near, partner), (far, partner), to_onward),
            8: ((near, partner), (near, partner), to_sibling),
            9: ((far, sub), (far, sub), to_sibling),
            10: ((far, partner), (far, partner), to_sibling),
        }[kind]
        source = own if source is None else table.at[source[0], source[1]]
        rows = pl.ds(piece * size, size)
        return remote(
            source.at[rows], table.at[slot[0], slot[1], rows],
            send_sems.at[kind, piece], recv_sems.at[kind, piece], device,
        )

    keep = pltpu.make_async_copy(own, table.at[1, sub], keep_sem)

    def start():
        for piece in range(PIECES):
            for kind in (0, 1, 2):
                move(kind, piece).start()
        keep.start()

    def relay(arrived, kinds, piece):
        move(arrived, piece).wait_recv()
        for kind in kinds:
            move(kind, piece).start()

    def one(piece):
        relay(0, (3, 4), piece)
        relay(1, (5, 6), piece)

    def two(piece):
        relay(3, (7, 8), piece)
        relay(5, (9,), piece)

    def three(piece):
        relay(7, (10,), piece)

    def drain():
        for kind in range(11):
            for piece in range(PIECES):
                if kind in (2, 4, 6, 8, 9, 10):
                    move(kind, piece).wait_recv()
                move(kind, piece).wait_send()
        keep.wait()

    return start, one, two, three, drain


def spread_scratch():
    return [
        pltpu.SemaphoreType.DMA,
        pltpu.SemaphoreType.DMA((11, PIECES)),
        pltpu.SemaphoreType.DMA((11, PIECES)),
    ]


def spread_kernel(own, table, *refs):
    at = places()
    meet((at["to_sibling"], at["to_partner"], at["to_beside"], at["to_source"]))
    start, one, two, three, drain = spread_moves(at, own, table, *refs)
    start()
    for stage in (one, two, three):
        for piece in range(PIECES):
            stage(piece)
    drain()


def spread(own, collective):
    rows, width = own.shape
    return pl.pallas_call(
        spread_kernel,
        in_specs=[pl.BlockSpec(memory_space=pltpu.VMEM)],
        out_specs=pl.BlockSpec(memory_space=pl.ANY),
        out_shape=jax.ShapeDtypeStruct((3, 4, rows, width), own.dtype),
        scratch_shapes=spread_scratch(),
        compiler_params=pltpu.CompilerParams(collective_id=collective, has_side_effects=True),
        name="spread_rows",
    )(own).reshape(12 * rows, width)


HALVES = 2
ORDER = (
    (0, 1, 0), (0, 1, 1), (1, 1, 0), (0, 0, 0), (1, 1, 1), (0, 0, 1),
    (1, 0, 0), (2, 1, 0), (1, 0, 1), (2, 1, 1), (2, 0, 0), (2, 0, 1),
)


def collect_scratch(rows, width, edges):
    return [
        pltpu.VMEM((edges, width), LOW),
        pltpu.VMEM((2, 3, 2, rows, width), WIDE),
        pltpu.VMEM((3, 2, rows, width), WIDE),
        pltpu.VMEM((2, rows, width), LOW),
        pltpu.VMEM((2, rows, width), LOW),
        pltpu.VMEM((2, rows, width), LOW),
        pltpu.VMEM((2, rows, width), LOW),
        pltpu.VMEM((rows, width), LOW),
        pltpu.VMEM((rows, width), LOW),
        pltpu.SemaphoreType.DMA,
        pltpu.SemaphoreType.DMA((3, 2, HALVES)),
        pltpu.SemaphoreType.DMA((3, 2, HALVES)),
        pltpu.SemaphoreType.DMA((5, PIECES)),
        pltpu.SemaphoreType.DMA((5, PIECES)),
    ]


def collect_moves(at, index, messages, out, refs):
    (
        held, parts, landed, far_out, far_in, near_out, near_in, pair_out, pair_in,
        load_sem, give_sems, take_sems, send_sems, recv_sems,
    ) = refs
    sub, partner, sibling = at["sub"], at["partner"], at["sibling"]
    rows = out.shape[0]
    size = rows // PIECES
    part_rows = rows // HALVES
    load = pltpu.make_async_copy(messages, held, load_sem)

    def piece_of(ref, piece):
        return ref.at[pl.ds(piece * size, size)]

    def give(role, side, half):
        span = pl.ds(pl.multiple_of(half * part_rows, part_rows), part_rows)
        return remote(
            parts.at[0, role, side, span], landed.at[role, side, span],
            give_sems.at[role, side, half], take_sems.at[role, side, half], at["to_sibling"],
        )

    def hop(kind, piece):
        source, target, device = {
            0: (far_out.at[0], far_in.at[0], at["to_source"]),
            1: (far_out.at[1], far_in.at[1], at["to_source"]),
            2: (near_out.at[0], near_in.at[0], at["to_beside"]),
            3: (near_out.at[1], near_in.at[1], at["to_beside"]),
            4: (pair_out, pair_in, at["to_partner"]),
        }[kind]
        return remote(
            piece_of(source, piece), piece_of(target, piece),
            send_sems.at[kind, piece], recv_sems.at[kind, piece], device,
        )

    def add_messages(step):
        def pick(column):
            return lax.rem(sum(int(item[column]) << (2 * i) for i, item in enumerate(ORDER)) >> (2 * step), 4)

        role, side, half = pick(0), pick(1), pick(2)
        relation = jnp.where(role == 0, at["far"], jnp.where(role == 1, at["near"], 1))
        span = pl.ds(pl.multiple_of(half * part_rows, part_rows), part_rows)

        def whose(w, carry):
            first = jnp.where(w == 0, sibling, sub)
            target = lax.rem(first + 2 * side, 4)
            base = (relation * 4 + target) * rows + half * part_rows
            node = lax.broadcasted_iota(jnp.int32, (part_rows, LANES), 0) + base
            chosen = jnp.concatenate(
                [jnp.where(node == index[j : j + 1, :], 1.0, 0.0).astype(LOW) for j in range(index.shape[0])], axis=1
            )
            parts[w, role, side, span, :] = dot(chosen, held[...])
            return carry

        lax.fori_loop(0, 2, whose, 0)
        give(role, side, half).start()

    def local(role, side, piece):
        span = pl.ds(piece * size, size)
        return parts[1, role, side, span, :] + landed[role, side, span, :]

    def arrived(kind, ref, piece):
        hop(kind, piece).wait_recv()
        return ref[pl.ds(piece * size, size), :].astype(WIDE)

    def pieces(half):
        return range(half * PIECES // HALVES, (half + 1) * PIECES // HALVES)

    def far_step(side, half):
        give(0, side, half).wait_recv()
        for piece in pieces(half):
            far_out[side, pl.ds(piece * size, size), :] = local(0, side, piece).astype(LOW)
            hop(side, piece).start()

    def near_step(side, half):
        give(1, side, half).wait_recv()
        for piece in pieces(half):
            value = local(1, side, piece) + arrived(side, far_in.at[side], piece)
            near_out[side, pl.ds(piece * size, size), :] = value.astype(LOW)
            hop(2 + side, piece).start()

    def pair_step(half):
        give(2, 1, half).wait_recv()
        for piece in pieces(half):
            value = local(2, 1, piece) + arrived(3, near_in.at[1], piece)
            pair_out[pl.ds(piece * size, size), :] = value.astype(LOW)
            hop(4, piece).start()

    def last_step(half):
        give(2, 0, half).wait_recv()
        for piece in pieces(half):
            value = local(2, 0, piece) + arrived(2, near_in.at[0], piece) + arrived(4, pair_in, piece)
            out[pl.ds(piece * size, size), :] = value

    def drain():
        for item in ORDER:
            give(*item).wait_send()
        for kind in range(5):
            for piece in range(PIECES):
                hop(kind, piece).wait_send()

    events = {
        1: [lambda: far_step(1, 0)],
        2: [lambda: far_step(1, 1)],
        3: [lambda: near_step(1, 0)],
        4: [lambda: far_step(0, 0)],
        5: [lambda: near_step(1, 1), lambda: far_step(0, 1)],
        7: [lambda: near_step(0, 0), lambda: pair_step(0)],
        9: [lambda: near_step(0, 1), lambda: pair_step(1)],
    }

    def run(more):
        def step(i, carry):
            add_messages(i)
            for k in sorted(set(events) | set(more)):
                @pl.when(i == k)
                def _():
                    for event in events.get(k, []) + more.get(k, []):
                        event()

            return carry

        lax.fori_loop(0, len(ORDER), step, 0)
        for half in range(HALVES):
            last_step(half)

    return load, run, drain


def collect_kernel(index, messages, out, *refs):
    at = places()
    load, run, drain = collect_moves(at, index, messages, out, refs)
    load.start()
    meet((at["to_sibling"], at["to_partner"], at["to_beside"], at["to_onward"]))
    load.wait()
    run({})
    drain()


def collect(index, messages, rows, collective):
    edges, width = messages.shape
    return pl.pallas_call(
        collect_kernel,
        in_specs=[pl.BlockSpec(memory_space=pltpu.VMEM), pl.BlockSpec(memory_space=pl.ANY)],
        out_specs=pl.BlockSpec(memory_space=pltpu.VMEM),
        out_shape=jax.ShapeDtypeStruct((rows, width), WIDE),
        scratch_shapes=collect_scratch(rows, width, edges),
        compiler_params=pltpu.CompilerParams(
            collective_id=collective, has_side_effects=True, vmem_limit_bytes=VMEM_BYTES
        ),
        name="collect_sums",
    )(index.reshape(edges // LANES, LANES), messages)


def exchange_scratch(rows, width, devices):
    slab = width // devices * (rows // LANES)
    return [
        pltpu.VMEM((devices * slab, LANES), WIDE),
        pltpu.VMEM((devices * slab, LANES), LOW),
        pltpu.VMEM((devices, slab, LANES), LOW),
        pltpu.VMEM((slab, LANES), WIDE),
        pltpu.SemaphoreType.DMA((devices - 1,)),
        pltpu.SemaphoreType.DMA((devices - 1,)),
    ]


def exchange_moves(residual, out, refs):
    flat, packed, landed, opened, send_sems, recv_sems = refs
    subs = lax.axis_size("sub")
    devices = lax.axis_size("blk") * subs
    here = lax.axis_index("blk") * subs + lax.axis_index("sub")
    slab = landed.shape[1]
    channels = out.shape[0]
    parts = slab // channels
    nodes = parts * LANES

    def move(k):
        there = lax.rem(here + k, devices)
        return remote(
            packed.at[pl.ds(pl.multiple_of(there * slab, slab), slab)], landed.at[here],
            send_sems.at[k - 1], recv_sems.at[k - 1], (there // subs, lax.rem(there, subs)),
        )

    def start(values):
        lay_rows(flat, 0, values.T)

        def cast(i, block):
            packed[pl.ds(i, block), :] = flat[pl.ds(i, block), :].astype(LOW)

        in_pieces(flat.shape[0], cast)

        def send(k, carry):
            move(k).start()
            return carry

        lax.fori_loop(1, devices, send, 0)

    def open_slab(source, device):
        opened[...] = source.astype(WIDE)
        for j in range(parts):
            columns = pl.ds(pl.multiple_of(device * nodes + j * LANES, LANES), LANES)
            out[:, columns] = residual[:, columns] + opened[pl.ds(j, channels, stride=parts), :]

    def last():
        open_slab(packed[pl.ds(pl.multiple_of(here * slab, slab), slab), :], here)

        def take(k, carry):
            move(k).wait_recv()
            device = lax.rem(here - k + devices, devices)
            open_slab(landed[device], device)
            return carry

        lax.fori_loop(1, devices, take, 0)

        def sent(k, carry):
            move(k).wait_send()
            return carry

        lax.fori_loop(1, devices, sent, 0)

    return start, last


def finish_kernel(
    cut, index, messages, grads, vectors, node_part, weight, residual, node_grad, reduced, reduced_vectors, total, *refs
):
    at = places()
    sizes = len(reducer_scratch(64, 128, 2))
    count = len(collect_scratch(64, 128, 64))
    load, run, drain = collect_moves(at, index, messages, total, refs[:count])
    load.start()
    meet_all()
    refs = refs[count:]
    steps = both([
        reducer(at, grads, reduced, 0, cut, False, refs[:sizes]),
        reducer(at, grads, reduced, cut, grads.shape[0] - cut, True, refs[sizes : 2 * sizes]),
    ])
    refs = refs[2 * sizes :]
    vector_steps = vector_reducer(at, vectors, reduced_vectors, refs[:4])
    exchange, receive = exchange_moves(residual, node_grad, refs[4:])
    steps[0]()
    vector_steps[0]()
    load.wait()
    run({
        1: [steps[1], vector_steps[1]],
        4: [steps[2], vector_steps[2]],
        6: [steps[3], vector_steps[3]],
        8: [steps[4]],
        10: [steps[5]],
    })
    high, rest = split_low(total[...])
    exchange(node_part[...] + dot_right(high, weight[...]) + dot_right(rest, weight[...]))
    for step in steps[6:8]:
        step()
    receive()
    steps[8]()
    vector_steps[4]()
    drain()
    steps[9]()


def finish(index, messages, grads, vectors, node_part, weight, residual, cut, collective):
    rows, width = node_part.shape
    edges = messages.shape[0]
    along = lax.axis_size("blk") // 2
    devices = lax.axis_size("blk") * lax.axis_size("sub")
    hold = pl.BlockSpec(memory_space=pltpu.VMEM)
    across = pl.BlockSpec(memory_space=pl.ANY)
    return pl.pallas_call(
        functools.partial(finish_kernel, cut),
        grid=(1,),
        in_specs=[
            hold, across, across, hold, hold, pl.BlockSpec((width, width), lambda i: (2, 0)), hold,
        ],
        out_specs=[hold] * 3,
        out_shape=[
            jax.ShapeDtypeStruct(residual.shape, WIDE),
            jax.ShapeDtypeStruct(grads.shape, LOW),
            jax.ShapeDtypeStruct(vectors.shape, WIDE),
        ],
        scratch_shapes=[
            pltpu.VMEM((rows, width), WIDE),
            *collect_scratch(rows, width, edges),
            *reducer_scratch(cut, width, along),
            *reducer_scratch(grads.shape[0] - cut, width, along),
            *vector_scratch(vectors.shape, along),
            *exchange_scratch(rows, width, devices),
        ],
        compiler_params=pltpu.CompilerParams(
            collective_id=collective, has_side_effects=True, vmem_limit_bytes=VMEM_BYTES
        ),
        name="finish_sums",
    )(index.reshape(edges // LANES, LANES), messages, grads, vectors, node_part, weight, residual)


def scatter_scratch(channels, nodes, devices):
    slab = channels * (nodes // LANES)
    return [
        pltpu.VMEM((devices * slab, LANES), WIDE),
        pltpu.VMEM((devices * slab, LANES), LOW),
        pltpu.VMEM((devices, slab, LANES), LOW),
        pltpu.VMEM((slab, LANES), WIDE),
        pltpu.VMEM((nodes // LANES * devices * channels, LANES), WIDE),
        pltpu.SemaphoreType.DMA((devices - 1,)),
        pltpu.SemaphoreType.DMA((devices - 1,)),
    ]


def scatter_moves(shard, refs):
    flat, packed, landed, opened, square, send_sems, recv_sems = refs
    subs = lax.axis_size("sub")
    devices = lax.axis_size("blk") * subs
    here = lax.axis_index("blk") * subs + lax.axis_index("sub")
    slab = landed.shape[1]
    channels = shard.shape[0]
    parts = slab // channels
    nodes = parts * LANES

    def move(k):
        there = lax.rem(here + k, devices)
        return remote(
            packed.at[pl.ds(pl.multiple_of(there * slab, slab), slab)], landed.at[here],
            send_sems.at[k - 1], recv_sems.at[k - 1], (there // subs, lax.rem(there, subs)),
        )

    def start():
        def pack(k, carry):
            device = lax.rem(here + k, devices)
            rows = pl.ds(pl.multiple_of(device * slab, slab), slab)
            for j in range(parts):
                columns = pl.ds(pl.multiple_of(device * nodes + j * LANES, LANES), LANES)
                flat[pl.ds(device * slab + j, channels, stride=parts), :] = shard[:, columns]
            packed[rows, :] = flat[rows, :].astype(LOW)
            return carry

        def send(k, carry):
            pack(k, carry)
            move(k).start()
            return carry

        lax.fori_loop(1, devices, send, 0)
        pack(0, 0)

    def open_slab(source, device):
        opened[...] = source.astype(WIDE)
        for j in range(parts):
            rows = pl.ds(pl.multiple_of((j * devices + device) * channels, channels), channels)
            square[rows, :] = opened[pl.ds(j, channels, stride=parts), :]

    def last(rows):
        open_slab(packed[pl.ds(pl.multiple_of(here * slab, slab), slab), :], here)

        def take(k, carry):
            move(k).wait_recv()
            device = lax.rem(here - k + devices, devices)
            open_slab(landed[device], device)
            return carry

        lax.fori_loop(1, devices, take, 0)
        width = devices * channels
        for j in range(parts):
            rows[j * LANES : (j + 1) * LANES, :] = square[j * width : (j + 1) * width, :].T.astype(LOW)

    def drain():
        def sent(k, carry):
            move(k).wait_send()
            return carry

        lax.fori_loop(1, devices, sent, 0)

    return start, last, drain


def begin_kernel(
    shard, later, senders, receivers, own, table, later_out, send_local, recv_wide, held, held_sem, *refs
):
    at = places()
    fetch = pltpu.make_async_copy(later, held, held_sem)
    fetch.start()
    meet_all()
    start, last, drain = scatter_moves(shard, refs[3:])
    start()
    last(own)
    begin, one, two, three, end = spread_moves(at, own, table, *refs[:3])
    begin()
    rows = own.shape[0]
    groups, subs = lax.axis_size("blk"), lax.axis_size("sub")
    send_local[...] = senders[...] - (at["group"] * subs + at["sub"]) * rows
    relative = lax.rem(receivers[...] // (rows * subs) - at["group"] + 1 + groups, groups)
    recv_wide[...] = relative * (rows * subs) + lax.rem(receivers[...], rows * subs)
    fetch.wait()
    give = pltpu.make_async_copy(held, later_out, held_sem)
    give.start()
    drain()
    for stage in (one, two, three):
        for piece in range(PIECES):
            stage(piece)
    give.wait()
    end()


def begin(shard, later, senders, receivers, rows, collective):
    channels, nodes = shard.shape
    devices = lax.axis_size("blk") * lax.axis_size("sub")
    width = channels * devices
    hold = pl.BlockSpec(memory_space=pltpu.VMEM)
    across = pl.BlockSpec(memory_space=pl.ANY)
    lines = (senders.shape[0] // LANES, LANES)
    own, table, later, send_local, recv_wide = pl.pallas_call(
        begin_kernel,
        in_specs=[hold, across, hold, hold],
        out_specs=[hold, across, across, hold, hold],
        out_shape=[
            jax.ShapeDtypeStruct((rows, width), LOW),
            jax.ShapeDtypeStruct((3, 4, rows, width), LOW),
            jax.ShapeDtypeStruct(later.shape, later.dtype),
            jax.ShapeDtypeStruct(lines, jnp.int32),
            jax.ShapeDtypeStruct(lines, jnp.int32),
        ],
        scratch_shapes=[
            pltpu.VMEM(later.shape, later.dtype),
            pltpu.SemaphoreType.DMA,
            *spread_scratch(),
            *scatter_scratch(channels, rows, devices),
        ],
        compiler_params=pltpu.CompilerParams(
            collective_id=collective, has_side_effects=True, vmem_limit_bytes=VMEM_BYTES
        ),
        name="begin_rows",
    )(shard, later, senders.reshape(lines), receivers.reshape(lines))
    return own, table.reshape(12 * rows, width), later, send_local, recv_wide


def shards(
    node_input,
    edge_input,
    senders,
    receivers,
    edge_count,
    edge_w_one,
    edge_b_one,
    edge_w_two,
    edge_b_two,
    edge_gain,
    edge_shift,
    node_w_one,
    node_b_one,
    node_w_two,
    node_b_two,
    node_gain,
    node_shift,
    node_cotangent,
    edge_cotangent,
):
    groups = lax.axis_size("blk")
    sub_count = lax.axis_size("sub")
    width = edge_input.shape[1]
    per_device = node_input.shape[1] // (groups * sub_count)
    node_low, wide_low, cotangent_later, send_local, recv_wide = begin(
        node_input, node_cotangent, senders, receivers, per_device, 0
    )
    node_upstream = to_nodes(cotangent_later).T
    recv_list = recv_wide.reshape(-1)
    edge_result, first_pre, second_pre, received, messages = edge_forward(
        edge_count, recv_list, send_local, edge_input, wide_low, node_low,
        edge_w_one, edge_b_one[None], edge_w_two, edge_b_two[None], edge_gain[None], edge_shift[None],
    )
    gathered = collect(recv_list, messages, per_device, 1)
    joined = jnp.concatenate([node_low, gathered.astype(jnp.bfloat16)], axis=1)
    third_pre = matmul(joined, node_w_one) + node_b_one
    third_act = jax.nn.silu(third_pre).astype(jnp.bfloat16)
    fourth_pre = matmul(third_act, node_w_two) + node_b_two
    node_branch, node_norm_back = jax.vjp(norm_apply, fourth_pre, node_gain, node_shift)
    grad_fourth, grad_node_gain, grad_node_shift = node_norm_back(node_upstream)
    fourth_low = grad_fourth.astype(jnp.bfloat16)
    grad_node_w_two = left_matmul(third_act, fourth_low)
    grad_node_b_two = jnp.sum(fourth_low.astype(jnp.float32), 0)
    grad_third = right_matmul(fourth_low, node_w_two) * silu_slope(third_pre)
    third_low = grad_third.astype(jnp.bfloat16)
    grad_node_w_one = left_matmul(joined, third_low)
    grad_node_b_one = jnp.sum(third_low.astype(jnp.float32), 0)
    grad_joined = right_matmul(third_low, node_w_one)
    grad_gathered = grad_joined[:, width:]
    wide_grad = spread(grad_gathered.astype(jnp.bfloat16), 2)
    node_out = node_input + to_channels(node_branch.T)
    edge_grad, messages, grads, vectors, node_part = edge_backward(
        edge_count, recv_list, send_local, edge_cotangent, edge_input, received, first_pre, second_pre,
        wide_grad, grad_node_w_one, grad_node_w_two, grad_joined[:, :width], node_low, edge_w_one, edge_w_two,
        edge_gain[None],
    )
    node_vectors = jnp.stack([grad_node_b_one, grad_node_b_two, grad_node_gain, grad_node_shift])
    node_grad, summed, vectors = finish(
        recv_list, messages, grads, jnp.concatenate([vectors[:4], node_vectors]), node_part, edge_w_one,
        node_cotangent, 4 * width, 3,
    )
    summed = summed.astype(jnp.float32)
    return (
        node_out,
        edge_result,
        node_grad,
        edge_grad,
        summed[: 3 * width],
        vectors[0],
        summed[3 * width : 4 * width],
        vectors[1],
        vectors[2],
        vectors[3],
        summed[4 * width : 6 * width],
        vectors[4],
        summed[6 * width : 7 * width],
        vectors[5],
        vectors[6],
        vectors[7],
    )


def solution(mesh):
    placed = (
        P(("blk", "sub"), None),
        P(("blk", "sub"), None),
        P(("blk", "sub")),
        P(("blk", "sub")),
        P(("blk", "sub")),
        P(),
        P(),
        P(),
        P(),
        P(),
        P(),
        P(),
        P(),
        P(),
        P(),
        P(),
        P(),
        P(("blk", "sub"), None),
        P(("blk", "sub"), None),
    )
    return jax.shard_map(
        shards,
        mesh=mesh,
        in_specs=placed,
        out_specs=(
            P(("blk", "sub"), None),
            P(("blk", "sub"), None),
            P(("blk", "sub"), None),
            P(("blk", "sub"), None),
            P(),
            P(),
            P(),
            P(),
            P(),
            P(),
            P(),
            P(),
            P(),
            P(),
            P(),
            P(),
        ),
        check_vma=False,
    )
```

```python
import math

import jax
import jax.numpy as jnp
from jax import lax
from jax.experimental import pallas as pl
from jax.experimental.pallas import tpu as pltpu
from jax.sharding import PartitionSpec as P

EPSILON = 1e-05


def to_nodes(channels):
    return lax.all_to_all(channels, ("blk", "sub"), split_axis=1, concat_axis=0, tiled=True)


TILE = 512
CHUNK = 512
LANES = 128
VMEM_BYTES = 60 * 2**20


def dot(left, right):
    return jnp.dot(left, right, preferred_element_type=jnp.float32)


def dot_left(left, right):
    return lax.dot_general(
        left, right, (((0,), (0,)), ((), ())), preferred_element_type=jnp.float32
    )


def dot_right(left, right):
    return lax.dot_general(
        left, right, (((1,), (1,)), ((), ())), preferred_element_type=jnp.float32
    )


def split_low(values):
    high = values.astype(jnp.bfloat16)
    return high, (values - high.astype(jnp.float32)).astype(jnp.bfloat16)


def lay_rows(target, start, values):
    count, width = values.shape
    parts = width // LANES
    for j in range(parts):
        target[pl.ds(start * parts + j, count, stride=parts), :] = values[:, j * LANES : (j + 1) * LANES]


def read_rows(source, start, count, parts):
    return jnp.concatenate(
        [source[pl.ds(start * parts + j, count, stride=parts), :] for j in range(parts)], axis=1
    )


def load_table(wide, table, stage, sems):
    steps = wide.shape[0] // CHUNK

    def fetch(i, slot):
        return pltpu.make_async_copy(wide.at[pl.ds(i * CHUNK, CHUNK)], stage.at[slot], sems.at[slot])

    fetch(0, 0).start()

    def body(i, carry):
        slot = lax.rem(i, 2)

        @pl.when(i + 1 < steps)
        def _():
            fetch(i + 1, 1 - slot).start()

        fetch(i, slot).wait()

        def piece(k, carry):
            values = stage[slot, pl.ds(k * 64, 64), :].astype(jnp.float32)
            lay_rows(table, i * CHUNK + k * 64, values)
            return carry

        return lax.fori_loop(0, CHUNK // 64, piece, carry)

    lax.fori_loop(0, steps, body, 0)


def gather_rows(index, base, table, rows, parts):
    count = rows.shape[0] // parts

    def body(i, carry):
        for u in range(16):
            slot = i * 16 + u
            place = index[base + slot]
            rows[pl.ds(pl.multiple_of(slot * parts, parts), parts), :] = table[
                pl.ds(pl.multiple_of(place * parts, parts), parts), :
            ]
        return carry

    lax.fori_loop(0, count // 16, body, 0)


def row_normal(values):
    average = jnp.mean(values, -1, keepdims=True)
    centred = values - average
    variance = jnp.mean(centred * centred, -1, keepdims=True)
    scale = lax.rsqrt(variance + EPSILON)
    return centred * scale, scale


def forward_kernel(
    count, recv, send, edge, wide, nodes, w_one, b_one, w_two, b_two, gain, shift,
    result, first, second, received, message,
    table, rows, stage, sems,
):
    step = pl.program_id(0)
    base = step * TILE
    width = nodes.shape[1]
    parts = width // LANES

    @pl.when(step == 0)
    def _():
        load_table(wide, table, stage, sems)

    gather_rows(recv, base, table, rows, parts)
    from_recv = read_rows(rows, 0, TILE, parts).astype(jnp.bfloat16)
    received[...] = from_recv
    lane = lax.broadcasted_iota(jnp.int32, (LANES, LANES), 1)
    chosen = []
    for i in range(TILE // LANES):
        column = jnp.broadcast_to(send[pl.ds(step * (TILE // LANES) + i, 1), :], (LANES, LANES)).T
        chosen.append(
            jnp.concatenate(
                [
                    jnp.where(column == lane + j * LANES, 1.0, 0.0).astype(jnp.bfloat16)
                    for j in range(nodes.shape[0] // LANES)
                ],
                axis=1,
            )
        )
    chosen = jnp.concatenate(chosen, axis=0)
    from_send = dot(chosen, nodes[...]).astype(jnp.bfloat16)
    pre = (
        dot(edge[...], w_one[:width])
        + dot(from_send, w_one[width : 2 * width])
        + dot(from_recv, w_one[2 * width :])
        + b_one[...]
    )
    first[...] = pre
    act = (pre * jax.nn.sigmoid(pre)).astype(jnp.bfloat16)
    post = dot(act, w_two[...]) + b_two[...]
    second[...] = post
    normal, _ = row_normal(post)
    branch = normal * gain[...] + shift[...]
    live = base + lax.broadcasted_iota(jnp.int32, (TILE, 1), 0) < count[0]
    outcome = edge[...].astype(jnp.float32) + jnp.where(live, branch, 0.0)
    result[...] = outcome
    message[...] = jnp.where(live, outcome, 0.0).astype(jnp.bfloat16)


def edge_forward(count, recv, send, edge, wide, nodes, w_one, b_one, w_two, b_two, gain, shift):
    edges, width = edge.shape
    steps = edges // TILE
    parts = width // LANES
    hold = pl.BlockSpec(memory_space=pltpu.VMEM)
    scalar = pl.BlockSpec(memory_space=pltpu.SMEM)
    tile = pl.BlockSpec((TILE, width), lambda i: (i, 0))
    return pl.pallas_call(
        forward_kernel,
        grid=(steps,),
        in_specs=[
            scalar, scalar, hold, tile,
            pl.BlockSpec(memory_space=pl.ANY), hold, hold, hold, hold, hold, hold, hold,
        ],
        out_specs=[tile] * 5,
        out_shape=[
            jax.ShapeDtypeStruct((edges, width), jnp.float32),
            jax.ShapeDtypeStruct((edges, width), jnp.float32),
            jax.ShapeDtypeStruct((edges, width), jnp.float32),
            jax.ShapeDtypeStruct((edges, width), jnp.bfloat16),
            jax.ShapeDtypeStruct((edges, width), jnp.bfloat16),
        ],
        scratch_shapes=[
            pltpu.VMEM((wide.shape[0] * parts, LANES), jnp.float32),
            pltpu.VMEM((TILE * parts, LANES), jnp.float32),
            pltpu.VMEM((2, CHUNK, width), jnp.bfloat16),
            pltpu.SemaphoreType.DMA((2,)),
        ],
        compiler_params=pltpu.CompilerParams(vmem_limit_bytes=VMEM_BYTES),
        cost_estimate=pl.CostEstimate(
            flops=20 * edges * width * width, bytes_accessed=40 * edges * width, transcendentals=2 * edges * width
        ),
        name="edge_forward",
    )(count, recv, send, edge, wide, nodes, w_one, b_one, w_two, b_two, gain, shift)


def backward_kernel(
    count, recv, send, cotangent, edge, received, first, second, wide, node_part, nodes, w_one, w_two, gain,
    grad, message, all_grads, vectors, sender_grad,
    table, rows, stage, sems, by_sender, grads, give_sem,
):
    step = pl.program_id(0)
    base = step * TILE
    width = nodes.shape[1]
    parts = width // LANES

    @pl.when(step == 0)
    def _():
        load_table(wide, table, stage, sems)
        grads[...] = jnp.zeros_like(grads)
        vectors[...] = jnp.zeros_like(vectors)
        by_sender[...] = jnp.zeros_like(by_sender)

    gather_rows(recv, base, table, rows, parts)
    live = base + lax.broadcasted_iota(jnp.int32, (TILE, 1), 0) < count[0]
    upstream = cotangent[...].astype(jnp.float32) + jnp.where(live, read_rows(rows, 0, TILE, parts), 0.0)
    masked = jnp.where(live, upstream, 0.0)
    normal, scale = row_normal(second[...])
    vectors[2:3, :] += jnp.sum(masked * normal, 0, keepdims=True)
    vectors[3:4, :] += jnp.sum(masked, 0, keepdims=True)
    scaled = masked * gain[...]
    slope = jnp.mean(scaled * normal, -1, keepdims=True)
    grad_second = scale * (scaled - jnp.mean(scaled, -1, keepdims=True) - normal * slope)
    second_low = grad_second.astype(jnp.bfloat16)
    vectors[1:2, :] += jnp.sum(second_low.astype(jnp.float32), 0, keepdims=True)
    pre = first[...]
    logistic = jax.nn.sigmoid(pre)
    act = (pre * logistic).astype(jnp.bfloat16)
    grads[3 * width : 4 * width] += dot_left(act, second_low)
    grad_first = dot_right(second_low, w_two[...]) * (logistic * (1.0 + pre * (1.0 - logistic)))
    first_low = grad_first.astype(jnp.bfloat16)
    message[...] = first_low
    vectors[0:1, :] += jnp.sum(first_low.astype(jnp.float32), 0, keepdims=True)
    grads[:width] += dot_left(edge[...], first_low)
    grads[2 * width : 3 * width] += dot_left(received[...], first_low)
    node = lax.broadcasted_iota(jnp.int32, (nodes.shape[0], LANES), 0)
    chosen = jnp.concatenate(
        [
            jnp.where(node == send[pl.ds(step * (TILE // LANES) + i, 1), :], 1.0, 0.0).astype(jnp.bfloat16)
            for i in range(TILE // LANES)
        ],
        axis=1,
    )
    by_sender[...] += dot(chosen, first_low)
    grad[...] = upstream + dot_right(first_low, w_one[:width])

    @pl.when(step == pl.num_programs(0) - 1)
    def _():
        high, rest = split_low(by_sender[...])
        grads[width : 2 * width] = dot_left(nodes[...], high) + dot_left(nodes[...], rest)
        give = pltpu.make_async_copy(grads, all_grads, give_sem)
        give.start()
        middle = w_one[width : 2 * width]
        sender_grad[...] = node_part[...] + dot_right(high, middle) + dot_right(rest, middle)
        give.wait()


def edge_backward(
    count, recv, send, cotangent, edge, received, first, second, wide, node_part, nodes, w_one, w_two, gain
):
    edges, width = edge.shape
    steps = edges // TILE
    parts = width // LANES
    per_device = nodes.shape[0]
    hold = pl.BlockSpec(memory_space=pltpu.VMEM)
    scalar = pl.BlockSpec(memory_space=pltpu.SMEM)
    tile = pl.BlockSpec((TILE, width), lambda i: (i, 0))

    across = pl.BlockSpec(memory_space=pl.ANY)

    def whole(rows):
        return pl.BlockSpec((rows, width), lambda i: (0, 0))

    return pl.pallas_call(
        backward_kernel,
        grid=(steps,),
        in_specs=[
            scalar, scalar, hold, tile, tile, tile, tile, tile,
            across, hold, hold, hold, hold, hold,
        ],
        out_specs=[
            tile, tile, across, whole(8), whole(per_device),
        ],
        out_shape=[
            jax.ShapeDtypeStruct((edges, width), jnp.float32),
            jax.ShapeDtypeStruct((edges, width), jnp.bfloat16),
            jax.ShapeDtypeStruct((4 * width, width), jnp.float32),
            jax.ShapeDtypeStruct((8, width), jnp.float32),
            jax.ShapeDtypeStruct((per_device, width), jnp.float32),
        ],
        scratch_shapes=[
            pltpu.VMEM((wide.shape[0] * parts, LANES), jnp.float32),
            pltpu.VMEM((TILE * parts, LANES), jnp.float32),
            pltpu.VMEM((2, CHUNK, width), jnp.bfloat16),
            pltpu.SemaphoreType.DMA((2,)),
            pltpu.VMEM((per_device, width), jnp.float32),
            pltpu.VMEM((4 * width, width), jnp.float32),
            pltpu.SemaphoreType.DMA,
        ],
        compiler_params=pltpu.CompilerParams(vmem_limit_bytes=VMEM_BYTES),
        cost_estimate=pl.CostEstimate(
            flops=24 * edges * width * width, bytes_accessed=40 * edges * width, transcendentals=2 * edges * width
        ),
        name="edge_backward",
    )(
        count, recv, send, cotangent, edge, received, first, second, wide,
        node_part, nodes, w_one, w_two, gain,
    )


MESH = pl.DeviceIdType.MESH
PIECES = 4
LOW = jnp.bfloat16
WIDE = jnp.float32


def places():
    groups = lax.axis_size("blk")
    group, sub = lax.axis_index("blk"), lax.axis_index("sub")
    odd = lax.rem(group, 2)
    along = groups // 2
    spot = group // 2
    beside = group + 1 - 2 * odd
    return dict(
        group=group,
        sub=sub,
        core=lax.rem(sub, 2),
        chip=sub // 2,
        odd=odd,
        spot=spot,
        along=along,
        sibling=sub + 1 - 2 * lax.rem(sub, 2),
        partner=lax.rem(sub + 2, 4),
        to_sibling=(group, sub + 1 - 2 * lax.rem(sub, 2)),
        to_partner=(group, lax.rem(sub + 2, 4)),
        to_beside=(beside, sub),
        to_onward=(lax.rem(group + 2 - 4 * odd + groups, groups), sub),
        to_source=(lax.rem(group - 2 + 4 * odd + groups, groups), sub),
        peers=[(2 * lax.rem(spot + k, along) + odd, sub) for k in range(1, along)],
        near=2 - 2 * odd,
        far=2 * odd,
    )


def meet(senders):
    barrier = pltpu.get_barrier_semaphore()
    for device in senders:
        pl.semaphore_signal(barrier, inc=1, device_id=device, device_id_type=MESH)
    pl.semaphore_wait(barrier, len(senders))


def meet_all():
    barrier = pltpu.get_barrier_semaphore()
    subs = lax.axis_size("sub")
    devices = lax.axis_size("blk") * subs
    here = lax.axis_index("blk") * subs + lax.axis_index("sub")

    def greet(k, carry):
        there = lax.rem(here + k, devices)
        pl.semaphore_signal(barrier, inc=1, device_id=(there // subs, lax.rem(there, subs)), device_id_type=MESH)
        return carry

    lax.fori_loop(1, devices, greet, 0)
    pl.semaphore_wait(barrier, devices - 1)


def remote(source, target, send, recv, device):
    return pltpu.make_async_remote_copy(
        src_ref=source, dst_ref=target, send_sem=send, recv_sem=recv, device_id=device, device_id_type=MESH
    )


def in_pieces(count, body):
    block = math.gcd(count, 128)

    def run(i, carry):
        body(pl.multiple_of(i * block, block), block)
        return carry

    lax.fori_loop(0, count // block, run, 0)


def streams_of(rows):
    unit = 64 * lax.axis_size("blk")
    first = -(-(rows // unit) // 2) * unit
    return [first, rows - first] if first < rows else [first]


def padded_rows(rows):
    unit = 64 * lax.axis_size("blk")
    return -(-rows // unit) * unit


def reducers_scratch(rows, width, along, loaded):
    return [
        ref for part in streams_of(rows) for ref in reducer_scratch(part, width, along, loaded)
    ]


def reducers(at, grads, reduced, refs, loaded):
    rows = grads.shape[0]
    count = 13 if loaded else 11
    made, first = [], 0
    for i, part in enumerate(streams_of(rows)):
        made.append(reducer(at, grads, reduced, first, part, i > 0, refs[i * count : (i + 1) * count]))
        first += part
    return both(made), refs[len(made) * count :]


def reducer_scratch(rows, width, along, loaded):
    return ([pltpu.VMEM((rows // 2, width), WIDE)] if loaded else []) + [
        pltpu.VMEM((rows // 2, width), WIDE),
        pltpu.VMEM((rows // 4, width), LOW),
        pltpu.VMEM((rows // 4, width), LOW),
        pltpu.VMEM((rows // 8, width), LOW),
        pltpu.VMEM((rows // 8, width), LOW),
        pltpu.VMEM((rows // 8, width), LOW),
        pltpu.VMEM((along - 1, rows // 8 // along, width), LOW),
    ] + ([pltpu.SemaphoreType.DMA] if loaded else []) + [
        pltpu.SemaphoreType.DMA((6,)),
        pltpu.SemaphoreType.DMA((6,)),
        pltpu.SemaphoreType.DMA((2, along - 1)),
        pltpu.SemaphoreType.DMA((2, along - 1)),
    ]


def reducer(at, grads, reduced, first, rows, swap, refs):
    (
        half, half_in, cross_out, cross_in, side_out, side_in, ring_out, ring_in,
        load_sem, step_send, step_recv, ring_send, ring_recv,
    ) = refs if len(refs) == 13 else (None, *refs[:7], None, *refs[7:])
    along, peers = at["along"], at["peers"]
    turns = [(at["chip"], at["to_partner"]), (at["odd"], at["to_beside"])]
    (bit_one, device_one), (bit_two, device_two) = turns[::-1] if swap else turns
    core, spot = at["core"], at["spot"]
    n_half, n_cross, n_side, n_ring = rows // 2, rows // 4, rows // 8, rows // 8 // along
    at_half = first + core * n_half
    at_cross = at_half + bit_one * n_cross
    at_side = at_cross + bit_two * n_side
    at_ring = at_side + spot * n_ring

    def span(start, count):
        return pl.ds(pl.multiple_of(start, 16), count)

    def step(kind):
        if kind == 0:
            source, target, device = grads.at[span(first + (1 - core) * n_half, n_half)], half_in, at["to_sibling"]
        elif kind == 1:
            source, target, device = cross_out, cross_in, device_one
        elif kind == 2:
            source, target, device = side_out, side_in, device_two
        else:
            start, count, device = {
                3: (at_side, n_side, device_two),
                4: (at_cross, n_cross, device_one),
                5: (at_half, n_half, at["to_sibling"]),
            }[kind]
            source = target = reduced.at[span(start, count)]
        return remote(source, target, step_send.at[kind], step_recv.at[kind], device)

    def ring(kind, k):
        if kind == 0:
            source = ring_out.at[span(lax.rem(spot + k, along) * n_ring, n_ring)]
            target = ring_in.at[k - 1]
        else:
            source = target = reduced.at[span(at_ring, n_ring)]
        return remote(source, target, ring_send.at[kind, k - 1], ring_recv.at[kind, k - 1], peers[k - 1])

    if half is None:
        half, load = grads.at[span(at_half, n_half)], None
    else:
        load = pltpu.make_async_copy(grads.at[span(at_half, n_half)], half, load_sem)

    def start():
        step(0).start()
        if load is not None:
            load.start()

    def add_half():
        if load is not None:
            load.wait()
        step(0).wait_recv()
        other = (1 - bit_one) * n_cross

        def part(i, block):
            here = pl.ds(pl.multiple_of(other + i, block), block)
            cross_out[pl.ds(i, block), :] = (half[here, :] + half_in[here, :]).astype(LOW)

        in_pieces(n_cross, part)
        step(1).start()

    def add_cross():
        mine, other = bit_one * n_cross, (1 - bit_two) * n_side
        step(1).wait_recv()

        def part(i, block):
            there = pl.ds(pl.multiple_of(other + i, block), block)
            here = pl.ds(pl.multiple_of(mine + other + i, block), block)
            side_out[pl.ds(i, block), :] = (half[here, :] + half_in[here, :] + cross_in[there, :].astype(WIDE)).astype(LOW)

        in_pieces(n_side, part)
        step(2).start()

    def add_side():
        mine, kept = bit_one * n_cross, bit_two * n_side
        step(2).wait_recv()

        def part(i, block):
            there = pl.ds(pl.multiple_of(kept + i, block), block)
            here = pl.ds(pl.multiple_of(mine + kept + i, block), block)
            flat = pl.ds(i, block)
            value = half[here, :] + half_in[here, :] + cross_in[there, :].astype(WIDE) + side_in[flat, :].astype(WIDE)
            half[here, :] = value
            ring_out[flat, :] = value.astype(LOW)

        in_pieces(n_side, part)
        for k in range(1, along):
            ring(0, k).start()

    def add_ring():
        value = half[span(bit_one * n_cross + bit_two * n_side + spot * n_ring, n_ring), :]
        for k in range(1, along):
            ring(0, k).wait_recv()
            value = value + ring_in[k - 1].astype(WIDE)
        reduced[span(at_ring, n_ring), :] = value.astype(LOW)
        for k in range(1, along):
            ring(1, k).start()

    def share_side():
        for k in range(1, along):
            ring(1, k).wait_recv()
        step(3).start()

    def share_cross():
        step(3).wait_recv()
        step(4).start()

    def share_half():
        step(4).wait_recv()
        step(5).start()

    def last():
        step(5).wait_recv()

    def drain():
        for kind in range(6):
            step(kind).wait_send()
        for k in range(1, along):
            ring(0, k).wait_send()
            ring(1, k).wait_send()

    return [start, add_half, add_cross, add_side, add_ring, share_side, share_cross, share_half, last, drain]


def vector_scratch(shape, along):
    return [
        pltpu.VMEM((4, *shape), WIDE),
        pltpu.VMEM((2 + along, *shape), WIDE),
        pltpu.SemaphoreType.DMA((2 + along,)),
        pltpu.SemaphoreType.DMA((2 + along,)),
    ]


def vector_reducer(at, vectors, reduced, refs):
    held, held_in, send_sems, recv_sems = refs
    along = at["along"]
    devices = (at["to_sibling"], at["to_partner"], at["to_beside"], *at["peers"])

    def move(kind):
        return remote(held.at[min(kind, 3)], held_in.at[kind], send_sems.at[kind], recv_sems.at[kind], devices[kind])

    def start():
        held[0] = vectors[...]
        move(0).start()

    def turn(kind):
        def run():
            move(kind).wait_recv()
            held[kind + 1] = held[kind] + held_in[kind]
            for k in range(kind + 1, kind + 2 if kind < 2 else 2 + along):
                move(k).start()

        return run

    def last():
        value = held[3]
        for k in range(3, 2 + along):
            move(k).wait_recv()
            value = value + held_in[k]
        reduced[...] = value
        for k in range(2 + along):
            move(k).wait_send()

    return [start, turn(0), turn(1), turn(2), last]


def both(streams):
    return [lambda steps=steps: [step() for step in steps] for steps in zip(*streams)]


def spread_moves(at, own, table, keep_sem, send_sems, recv_sems):
    sub, partner, near, far = at["sub"], at["partner"], at["near"], at["far"]
    to_sibling, to_partner, to_beside, to_onward = (
        at["to_sibling"], at["to_partner"], at["to_beside"], at["to_onward"]
    )
    size = own.shape[0] // PIECES

    def move(kind, piece):
        source, slot, device = {
            0: (None, (1, sub), to_partner),
            1: (None, (far, sub), to_beside),
            2: (None, (1, sub), to_sibling),
            3: ((1, partner), (far, partner), to_beside),
            4: ((1, partner), (1, partner), to_sibling),
            5: ((near, sub), (far, sub), to_onward),
            6: ((near, sub), (near, sub), to_sibling),
            7: ((near, partner), (far, partner), to_onward),
            8: ((near, partner), (near, partner), to_sibling),
            9: ((far, sub), (far, sub), to_sibling),
            10: ((far, partner), (far, partner), to_sibling),
        }[kind]
        source = own if source is None else table.at[source[0], source[1]]
        rows = pl.ds(piece * size, size)
        return remote(
            source.at[rows], table.at[slot[0], slot[1], rows],
            send_sems.at[kind, piece], recv_sems.at[kind, piece], device,
        )

    keep = pltpu.make_async_copy(own, table.at[1, sub], keep_sem)

    def start():
        for piece in range(PIECES):
            for kind in (0, 1, 2):
                move(kind, piece).start()
        keep.start()

    def relay(arrived, kinds, piece):
        move(arrived, piece).wait_recv()
        for kind in kinds:
            move(kind, piece).start()

    def one(piece):
        relay(0, (3, 4), piece)
        relay(1, (5, 6), piece)

    def two(piece):
        relay(3, (7, 8), piece)
        relay(5, (9,), piece)

    def three(piece):
        relay(7, (10,), piece)

    def drain():
        for kind in range(11):
            for piece in range(PIECES):
                if kind in (2, 4, 6, 8, 9, 10):
                    move(kind, piece).wait_recv()
                move(kind, piece).wait_send()
        keep.wait()

    return start, one, two, three, drain


def spread_scratch():
    return [
        pltpu.SemaphoreType.DMA,
        pltpu.SemaphoreType.DMA((11, PIECES)),
        pltpu.SemaphoreType.DMA((11, PIECES)),
    ]


HALVES = 2
ORDER = (
    (0, 1, 0), (0, 1, 1), (1, 1, 0), (0, 0, 0), (1, 1, 1), (0, 0, 1),
    (1, 0, 0), (2, 1, 0), (1, 0, 1), (2, 1, 1), (2, 0, 0), (2, 0, 1),
)


def collect_scratch(rows, width, edges):
    return [
        pltpu.VMEM((edges, width), LOW),
        pltpu.VMEM((2, 3, 2, rows, width), WIDE),
        pltpu.VMEM((3, 2, rows, width), WIDE),
        pltpu.VMEM((2, rows, width), LOW),
        pltpu.VMEM((2, rows, width), LOW),
        pltpu.VMEM((2, rows, width), LOW),
        pltpu.VMEM((2, rows, width), LOW),
        pltpu.VMEM((rows, width), LOW),
        pltpu.VMEM((rows, width), LOW),
        pltpu.SemaphoreType.DMA,
        pltpu.SemaphoreType.DMA((3, 2, HALVES)),
        pltpu.SemaphoreType.DMA((3, 2, HALVES)),
        pltpu.SemaphoreType.DMA((5, PIECES)),
        pltpu.SemaphoreType.DMA((5, PIECES)),
    ]


def collect_moves(at, index, messages, out, refs):
    (
        held, parts, landed, far_out, far_in, near_out, near_in, pair_out, pair_in,
        load_sem, give_sems, take_sems, send_sems, recv_sems,
    ) = refs
    sub, partner, sibling = at["sub"], at["partner"], at["sibling"]
    rows = out.shape[0]
    size = rows // PIECES
    part_rows = rows // HALVES
    load = pltpu.make_async_copy(messages, held, load_sem)

    def piece_of(ref, piece):
        return ref.at[pl.ds(piece * size, size)]

    def give(role, side, half):
        span = pl.ds(pl.multiple_of(half * part_rows, part_rows), part_rows)
        return remote(
            parts.at[0, role, side, span], landed.at[role, side, span],
            give_sems.at[role, side, half], take_sems.at[role, side, half], at["to_sibling"],
        )

    def hop(kind, piece):
        source, target, device = {
            0: (far_out.at[0], far_in.at[0], at["to_source"]),
            1: (far_out.at[1], far_in.at[1], at["to_source"]),
            2: (near_out.at[0], near_in.at[0], at["to_beside"]),
            3: (near_out.at[1], near_in.at[1], at["to_beside"]),
            4: (pair_out, pair_in, at["to_partner"]),
        }[kind]
        return remote(
            piece_of(source, piece), piece_of(target, piece),
            send_sems.at[kind, piece], recv_sems.at[kind, piece], device,
        )

    def add_messages(step):
        def pick(column):
            return lax.rem(sum(int(item[column]) << (2 * i) for i, item in enumerate(ORDER)) >> (2 * step), 4)

        role, side, half = pick(0), pick(1), pick(2)
        relation = jnp.where(role == 0, at["far"], jnp.where(role == 1, at["near"], 1))
        span = pl.ds(pl.multiple_of(half * part_rows, part_rows), part_rows)

        def whose(w, carry):
            first = jnp.where(w == 0, sibling, sub)
            target = lax.rem(first + 2 * side, 4)
            base = (relation * 4 + target) * rows + half * part_rows
            node = lax.broadcasted_iota(jnp.int32, (part_rows, LANES), 0) + base
            chosen = jnp.concatenate(
                [jnp.where(node == index[j : j + 1, :], 1.0, 0.0).astype(LOW) for j in range(index.shape[0])], axis=1
            )
            parts[w, role, side, span, :] = dot(chosen, held[...])
            return carry

        lax.fori_loop(0, 2, whose, 0)
        give(role, side, half).start()

    def local(role, side, piece):
        span = pl.ds(piece * size, size)
        return parts[1, role, side, span, :] + landed[role, side, span, :]

    def arrived(kind, ref, piece):
        hop(kind, piece).wait_recv()
        return ref[pl.ds(piece * size, size), :].astype(WIDE)

    def pieces(half):
        return range(half * PIECES // HALVES, (half + 1) * PIECES // HALVES)

    def far_step(side, half):
        give(0, side, half).wait_recv()
        for piece in pieces(half):
            far_out[side, pl.ds(piece * size, size), :] = local(0, side, piece).astype(LOW)
            hop(side, piece).start()

    def near_step(side, half):
        give(1, side, half).wait_recv()
        for piece in pieces(half):
            value = local(1, side, piece) + arrived(side, far_in.at[side], piece)
            near_out[side, pl.ds(piece * size, size), :] = value.astype(LOW)
            hop(2 + side, piece).start()

    def pair_step(half):
        give(2, 1, half).wait_recv()
        for piece in pieces(half):
            value = local(2, 1, piece) + arrived(3, near_in.at[1], piece)
            pair_out[pl.ds(piece * size, size), :] = value.astype(LOW)
            hop(4, piece).start()

    def last_step(half):
        give(2, 0, half).wait_recv()
        for piece in pieces(half):
            value = local(2, 0, piece) + arrived(2, near_in.at[0], piece) + arrived(4, pair_in, piece)
            out[pl.ds(piece * size, size), :] = value

    def drain():
        for item in ORDER:
            give(*item).wait_send()
        for kind in range(5):
            for piece in range(PIECES):
                hop(kind, piece).wait_send()

    events = {
        1: [lambda: far_step(1, 0)],
        2: [lambda: far_step(1, 1)],
        3: [lambda: near_step(1, 0)],
        4: [lambda: far_step(0, 0)],
        5: [lambda: near_step(1, 1), lambda: far_step(0, 1)],
        7: [lambda: near_step(0, 0), lambda: pair_step(0)],
        9: [lambda: near_step(0, 1), lambda: pair_step(1)],
    }

    def run(more):
        def step(i, carry):
            add_messages(i)
            for k in sorted(set(events) | set(more)):
                @pl.when(i == k)
                def _():
                    for event in events.get(k, []) + more.get(k, []):
                        event()

            return carry

        lax.fori_loop(0, len(ORDER), step, 0)
        for half in range(HALVES):
            last_step(half)

    return load, run, drain


def exchange_scratch(rows, width, devices):
    slab = width // devices * (rows // LANES)
    return [
        pltpu.VMEM((devices * slab, LANES), WIDE),
        pltpu.VMEM((devices * slab, LANES), LOW),
        pltpu.VMEM((devices, slab, LANES), LOW),
        pltpu.VMEM((slab, LANES), WIDE),
        pltpu.SemaphoreType.DMA((devices - 1,)),
        pltpu.SemaphoreType.DMA((devices - 1,)),
    ]


def exchange_moves(residual, out, refs):
    flat, packed, landed, opened, send_sems, recv_sems = refs
    subs = lax.axis_size("sub")
    devices = lax.axis_size("blk") * subs
    here = lax.axis_index("blk") * subs + lax.axis_index("sub")
    slab = landed.shape[1]
    channels = out.shape[0]
    parts = slab // channels
    nodes = parts * LANES

    def move(k):
        there = lax.rem(here + k, devices)
        return remote(
            packed.at[pl.ds(pl.multiple_of(there * slab, slab), slab)], landed.at[here],
            send_sems.at[k - 1], recv_sems.at[k - 1], (there // subs, lax.rem(there, subs)),
        )

    def start(values):
        lay_rows(flat, 0, values.T)

        def cast(i, block):
            packed[pl.ds(i, block), :] = flat[pl.ds(i, block), :].astype(LOW)

        in_pieces(flat.shape[0], cast)

        def send(k, carry):
            move(k).start()
            return carry

        lax.fori_loop(1, devices, send, 0)

    def open_slab(source, device):
        opened[...] = source.astype(WIDE)
        for j in range(parts):
            columns = pl.ds(pl.multiple_of(device * nodes + j * LANES, LANES), LANES)
            out[:, columns] = residual[:, columns] + opened[pl.ds(j, channels, stride=parts), :]

    def last():
        open_slab(packed[pl.ds(pl.multiple_of(here * slab, slab), slab), :], here)

        def take(k, carry):
            move(k).wait_recv()
            device = lax.rem(here - k + devices, devices)
            open_slab(landed[device], device)
            return carry

        lax.fori_loop(1, devices, take, 0)

        def sent(k, carry):
            move(k).wait_send()
            return carry

        lax.fori_loop(1, devices, sent, 0)

    return start, last


def finish_kernel(
    index, messages, grads, vectors, node_part, weight, residual, node_grad, reduced, reduced_vectors, total, *refs
):
    at = places()
    count = len(collect_scratch(64, 128, 64))
    load, run, drain = collect_moves(at, index, messages, total, refs[:count])
    load.start()
    meet_all()
    steps, refs = reducers(at, grads, reduced, refs[count:], True)
    vector_steps = vector_reducer(at, vectors, reduced_vectors, refs[:4])
    exchange, receive = exchange_moves(residual, node_grad, refs[4:])
    steps[0]()
    vector_steps[0]()
    load.wait()
    run({
        1: [steps[1], vector_steps[1]],
        4: [steps[2], vector_steps[2]],
        6: [steps[3], vector_steps[3]],
        8: [steps[4]],
        10: [steps[5]],
    })
    high, rest = split_low(total[...])
    exchange(node_part[...] + dot_right(high, weight[...]) + dot_right(rest, weight[...]))
    for step in steps[6:8]:
        step()
    receive()
    steps[8]()
    vector_steps[4]()
    drain()
    steps[9]()


def finish(index, messages, grads, vectors, node_part, weight, residual, collective):
    rows, width = node_part.shape
    edges = messages.shape[0]
    along = lax.axis_size("blk") // 2
    devices = lax.axis_size("blk") * lax.axis_size("sub")
    hold = pl.BlockSpec(memory_space=pltpu.VMEM)
    across = pl.BlockSpec(memory_space=pl.ANY)
    return pl.pallas_call(
        finish_kernel,
        grid=(1,),
        in_specs=[
            hold, across, across, hold, hold, pl.BlockSpec((width, width), lambda i: (2, 0)), hold,
        ],
        out_specs=[hold] * 3,
        out_shape=[
            jax.ShapeDtypeStruct(residual.shape, WIDE),
            jax.ShapeDtypeStruct(grads.shape, LOW),
            jax.ShapeDtypeStruct(vectors.shape, WIDE),
        ],
        scratch_shapes=[
            pltpu.VMEM((rows, width), WIDE),
            *collect_scratch(rows, width, edges),
            *reducers_scratch(grads.shape[0], width, along, True),
            *vector_scratch(vectors.shape, along),
            *exchange_scratch(rows, width, devices),
        ],
        compiler_params=pltpu.CompilerParams(
            collective_id=collective, has_side_effects=True, vmem_limit_bytes=VMEM_BYTES
        ),
        name="finish_sums",
    )(index.reshape(edges // LANES, LANES), messages, grads, vectors, node_part, weight, residual)


def middle_kernel(
    index, messages, node_low, upstream, w_one, b_one, w_two, b_two, gain, shift, residual,
    table, node_part, node_out, reduced, reduced_vectors, total, sent, grads, vectors, *refs
):
    at = places()
    count = len(collect_scratch(64, 128, 64))
    load, run, drain = collect_moves(at, index, messages, total, refs[:count])
    load.start()
    meet_all()
    refs = refs[count:]
    start, one, two, three, end = spread_moves(at, sent, table, *refs[:3])
    steps, refs = reducers(at, grads, reduced, refs[3:], False)
    vector_steps = vector_reducer(at, vectors, reduced_vectors, refs[:4])
    exchange, receive = exchange_moves(residual, node_out, refs[4:])
    load.wait()
    run({})

    width = total.shape[1]
    low = total[...].astype(LOW)
    pre = dot(node_low[...], w_one[:width]) + dot(low, w_one[width:]) + b_one[...]
    logistic = jax.nn.sigmoid(pre)
    act = (pre * logistic).astype(LOW)
    normal, scale = row_normal(dot(act, w_two[...]) + b_two[...])
    given = upstream[...].T
    scaled = given * gain[...]
    slope = jnp.mean(scaled * normal, -1, keepdims=True)
    fourth = scale * (scaled - jnp.mean(scaled, -1, keepdims=True) - normal * slope)
    fourth_low = fourth.astype(LOW)
    third = dot_right(fourth_low, w_two[...]) * (logistic * (1.0 + pre * (1.0 - logistic)))
    third_low = third.astype(LOW)
    sent[...] = dot_right(third_low, w_one[width:]).astype(LOW)
    start()
    grads[:width] = dot_left(node_low[...], third_low)
    grads[width : 2 * width] = dot_left(low, third_low)
    grads[2 * width : 3 * width] = dot_left(act, fourth_low)
    steps[0]()
    vectors[...] = jnp.zeros_like(vectors)
    vectors[0:1] = jnp.sum(third_low.astype(WIDE), 0, keepdims=True)
    vectors[1:2] = jnp.sum(fourth_low.astype(WIDE), 0, keepdims=True)
    vectors[2:3] = jnp.sum(given * normal, 0, keepdims=True)
    vectors[3:4] = jnp.sum(given, 0, keepdims=True)
    vector_steps[0]()
    node_part[...] = dot_right(third_low, w_one[:width])
    exchange(normal * gain[...] + shift[...])

    one(0)
    steps[1]()
    vector_steps[1]()
    one(1)
    one(2)
    steps[2]()
    vector_steps[2]()
    one(3)
    two(0)
    steps[3]()
    vector_steps[3]()
    two(1)
    two(2)
    steps[4]()
    two(3)
    steps[5]()
    three(0)
    three(1)
    steps[6]()
    three(2)
    three(3)
    steps[7]()
    receive()
    vector_steps[4]()
    end()
    steps[8]()
    steps[9]()
    drain()


def middle(index, messages, node_low, upstream, w_one, b_one, w_two, b_two, gain, shift, residual, collective):
    rows, width = node_low.shape
    edges = messages.shape[0]
    along = lax.axis_size("blk") // 2
    devices = lax.axis_size("blk") * lax.axis_size("sub")
    grad_rows = padded_rows(3 * width)
    hold = pl.BlockSpec(memory_space=pltpu.VMEM)
    across = pl.BlockSpec(memory_space=pl.ANY)
    table, node_part, node_out, reduced, reduced_vectors = pl.pallas_call(
        middle_kernel,
        in_specs=[hold, across] + [hold] * 9,
        out_specs=[across] + [hold] * 4,
        out_shape=[
            jax.ShapeDtypeStruct((3, 4, rows, width), LOW),
            jax.ShapeDtypeStruct((rows, width), WIDE),
            jax.ShapeDtypeStruct(residual.shape, WIDE),
            jax.ShapeDtypeStruct((grad_rows, width), LOW),
            jax.ShapeDtypeStruct((8, width), WIDE),
        ],
        scratch_shapes=[
            pltpu.VMEM((rows, width), WIDE),
            pltpu.VMEM((rows, width), LOW),
            pltpu.VMEM((grad_rows, width), WIDE),
            pltpu.VMEM((8, width), WIDE),
            *collect_scratch(rows, width, edges),
            *spread_scratch(),
            *reducers_scratch(grad_rows, width, along, False),
            *vector_scratch((8, width), along),
            *exchange_scratch(rows, width, devices),
        ],
        compiler_params=pltpu.CompilerParams(
            collective_id=collective, has_side_effects=True, vmem_limit_bytes=VMEM_BYTES
        ),
        name="middle_nodes",
    )(
        index.reshape(edges // LANES, LANES), messages, node_low, upstream,
        w_one, b_one, w_two, b_two, gain, shift, residual,
    )
    return table.reshape(12 * rows, width), node_part, node_out, reduced, reduced_vectors


def scatter_scratch(channels, nodes, devices):
    slab = channels * (nodes // LANES)
    return [
        pltpu.VMEM((devices * slab, LANES), WIDE),
        pltpu.VMEM((devices * slab, LANES), LOW),
        pltpu.VMEM((devices, slab, LANES), LOW),
        pltpu.VMEM((slab, LANES), WIDE),
        pltpu.VMEM((nodes // LANES * devices * channels, LANES), WIDE),
        pltpu.SemaphoreType.DMA((devices - 1,)),
        pltpu.SemaphoreType.DMA((devices - 1,)),
    ]


def scatter_moves(shard, refs):
    flat, packed, landed, opened, square, send_sems, recv_sems = refs
    subs = lax.axis_size("sub")
    devices = lax.axis_size("blk") * subs
    here = lax.axis_index("blk") * subs + lax.axis_index("sub")
    slab = landed.shape[1]
    channels = shard.shape[0]
    parts = slab // channels
    nodes = parts * LANES

    def move(k):
        there = lax.rem(here + k, devices)
        return remote(
            packed.at[pl.ds(pl.multiple_of(there * slab, slab), slab)], landed.at[here],
            send_sems.at[k - 1], recv_sems.at[k - 1], (there // subs, lax.rem(there, subs)),
        )

    def start():
        def pack(k, carry):
            device = lax.rem(here + k, devices)
            rows = pl.ds(pl.multiple_of(device * slab, slab), slab)
            for j in range(parts):
                columns = pl.ds(pl.multiple_of(device * nodes + j * LANES, LANES), LANES)
                flat[pl.ds(device * slab + j, channels, stride=parts), :] = shard[:, columns]
            packed[rows, :] = flat[rows, :].astype(LOW)
            return carry

        def send(k, carry):
            pack(k, carry)
            move(k).start()
            return carry

        lax.fori_loop(1, devices, send, 0)
        pack(0, 0)

    def open_slab(source, device):
        opened[...] = source.astype(WIDE)
        for j in range(parts):
            rows = pl.ds(pl.multiple_of((j * devices + device) * channels, channels), channels)
            square[rows, :] = opened[pl.ds(j, channels, stride=parts), :]

    def last(rows):
        open_slab(packed[pl.ds(pl.multiple_of(here * slab, slab), slab), :], here)

        def take(k, carry):
            move(k).wait_recv()
            device = lax.rem(here - k + devices, devices)
            open_slab(landed[device], device)
            return carry

        lax.fori_loop(1, devices, take, 0)
        width = devices * channels
        for j in range(parts):
            rows[j * LANES : (j + 1) * LANES, :] = square[j * width : (j + 1) * width, :].T.astype(LOW)

    def drain():
        def sent(k, carry):
            move(k).wait_send()
            return carry

        lax.fori_loop(1, devices, sent, 0)

    return start, last, drain


def begin_kernel(
    shard, later, senders, receivers, own, table, later_out, send_local, recv_wide, held, held_sem, *refs
):
    at = places()
    fetch = pltpu.make_async_copy(later, held, held_sem)
    fetch.start()
    meet_all()
    start, last, drain = scatter_moves(shard, refs[3:])
    start()
    last(own)
    begin, one, two, three, end = spread_moves(at, own, table, *refs[:3])
    begin()
    rows = own.shape[0]
    groups, subs = lax.axis_size("blk"), lax.axis_size("sub")
    send_local[...] = senders[...] - (at["group"] * subs + at["sub"]) * rows
    relative = lax.rem(receivers[...] // (rows * subs) - at["group"] + 1 + groups, groups)
    recv_wide[...] = relative * (rows * subs) + lax.rem(receivers[...], rows * subs)
    fetch.wait()
    give = pltpu.make_async_copy(held, later_out, held_sem)
    give.start()
    drain()
    for stage in (one, two, three):
        for piece in range(PIECES):
            stage(piece)
    give.wait()
    end()


def begin(shard, later, senders, receivers, rows, collective):
    channels, nodes = shard.shape
    devices = lax.axis_size("blk") * lax.axis_size("sub")
    width = channels * devices
    hold = pl.BlockSpec(memory_space=pltpu.VMEM)
    across = pl.BlockSpec(memory_space=pl.ANY)
    lines = (senders.shape[0] // LANES, LANES)
    own, table, later, send_local, recv_wide = pl.pallas_call(
        begin_kernel,
        in_specs=[hold, across, hold, hold],
        out_specs=[hold, across, across, hold, hold],
        out_shape=[
            jax.ShapeDtypeStruct((rows, width), LOW),
            jax.ShapeDtypeStruct((3, 4, rows, width), LOW),
            jax.ShapeDtypeStruct(later.shape, later.dtype),
            jax.ShapeDtypeStruct(lines, jnp.int32),
            jax.ShapeDtypeStruct(lines, jnp.int32),
        ],
        scratch_shapes=[
            pltpu.VMEM(later.shape, later.dtype),
            pltpu.SemaphoreType.DMA,
            *spread_scratch(),
            *scatter_scratch(channels, rows, devices),
        ],
        compiler_params=pltpu.CompilerParams(
            collective_id=collective, has_side_effects=True, vmem_limit_bytes=VMEM_BYTES
        ),
        name="begin_rows",
    )(shard, later, senders.reshape(lines), receivers.reshape(lines))
    return own, table.reshape(12 * rows, width), later, send_local, recv_wide


def shards(
    node_input,
    edge_input,
    senders,
    receivers,
    edge_count,
    edge_w_one,
    edge_b_one,
    edge_w_two,
    edge_b_two,
    edge_gain,
    edge_shift,
    node_w_one,
    node_b_one,
    node_w_two,
    node_b_two,
    node_gain,
    node_shift,
    node_cotangent,
    edge_cotangent,
):
    groups = lax.axis_size("blk")
    sub_count = lax.axis_size("sub")
    width = edge_input.shape[1]
    per_device = node_input.shape[1] // (groups * sub_count)
    node_low, wide_low, cotangent_later, send_local, recv_wide = begin(
        node_input, node_cotangent, senders, receivers, per_device, 0
    )
    node_upstream = to_nodes(cotangent_later)
    recv_list = recv_wide.reshape(-1)
    edge_result, first_pre, second_pre, received, messages = edge_forward(
        edge_count, recv_list, send_local, edge_input, wide_low, node_low,
        edge_w_one, edge_b_one[None], edge_w_two, edge_b_two[None], edge_gain[None], edge_shift[None],
    )
    wide_grad, node_part, node_out, node_summed, node_vectors = middle(
        recv_list, messages, node_low, node_upstream, node_w_one, node_b_one[None], node_w_two, node_b_two[None],
        node_gain[None], node_shift[None], node_input, 1,
    )
    edge_grad, messages, grads, vectors, node_part = edge_backward(
        edge_count, recv_list, send_local, edge_cotangent, edge_input, received, first_pre, second_pre,
        wide_grad, node_part, node_low, edge_w_one, edge_w_two,
        edge_gain[None],
    )
    node_grad, summed, vectors = finish(
        recv_list, messages, grads, vectors, node_part, edge_w_one, node_cotangent, 3
    )
    summed = summed.astype(jnp.float32)
    node_summed = node_summed.astype(jnp.float32)
    return (
        node_out,
        edge_result,
        node_grad,
        edge_grad,
        summed[: 3 * width],
        vectors[0],
        summed[3 * width :],
        vectors[1],
        vectors[2],
        vectors[3],
        node_summed[: 2 * width],
        node_vectors[0],
        node_summed[2 * width : 3 * width],
        node_vectors[1],
        node_vectors[2],
        node_vectors[3],
    )


def solution(mesh):
    placed = (
        P(("blk", "sub"), None),
        P(("blk", "sub"), None),
        P(("blk", "sub")),
        P(("blk", "sub")),
        P(("blk", "sub")),
        P(),
        P(),
        P(),
        P(),
        P(),
        P(),
        P(),
        P(),
        P(),
        P(),
        P(),
        P(),
        P(("blk", "sub"), None),
        P(("blk", "sub"), None),
    )
    return jax.shard_map(
        shards,
        mesh=mesh,
        in_specs=placed,
        out_specs=(
            P(("blk", "sub"), None),
            P(("blk", "sub"), None),
            P(("blk", "sub"), None),
            P(("blk", "sub"), None),
            P(),
            P(),
            P(),
            P(),
            P(),
            P(),
            P(),
            P(),
            P(),
            P(),
            P(),
            P(),
        ),
        check_vma=False,
    )
```

```python
import math

import jax
import jax.numpy as jnp
from jax import lax
from jax.experimental import pallas as pl
from jax.experimental.pallas import tpu as pltpu
from jax.sharding import PartitionSpec as P

EPSILON = 1e-05


def to_nodes(channels):
    return lax.all_to_all(channels, ("blk", "sub"), split_axis=1, concat_axis=0, tiled=True)


TILE = 512
CHUNK = 512
LANES = 128
VMEM_BYTES = 60 * 2**20


def dot(left, right):
    return jnp.dot(left, right, preferred_element_type=jnp.float32)


def dot_left(left, right):
    return lax.dot_general(
        left, right, (((0,), (0,)), ((), ())), preferred_element_type=jnp.float32
    )


def dot_right(left, right):
    return lax.dot_general(
        left, right, (((1,), (1,)), ((), ())), preferred_element_type=jnp.float32
    )


def split_low(values):
    high = values.astype(jnp.bfloat16)
    return high, (values - high.astype(jnp.float32)).astype(jnp.bfloat16)


def lay_rows(target, start, values):
    count, width = values.shape
    parts = width // LANES
    for j in range(parts):
        target[pl.ds(start * parts + j, count, stride=parts), :] = values[:, j * LANES : (j + 1) * LANES]


def read_rows(source, start, count, parts):
    return jnp.concatenate(
        [source[pl.ds(start * parts + j, count, stride=parts), :] for j in range(parts)], axis=1
    )


def load_table(wide, table, stage, sems):
    parts = table.shape[1]
    steps = wide.shape[0] // CHUNK

    def fetch(i, slot):
        return pltpu.make_async_copy(wide.at[pl.ds(i * CHUNK, CHUNK)], stage.at[slot], sems.at[slot])

    fetch(0, 0).start()

    def body(i, carry):
        slot = lax.rem(i, 2)

        @pl.when(i + 1 < steps)
        def _():
            fetch(i + 1, 1 - slot).start()

        fetch(i, slot).wait()

        def piece(k, carry):
            values = stage[slot, pl.ds(k * 64, 64), :].astype(jnp.float32)
            for j in range(parts):
                table[pl.ds(i * CHUNK + k * 64, 64), j, :] = values[:, j * LANES : (j + 1) * LANES]
            return carry

        return lax.fori_loop(0, CHUNK // 64, piece, carry)

    lax.fori_loop(0, steps, body, 0)


def gather_rows(index, base, table, rows, parts):
    count = rows.shape[0] // parts

    def body(i, carry):
        for u in range(16):
            slot = i * 16 + u
            rows[pl.ds(pl.multiple_of(slot * parts, parts), parts), :] = table[index[base + slot]]
        return carry

    lax.fori_loop(0, count // 16, body, 0)


def row_normal(values):
    average = jnp.mean(values, -1, keepdims=True)
    centred = values - average
    variance = jnp.mean(centred * centred, -1, keepdims=True)
    scale = lax.rsqrt(variance + EPSILON)
    return centred * scale, scale


def forward_kernel(
    count, recv, send, edge, wide, nodes, w_one, b_one, w_two, b_two, gain, shift,
    result, first, second, received, message,
    table, rows, stage, sems,
):
    step = pl.program_id(0)
    base = step * TILE
    width = nodes.shape[1]
    parts = width // LANES

    @pl.when(step == 0)
    def _():
        load_table(wide, table, stage, sems)

    gather_rows(recv, base, table, rows, parts)
    from_recv = read_rows(rows, 0, TILE, parts).astype(jnp.bfloat16)
    received[...] = from_recv
    lane = lax.broadcasted_iota(jnp.int32, (LANES, LANES), 1)
    chosen = []
    for i in range(TILE // LANES):
        column = jnp.broadcast_to(send[pl.ds(step * (TILE // LANES) + i, 1), :], (LANES, LANES)).T
        chosen.append(
            jnp.concatenate(
                [
                    jnp.where(column == lane + j * LANES, 1.0, 0.0).astype(jnp.bfloat16)
                    for j in range(nodes.shape[0] // LANES)
                ],
                axis=1,
            )
        )
    chosen = jnp.concatenate(chosen, axis=0)
    from_send = dot(chosen, nodes[...]).astype(jnp.bfloat16)
    pre = (
        dot(edge[...], w_one[:width])
        + dot(from_send, w_one[width : 2 * width])
        + dot(from_recv, w_one[2 * width :])
        + b_one[...]
    )
    first[...] = pre
    act = (pre * jax.nn.sigmoid(pre)).astype(jnp.bfloat16)
    post = dot(act, w_two[...]) + b_two[...]
    second[...] = post
    normal, _ = row_normal(post)
    branch = normal * gain[...] + shift[...]
    live = base + lax.broadcasted_iota(jnp.int32, (TILE, 1), 0) < count[0]
    outcome = edge[...].astype(jnp.float32) + jnp.where(live, branch, 0.0)
    result[...] = outcome
    message[...] = jnp.where(live, outcome, 0.0).astype(jnp.bfloat16)


def edge_forward(count, recv, send, edge, wide, nodes, w_one, b_one, w_two, b_two, gain, shift):
    edges, width = edge.shape
    steps = edges // TILE
    parts = width // LANES
    hold = pl.BlockSpec(memory_space=pltpu.VMEM)
    scalar = pl.BlockSpec(memory_space=pltpu.SMEM)
    tile = pl.BlockSpec((TILE, width), lambda i: (i, 0))
    return pl.pallas_call(
        forward_kernel,
        grid=(steps,),
        in_specs=[
            scalar, scalar, hold, tile,
            pl.BlockSpec(memory_space=pl.ANY), hold, hold, hold, hold, hold, hold, hold,
        ],
        out_specs=[tile] * 5,
        out_shape=[
            jax.ShapeDtypeStruct((edges, width), jnp.float32),
            jax.ShapeDtypeStruct((edges, width), jnp.float32),
            jax.ShapeDtypeStruct((edges, width), jnp.float32),
            jax.ShapeDtypeStruct((edges, width), jnp.bfloat16),
            jax.ShapeDtypeStruct((edges, width), jnp.bfloat16),
        ],
        scratch_shapes=[
            pltpu.VMEM((wide.shape[0], parts, LANES), jnp.float32),
            pltpu.VMEM((TILE * parts, LANES), jnp.float32),
            pltpu.VMEM((2, CHUNK, width), jnp.bfloat16),
            pltpu.SemaphoreType.DMA((2,)),
        ],
        compiler_params=pltpu.CompilerParams(vmem_limit_bytes=VMEM_BYTES),
        cost_estimate=pl.CostEstimate(
            flops=20 * edges * width * width, bytes_accessed=40 * edges * width, transcendentals=2 * edges * width
        ),
        name="edge_forward",
    )(count, recv, send, edge, wide, nodes, w_one, b_one, w_two, b_two, gain, shift)


def backward_kernel(
    count, recv, send, cotangent, edge, received, first, second, wide, node_part, nodes, w_one, w_two, gain,
    node_grads, node_vectors,
    grad, message, all_grads, vectors, sender_grad, node_reduced, vectors_reduced,
    table, rows, stage, sems, by_sender, grads, give_sem, reduced, reduced_sem, *refs,
):
    step = pl.program_id(0)
    at = places()
    moves, refs = reducers(at, node_grads, reduced, refs, True)
    vector_moves = vector_reducer(at, node_vectors, vectors_reduced, refs)

    @pl.when(step == 0)
    def _():
        meet((at["to_sibling"], at["to_partner"], at["to_beside"], *at["peers"]))
        moves[0]()
        vector_moves[0]()

    for when, events in (
        (1, [moves[1], vector_moves[1]]),
        (2, [moves[2], vector_moves[2]]),
        (4, [moves[3], vector_moves[3]]),
        (5, [moves[4]]),
        (6, [moves[5]]),
        (7, [moves[6]]),
        (8, [moves[7], vector_moves[4]]),
    ):

        @pl.when(step == when)
        def _():
            for event in events:
                event()

    base = step * TILE
    width = nodes.shape[1]
    parts = width // LANES

    @pl.when(step == 0)
    def _():
        load_table(wide, table, stage, sems)
        grads[...] = jnp.zeros_like(grads)
        vectors[...] = jnp.zeros_like(vectors)
        by_sender[...] = jnp.zeros_like(by_sender)

    gather_rows(recv, base, table, rows, parts)
    live = base + lax.broadcasted_iota(jnp.int32, (TILE, 1), 0) < count[0]
    upstream = cotangent[...].astype(jnp.float32) + jnp.where(live, read_rows(rows, 0, TILE, parts), 0.0)
    masked = jnp.where(live, upstream, 0.0)
    normal, scale = row_normal(second[...])
    vectors[2:3, :] += jnp.sum(masked * normal, 0, keepdims=True)
    vectors[3:4, :] += jnp.sum(masked, 0, keepdims=True)
    scaled = masked * gain[...]
    slope = jnp.mean(scaled * normal, -1, keepdims=True)
    grad_second = scale * (scaled - jnp.mean(scaled, -1, keepdims=True) - normal * slope)
    second_low = grad_second.astype(jnp.bfloat16)
    vectors[1:2, :] += jnp.sum(second_low.astype(jnp.float32), 0, keepdims=True)
    pre = first[...]
    logistic = jax.nn.sigmoid(pre)
    act = (pre * logistic).astype(jnp.bfloat16)
    grads[3 * width : 4 * width] += dot_left(act, second_low)
    grad_first = dot_right(second_low, w_two[...]) * (logistic * (1.0 + pre * (1.0 - logistic)))
    first_low = grad_first.astype(jnp.bfloat16)
    message[...] = first_low
    vectors[0:1, :] += jnp.sum(first_low.astype(jnp.float32), 0, keepdims=True)
    grads[:width] += dot_left(edge[...], first_low)
    grads[2 * width : 3 * width] += dot_left(received[...], first_low)
    node = lax.broadcasted_iota(jnp.int32, (nodes.shape[0], LANES), 0)
    chosen = jnp.concatenate(
        [
            jnp.where(node == send[pl.ds(step * (TILE // LANES) + i, 1), :], 1.0, 0.0).astype(jnp.bfloat16)
            for i in range(TILE // LANES)
        ],
        axis=1,
    )
    by_sender[...] += dot(chosen, first_low)
    grad[...] = upstream + dot_right(first_low, w_one[:width])

    @pl.when(step == pl.num_programs(0) - 1)
    def _():
        high, rest = split_low(by_sender[...])
        grads[width : 2 * width] = dot_left(nodes[...], high) + dot_left(nodes[...], rest)
        give = pltpu.make_async_copy(grads, all_grads, give_sem)
        give.start()
        middle = w_one[width : 2 * width]
        sender_grad[...] = node_part[...] + dot_right(high, middle) + dot_right(rest, middle)
        moves[8]()
        give_reduced = pltpu.make_async_copy(reduced, node_reduced, reduced_sem)
        give_reduced.start()
        moves[9]()
        give.wait()
        give_reduced.wait()


def edge_backward(
    count, recv, send, cotangent, edge, received, first, second, wide, node_part, nodes, w_one, w_two, gain,
    node_grads, node_vectors, collective,
):
    edges, width = edge.shape
    steps = edges // TILE
    parts = width // LANES
    per_device = nodes.shape[0]
    along = lax.axis_size("blk") // 2
    node_rows = node_grads.shape[0]
    hold = pl.BlockSpec(memory_space=pltpu.VMEM)
    scalar = pl.BlockSpec(memory_space=pltpu.SMEM)
    tile = pl.BlockSpec((TILE, width), lambda i: (i, 0))

    across = pl.BlockSpec(memory_space=pl.ANY)

    def whole(rows):
        return pl.BlockSpec((rows, width), lambda i: (0, 0))

    return pl.pallas_call(
        backward_kernel,
        grid=(steps,),
        in_specs=[
            scalar, scalar, hold, tile, tile, tile, tile, tile,
            across, hold, hold, hold, hold, hold, across, hold,
        ],
        out_specs=[
            tile, tile, across, whole(8), whole(per_device), across, whole(8),
        ],
        out_shape=[
            jax.ShapeDtypeStruct((edges, width), jnp.float32),
            jax.ShapeDtypeStruct((edges, width), jnp.bfloat16),
            jax.ShapeDtypeStruct((4 * width, width), jnp.float32),
            jax.ShapeDtypeStruct((8, width), jnp.float32),
            jax.ShapeDtypeStruct((per_device, width), jnp.float32),
            jax.ShapeDtypeStruct((node_rows, width), jnp.bfloat16),
            jax.ShapeDtypeStruct((8, width), jnp.float32),
        ],
        scratch_shapes=[
            pltpu.VMEM((wide.shape[0], parts, LANES), jnp.float32),
            pltpu.VMEM((TILE * parts, LANES), jnp.float32),
            pltpu.VMEM((2, CHUNK, width), jnp.bfloat16),
            pltpu.SemaphoreType.DMA((2,)),
            pltpu.VMEM((per_device, width), jnp.float32),
            pltpu.VMEM((4 * width, width), jnp.float32),
            pltpu.SemaphoreType.DMA,
            pltpu.VMEM((node_rows, width), jnp.bfloat16),
            pltpu.SemaphoreType.DMA,
            *reducers_scratch(node_rows, width, along, True),
            *vector_scratch((8, width), along),
        ],
        compiler_params=pltpu.CompilerParams(
            collective_id=collective, has_side_effects=True, vmem_limit_bytes=VMEM_BYTES
        ),
        cost_estimate=pl.CostEstimate(
            flops=24 * edges * width * width, bytes_accessed=40 * edges * width, transcendentals=2 * edges * width
        ),
        name="edge_backward",
    )(
        count, recv, send, cotangent, edge, received, first, second, wide,
        node_part, nodes, w_one, w_two, gain, node_grads, node_vectors,
    )


MESH = pl.DeviceIdType.MESH
PIECES = 4
LOW = jnp.bfloat16
WIDE = jnp.float32


def places():
    groups = lax.axis_size("blk")
    group, sub = lax.axis_index("blk"), lax.axis_index("sub")
    odd = lax.rem(group, 2)
    along = groups // 2
    spot = group // 2
    beside = group + 1 - 2 * odd
    return dict(
        group=group,
        sub=sub,
        core=lax.rem(sub, 2),
        chip=sub // 2,
        odd=odd,
        spot=spot,
        along=along,
        sibling=sub + 1 - 2 * lax.rem(sub, 2),
        partner=lax.rem(sub + 2, 4),
        to_sibling=(group, sub + 1 - 2 * lax.rem(sub, 2)),
        to_partner=(group, lax.rem(sub + 2, 4)),
        to_beside=(beside, sub),
        to_onward=(lax.rem(group + 2 - 4 * odd + groups, groups), sub),
        to_source=(lax.rem(group - 2 + 4 * odd + groups, groups), sub),
        peers=[(2 * lax.rem(spot + k, along) + odd, sub) for k in range(1, along)],
        near=2 - 2 * odd,
        far=2 * odd,
    )


def meet(senders):
    barrier = pltpu.get_barrier_semaphore()
    for device in senders:
        pl.semaphore_signal(barrier, inc=1, device_id=device, device_id_type=MESH)
    pl.semaphore_wait(barrier, len(senders))


def meet_all():
    barrier = pltpu.get_barrier_semaphore()
    subs = lax.axis_size("sub")
    devices = lax.axis_size("blk") * subs
    here = lax.axis_index("blk") * subs + lax.axis_index("sub")

    def greet(k, carry):
        there = lax.rem(here + k, devices)
        pl.semaphore_signal(barrier, inc=1, device_id=(there // subs, lax.rem(there, subs)), device_id_type=MESH)
        return carry

    lax.fori_loop(1, devices, greet, 0)
    pl.semaphore_wait(barrier, devices - 1)


def remote(source, target, send, recv, device):
    return pltpu.make_async_remote_copy(
        src_ref=source, dst_ref=target, send_sem=send, recv_sem=recv, device_id=device, device_id_type=MESH
    )


def in_pieces(count, body):
    block = math.gcd(count, 128)

    def run(i, carry):
        body(pl.multiple_of(i * block, block), block)
        return carry

    lax.fori_loop(0, count // block, run, 0)


def streams_of(rows):
    unit = 64 * lax.axis_size("blk")
    first = -(-(rows // unit) // 2) * unit
    return [first, rows - first] if first < rows else [first]


def padded_rows(rows):
    unit = 64 * lax.axis_size("blk")
    return -(-rows // unit) * unit


def reducers_scratch(rows, width, along, loaded):
    return [
        ref for part in streams_of(rows) for ref in reducer_scratch(part, width, along, loaded)
    ]


def reducers(at, grads, reduced, refs, loaded):
    rows = grads.shape[0]
    count = 13 if loaded else 11
    made, first = [], 0
    for i, part in enumerate(streams_of(rows)):
        made.append(reducer(at, grads, reduced, first, part, i > 0, refs[i * count : (i + 1) * count]))
        first += part
    return both(made), refs[len(made) * count :]


def reducer_scratch(rows, width, along, loaded):
    return ([pltpu.VMEM((rows // 2, width), WIDE)] if loaded else []) + [
        pltpu.VMEM((rows // 2, width), WIDE),
        pltpu.VMEM((rows // 4, width), LOW),
        pltpu.VMEM((rows // 4, width), LOW),
        pltpu.VMEM((rows // 8, width), LOW),
        pltpu.VMEM((rows // 8, width), LOW),
        pltpu.VMEM((rows // 8, width), LOW),
        pltpu.VMEM((along - 1, rows // 8 // along, width), LOW),
    ] + ([pltpu.SemaphoreType.DMA] if loaded else []) + [
        pltpu.SemaphoreType.DMA((6,)),
        pltpu.SemaphoreType.DMA((6,)),
        pltpu.SemaphoreType.DMA((2, along - 1)),
        pltpu.SemaphoreType.DMA((2, along - 1)),
    ]


def reducer(at, grads, reduced, first, rows, swap, refs):
    (
        half, half_in, cross_out, cross_in, side_out, side_in, ring_out, ring_in,
        load_sem, step_send, step_recv, ring_send, ring_recv,
    ) = refs if len(refs) == 13 else (None, *refs[:7], None, *refs[7:])
    along, peers = at["along"], at["peers"]
    turns = [(at["chip"], at["to_partner"]), (at["odd"], at["to_beside"])]
    (bit_one, device_one), (bit_two, device_two) = turns[::-1] if swap else turns
    core, spot = at["core"], at["spot"]
    n_half, n_cross, n_side, n_ring = rows // 2, rows // 4, rows // 8, rows // 8 // along
    at_half = first + core * n_half
    at_cross = at_half + bit_one * n_cross
    at_side = at_cross + bit_two * n_side
    at_ring = at_side + spot * n_ring

    def span(start, count):
        return pl.ds(pl.multiple_of(start, 16), count)

    def step(kind):
        if kind == 0:
            source, target, device = grads.at[span(first + (1 - core) * n_half, n_half)], half_in, at["to_sibling"]
        elif kind == 1:
            source, target, device = cross_out, cross_in, device_one
        elif kind == 2:
            source, target, device = side_out, side_in, device_two
        else:
            start, count, device = {
                3: (at_side, n_side, device_two),
                4: (at_cross, n_cross, device_one),
                5: (at_half, n_half, at["to_sibling"]),
            }[kind]
            source = target = reduced.at[span(start, count)]
        return remote(source, target, step_send.at[kind], step_recv.at[kind], device)

    def ring(kind, k):
        if kind == 0:
            source = ring_out.at[span(lax.rem(spot + k, along) * n_ring, n_ring)]
            target = ring_in.at[k - 1]
        else:
            source = target = reduced.at[span(at_ring, n_ring)]
        return remote(source, target, ring_send.at[kind, k - 1], ring_recv.at[kind, k - 1], peers[k - 1])

    if half is None:
        half, load = grads.at[span(at_half, n_half)], None
    else:
        load = pltpu.make_async_copy(grads.at[span(at_half, n_half)], half, load_sem)

    def start():
        step(0).start()
        if load is not None:
            load.start()

    def add_half():
        if load is not None:
            load.wait()
        step(0).wait_recv()
        other = (1 - bit_one) * n_cross

        def part(i, block):
            here = pl.ds(pl.multiple_of(other + i, block), block)
            cross_out[pl.ds(i, block), :] = (half[here, :] + half_in[here, :]).astype(LOW)

        in_pieces(n_cross, part)
        step(1).start()

    def add_cross():
        mine, other = bit_one * n_cross, (1 - bit_two) * n_side
        step(1).wait_recv()

        def part(i, block):
            there = pl.ds(pl.multiple_of(other + i, block), block)
            here = pl.ds(pl.multiple_of(mine + other + i, block), block)
            side_out[pl.ds(i, block), :] = (half[here, :] + half_in[here, :] + cross_in[there, :].astype(WIDE)).astype(LOW)

        in_pieces(n_side, part)
        step(2).start()

    def add_side():
        mine, kept = bit_one * n_cross, bit_two * n_side
        step(2).wait_recv()

        def part(i, block):
            there = pl.ds(pl.multiple_of(kept + i, block), block)
            here = pl.ds(pl.multiple_of(mine + kept + i, block), block)
            flat = pl.ds(i, block)
            value = half[here, :] + half_in[here, :] + cross_in[there, :].astype(WIDE) + side_in[flat, :].astype(WIDE)
            half[here, :] = value
            ring_out[flat, :] = value.astype(LOW)

        in_pieces(n_side, part)
        for k in range(1, along):
            ring(0, k).start()

    def add_ring():
        value = half[span(bit_one * n_cross + bit_two * n_side + spot * n_ring, n_ring), :]
        for k in range(1, along):
            ring(0, k).wait_recv()
            value = value + ring_in[k - 1].astype(WIDE)
        reduced[span(at_ring, n_ring), :] = value.astype(LOW)
        for k in range(1, along):
            ring(1, k).start()

    def share_side():
        for k in range(1, along):
            ring(1, k).wait_recv()
        step(3).start()

    def share_cross():
        step(3).wait_recv()
        step(4).start()

    def share_half():
        step(4).wait_recv()
        step(5).start()

    def last():
        step(5).wait_recv()

    def drain():
        for kind in range(6):
            step(kind).wait_send()
        for k in range(1, along):
            ring(0, k).wait_send()
            ring(1, k).wait_send()

    return [start, add_half, add_cross, add_side, add_ring, share_side, share_cross, share_half, last, drain]


def vector_scratch(shape, along):
    return [
        pltpu.VMEM((4, *shape), WIDE),
        pltpu.VMEM((2 + along, *shape), WIDE),
        pltpu.SemaphoreType.DMA((2 + along,)),
        pltpu.SemaphoreType.DMA((2 + along,)),
    ]


def vector_reducer(at, vectors, reduced, refs):
    held, held_in, send_sems, recv_sems = refs
    along = at["along"]
    devices = (at["to_sibling"], at["to_partner"], at["to_beside"], *at["peers"])

    def move(kind):
        return remote(held.at[min(kind, 3)], held_in.at[kind], send_sems.at[kind], recv_sems.at[kind], devices[kind])

    def start():
        held[0] = vectors[...]
        move(0).start()

    def turn(kind):
        def run():
            move(kind).wait_recv()
            held[kind + 1] = held[kind] + held_in[kind]
            for k in range(kind + 1, kind + 2 if kind < 2 else 2 + along):
                move(k).start()

        return run

    def last():
        value = held[3]
        for k in range(3, 2 + along):
            move(k).wait_recv()
            value = value + held_in[k]
        reduced[...] = value
        for k in range(2 + along):
            move(k).wait_send()

    return [start, turn(0), turn(1), turn(2), last]


def both(streams):
    return [lambda steps=steps: [step() for step in steps] for steps in zip(*streams)]


def spread_moves(at, own, table, keep_sem, send_sems, recv_sems):
    sub, partner, near, far = at["sub"], at["partner"], at["near"], at["far"]
    to_sibling, to_partner, to_beside, to_onward = (
        at["to_sibling"], at["to_partner"], at["to_beside"], at["to_onward"]
    )
    size = own.shape[0] // PIECES

    def move(kind, piece):
        source, slot, device = {
            0: (None, (1, sub), to_partner),
            1: (None, (far, sub), to_beside),
            2: (None, (1, sub), to_sibling),
            3: ((1, partner), (far, partner), to_beside),
            4: ((1, partner), (1, partner), to_sibling),
            5: ((near, sub), (far, sub), to_onward),
            6: ((near, sub), (near, sub), to_sibling),
            7: ((near, partner), (far, partner), to_onward),
            8: ((near, partner), (near, partner), to_sibling),
            9: ((far, sub), (far, sub), to_sibling),
            10: ((far, partner), (far, partner), to_sibling),
        }[kind]
        source = own if source is None else table.at[source[0], source[1]]
        rows = pl.ds(piece * size, size)
        return remote(
            source.at[rows], table.at[slot[0], slot[1], rows],
            send_sems.at[kind, piece], recv_sems.at[kind, piece], device,
        )

    keep = pltpu.make_async_copy(own, table.at[1, sub], keep_sem)

    def start():
        for piece in range(PIECES):
            for kind in (0, 1, 2):
                move(kind, piece).start()
        keep.start()

    def relay(arrived, kinds, piece):
        move(arrived, piece).wait_recv()
        for kind in kinds:
            move(kind, piece).start()

    def one(piece):
        relay(0, (3, 4), piece)
        relay(1, (5, 6), piece)

    def two(piece):
        relay(3, (7, 8), piece)
        relay(5, (9,), piece)

    def three(piece):
        relay(7, (10,), piece)

    def drain():
        for kind in range(11):
            for piece in range(PIECES):
                if kind in (2, 4, 6, 8, 9, 10):
                    move(kind, piece).wait_recv()
                move(kind, piece).wait_send()
        keep.wait()

    return start, one, two, three, drain


def spread_scratch():
    return [
        pltpu.SemaphoreType.DMA,
        pltpu.SemaphoreType.DMA((11, PIECES)),
        pltpu.SemaphoreType.DMA((11, PIECES)),
    ]


HALVES = 2
ORDER = (
    (0, 1, 0), (0, 1, 1), (1, 1, 0), (0, 0, 0), (1, 1, 1), (0, 0, 1),
    (1, 0, 0), (2, 1, 0), (1, 0, 1), (2, 1, 1), (2, 0, 0), (2, 0, 1),
)


def collect_scratch(rows, width, edges):
    return [
        pltpu.VMEM((edges, width), LOW),
        pltpu.VMEM((2, 3, 2, rows, width), WIDE),
        pltpu.VMEM((3, 2, rows, width), WIDE),
        pltpu.VMEM((2, rows, width), LOW),
        pltpu.VMEM((2, rows, width), LOW),
        pltpu.VMEM((2, rows, width), LOW),
        pltpu.VMEM((2, rows, width), LOW),
        pltpu.VMEM((rows, width), LOW),
        pltpu.VMEM((rows, width), LOW),
        pltpu.SemaphoreType.DMA,
        pltpu.SemaphoreType.DMA((3, 2, HALVES)),
        pltpu.SemaphoreType.DMA((3, 2, HALVES)),
        pltpu.SemaphoreType.DMA((5, PIECES)),
        pltpu.SemaphoreType.DMA((5, PIECES)),
    ]


def collect_moves(at, index, messages, out, refs):
    (
        held, parts, landed, far_out, far_in, near_out, near_in, pair_out, pair_in,
        load_sem, give_sems, take_sems, send_sems, recv_sems,
    ) = refs
    sub, partner, sibling = at["sub"], at["partner"], at["sibling"]
    rows = out.shape[0]
    size = rows // PIECES
    part_rows = rows // HALVES
    load = pltpu.make_async_copy(messages, held, load_sem)

    def piece_of(ref, piece):
        return ref.at[pl.ds(piece * size, size)]

    def give(role, side, half):
        span = pl.ds(pl.multiple_of(half * part_rows, part_rows), part_rows)
        return remote(
            parts.at[0, role, side, span], landed.at[role, side, span],
            give_sems.at[role, side, half], take_sems.at[role, side, half], at["to_sibling"],
        )

    def hop(kind, piece):
        source, target, device = {
            0: (far_out.at[0], far_in.at[0], at["to_source"]),
            1: (far_out.at[1], far_in.at[1], at["to_source"]),
            2: (near_out.at[0], near_in.at[0], at["to_beside"]),
            3: (near_out.at[1], near_in.at[1], at["to_beside"]),
            4: (pair_out, pair_in, at["to_partner"]),
        }[kind]
        return remote(
            piece_of(source, piece), piece_of(target, piece),
            send_sems.at[kind, piece], recv_sems.at[kind, piece], device,
        )

    def add_messages(step):
        def pick(column):
            return lax.rem(sum(int(item[column]) << (2 * i) for i, item in enumerate(ORDER)) >> (2 * step), 4)

        role, side, half = pick(0), pick(1), pick(2)
        relation = jnp.where(role == 0, at["far"], jnp.where(role == 1, at["near"], 1))
        span = pl.ds(pl.multiple_of(half * part_rows, part_rows), part_rows)

        def whose(w, carry):
            first = jnp.where(w == 0, sibling, sub)
            target = lax.rem(first + 2 * side, 4)
            base = (relation * 4 + target) * rows + half * part_rows
            node = lax.broadcasted_iota(jnp.int32, (part_rows, LANES), 0) + base
            chosen = jnp.concatenate(
                [jnp.where(node == index[j : j + 1, :], 1.0, 0.0).astype(LOW) for j in range(index.shape[0])], axis=1
            )
            parts[w, role, side, span, :] = dot(chosen, held[...])
            return carry

        lax.fori_loop(0, 2, whose, 0)
        give(role, side, half).start()

    def local(role, side, piece):
        span = pl.ds(piece * size, size)
        return parts[1, role, side, span, :] + landed[role, side, span, :]

    def arrived(kind, ref, piece):
        hop(kind, piece).wait_recv()
        return ref[pl.ds(piece * size, size), :].astype(WIDE)

    def pieces(half):
        return range(half * PIECES // HALVES, (half + 1) * PIECES // HALVES)

    def far_step(side, half):
        give(0, side, half).wait_recv()
        for piece in pieces(half):
            far_out[side, pl.ds(piece * size, size), :] = local(0, side, piece).astype(LOW)
            hop(side, piece).start()

    def near_step(side, half):
        give(1, side, half).wait_recv()
        for piece in pieces(half):
            value = local(1, side, piece) + arrived(side, far_in.at[side], piece)
            near_out[side, pl.ds(piece * size, size), :] = value.astype(LOW)
            hop(2 + side, piece).start()

    def pair_step(half):
        give(2, 1, half).wait_recv()
        for piece in pieces(half):
            value = local(2, 1, piece) + arrived(3, near_in.at[1], piece)
            pair_out[pl.ds(piece * size, size), :] = value.astype(LOW)
            hop(4, piece).start()

    def last_step(half):
        give(2, 0, half).wait_recv()
        for piece in pieces(half):
            value = local(2, 0, piece) + arrived(2, near_in.at[0], piece) + arrived(4, pair_in, piece)
            out[pl.ds(piece * size, size), :] = value

    def drain():
        for item in ORDER:
            give(*item).wait_send()
        for kind in range(5):
            for piece in range(PIECES):
                hop(kind, piece).wait_send()

    events = {
        1: [lambda: far_step(1, 0)],
        2: [lambda: far_step(1, 1)],
        3: [lambda: near_step(1, 0)],
        4: [lambda: far_step(0, 0)],
        5: [lambda: near_step(1, 1), lambda: far_step(0, 1)],
        7: [lambda: near_step(0, 0), lambda: pair_step(0)],
        9: [lambda: near_step(0, 1), lambda: pair_step(1)],
    }

    def run(more):
        def step(i, carry):
            add_messages(i)
            for k in sorted(set(events) | set(more)):
                @pl.when(i == k)
                def _():
                    for event in events.get(k, []) + more.get(k, []):
                        event()

            return carry

        lax.fori_loop(0, len(ORDER), step, 0)
        for half in range(HALVES):
            last_step(half)

    return load, run, drain


def exchange_scratch(rows, width, devices):
    slab = width // devices * (rows // LANES)
    return [
        pltpu.VMEM((devices * slab, LANES), WIDE),
        pltpu.VMEM((devices * slab, LANES), LOW),
        pltpu.VMEM((devices, slab, LANES), LOW),
        pltpu.VMEM((slab, LANES), WIDE),
        pltpu.SemaphoreType.DMA((devices - 1,)),
        pltpu.SemaphoreType.DMA((devices - 1,)),
    ]


def exchange_moves(residual, out, refs):
    flat, packed, landed, opened, send_sems, recv_sems = refs
    subs = lax.axis_size("sub")
    devices = lax.axis_size("blk") * subs
    here = lax.axis_index("blk") * subs + lax.axis_index("sub")
    slab = landed.shape[1]
    channels = out.shape[0]
    parts = slab // channels
    nodes = parts * LANES

    def move(k):
        there = lax.rem(here + k, devices)
        return remote(
            packed.at[pl.ds(pl.multiple_of(there * slab, slab), slab)], landed.at[here],
            send_sems.at[k - 1], recv_sems.at[k - 1], (there // subs, lax.rem(there, subs)),
        )

    def start(values):
        lay_rows(flat, 0, values.T)

        def cast(i, block):
            packed[pl.ds(i, block), :] = flat[pl.ds(i, block), :].astype(LOW)

        in_pieces(flat.shape[0], cast)

        def send(k, carry):
            move(k).start()
            return carry

        lax.fori_loop(1, devices, send, 0)

    def open_slab(source, device):
        opened[...] = source.astype(WIDE)
        for j in range(parts):
            columns = pl.ds(pl.multiple_of(device * nodes + j * LANES, LANES), LANES)
            out[:, columns] = residual[:, columns] + opened[pl.ds(j, channels, stride=parts), :]

    def last():
        open_slab(packed[pl.ds(pl.multiple_of(here * slab, slab), slab), :], here)

        def take(k, carry):
            move(k).wait_recv()
            device = lax.rem(here - k + devices, devices)
            open_slab(landed[device], device)
            return carry

        lax.fori_loop(1, devices, take, 0)

        def sent(k, carry):
            move(k).wait_send()
            return carry

        lax.fori_loop(1, devices, sent, 0)

    return start, last


def finish_kernel(
    index, messages, grads, vectors, node_part, weight, residual, node_grad, reduced, reduced_vectors, total, *refs
):
    at = places()
    count = len(collect_scratch(64, 128, 64))
    load, run, drain = collect_moves(at, index, messages, total, refs[:count])
    load.start()
    meet_all()
    steps, refs = reducers(at, grads, reduced, refs[count:], True)
    vector_steps = vector_reducer(at, vectors, reduced_vectors, refs[:4])
    exchange, receive = exchange_moves(residual, node_grad, refs[4:])
    steps[0]()
    vector_steps[0]()
    load.wait()
    run({
        1: [steps[1], vector_steps[1]],
        4: [steps[2], vector_steps[2]],
        6: [steps[3], vector_steps[3]],
        8: [steps[4]],
        10: [steps[5]],
    })
    high, rest = split_low(total[...])
    exchange(node_part[...] + dot_right(high, weight[...]) + dot_right(rest, weight[...]))
    for step in steps[6:8]:
        step()
    receive()
    steps[8]()
    vector_steps[4]()
    drain()
    steps[9]()


def finish(index, messages, grads, vectors, node_part, weight, residual, collective):
    rows, width = node_part.shape
    edges = messages.shape[0]
    along = lax.axis_size("blk") // 2
    devices = lax.axis_size("blk") * lax.axis_size("sub")
    hold = pl.BlockSpec(memory_space=pltpu.VMEM)
    across = pl.BlockSpec(memory_space=pl.ANY)
    return pl.pallas_call(
        finish_kernel,
        grid=(1,),
        in_specs=[
            hold, across, across, hold, hold, pl.BlockSpec((width, width), lambda i: (2, 0)), hold,
        ],
        out_specs=[hold] * 3,
        out_shape=[
            jax.ShapeDtypeStruct(residual.shape, WIDE),
            jax.ShapeDtypeStruct(grads.shape, LOW),
            jax.ShapeDtypeStruct(vectors.shape, WIDE),
        ],
        scratch_shapes=[
            pltpu.VMEM((rows, width), WIDE),
            *collect_scratch(rows, width, edges),
            *reducers_scratch(grads.shape[0], width, along, True),
            *vector_scratch(vectors.shape, along),
            *exchange_scratch(rows, width, devices),
        ],
        compiler_params=pltpu.CompilerParams(
            collective_id=collective, has_side_effects=True, vmem_limit_bytes=VMEM_BYTES
        ),
        name="finish_sums",
    )(index.reshape(edges // LANES, LANES), messages, grads, vectors, node_part, weight, residual)


def middle_kernel(
    index, messages, node_low, upstream, w_one, b_one, w_two, b_two, gain, shift, residual,
    table, node_part, node_out, grads, vectors, total, sent, *refs
):
    at = places()
    count = len(collect_scratch(64, 128, 64))
    load, run, drain = collect_moves(at, index, messages, total, refs[:count])
    load.start()
    meet_all()
    refs = refs[count:]
    start, one, two, three, end = spread_moves(at, sent, table, *refs[:3])
    exchange, receive = exchange_moves(residual, node_out, refs[3:])
    load.wait()
    run({})

    width = total.shape[1]
    low = total[...].astype(LOW)
    pre = dot(node_low[...], w_one[:width]) + dot(low, w_one[width:]) + b_one[...]
    logistic = jax.nn.sigmoid(pre)
    act = (pre * logistic).astype(LOW)
    normal, scale = row_normal(dot(act, w_two[...]) + b_two[...])
    given = upstream[...].T
    scaled = given * gain[...]
    slope = jnp.mean(scaled * normal, -1, keepdims=True)
    fourth = scale * (scaled - jnp.mean(scaled, -1, keepdims=True) - normal * slope)
    fourth_low = fourth.astype(LOW)
    third = dot_right(fourth_low, w_two[...]) * (logistic * (1.0 + pre * (1.0 - logistic)))
    third_low = third.astype(LOW)
    sent[...] = dot_right(third_low, w_one[width:]).astype(LOW)
    start()
    grads[:width] = dot_left(node_low[...], third_low)
    grads[width : 2 * width] = dot_left(low, third_low)
    grads[2 * width : 3 * width] = dot_left(act, fourth_low)
    vectors[...] = jnp.zeros_like(vectors)
    vectors[0:1] = jnp.sum(third_low.astype(WIDE), 0, keepdims=True)
    vectors[1:2] = jnp.sum(fourth_low.astype(WIDE), 0, keepdims=True)
    vectors[2:3] = jnp.sum(given * normal, 0, keepdims=True)
    vectors[3:4] = jnp.sum(given, 0, keepdims=True)
    node_part[...] = dot_right(third_low, w_one[:width])
    exchange(normal * gain[...] + shift[...])

    for stage in (one, two, three):
        for piece in range(PIECES):
            stage(piece)
    receive()
    end()
    drain()


def middle(index, messages, node_low, upstream, w_one, b_one, w_two, b_two, gain, shift, residual, collective):
    rows, width = node_low.shape
    edges = messages.shape[0]
    devices = lax.axis_size("blk") * lax.axis_size("sub")
    grad_rows = padded_rows(3 * width)
    hold = pl.BlockSpec(memory_space=pltpu.VMEM)
    across = pl.BlockSpec(memory_space=pl.ANY)
    table, node_part, node_out, grads, vectors = pl.pallas_call(
        middle_kernel,
        in_specs=[hold, across] + [hold] * 9,
        out_specs=[across] + [hold] * 4,
        out_shape=[
            jax.ShapeDtypeStruct((3, 4, rows, width), LOW),
            jax.ShapeDtypeStruct((rows, width), WIDE),
            jax.ShapeDtypeStruct(residual.shape, WIDE),
            jax.ShapeDtypeStruct((grad_rows, width), WIDE),
            jax.ShapeDtypeStruct((8, width), WIDE),
        ],
        scratch_shapes=[
            pltpu.VMEM((rows, width), WIDE),
            pltpu.VMEM((rows, width), LOW),
            *collect_scratch(rows, width, edges),
            *spread_scratch(),
            *exchange_scratch(rows, width, devices),
        ],
        compiler_params=pltpu.CompilerParams(
            collective_id=collective, has_side_effects=True, vmem_limit_bytes=VMEM_BYTES
        ),
        name="middle_nodes",
    )(
        index.reshape(edges // LANES, LANES), messages, node_low, upstream,
        w_one, b_one, w_two, b_two, gain, shift, residual,
    )
    return table.reshape(12 * rows, width), node_part, node_out, grads, vectors


def scatter_scratch(channels, nodes, devices):
    slab = channels * (nodes // LANES)
    return [
        pltpu.VMEM((devices * slab, LANES), WIDE),
        pltpu.VMEM((devices * slab, LANES), LOW),
        pltpu.VMEM((devices, slab, LANES), LOW),
        pltpu.VMEM((slab, LANES), WIDE),
        pltpu.VMEM((nodes // LANES * devices * channels, LANES), WIDE),
        pltpu.SemaphoreType.DMA((devices - 1,)),
        pltpu.SemaphoreType.DMA((devices - 1,)),
    ]


def scatter_moves(shard, refs):
    flat, packed, landed, opened, square, send_sems, recv_sems = refs
    subs = lax.axis_size("sub")
    devices = lax.axis_size("blk") * subs
    here = lax.axis_index("blk") * subs + lax.axis_index("sub")
    slab = landed.shape[1]
    channels = shard.shape[0]
    parts = slab // channels
    nodes = parts * LANES

    def move(k):
        there = lax.rem(here + k, devices)
        return remote(
            packed.at[pl.ds(pl.multiple_of(there * slab, slab), slab)], landed.at[here],
            send_sems.at[k - 1], recv_sems.at[k - 1], (there // subs, lax.rem(there, subs)),
        )

    def start():
        def pack(k, carry):
            device = lax.rem(here + k, devices)
            rows = pl.ds(pl.multiple_of(device * slab, slab), slab)
            for j in range(parts):
                columns = pl.ds(pl.multiple_of(device * nodes + j * LANES, LANES), LANES)
                flat[pl.ds(device * slab + j, channels, stride=parts), :] = shard[:, columns]
            packed[rows, :] = flat[rows, :].astype(LOW)
            return carry

        def send(k, carry):
            pack(k, carry)
            move(k).start()
            return carry

        lax.fori_loop(1, devices, send, 0)
        pack(0, 0)

    def open_slab(source, device):
        opened[...] = source.astype(WIDE)
        for j in range(parts):
            rows = pl.ds(pl.multiple_of((j * devices + device) * channels, channels), channels)
            square[rows, :] = opened[pl.ds(j, channels, stride=parts), :]

    def last(rows):
        open_slab(packed[pl.ds(pl.multiple_of(here * slab, slab), slab), :], here)

        def take(k, carry):
            move(k).wait_recv()
            device = lax.rem(here - k + devices, devices)
            open_slab(landed[device], device)
            return carry

        lax.fori_loop(1, devices, take, 0)
        width = devices * channels
        for j in range(parts):
            rows[j * LANES : (j + 1) * LANES, :] = square[j * width : (j + 1) * width, :].T.astype(LOW)

    def drain():
        def sent(k, carry):
            move(k).wait_send()
            return carry

        lax.fori_loop(1, devices, sent, 0)

    return start, last, drain


def begin_kernel(
    shard, later, senders, receivers, own, table, later_out, send_local, recv_wide, held, held_sem, *refs
):
    at = places()
    fetch = pltpu.make_async_copy(later, held, held_sem)
    fetch.start()
    meet_all()
    start, last, drain = scatter_moves(shard, refs[3:])
    start()
    last(own)
    begin, one, two, three, end = spread_moves(at, own, table, *refs[:3])
    begin()
    rows = own.shape[0]
    groups, subs = lax.axis_size("blk"), lax.axis_size("sub")
    send_local[...] = senders[...] - (at["group"] * subs + at["sub"]) * rows
    relative = lax.rem(receivers[...] // (rows * subs) - at["group"] + 1 + groups, groups)
    recv_wide[...] = relative * (rows * subs) + lax.rem(receivers[...], rows * subs)
    fetch.wait()
    give = pltpu.make_async_copy(held, later_out, held_sem)
    give.start()
    drain()
    for stage in (one, two, three):
        for piece in range(PIECES):
            stage(piece)
    give.wait()
    end()


def begin(shard, later, senders, receivers, rows, collective):
    channels, nodes = shard.shape
    devices = lax.axis_size("blk") * lax.axis_size("sub")
    width = channels * devices
    hold = pl.BlockSpec(memory_space=pltpu.VMEM)
    across = pl.BlockSpec(memory_space=pl.ANY)
    lines = (senders.shape[0] // LANES, LANES)
    own, table, later, send_local, recv_wide = pl.pallas_call(
        begin_kernel,
        in_specs=[hold, across, hold, hold],
        out_specs=[hold, across, across, hold, hold],
        out_shape=[
            jax.ShapeDtypeStruct((rows, width), LOW),
            jax.ShapeDtypeStruct((3, 4, rows, width), LOW),
            jax.ShapeDtypeStruct(later.shape, later.dtype),
            jax.ShapeDtypeStruct(lines, jnp.int32),
            jax.ShapeDtypeStruct(lines, jnp.int32),
        ],
        scratch_shapes=[
            pltpu.VMEM(later.shape, later.dtype),
            pltpu.SemaphoreType.DMA,
            *spread_scratch(),
            *scatter_scratch(channels, rows, devices),
        ],
        compiler_params=pltpu.CompilerParams(
            collective_id=collective, has_side_effects=True, vmem_limit_bytes=VMEM_BYTES
        ),
        name="begin_rows",
    )(shard, later, senders.reshape(lines), receivers.reshape(lines))
    return own, table.reshape(12 * rows, width), later, send_local, recv_wide


def shards(
    node_input,
    edge_input,
    senders,
    receivers,
    edge_count,
    edge_w_one,
    edge_b_one,
    edge_w_two,
    edge_b_two,
    edge_gain,
    edge_shift,
    node_w_one,
    node_b_one,
    node_w_two,
    node_b_two,
    node_gain,
    node_shift,
    node_cotangent,
    edge_cotangent,
):
    groups = lax.axis_size("blk")
    sub_count = lax.axis_size("sub")
    width = edge_input.shape[1]
    per_device = node_input.shape[1] // (groups * sub_count)
    node_low, wide_low, cotangent_later, send_local, recv_wide = begin(
        node_input, node_cotangent, senders, receivers, per_device, 0
    )
    node_upstream = to_nodes(cotangent_later)
    recv_list = recv_wide.reshape(-1)
    edge_result, first_pre, second_pre, received, messages = edge_forward(
        edge_count, recv_list, send_local, edge_input, wide_low, node_low,
        edge_w_one, edge_b_one[None], edge_w_two, edge_b_two[None], edge_gain[None], edge_shift[None],
    )
    wide_grad, node_part, node_out, node_grads, node_vectors = middle(
        recv_list, messages, node_low, node_upstream, node_w_one, node_b_one[None], node_w_two, node_b_two[None],
        node_gain[None], node_shift[None], node_input, 1,
    )
    edge_grad, messages, grads, vectors, node_part, node_summed, node_vectors = edge_backward(
        edge_count, recv_list, send_local, edge_cotangent, edge_input, received, first_pre, second_pre,
        wide_grad, node_part, node_low, edge_w_one, edge_w_two,
        edge_gain[None], node_grads, node_vectors, 2,
    )
    node_grad, summed, vectors = finish(
        recv_list, messages, grads, vectors, node_part, edge_w_one, node_cotangent, 3
    )
    summed = summed.astype(jnp.float32)
    node_summed = node_summed.astype(jnp.float32)
    return (
        node_out,
        edge_result,
        node_grad,
        edge_grad,
        summed[: 3 * width],
        vectors[0],
        summed[3 * width :],
        vectors[1],
        vectors[2],
        vectors[3],
        node_summed[: 2 * width],
        node_vectors[0],
        node_summed[2 * width : 3 * width],
        node_vectors[1],
        node_vectors[2],
        node_vectors[3],
    )


def solution(mesh):
    placed = (
        P(("blk", "sub"), None),
        P(("blk", "sub"), None),
        P(("blk", "sub")),
        P(("blk", "sub")),
        P(("blk", "sub")),
        P(),
        P(),
        P(),
        P(),
        P(),
        P(),
        P(),
        P(),
        P(),
        P(),
        P(),
        P(),
        P(("blk", "sub"), None),
        P(("blk", "sub"), None),
    )
    return jax.shard_map(
        shards,
        mesh=mesh,
        in_specs=placed,
        out_specs=(
            P(("blk", "sub"), None),
            P(("blk", "sub"), None),
            P(("blk", "sub"), None),
            P(("blk", "sub"), None),
            P(),
            P(),
            P(),
            P(),
            P(),
            P(),
            P(),
            P(),
            P(),
            P(),
            P(),
            P(),
        ),
        check_vma=False,
    )
```

```python
import math

import jax
import jax.numpy as jnp
from jax import lax
from jax.experimental import pallas as pl
from jax.experimental.pallas import tpu as pltpu
from jax.sharding import PartitionSpec as P

EPSILON = 1e-05


TILE = 512
CHUNK = 512
LANES = 128
VMEM_BYTES = 60 * 2**20


def dot(left, right):
    return jnp.dot(left, right, preferred_element_type=jnp.float32)


def dot_left(left, right):
    return lax.dot_general(
        left, right, (((0,), (0,)), ((), ())), preferred_element_type=jnp.float32
    )


def dot_right(left, right):
    return lax.dot_general(
        left, right, (((1,), (1,)), ((), ())), preferred_element_type=jnp.float32
    )


def split_low(values):
    high = values.astype(jnp.bfloat16)
    return high, (values - high.astype(jnp.float32)).astype(jnp.bfloat16)


def lay_rows(target, start, values):
    count, width = values.shape
    parts = width // LANES
    for j in range(parts):
        target[pl.ds(start * parts + j, count, stride=parts), :] = values[:, j * LANES : (j + 1) * LANES]


def read_rows(source, start, count, parts):
    return jnp.concatenate(
        [source[pl.ds(start * parts + j, count, stride=parts), :] for j in range(parts)], axis=1
    )


def load_table(wide, table, stage, sems):
    steps = wide.shape[0] // CHUNK

    def fetch(i, slot):
        return pltpu.make_async_copy(wide.at[pl.ds(i * CHUNK, CHUNK)], stage.at[slot], sems.at[slot])

    fetch(0, 0).start()

    def body(i, carry):
        slot = lax.rem(i, 2)

        @pl.when(i + 1 < steps)
        def _():
            fetch(i + 1, 1 - slot).start()

        fetch(i, slot).wait()

        def piece(k, carry):
            values = stage[slot, pl.ds(k * 64, 64), :].astype(jnp.float32)
            lay_rows(table, i * CHUNK + k * 64, values)
            return carry

        return lax.fori_loop(0, CHUNK // 64, piece, carry)

    lax.fori_loop(0, steps, body, 0)


def gather_rows(index, base, table, rows, parts):
    count = rows.shape[0] // parts

    def body(i, carry):
        for u in range(16):
            slot = i * 16 + u
            place = index[base + slot]
            rows[pl.ds(pl.multiple_of(slot * parts, parts), parts), :] = table[
                pl.ds(pl.multiple_of(place * parts, parts), parts), :
            ]
        return carry

    lax.fori_loop(0, count // 16, body, 0)


def row_normal(values):
    average = jnp.mean(values, -1, keepdims=True)
    centred = values - average
    variance = jnp.mean(centred * centred, -1, keepdims=True)
    scale = lax.rsqrt(variance + EPSILON)
    return centred * scale, scale


def forward_kernel(
    count, recv, send, edge, wide, nodes, w_one, b_one, w_two, b_two, gain, shift,
    result, first, second, received, message,
    table, rows, stage, sems,
):
    step = pl.program_id(0)
    base = step * TILE
    width = nodes.shape[1]
    parts = width // LANES

    @pl.when(step == 0)
    def _():
        load_table(wide, table, stage, sems)

    gather_rows(recv, base, table, rows, parts)
    from_recv = read_rows(rows, 0, TILE, parts).astype(jnp.bfloat16)
    received[...] = from_recv
    lane = lax.broadcasted_iota(jnp.int32, (LANES, LANES), 1)
    chosen = []
    for i in range(TILE // LANES):
        column = jnp.broadcast_to(send[pl.ds(step * (TILE // LANES) + i, 1), :], (LANES, LANES)).T
        chosen.append(
            jnp.concatenate(
                [
                    jnp.where(column == lane + j * LANES, 1.0, 0.0).astype(jnp.bfloat16)
                    for j in range(nodes.shape[0] // LANES)
                ],
                axis=1,
            )
        )
    chosen = jnp.concatenate(chosen, axis=0)
    from_send = dot(chosen, nodes[...]).astype(jnp.bfloat16)
    pre = (
        dot(edge[...], w_one[:width])
        + dot(from_send, w_one[width : 2 * width])
        + dot(from_recv, w_one[2 * width :])
        + b_one[...]
    )
    first[...] = pre
    act = (pre * jax.nn.sigmoid(pre)).astype(jnp.bfloat16)
    post = dot(act, w_two[...]) + b_two[...]
    second[...] = post
    normal, _ = row_normal(post)
    branch = normal * gain[...] + shift[...]
    live = base + lax.broadcasted_iota(jnp.int32, (TILE, 1), 0) < count[0]
    outcome = edge[...].astype(jnp.float32) + jnp.where(live, branch, 0.0)
    result[...] = outcome
    message[...] = jnp.where(live, outcome, 0.0).astype(jnp.bfloat16)


def edge_forward(count, recv, send, edge, wide, nodes, w_one, b_one, w_two, b_two, gain, shift):
    edges, width = edge.shape
    steps = edges // TILE
    parts = width // LANES
    hold = pl.BlockSpec(memory_space=pltpu.VMEM)
    scalar = pl.BlockSpec(memory_space=pltpu.SMEM)
    tile = pl.BlockSpec((TILE, width), lambda i: (i, 0))
    return pl.pallas_call(
        forward_kernel,
        grid=(steps,),
        in_specs=[
            scalar, scalar, hold, tile,
            pl.BlockSpec(memory_space=pl.ANY), hold, hold, hold, hold, hold, hold, hold,
        ],
        out_specs=[tile] * 5,
        out_shape=[
            jax.ShapeDtypeStruct((edges, width), jnp.float32),
            jax.ShapeDtypeStruct((edges, width), jnp.float32),
            jax.ShapeDtypeStruct((edges, width), jnp.float32),
            jax.ShapeDtypeStruct((edges, width), jnp.bfloat16),
            jax.ShapeDtypeStruct((edges, width), jnp.bfloat16),
        ],
        scratch_shapes=[
            pltpu.VMEM((wide.shape[0] * parts, LANES), jnp.float32),
            pltpu.VMEM((TILE * parts, LANES), jnp.float32),
            pltpu.VMEM((2, CHUNK, width), jnp.bfloat16),
            pltpu.SemaphoreType.DMA((2,)),
        ],
        compiler_params=pltpu.CompilerParams(vmem_limit_bytes=VMEM_BYTES),
        cost_estimate=pl.CostEstimate(
            flops=20 * edges * width * width, bytes_accessed=40 * edges * width, transcendentals=2 * edges * width
        ),
        name="edge_forward",
    )(count, recv, send, edge, wide, nodes, w_one, b_one, w_two, b_two, gain, shift)


def backward_kernel(
    count, recv, send, cotangent, edge, received, first, second, wide, node_part, nodes, w_one, w_two, gain,
    grad, message, all_grads, vectors, sender_grad,
    table, rows, stage, sems, by_sender, grads, give_sem,
):
    step = pl.program_id(0)
    base = step * TILE
    width = nodes.shape[1]
    parts = width // LANES

    @pl.when(step == 0)
    def _():
        load_table(wide, table, stage, sems)
        grads[...] = jnp.zeros_like(grads)
        vectors[...] = jnp.zeros_like(vectors)
        by_sender[...] = jnp.zeros_like(by_sender)

    gather_rows(recv, base, table, rows, parts)
    live = base + lax.broadcasted_iota(jnp.int32, (TILE, 1), 0) < count[0]
    upstream = cotangent[...].astype(jnp.float32) + jnp.where(live, read_rows(rows, 0, TILE, parts), 0.0)
    masked = jnp.where(live, upstream, 0.0)
    normal, scale = row_normal(second[...])
    vectors[2:3, :] += jnp.sum(masked * normal, 0, keepdims=True)
    vectors[3:4, :] += jnp.sum(masked, 0, keepdims=True)
    scaled = masked * gain[...]
    slope = jnp.mean(scaled * normal, -1, keepdims=True)
    grad_second = scale * (scaled - jnp.mean(scaled, -1, keepdims=True) - normal * slope)
    second_low = grad_second.astype(jnp.bfloat16)
    vectors[1:2, :] += jnp.sum(second_low.astype(jnp.float32), 0, keepdims=True)
    pre = first[...]
    logistic = jax.nn.sigmoid(pre)
    act = (pre * logistic).astype(jnp.bfloat16)
    grads[3 * width : 4 * width] += dot_left(act, second_low)
    grad_first = dot_right(second_low, w_two[...]) * (logistic * (1.0 + pre * (1.0 - logistic)))
    first_low = grad_first.astype(jnp.bfloat16)
    message[...] = first_low
    vectors[0:1, :] += jnp.sum(first_low.astype(jnp.float32), 0, keepdims=True)
    grads[:width] += dot_left(edge[...], first_low)
    grads[2 * width : 3 * width] += dot_left(received[...], first_low)
    node = lax.broadcasted_iota(jnp.int32, (nodes.shape[0], LANES), 0)
    chosen = jnp.concatenate(
        [
            jnp.where(node == send[pl.ds(step * (TILE // LANES) + i, 1), :], 1.0, 0.0).astype(jnp.bfloat16)
            for i in range(TILE // LANES)
        ],
        axis=1,
    )
    by_sender[...] += dot(chosen, first_low)
    grad[...] = upstream + dot_right(first_low, w_one[:width])

    @pl.when(step == pl.num_programs(0) - 1)
    def _():
        high, rest = split_low(by_sender[...])
        grads[width : 2 * width] = dot_left(nodes[...], high) + dot_left(nodes[...], rest)
        give = pltpu.make_async_copy(grads, all_grads, give_sem)
        give.start()
        middle = w_one[width : 2 * width]
        sender_grad[...] = node_part[...] + dot_right(high, middle) + dot_right(rest, middle)
        give.wait()


def edge_backward(
    count, recv, send, cotangent, edge, received, first, second, wide, node_part, nodes, w_one, w_two, gain
):
    edges, width = edge.shape
    steps = edges // TILE
    parts = width // LANES
    per_device = nodes.shape[0]
    hold = pl.BlockSpec(memory_space=pltpu.VMEM)
    scalar = pl.BlockSpec(memory_space=pltpu.SMEM)
    tile = pl.BlockSpec((TILE, width), lambda i: (i, 0))

    across = pl.BlockSpec(memory_space=pl.ANY)

    def whole(rows):
        return pl.BlockSpec((rows, width), lambda i: (0, 0))

    return pl.pallas_call(
        backward_kernel,
        grid=(steps,),
        in_specs=[
            scalar, scalar, hold, tile, tile, tile, tile, tile,
            across, hold, hold, hold, hold, hold,
        ],
        out_specs=[
            tile, tile, across, whole(8), whole(per_device),
        ],
        out_shape=[
            jax.ShapeDtypeStruct((edges, width), jnp.float32),
            jax.ShapeDtypeStruct((edges, width), jnp.bfloat16),
            jax.ShapeDtypeStruct((4 * width, width), jnp.float32),
            jax.ShapeDtypeStruct((8, width), jnp.float32),
            jax.ShapeDtypeStruct((per_device, width), jnp.float32),
        ],
        scratch_shapes=[
            pltpu.VMEM((wide.shape[0] * parts, LANES), jnp.float32),
            pltpu.VMEM((TILE * parts, LANES), jnp.float32),
            pltpu.VMEM((2, CHUNK, width), jnp.bfloat16),
            pltpu.SemaphoreType.DMA((2,)),
            pltpu.VMEM((per_device, width), jnp.float32),
            pltpu.VMEM((4 * width, width), jnp.float32),
            pltpu.SemaphoreType.DMA,
        ],
        compiler_params=pltpu.CompilerParams(vmem_limit_bytes=VMEM_BYTES),
        cost_estimate=pl.CostEstimate(
            flops=24 * edges * width * width, bytes_accessed=40 * edges * width, transcendentals=2 * edges * width
        ),
        name="edge_backward",
    )(
        count, recv, send, cotangent, edge, received, first, second, wide,
        node_part, nodes, w_one, w_two, gain,
    )


MESH = pl.DeviceIdType.MESH
PIECES = 4
SPLIT = False
LOW = jnp.bfloat16
WIDE = jnp.float32


def places():
    groups = lax.axis_size("blk")
    group, sub = lax.axis_index("blk"), lax.axis_index("sub")
    odd = lax.rem(group, 2)
    along = groups // 2
    spot = group // 2
    beside = group + 1 - 2 * odd
    return dict(
        group=group,
        sub=sub,
        core=lax.rem(sub, 2),
        chip=sub // 2,
        odd=odd,
        spot=spot,
        along=along,
        sibling=sub + 1 - 2 * lax.rem(sub, 2),
        partner=lax.rem(sub + 2, 4),
        to_sibling=(group, sub + 1 - 2 * lax.rem(sub, 2)),
        to_partner=(group, lax.rem(sub + 2, 4)),
        to_beside=(beside, sub),
        to_onward=(lax.rem(group + 2 - 4 * odd + groups, groups), sub),
        to_source=(lax.rem(group - 2 + 4 * odd + groups, groups), sub),
        peers=[(2 * lax.rem(spot + k, along) + odd, sub) for k in range(1, along)],
        near=2 - 2 * odd,
        far=2 * odd,
    )


def meet(senders):
    barrier = pltpu.get_barrier_semaphore()
    for device in senders:
        pl.semaphore_signal(barrier, inc=1, device_id=device, device_id_type=MESH)
    pl.semaphore_wait(barrier, len(senders))


def meet_all():
    barrier = pltpu.get_barrier_semaphore()
    subs = lax.axis_size("sub")
    devices = lax.axis_size("blk") * subs
    here = lax.axis_index("blk") * subs + lax.axis_index("sub")

    def greet(k, carry):
        there = lax.rem(here + k, devices)
        pl.semaphore_signal(barrier, inc=1, device_id=(there // subs, lax.rem(there, subs)), device_id_type=MESH)
        return carry

    lax.fori_loop(1, devices, greet, 0)
    pl.semaphore_wait(barrier, devices - 1)


def remote(source, target, send, recv, device):
    return pltpu.make_async_remote_copy(
        src_ref=source, dst_ref=target, send_sem=send, recv_sem=recv, device_id=device, device_id_type=MESH
    )


def in_pieces(count, body):
    block = math.gcd(count, 128)

    def run(i, carry):
        body(pl.multiple_of(i * block, block), block)
        return carry

    lax.fori_loop(0, count // block, run, 0)


def padded_rows(rows):
    unit = 64 * lax.axis_size("blk")
    return -(-rows // unit) * unit


def streams_of(sources):
    unit = 64 * lax.axis_size("blk")
    streams = []
    for i, rows in enumerate(sources):
        first = -(-(rows // unit) // 2) * unit if SPLIT else rows
        streams.append((i, 0, first))
        if first < rows:
            streams.append((i, first, rows - first))
    return streams


def reducers_scratch(sources, width, along):
    return [ref for _, _, rows in streams_of(sources) for ref in reducer_scratch(rows, width, along)]


def reducers(at, sources, reduced, refs):
    made = []
    for i, (which, start, rows) in enumerate(streams_of([source.shape[0] for source in sources])):
        first = start + sum(source.shape[0] for source in sources[:which])
        made.append(reducer(at, sources[which], start, reduced, first, rows, i % 2 > 0, refs[i * 13 : i * 13 + 13]))
    return both(made), refs[len(made) * 13 :]


def reducer_scratch(rows, width, along):
    return [
        pltpu.VMEM((rows // 2, width), WIDE),
        pltpu.VMEM((rows // 2, width), WIDE),
        pltpu.VMEM((rows // 4, width), LOW),
        pltpu.VMEM((rows // 4, width), LOW),
        pltpu.VMEM((rows // 8, width), LOW),
        pltpu.VMEM((rows // 8, width), LOW),
        pltpu.VMEM((rows // 8, width), LOW),
        pltpu.VMEM((along - 1, rows // 8 // along, width), LOW),
        pltpu.SemaphoreType.DMA,
        pltpu.SemaphoreType.DMA((6,)),
        pltpu.SemaphoreType.DMA((6,)),
        pltpu.SemaphoreType.DMA((2, along - 1)),
        pltpu.SemaphoreType.DMA((2, along - 1)),
    ]


def reducer(at, grads, source_first, reduced, first, rows, swap, refs):
    (
        half, half_in, cross_out, cross_in, side_out, side_in, ring_out, ring_in,
        load_sem, step_send, step_recv, ring_send, ring_recv,
    ) = refs
    along, peers = at["along"], at["peers"]
    turns = [(at["chip"], at["to_partner"]), (at["odd"], at["to_beside"])]
    (bit_one, device_one), (bit_two, device_two) = turns[::-1] if swap else turns
    core, spot = at["core"], at["spot"]
    n_half, n_cross, n_side, n_ring = rows // 2, rows // 4, rows // 8, rows // 8 // along
    at_half = first + core * n_half
    at_cross = at_half + bit_one * n_cross
    at_side = at_cross + bit_two * n_side
    at_ring = at_side + spot * n_ring

    def span(start, count):
        return pl.ds(pl.multiple_of(start, 16), count)

    def step(kind):
        if kind == 0:
            other = span(source_first + (1 - core) * n_half, n_half)
            source, target, device = grads.at[other], half_in, at["to_sibling"]
        elif kind == 1:
            source, target, device = cross_out, cross_in, device_one
        elif kind == 2:
            source, target, device = side_out, side_in, device_two
        else:
            start, count, device = {
                3: (at_side, n_side, device_two),
                4: (at_cross, n_cross, device_one),
                5: (at_half, n_half, at["to_sibling"]),
            }[kind]
            source = target = reduced.at[span(start, count)]
        return remote(source, target, step_send.at[kind], step_recv.at[kind], device)

    def ring(kind, k):
        if kind == 0:
            source = ring_out.at[span(lax.rem(spot + k, along) * n_ring, n_ring)]
            target = ring_in.at[k - 1]
        else:
            source = target = reduced.at[span(at_ring, n_ring)]
        return remote(source, target, ring_send.at[kind, k - 1], ring_recv.at[kind, k - 1], peers[k - 1])

    load = pltpu.make_async_copy(grads.at[span(source_first + core * n_half, n_half)], half, load_sem)

    def start():
        step(0).start()
        load.start()

    def add_half():
        load.wait()
        step(0).wait_recv()
        other = (1 - bit_one) * n_cross

        def part(i, block):
            here = pl.ds(pl.multiple_of(other + i, block), block)
            cross_out[pl.ds(i, block), :] = (half[here, :] + half_in[here, :]).astype(LOW)

        in_pieces(n_cross, part)
        step(1).start()

    def add_cross():
        mine, other = bit_one * n_cross, (1 - bit_two) * n_side
        step(1).wait_recv()

        def part(i, block):
            there = pl.ds(pl.multiple_of(other + i, block), block)
            here = pl.ds(pl.multiple_of(mine + other + i, block), block)
            side_out[pl.ds(i, block), :] = (half[here, :] + half_in[here, :] + cross_in[there, :].astype(WIDE)).astype(LOW)

        in_pieces(n_side, part)
        step(2).start()

    def add_side():
        mine, kept = bit_one * n_cross, bit_two * n_side
        step(2).wait_recv()

        def part(i, block):
            there = pl.ds(pl.multiple_of(kept + i, block), block)
            here = pl.ds(pl.multiple_of(mine + kept + i, block), block)
            flat = pl.ds(i, block)
            value = half[here, :] + half_in[here, :] + cross_in[there, :].astype(WIDE) + side_in[flat, :].astype(WIDE)
            half[here, :] = value
            ring_out[flat, :] = value.astype(LOW)

        in_pieces(n_side, part)
        for k in range(1, along):
            ring(0, k).start()

    def add_ring():
        value = half[span(bit_one * n_cross + bit_two * n_side + spot * n_ring, n_ring), :]
        for k in range(1, along):
            ring(0, k).wait_recv()
            value = value + ring_in[k - 1].astype(WIDE)
        reduced[span(at_ring, n_ring), :] = value.astype(LOW)
        for k in range(1, along):
            ring(1, k).start()

    def share_side():
        for k in range(1, along):
            ring(1, k).wait_recv()
        step(3).start()

    def share_cross():
        step(3).wait_recv()
        step(4).start()

    def share_half():
        step(4).wait_recv()
        step(5).start()

    def last():
        step(5).wait_recv()

    def drain():
        for kind in range(6):
            step(kind).wait_send()
        for k in range(1, along):
            ring(0, k).wait_send()
            ring(1, k).wait_send()

    return [start, add_half, add_cross, add_side, add_ring, share_side, share_cross, share_half, last, drain]


def vector_scratch(shape, along):
    return [
        pltpu.VMEM((4, *shape), WIDE),
        pltpu.VMEM((2 + along, *shape), WIDE),
        pltpu.SemaphoreType.DMA((2 + along,)),
        pltpu.SemaphoreType.DMA((2 + along,)),
    ]


def vector_reducer(at, vectors, reduced, refs):
    held, held_in, send_sems, recv_sems = refs
    along = at["along"]
    devices = (at["to_sibling"], at["to_partner"], at["to_beside"], *at["peers"])

    def move(kind):
        return remote(held.at[min(kind, 3)], held_in.at[kind], send_sems.at[kind], recv_sems.at[kind], devices[kind])

    def start():
        held[0] = vectors[...]
        move(0).start()

    def turn(kind):
        def run():
            move(kind).wait_recv()
            held[kind + 1] = held[kind] + held_in[kind]
            for k in range(kind + 1, kind + 2 if kind < 2 else 2 + along):
                move(k).start()

        return run

    def last():
        value = held[3]
        for k in range(3, 2 + along):
            move(k).wait_recv()
            value = value + held_in[k]
        reduced[...] = value
        for k in range(2 + along):
            move(k).wait_send()

    return [start, turn(0), turn(1), turn(2), last]


def both(streams):
    return [lambda steps=steps: [step() for step in steps] for steps in zip(*streams)]


def spread_moves(at, own, table, keep_sem, send_sems, recv_sems):
    sub, partner, near, far = at["sub"], at["partner"], at["near"], at["far"]
    to_sibling, to_partner, to_beside, to_onward = (
        at["to_sibling"], at["to_partner"], at["to_beside"], at["to_onward"]
    )
    size = own.shape[0] // PIECES

    def move(kind, piece):
        source, slot, device = {
            0: (None, (1, sub), to_partner),
            1: (None, (far, sub), to_beside),
            2: (None, (1, sub), to_sibling),
            3: ((1, partner), (far, partner), to_beside),
            4: ((1, partner), (1, partner), to_sibling),
            5: ((near, sub), (far, sub), to_onward),
            6: ((near, sub), (near, sub), to_sibling),
            7: ((near, partner), (far, partner), to_onward),
            8: ((near, partner), (near, partner), to_sibling),
            9: ((far, sub), (far, sub), to_sibling),
            10: ((far, partner), (far, partner), to_sibling),
        }[kind]
        source = own if source is None else table.at[source[0], source[1]]
        rows = pl.ds(piece * size, size)
        return remote(
            source.at[rows], table.at[slot[0], slot[1], rows],
            send_sems.at[kind, piece], recv_sems.at[kind, piece], device,
        )

    keep = pltpu.make_async_copy(own, table.at[1, sub], keep_sem)

    def start():
        for piece in range(PIECES):
            for kind in (0, 1, 2):
                move(kind, piece).start()
        keep.start()

    def relay(arrived, kinds, piece):
        move(arrived, piece).wait_recv()
        for kind in kinds:
            move(kind, piece).start()

    def one(piece):
        relay(0, (3, 4), piece)
        relay(1, (5, 6), piece)

    def two(piece):
        relay(3, (7, 8), piece)
        relay(5, (9,), piece)

    def three(piece):
        relay(7, (10,), piece)

    def drain():
        for kind in range(11):
            for piece in range(PIECES):
                if kind in (2, 4, 6, 8, 9, 10):
                    move(kind, piece).wait_recv()
                move(kind, piece).wait_send()
        keep.wait()

    return start, one, two, three, drain


def spread_scratch():
    return [
        pltpu.SemaphoreType.DMA,
        pltpu.SemaphoreType.DMA((11, PIECES)),
        pltpu.SemaphoreType.DMA((11, PIECES)),
    ]


HALVES = 2
ORDER = (
    (0, 1, 0), (0, 1, 1), (1, 1, 0), (0, 0, 0), (1, 1, 1), (0, 0, 1),
    (1, 0, 0), (2, 1, 0), (1, 0, 1), (2, 1, 1), (2, 0, 0), (2, 0, 1),
)


def collect_scratch(rows, width, edges):
    return [
        pltpu.VMEM((edges, width), LOW),
        pltpu.VMEM((2, 3, 2, rows, width), WIDE),
        pltpu.VMEM((3, 2, rows, width), WIDE),
        pltpu.VMEM((2, rows, width), LOW),
        pltpu.VMEM((2, rows, width), LOW),
        pltpu.VMEM((2, rows, width), LOW),
        pltpu.VMEM((2, rows, width), LOW),
        pltpu.VMEM((rows, width), LOW),
        pltpu.VMEM((rows, width), LOW),
        pltpu.SemaphoreType.DMA,
        pltpu.SemaphoreType.DMA((3, 2, HALVES)),
        pltpu.SemaphoreType.DMA((3, 2, HALVES)),
        pltpu.SemaphoreType.DMA((5, PIECES)),
        pltpu.SemaphoreType.DMA((5, PIECES)),
    ]


def collect_moves(at, index, messages, out, refs):
    (
        held, parts, landed, far_out, far_in, near_out, near_in, pair_out, pair_in,
        load_sem, give_sems, take_sems, send_sems, recv_sems,
    ) = refs
    sub, partner, sibling = at["sub"], at["partner"], at["sibling"]
    rows = out.shape[0]
    size = rows // PIECES
    part_rows = rows // HALVES
    load = pltpu.make_async_copy(messages, held, load_sem)

    def piece_of(ref, piece):
        return ref.at[pl.ds(piece * size, size)]

    def give(role, side, half):
        span = pl.ds(pl.multiple_of(half * part_rows, part_rows), part_rows)
        return remote(
            parts.at[0, role, side, span], landed.at[role, side, span],
            give_sems.at[role, side, half], take_sems.at[role, side, half], at["to_sibling"],
        )

    def hop(kind, piece):
        source, target, device = {
            0: (far_out.at[0], far_in.at[0], at["to_source"]),
            1: (far_out.at[1], far_in.at[1], at["to_source"]),
            2: (near_out.at[0], near_in.at[0], at["to_beside"]),
            3: (near_out.at[1], near_in.at[1], at["to_beside"]),
            4: (pair_out, pair_in, at["to_partner"]),
        }[kind]
        return remote(
            piece_of(source, piece), piece_of(target, piece),
            send_sems.at[kind, piece], recv_sems.at[kind, piece], device,
        )

    def add_messages(step):
        def pick(column):
            return lax.rem(sum(int(item[column]) << (2 * i) for i, item in enumerate(ORDER)) >> (2 * step), 4)

        role, side, half = pick(0), pick(1), pick(2)
        relation = jnp.where(role == 0, at["far"], jnp.where(role == 1, at["near"], 1))
        span = pl.ds(pl.multiple_of(half * part_rows, part_rows), part_rows)

        def whose(w, carry):
            first = jnp.where(w == 0, sibling, sub)
            target = lax.rem(first + 2 * side, 4)
            base = (relation * 4 + target) * rows + half * part_rows
            node = lax.broadcasted_iota(jnp.int32, (part_rows, LANES), 0) + base
            chosen = jnp.concatenate(
                [jnp.where(node == index[j : j + 1, :], 1.0, 0.0).astype(LOW) for j in range(index.shape[0])], axis=1
            )
            parts[w, role, side, span, :] = dot(chosen, held[...])
            return carry

        lax.fori_loop(0, 2, whose, 0)
        give(role, side, half).start()

    def local(role, side, piece):
        span = pl.ds(piece * size, size)
        return parts[1, role, side, span, :] + landed[role, side, span, :]

    def arrived(kind, ref, piece):
        hop(kind, piece).wait_recv()
        return ref[pl.ds(piece * size, size), :].astype(WIDE)

    def pieces(half):
        return range(half * PIECES // HALVES, (half + 1) * PIECES // HALVES)

    def far_step(side, half):
        give(0, side, half).wait_recv()
        for piece in pieces(half):
            far_out[side, pl.ds(piece * size, size), :] = local(0, side, piece).astype(LOW)
            hop(side, piece).start()

    def near_step(side, half):
        give(1, side, half).wait_recv()
        for piece in pieces(half):
            value = local(1, side, piece) + arrived(side, far_in.at[side], piece)
            near_out[side, pl.ds(piece * size, size), :] = value.astype(LOW)
            hop(2 + side, piece).start()

    def pair_step(half):
        give(2, 1, half).wait_recv()
        for piece in pieces(half):
            value = local(2, 1, piece) + arrived(3, near_in.at[1], piece)
            pair_out[pl.ds(piece * size, size), :] = value.astype(LOW)
            hop(4, piece).start()

    def last_step(half):
        give(2, 0, half).wait_recv()
        for piece in pieces(half):
            value = local(2, 0, piece) + arrived(2, near_in.at[0], piece) + arrived(4, pair_in, piece)
            out[pl.ds(piece * size, size), :] = value

    def drain():
        for item in ORDER:
            give(*item).wait_send()
        for kind in range(5):
            for piece in range(PIECES):
                hop(kind, piece).wait_send()

    events = {
        1: [lambda: far_step(1, 0)],
        2: [lambda: far_step(1, 1)],
        3: [lambda: near_step(1, 0)],
        4: [lambda: far_step(0, 0)],
        5: [lambda: near_step(1, 1), lambda: far_step(0, 1)],
        7: [lambda: near_step(0, 0), lambda: pair_step(0)],
        9: [lambda: near_step(0, 1), lambda: pair_step(1)],
    }

    def run(more):
        def step(i, carry):
            add_messages(i)
            for k in sorted(set(events) | set(more)):
                @pl.when(i == k)
                def _():
                    for event in events.get(k, []) + more.get(k, []):
                        event()

            return carry

        lax.fori_loop(0, len(ORDER), step, 0)
        for half in range(HALVES):
            last_step(half)

    return load, run, drain


def exchange_scratch(rows, width, devices):
    slab = width // devices * (rows // LANES)
    return [
        pltpu.VMEM((devices * slab, LANES), WIDE),
        pltpu.VMEM((devices * slab, LANES), LOW),
        pltpu.VMEM((devices, slab, LANES), LOW),
        pltpu.VMEM((slab, LANES), WIDE),
        pltpu.SemaphoreType.DMA((devices - 1,)),
        pltpu.SemaphoreType.DMA((devices - 1,)),
    ]


def exchange_moves(residual, out, refs):
    flat, packed, landed, opened, send_sems, recv_sems = refs
    subs = lax.axis_size("sub")
    devices = lax.axis_size("blk") * subs
    here = lax.axis_index("blk") * subs + lax.axis_index("sub")
    slab = landed.shape[1]
    channels = out.shape[0]
    parts = slab // channels
    nodes = parts * LANES

    def move(k):
        there = lax.rem(here + k, devices)
        return remote(
            packed.at[pl.ds(pl.multiple_of(there * slab, slab), slab)], landed.at[here],
            send_sems.at[k - 1], recv_sems.at[k - 1], (there // subs, lax.rem(there, subs)),
        )

    def start(values):
        lay_rows(flat, 0, values.T)

        def cast(i, block):
            packed[pl.ds(i, block), :] = flat[pl.ds(i, block), :].astype(LOW)

        in_pieces(flat.shape[0], cast)

        def send(k, carry):
            move(k).start()
            return carry

        lax.fori_loop(1, devices, send, 0)

    def open_slab(source, device):
        opened[...] = source.astype(WIDE)
        for j in range(parts):
            columns = pl.ds(pl.multiple_of(device * nodes + j * LANES, LANES), LANES)
            out[:, columns] = residual[:, columns] + opened[pl.ds(j, channels, stride=parts), :]

    def last():
        open_slab(packed[pl.ds(pl.multiple_of(here * slab, slab), slab), :], here)

        def take(k, carry):
            move(k).wait_recv()
            device = lax.rem(here - k + devices, devices)
            open_slab(landed[device], device)
            return carry

        lax.fori_loop(1, devices, take, 0)

        def sent(k, carry):
            move(k).wait_send()
            return carry

        lax.fori_loop(1, devices, sent, 0)

    return start, last


def finish_kernel(
    index, messages, edge_grads, node_grads, vectors, node_part, weight, residual,
    node_grad, reduced, reduced_vectors, total, *refs,
):
    at = places()
    count = len(collect_scratch(64, 128, 64))
    load, run, drain = collect_moves(at, index, messages, total, refs[:count])
    load.start()
    meet_all()
    steps, refs = reducers(at, (edge_grads, node_grads), reduced, refs[count:])
    vector_steps = vector_reducer(at, vectors, reduced_vectors, refs[:4])
    exchange, receive = exchange_moves(residual, node_grad, refs[4:])
    steps[0]()
    vector_steps[0]()
    load.wait()
    run({
        1: [steps[1], vector_steps[1]],
        4: [steps[2], vector_steps[2]],
        6: [steps[3], vector_steps[3]],
        8: [steps[4]],
        10: [steps[5]],
    })
    high, rest = split_low(total[...])
    exchange(node_part[...] + dot_right(high, weight[...]) + dot_right(rest, weight[...]))
    for step in steps[6:8]:
        step()
    receive()
    steps[8]()
    vector_steps[4]()
    drain()
    steps[9]()


def finish(index, messages, edge_grads, node_grads, vectors, node_part, weight, residual, collective):
    rows, width = node_part.shape
    edges = messages.shape[0]
    sources = [edge_grads.shape[0], node_grads.shape[0]]
    along = lax.axis_size("blk") // 2
    devices = lax.axis_size("blk") * lax.axis_size("sub")
    hold = pl.BlockSpec(memory_space=pltpu.VMEM)
    across = pl.BlockSpec(memory_space=pl.ANY)
    return pl.pallas_call(
        finish_kernel,
        grid=(1,),
        in_specs=[
            hold, across, across, across, hold, hold, pl.BlockSpec((width, width), lambda i: (2, 0)), hold,
        ],
        out_specs=[hold] * 3,
        out_shape=[
            jax.ShapeDtypeStruct(residual.shape, WIDE),
            jax.ShapeDtypeStruct((sum(sources), width), LOW),
            jax.ShapeDtypeStruct(vectors.shape, WIDE),
        ],
        scratch_shapes=[
            pltpu.VMEM((rows, width), WIDE),
            *collect_scratch(rows, width, edges),
            *reducers_scratch(sources, width, along),
            *vector_scratch(vectors.shape, along),
            *exchange_scratch(rows, width, devices),
        ],
        compiler_params=pltpu.CompilerParams(
            collective_id=collective, has_side_effects=True, vmem_limit_bytes=VMEM_BYTES
        ),
        name="finish_sums",
    )(index.reshape(edges // LANES, LANES), messages, edge_grads, node_grads, vectors, node_part, weight, residual)


def middle_kernel(
    index, messages, node_low, upstream, w_one, b_one, w_two, b_two, gain, shift, residual,
    table, node_part, node_out, grads, vectors, total, sent, *refs
):
    at = places()
    count = len(collect_scratch(64, 128, 64))
    load, run, drain = collect_moves(at, index, messages, total, refs[:count])
    load.start()
    meet_all()
    refs = refs[count:]
    start, one, two, three, end = spread_moves(at, sent, table, *refs[:3])
    exchange, receive = exchange_moves(residual, node_out, refs[3:])
    load.wait()
    run({})

    width = total.shape[1]
    low = total[...].astype(LOW)
    pre = dot(node_low[...], w_one[:width]) + dot(low, w_one[width:]) + b_one[...]
    logistic = jax.nn.sigmoid(pre)
    act = (pre * logistic).astype(LOW)
    normal, scale = row_normal(dot(act, w_two[...]) + b_two[...])
    given = upstream[...].T
    scaled = given * gain[...]
    slope = jnp.mean(scaled * normal, -1, keepdims=True)
    fourth = scale * (scaled - jnp.mean(scaled, -1, keepdims=True) - normal * slope)
    fourth_low = fourth.astype(LOW)
    third = dot_right(fourth_low, w_two[...]) * (logistic * (1.0 + pre * (1.0 - logistic)))
    third_low = third.astype(LOW)
    sent[...] = dot_right(third_low, w_one[width:]).astype(LOW)
    start()
    grads[:width] = dot_left(node_low[...], third_low)
    grads[width : 2 * width] = dot_left(low, third_low)
    grads[2 * width : 3 * width] = dot_left(act, fourth_low)
    vectors[...] = jnp.zeros_like(vectors)
    vectors[0:1] = jnp.sum(third_low.astype(WIDE), 0, keepdims=True)
    vectors[1:2] = jnp.sum(fourth_low.astype(WIDE), 0, keepdims=True)
    vectors[2:3] = jnp.sum(given * normal, 0, keepdims=True)
    vectors[3:4] = jnp.sum(given, 0, keepdims=True)
    node_part[...] = dot_right(third_low, w_one[:width])
    exchange(normal * gain[...] + shift[...])

    for stage in (one, two, three):
        for piece in range(PIECES):
            stage(piece)
    receive()
    end()
    drain()


def middle(index, messages, node_low, upstream, w_one, b_one, w_two, b_two, gain, shift, residual, collective):
    rows, width = node_low.shape
    edges = messages.shape[0]
    devices = lax.axis_size("blk") * lax.axis_size("sub")
    grad_rows = padded_rows(3 * width)
    hold = pl.BlockSpec(memory_space=pltpu.VMEM)
    across = pl.BlockSpec(memory_space=pl.ANY)
    table, node_part, node_out, grads, vectors = pl.pallas_call(
        middle_kernel,
        in_specs=[hold, across] + [hold] * 9,
        out_specs=[across] + [hold] * 4,
        out_shape=[
            jax.ShapeDtypeStruct((3, 4, rows, width), LOW),
            jax.ShapeDtypeStruct((rows, width), WIDE),
            jax.ShapeDtypeStruct(residual.shape, WIDE),
            jax.ShapeDtypeStruct((grad_rows, width), WIDE),
            jax.ShapeDtypeStruct((8, width), WIDE),
        ],
        scratch_shapes=[
            pltpu.VMEM((rows, width), WIDE),
            pltpu.VMEM((rows, width), LOW),
            *collect_scratch(rows, width, edges),
            *spread_scratch(),
            *exchange_scratch(rows, width, devices),
        ],
        compiler_params=pltpu.CompilerParams(
            collective_id=collective, has_side_effects=True, vmem_limit_bytes=VMEM_BYTES
        ),
        name="middle_nodes",
    )(
        index.reshape(edges // LANES, LANES), messages, node_low, upstream,
        w_one, b_one, w_two, b_two, gain, shift, residual,
    )
    return table.reshape(12 * rows, width), node_part, node_out, grads, vectors


def scatter_scratch(channels, nodes, devices):
    slab = channels * (nodes // LANES)
    return [
        pltpu.VMEM((devices * slab, LANES), WIDE),
        pltpu.VMEM((devices * slab, LANES), LOW),
        pltpu.VMEM((devices, slab, LANES), LOW),
        pltpu.VMEM((slab, LANES), WIDE),
        pltpu.VMEM((nodes // LANES * devices * channels, LANES), WIDE),
        pltpu.SemaphoreType.DMA((devices - 1,)),
        pltpu.SemaphoreType.DMA((devices - 1,)),
    ]


def scatter_moves(shard, refs):
    flat, packed, landed, opened, square, send_sems, recv_sems = refs
    subs = lax.axis_size("sub")
    devices = lax.axis_size("blk") * subs
    here = lax.axis_index("blk") * subs + lax.axis_index("sub")
    slab = landed.shape[1]
    channels = shard.shape[0]
    parts = slab // channels
    nodes = parts * LANES

    def move(k):
        there = lax.rem(here + k, devices)
        return remote(
            packed.at[pl.ds(pl.multiple_of(there * slab, slab), slab)], landed.at[here],
            send_sems.at[k - 1], recv_sems.at[k - 1], (there // subs, lax.rem(there, subs)),
        )

    def start():
        def pack(k, carry):
            device = lax.rem(here + k, devices)
            rows = pl.ds(pl.multiple_of(device * slab, slab), slab)
            for j in range(parts):
                columns = pl.ds(pl.multiple_of(device * nodes + j * LANES, LANES), LANES)
                flat[pl.ds(device * slab + j, channels, stride=parts), :] = shard[:, columns]
            packed[rows, :] = flat[rows, :].astype(LOW)
            return carry

        def send(k, carry):
            pack(k, carry)
            move(k).start()
            return carry

        lax.fori_loop(1, devices, send, 0)
        pack(0, 0)

    def open_slab(source, device):
        opened[...] = source.astype(WIDE)
        for j in range(parts):
            rows = pl.ds(pl.multiple_of((j * devices + device) * channels, channels), channels)
            square[rows, :] = opened[pl.ds(j, channels, stride=parts), :]

    def last(rows):
        open_slab(packed[pl.ds(pl.multiple_of(here * slab, slab), slab), :], here)

        def take(k, carry):
            move(k).wait_recv()
            device = lax.rem(here - k + devices, devices)
            open_slab(landed[device], device)
            return carry

        lax.fori_loop(1, devices, take, 0)
        width = devices * channels
        for j in range(parts):
            rows[j * LANES : (j + 1) * LANES, :] = square[j * width : (j + 1) * width, :].T.astype(LOW)

    def drain():
        def sent(k, carry):
            move(k).wait_send()
            return carry

        lax.fori_loop(1, devices, sent, 0)

    return start, last, drain


def begin_kernel(
    shard, later, senders, receivers, own, table, later_out, send_local, recv_wide, held, held_sem, slab_sems, *refs
):
    at = places()
    fetch = pltpu.make_async_copy(later, held, held_sem)
    fetch.start()
    meet_all()
    start, last, drain = scatter_moves(shard, refs[3:])
    start()
    last(own)
    begin, one, two, three, end = spread_moves(at, own, table, *refs[:3])
    begin()
    rows = own.shape[0]
    groups, subs = lax.axis_size("blk"), lax.axis_size("sub")
    send_local[...] = senders[...] - (at["group"] * subs + at["sub"]) * rows
    relative = lax.rem(receivers[...] // (rows * subs) - at["group"] + 1 + groups, groups)
    recv_wide[...] = relative * (rows * subs) + lax.rem(receivers[...], rows * subs)
    fetch.wait()
    devices, _, nodes = later_out.shape

    def slab(k):
        columns = pl.ds(pl.multiple_of(k * nodes, LANES), nodes)
        return pltpu.make_async_copy(held.at[:, columns], later_out.at[k], slab_sems.at[k])

    def give(k, carry):
        slab(k).start()
        return carry

    def given(k, carry):
        slab(k).wait()
        return carry

    lax.fori_loop(0, devices, give, 0)
    drain()
    for stage in (one, two, three):
        for piece in range(PIECES):
            stage(piece)
    lax.fori_loop(0, devices, given, 0)
    end()


def begin(shard, later, senders, receivers, rows, collective):
    channels, nodes = shard.shape
    devices = lax.axis_size("blk") * lax.axis_size("sub")
    width = channels * devices
    hold = pl.BlockSpec(memory_space=pltpu.VMEM)
    across = pl.BlockSpec(memory_space=pl.ANY)
    lines = (senders.shape[0] // LANES, LANES)
    own, table, later, send_local, recv_wide = pl.pallas_call(
        begin_kernel,
        in_specs=[hold, across, hold, hold],
        out_specs=[hold, across, across, hold, hold],
        out_shape=[
            jax.ShapeDtypeStruct((rows, width), LOW),
            jax.ShapeDtypeStruct((3, 4, rows, width), LOW),
            jax.ShapeDtypeStruct((devices, channels, rows), later.dtype),
            jax.ShapeDtypeStruct(lines, jnp.int32),
            jax.ShapeDtypeStruct(lines, jnp.int32),
        ],
        scratch_shapes=[
            pltpu.VMEM(later.shape, later.dtype),
            pltpu.SemaphoreType.DMA,
            pltpu.SemaphoreType.DMA((devices,)),
            *spread_scratch(),
            *scatter_scratch(channels, rows, devices),
        ],
        compiler_params=pltpu.CompilerParams(
            collective_id=collective, has_side_effects=True, vmem_limit_bytes=VMEM_BYTES
        ),
        name="begin_rows",
    )(shard, later, senders.reshape(lines), receivers.reshape(lines))
    return own, table.reshape(12 * rows, width), later, send_local, recv_wide


def shards(
    node_input,
    edge_input,
    senders,
    receivers,
    edge_count,
    edge_w_one,
    edge_b_one,
    edge_w_two,
    edge_b_two,
    edge_gain,
    edge_shift,
    node_w_one,
    node_b_one,
    node_w_two,
    node_b_two,
    node_gain,
    node_shift,
    node_cotangent,
    edge_cotangent,
):
    groups = lax.axis_size("blk")
    sub_count = lax.axis_size("sub")
    width = edge_input.shape[1]
    per_device = node_input.shape[1] // (groups * sub_count)
    node_low, wide_low, cotangent_later, send_local, recv_wide = begin(
        node_input, node_cotangent, senders, receivers, per_device, 0
    )
    node_upstream = lax.all_to_all(
        cotangent_later, ("blk", "sub"), split_axis=0, concat_axis=0, tiled=True
    ).reshape(width, per_device)
    recv_list = recv_wide.reshape(-1)
    edge_result, first_pre, second_pre, received, messages = edge_forward(
        edge_count, recv_list, send_local, edge_input, wide_low, node_low,
        edge_w_one, edge_b_one[None], edge_w_two, edge_b_two[None], edge_gain[None], edge_shift[None],
    )
    wide_grad, node_part, node_out, node_grads, node_vectors = middle(
        recv_list, messages, node_low, node_upstream, node_w_one, node_b_one[None], node_w_two, node_b_two[None],
        node_gain[None], node_shift[None], node_input, 1,
    )
    edge_grad, messages, edge_grads, vectors, node_part = edge_backward(
        edge_count, recv_list, send_local, edge_cotangent, edge_input, received, first_pre, second_pre,
        wide_grad, node_part, node_low, edge_w_one, edge_w_two, edge_gain[None],
    )
    node_grad, summed, vectors = finish(
        recv_list, messages, edge_grads, node_grads, jnp.concatenate([vectors[:4], node_vectors[:4]]), node_part,
        edge_w_one, node_cotangent, 3,
    )
    summed = summed.astype(jnp.float32)
    return (
        node_out,
        edge_result,
        node_grad,
        edge_grad,
        summed[: 3 * width],
        vectors[0],
        summed[3 * width : 4 * width],
        vectors[1],
        vectors[2],
        vectors[3],
        summed[4 * width : 6 * width],
        vectors[4],
        summed[6 * width : 7 * width],
        vectors[5],
        vectors[6],
        vectors[7],
    )


def solution(mesh):
    placed = (
        P(("blk", "sub"), None),
        P(("blk", "sub"), None),
        P(("blk", "sub")),
        P(("blk", "sub")),
        P(("blk", "sub")),
        P(),
        P(),
        P(),
        P(),
        P(),
        P(),
        P(),
        P(),
        P(),
        P(),
        P(),
        P(),
        P(("blk", "sub"), None),
        P(("blk", "sub"), None),
    )
    return jax.shard_map(
        shards,
        mesh=mesh,
        in_specs=placed,
        out_specs=(
            P(("blk", "sub"), None),
            P(("blk", "sub"), None),
            P(("blk", "sub"), None),
            P(("blk", "sub"), None),
            P(),
            P(),
            P(),
            P(),
            P(),
            P(),
            P(),
            P(),
            P(),
            P(),
            P(),
            P(),
        ),
        check_vma=False,
    )
```

```python
import math

import jax
import jax.numpy as jnp
from jax import lax
from jax.experimental import pallas as pl
from jax.experimental.pallas import tpu as pltpu
from jax.sharding import PartitionSpec as P

EPSILON = 1e-05


TILE = 512
CHUNK = 512
LANES = 128
VMEM_BYTES = 60 * 2**20


def dot(left, right):
    return jnp.dot(left, right, preferred_element_type=jnp.float32)


def dot_left(left, right):
    return lax.dot_general(
        left, right, (((0,), (0,)), ((), ())), preferred_element_type=jnp.float32
    )


def dot_right(left, right):
    return lax.dot_general(
        left, right, (((1,), (1,)), ((), ())), preferred_element_type=jnp.float32
    )


def split_low(values):
    high = values.astype(jnp.bfloat16)
    return high, (values - high.astype(jnp.float32)).astype(jnp.bfloat16)


def lay_rows(target, start, values):
    count, width = values.shape
    parts = width // LANES
    for j in range(parts):
        target[pl.ds(start * parts + j, count, stride=parts), :] = values[:, j * LANES : (j + 1) * LANES]


def read_rows(source, start, count, parts):
    return jnp.concatenate(
        [source[pl.ds(start * parts + j, count, stride=parts), :] for j in range(parts)], axis=1
    )


def load_table(wide, table, stage, sems):
    steps = wide.shape[0] // CHUNK

    def fetch(i, slot):
        return pltpu.make_async_copy(wide.at[pl.ds(i * CHUNK, CHUNK)], stage.at[slot], sems.at[slot])

    for i in range(3):
        fetch(i, i).start()

    def body(i, carry):
        slot = lax.rem(i, 4)

        @pl.when(i + 3 < steps)
        def _():
            fetch(i + 3, lax.rem(i + 3, 4)).start()

        fetch(i, slot).wait()

        def piece(k, carry):
            values = stage[slot, pl.ds(k * 64, 64), :].astype(jnp.float32)
            lay_rows(table, i * CHUNK + k * 64, values)
            return carry

        return lax.fori_loop(0, CHUNK // 64, piece, carry)

    lax.fori_loop(0, steps, body, 0)


def gather_rows(index, base, table, rows, parts):
    count = rows.shape[0] // parts

    def body(i, carry):
        for u in range(16):
            slot = i * 16 + u
            place = index[base + slot]
            rows[pl.ds(pl.multiple_of(slot * parts, parts), parts), :] = table[
                pl.ds(pl.multiple_of(place * parts, parts), parts), :
            ]
        return carry

    lax.fori_loop(0, count // 16, body, 0)


def gather_inline(index, base, table, rows, parts):
    for slot in range(rows.shape[0] // parts):
        place = index[base + slot]
        rows[slot * parts : (slot + 1) * parts, :] = table[pl.ds(pl.multiple_of(place * parts, parts), parts), :]


def row_normal(values):
    average = jnp.mean(values, -1, keepdims=True)
    centred = values - average
    variance = jnp.mean(centred * centred, -1, keepdims=True)
    scale = lax.rsqrt(variance + EPSILON)
    return centred * scale, scale


def forward_kernel(
    count, recv, send, edge, wide, nodes, w_one, b_one, w_two, b_two, gain, shift,
    result, first, second, received, message,
    table, rows, stage, sems,
):
    step = pl.program_id(0)
    base = step * TILE
    width = nodes.shape[1]
    parts = width // LANES

    @pl.when(step == 0)
    def _():
        load_table(wide, table, stage, sems)
        gather_rows(recv, base, table, rows, parts)

    later = jnp.where(step + 1 < pl.num_programs(0), base + TILE, 0)
    received[...] = read_rows(rows, 0, TILE, parts).astype(jnp.bfloat16)
    gather_inline(recv, later, table, rows, parts)
    from_recv = received[...]
    lane = lax.broadcasted_iota(jnp.int32, (LANES, LANES), 1)
    chosen = []
    for i in range(TILE // LANES):
        column = jnp.broadcast_to(send[pl.ds(step * (TILE // LANES) + i, 1), :], (LANES, LANES)).T
        chosen.append(
            jnp.concatenate(
                [
                    jnp.where(column == lane + j * LANES, 1.0, 0.0).astype(jnp.bfloat16)
                    for j in range(nodes.shape[0] // LANES)
                ],
                axis=1,
            )
        )
    chosen = jnp.concatenate(chosen, axis=0)
    from_send = dot(chosen, nodes[...]).astype(jnp.bfloat16)
    pre = (
        dot(edge[...], w_one[:width])
        + dot(from_send, w_one[width : 2 * width])
        + dot(from_recv, w_one[2 * width :])
        + b_one[...]
    )
    first[...] = pre
    act = (pre * jax.nn.sigmoid(pre)).astype(jnp.bfloat16)
    post = dot(act, w_two[...]) + b_two[...]
    second[...] = post
    normal, _ = row_normal(post)
    branch = normal * gain[...] + shift[...]
    live = base + lax.broadcasted_iota(jnp.int32, (TILE, 1), 0) < count[0]
    outcome = edge[...].astype(jnp.float32) + jnp.where(live, branch, 0.0)
    result[...] = outcome
    message[...] = jnp.where(live, outcome, 0.0).astype(jnp.bfloat16)


def edge_forward(count, recv, send, edge, wide, nodes, w_one, b_one, w_two, b_two, gain, shift):
    edges, width = edge.shape
    steps = edges // TILE
    parts = width // LANES
    hold = pl.BlockSpec(memory_space=pltpu.VMEM)
    scalar = pl.BlockSpec(memory_space=pltpu.SMEM)
    tile = pl.BlockSpec((TILE, width), lambda i: (i, 0))
    return pl.pallas_call(
        forward_kernel,
        grid=(steps,),
        in_specs=[
            scalar, scalar, hold, tile,
            pl.BlockSpec(memory_space=pl.ANY), hold, hold, hold, hold, hold, hold, hold,
        ],
        out_specs=[tile] * 5,
        out_shape=[
            jax.ShapeDtypeStruct((edges, width), jnp.float32),
            jax.ShapeDtypeStruct((edges, width), jnp.float32),
            jax.ShapeDtypeStruct((edges, width), jnp.float32),
            jax.ShapeDtypeStruct((edges, width), jnp.bfloat16),
            jax.ShapeDtypeStruct((edges, width), jnp.bfloat16),
        ],
        scratch_shapes=[
            pltpu.VMEM((wide.shape[0] * parts, LANES), jnp.float32),
            pltpu.VMEM((TILE * parts, LANES), jnp.float32),
            pltpu.VMEM((4, CHUNK, width), jnp.bfloat16),
            pltpu.SemaphoreType.DMA((4,)),
        ],
        compiler_params=pltpu.CompilerParams(vmem_limit_bytes=VMEM_BYTES),
        cost_estimate=pl.CostEstimate(
            flops=20 * edges * width * width, bytes_accessed=40 * edges * width, transcendentals=2 * edges * width
        ),
        name="edge_forward",
    )(count, recv, send, edge, wide, nodes, w_one, b_one, w_two, b_two, gain, shift)


def backward_kernel(
    count, recv, send, cotangent, edge, received, first, second, wide, node_part, nodes, w_one, w_two, gain,
    grad, message, all_grads, vectors, sender_grad,
    table, rows, stage, sems, by_sender, grads, give_sem,
):
    step = pl.program_id(0)
    base = step * TILE
    width = nodes.shape[1]
    parts = width // LANES

    @pl.when(step == 0)
    def _():
        load_table(wide, table, stage, sems)
        grads[...] = jnp.zeros_like(grads)
        vectors[...] = jnp.zeros_like(vectors)
        by_sender[...] = jnp.zeros_like(by_sender)
        gather_rows(recv, base, table, rows, parts)

    live = base + lax.broadcasted_iota(jnp.int32, (TILE, 1), 0) < count[0]
    upstream = cotangent[...].astype(jnp.float32) + jnp.where(live, read_rows(rows, 0, TILE, parts), 0.0)
    grad[...] = upstream
    later = jnp.where(step + 1 < pl.num_programs(0), base + TILE, 0)
    gather_inline(recv, later, table, rows, parts)
    masked = jnp.where(live, upstream, 0.0)
    normal, scale = row_normal(second[...])
    vectors[2:3, :] += jnp.sum(masked * normal, 0, keepdims=True)
    vectors[3:4, :] += jnp.sum(masked, 0, keepdims=True)
    scaled = masked * gain[...]
    slope = jnp.mean(scaled * normal, -1, keepdims=True)
    grad_second = scale * (scaled - jnp.mean(scaled, -1, keepdims=True) - normal * slope)
    second_low = grad_second.astype(jnp.bfloat16)
    vectors[1:2, :] += jnp.sum(second_low.astype(jnp.float32), 0, keepdims=True)
    pre = first[...]
    logistic = jax.nn.sigmoid(pre)
    act = (pre * logistic).astype(jnp.bfloat16)
    grads[3 * width : 4 * width] += dot_left(act, second_low)
    grad_first = dot_right(second_low, w_two[...]) * (logistic * (1.0 + pre * (1.0 - logistic)))
    first_low = grad_first.astype(jnp.bfloat16)
    message[...] = first_low
    vectors[0:1, :] += jnp.sum(first_low.astype(jnp.float32), 0, keepdims=True)
    grads[:width] += dot_left(edge[...], first_low)
    grads[2 * width : 3 * width] += dot_left(received[...], first_low)
    node = lax.broadcasted_iota(jnp.int32, (nodes.shape[0], LANES), 0)
    chosen = jnp.concatenate(
        [
            jnp.where(node == send[pl.ds(step * (TILE // LANES) + i, 1), :], 1.0, 0.0).astype(jnp.bfloat16)
            for i in range(TILE // LANES)
        ],
        axis=1,
    )
    by_sender[...] += dot(chosen, first_low)
    grad[...] += dot_right(first_low, w_one[:width])

    @pl.when(step == pl.num_programs(0) - 1)
    def _():
        high, rest = split_low(by_sender[...])
        grads[width : 2 * width] = dot_left(nodes[...], high) + dot_left(nodes[...], rest)
        give = pltpu.make_async_copy(grads, all_grads, give_sem)
        give.start()
        middle = w_one[width : 2 * width]
        sender_grad[...] = node_part[...] + dot_right(high, middle) + dot_right(rest, middle)
        give.wait()


def edge_backward(
    count, recv, send, cotangent, edge, received, first, second, wide, node_part, nodes, w_one, w_two, gain
):
    edges, width = edge.shape
    steps = edges // TILE
    parts = width // LANES
    per_device = nodes.shape[0]
    hold = pl.BlockSpec(memory_space=pltpu.VMEM)
    scalar = pl.BlockSpec(memory_space=pltpu.SMEM)
    tile = pl.BlockSpec((TILE, width), lambda i: (i, 0))

    across = pl.BlockSpec(memory_space=pl.ANY)

    def whole(rows):
        return pl.BlockSpec((rows, width), lambda i: (0, 0))

    return pl.pallas_call(
        backward_kernel,
        grid=(steps,),
        in_specs=[
            scalar, scalar, hold, tile, tile, tile, tile, tile,
            across, hold, hold, hold, hold, hold,
        ],
        out_specs=[
            tile, tile, across, whole(8), whole(per_device),
        ],
        out_shape=[
            jax.ShapeDtypeStruct((edges, width), jnp.float32),
            jax.ShapeDtypeStruct((edges, width), jnp.bfloat16),
            jax.ShapeDtypeStruct((4 * width, width), jnp.float32),
            jax.ShapeDtypeStruct((8, width), jnp.float32),
            jax.ShapeDtypeStruct((per_device, width), jnp.float32),
        ],
        scratch_shapes=[
            pltpu.VMEM((wide.shape[0] * parts, LANES), jnp.float32),
            pltpu.VMEM((TILE * parts, LANES), jnp.float32),
            pltpu.VMEM((4, CHUNK, width), jnp.bfloat16),
            pltpu.SemaphoreType.DMA((4,)),
            pltpu.VMEM((per_device, width), jnp.float32),
            pltpu.VMEM((4 * width, width), jnp.float32),
            pltpu.SemaphoreType.DMA,
        ],
        compiler_params=pltpu.CompilerParams(vmem_limit_bytes=VMEM_BYTES),
        cost_estimate=pl.CostEstimate(
            flops=24 * edges * width * width, bytes_accessed=40 * edges * width, transcendentals=2 * edges * width
        ),
        name="edge_backward",
    )(
        count, recv, send, cotangent, edge, received, first, second, wide,
        node_part, nodes, w_one, w_two, gain,
    )


MESH = pl.DeviceIdType.MESH
PIECES = 4
SPLIT = True
LOW = jnp.bfloat16
WIDE = jnp.float32


def places():
    groups = lax.axis_size("blk")
    group, sub = lax.axis_index("blk"), lax.axis_index("sub")
    odd = lax.rem(group, 2)
    along = groups // 2
    spot = group // 2
    beside = group + 1 - 2 * odd
    return dict(
        group=group,
        sub=sub,
        core=lax.rem(sub, 2),
        chip=sub // 2,
        odd=odd,
        spot=spot,
        along=along,
        sibling=sub + 1 - 2 * lax.rem(sub, 2),
        partner=lax.rem(sub + 2, 4),
        to_sibling=(group, sub + 1 - 2 * lax.rem(sub, 2)),
        to_partner=(group, lax.rem(sub + 2, 4)),
        to_beside=(beside, sub),
        to_onward=(lax.rem(group + 2 - 4 * odd + groups, groups), sub),
        to_source=(lax.rem(group - 2 + 4 * odd + groups, groups), sub),
        peers=[(2 * lax.rem(spot + k, along) + odd, sub) for k in range(1, along)],
        near=2 - 2 * odd,
        far=2 * odd,
    )


def meet(senders):
    barrier = pltpu.get_barrier_semaphore()
    for device in senders:
        pl.semaphore_signal(barrier, inc=1, device_id=device, device_id_type=MESH)
    pl.semaphore_wait(barrier, len(senders))


def meet_all():
    barrier = pltpu.get_barrier_semaphore()
    subs = lax.axis_size("sub")
    devices = lax.axis_size("blk") * subs
    here = lax.axis_index("blk") * subs + lax.axis_index("sub")

    def greet(k, carry):
        there = lax.rem(here + k, devices)
        pl.semaphore_signal(barrier, inc=1, device_id=(there // subs, lax.rem(there, subs)), device_id_type=MESH)
        return carry

    lax.fori_loop(1, devices, greet, 0)
    pl.semaphore_wait(barrier, devices - 1)


def remote(source, target, send, recv, device):
    return pltpu.make_async_remote_copy(
        src_ref=source, dst_ref=target, send_sem=send, recv_sem=recv, device_id=device, device_id_type=MESH
    )


def in_pieces(count, body):
    block = math.gcd(count, 128)

    def run(i, carry):
        body(pl.multiple_of(i * block, block), block)
        return carry

    lax.fori_loop(0, count // block, run, 0)


def padded_rows(rows):
    unit = 64 * lax.axis_size("blk")
    return -(-rows // unit) * unit


def streams_of(sources):
    unit = 64 * lax.axis_size("blk")
    streams = []
    for i, rows in enumerate(sources):
        first = -(-(rows // unit) // 2) * unit if SPLIT else rows
        streams.append((i, 0, first))
        if first < rows:
            streams.append((i, first, rows - first))
    return streams


def reducers_scratch(sources, width, along):
    return [ref for _, _, rows in streams_of(sources) for ref in reducer_scratch(rows, width, along)]


def reducers(at, sources, reduced, refs):
    made = []
    for i, (which, start, rows) in enumerate(streams_of([source.shape[0] for source in sources])):
        first = start + sum(source.shape[0] for source in sources[:which])
        made.append(reducer(at, sources[which], start, reduced, first, rows, i % 2 > 0, refs[i * 13 : i * 13 + 13]))
    return both(made), refs[len(made) * 13 :]


def reducer_scratch(rows, width, along):
    return [
        pltpu.VMEM((rows // 2, width), WIDE),
        pltpu.VMEM((rows // 2, width), WIDE),
        pltpu.VMEM((rows // 4, width), LOW),
        pltpu.VMEM((rows // 4, width), LOW),
        pltpu.VMEM((rows // 8, width), LOW),
        pltpu.VMEM((rows // 8, width), LOW),
        pltpu.VMEM((rows // 8, width), LOW),
        pltpu.VMEM((along - 1, rows // 8 // along, width), LOW),
        pltpu.SemaphoreType.DMA,
        pltpu.SemaphoreType.DMA((6,)),
        pltpu.SemaphoreType.DMA((6,)),
        pltpu.SemaphoreType.DMA((2, along - 1)),
        pltpu.SemaphoreType.DMA((2, along - 1)),
    ]


def reducer(at, grads, source_first, reduced, first, rows, swap, refs):
    (
        half, half_in, cross_out, cross_in, side_out, side_in, ring_out, ring_in,
        load_sem, step_send, step_recv, ring_send, ring_recv,
    ) = refs
    along, peers = at["along"], at["peers"]
    turns = [(at["chip"], at["to_partner"]), (at["odd"], at["to_beside"])]
    (bit_one, device_one), (bit_two, device_two) = turns[::-1] if swap else turns
    core, spot = at["core"], at["spot"]
    n_half, n_cross, n_side, n_ring = rows // 2, rows // 4, rows // 8, rows // 8 // along
    at_half = first + core * n_half
    at_cross = at_half + bit_one * n_cross
    at_side = at_cross + bit_two * n_side
    at_ring = at_side + spot * n_ring

    def span(start, count):
        return pl.ds(pl.multiple_of(start, 16), count)

    def step(kind):
        if kind == 0:
            other = span(source_first + (1 - core) * n_half, n_half)
            source, target, device = grads.at[other], half_in, at["to_sibling"]
        elif kind == 1:
            source, target, device = cross_out, cross_in, device_one
        elif kind == 2:
            source, target, device = side_out, side_in, device_two
        else:
            start, count, device = {
                3: (at_side, n_side, device_two),
                4: (at_cross, n_cross, device_one),
                5: (at_half, n_half, at["to_sibling"]),
            }[kind]
            source = target = reduced.at[span(start, count)]
        return remote(source, target, step_send.at[kind], step_recv.at[kind], device)

    def ring(kind, k):
        if kind == 0:
            source = ring_out.at[span(lax.rem(spot + k, along) * n_ring, n_ring)]
            target = ring_in.at[k - 1]
        else:
            source = target = reduced.at[span(at_ring, n_ring)]
        return remote(source, target, ring_send.at[kind, k - 1], ring_recv.at[kind, k - 1], peers[k - 1])

    load = pltpu.make_async_copy(grads.at[span(source_first + core * n_half, n_half)], half, load_sem)

    def start():
        step(0).start()
        load.start()

    def add_half():
        load.wait()
        step(0).wait_recv()
        other = (1 - bit_one) * n_cross

        def part(i, block):
            here = pl.ds(pl.multiple_of(other + i, block), block)
            cross_out[pl.ds(i, block), :] = (half[here, :] + half_in[here, :]).astype(LOW)

        in_pieces(n_cross, part)
        step(1).start()

    def add_cross():
        mine, other = bit_one * n_cross, (1 - bit_two) * n_side
        step(1).wait_recv()

        def part(i, block):
            there = pl.ds(pl.multiple_of(other + i, block), block)
            here = pl.ds(pl.multiple_of(mine + other + i, block), block)
            side_out[pl.ds(i, block), :] = (half[here, :] + half_in[here, :] + cross_in[there, :].astype(WIDE)).astype(LOW)

        in_pieces(n_side, part)
        step(2).start()

    def add_side():
        mine, kept = bit_one * n_cross, bit_two * n_side
        step(2).wait_recv()

        def part(i, block):
            there = pl.ds(pl.multiple_of(kept + i, block), block)
            here = pl.ds(pl.multiple_of(mine + kept + i, block), block)
            flat = pl.ds(i, block)
            value = half[here, :] + half_in[here, :] + cross_in[there, :].astype(WIDE) + side_in[flat, :].astype(WIDE)
            half[here, :] = value
            ring_out[flat, :] = value.astype(LOW)

        in_pieces(n_side, part)
        for k in range(1, along):
            ring(0, k).start()

    def add_ring():
        value = half[span(bit_one * n_cross + bit_two * n_side + spot * n_ring, n_ring), :]
        for k in range(1, along):
            ring(0, k).wait_recv()
            value = value + ring_in[k - 1].astype(WIDE)
        reduced[span(at_ring, n_ring), :] = value.astype(LOW)
        for k in range(1, along):
            ring(1, k).start()

    def share_side():
        for k in range(1, along):
            ring(1, k).wait_recv()
        step(3).start()

    def share_cross():
        step(3).wait_recv()
        step(4).start()

    def share_half():
        step(4).wait_recv()
        step(5).start()

    def last():
        step(5).wait_recv()

    def drain():
        for kind in range(6):
            step(kind).wait_send()
        for k in range(1, along):
            ring(0, k).wait_send()
            ring(1, k).wait_send()

    return [start, add_half, add_cross, add_side, add_ring, share_side, share_cross, share_half, last, drain]


def vector_scratch(shape, along):
    return [
        pltpu.VMEM((4, *shape), WIDE),
        pltpu.VMEM((2 + along, *shape), WIDE),
        pltpu.SemaphoreType.DMA((2 + along,)),
        pltpu.SemaphoreType.DMA((2 + along,)),
    ]


def vector_reducer(at, vectors, reduced, refs):
    held, held_in, send_sems, recv_sems = refs
    along = at["along"]
    devices = (at["to_sibling"], at["to_partner"], at["to_beside"], *at["peers"])

    def move(kind):
        return remote(held.at[min(kind, 3)], held_in.at[kind], send_sems.at[kind], recv_sems.at[kind], devices[kind])

    def start():
        held[0] = vectors[...]
        move(0).start()

    def turn(kind):
        def run():
            move(kind).wait_recv()
            held[kind + 1] = held[kind] + held_in[kind]
            for k in range(kind + 1, kind + 2 if kind < 2 else 2 + along):
                move(k).start()

        return run

    def last():
        value = held[3]
        for k in range(3, 2 + along):
            move(k).wait_recv()
            value = value + held_in[k]
        reduced[...] = value
        for k in range(2 + along):
            move(k).wait_send()

    return [start, turn(0), turn(1), turn(2), last]


def both(streams):
    return [lambda steps=steps: [step() for step in steps] for steps in zip(*streams)]


def spread_moves(at, own, table, keep_sem, send_sems, recv_sems):
    sub, partner, near, far = at["sub"], at["partner"], at["near"], at["far"]
    to_sibling, to_partner, to_beside, to_onward = (
        at["to_sibling"], at["to_partner"], at["to_beside"], at["to_onward"]
    )
    size = own.shape[0] // PIECES

    def move(kind, piece):
        source, slot, device = {
            0: (None, (1, sub), to_partner),
            1: (None, (far, sub), to_beside),
            2: (None, (1, sub), to_sibling),
            3: ((1, partner), (far, partner), to_beside),
            4: ((1, partner), (1, partner), to_sibling),
            5: ((near, sub), (far, sub), to_onward),
            6: ((near, sub), (near, sub), to_sibling),
            7: ((near, partner), (far, partner), to_onward),
            8: ((near, partner), (near, partner), to_sibling),
            9: ((far, sub), (far, sub), to_sibling),
            10: ((far, partner), (far, partner), to_sibling),
        }[kind]
        source = own if source is None else table.at[source[0], source[1]]
        rows = pl.ds(piece * size, size)
        return remote(
            source.at[rows], table.at[slot[0], slot[1], rows],
            send_sems.at[kind, piece], recv_sems.at[kind, piece], device,
        )

    keep = pltpu.make_async_copy(own, table.at[1, sub], keep_sem)

    def start():
        for piece in range(PIECES):
            for kind in (0, 1, 2):
                move(kind, piece).start()
        keep.start()

    def relay(arrived, kinds, piece):
        move(arrived, piece).wait_recv()
        for kind in kinds:
            move(kind, piece).start()

    def one(piece):
        relay(0, (3, 4), piece)
        relay(1, (5, 6), piece)

    def two(piece):
        relay(3, (7, 8), piece)
        relay(5, (9,), piece)

    def three(piece):
        relay(7, (10,), piece)

    def drain():
        for kind in range(11):
            for piece in range(PIECES):
                if kind in (2, 4, 6, 8, 9, 10):
                    move(kind, piece).wait_recv()
                move(kind, piece).wait_send()
        keep.wait()

    return start, one, two, three, drain


def spread_scratch():
    return [
        pltpu.SemaphoreType.DMA,
        pltpu.SemaphoreType.DMA((11, PIECES)),
        pltpu.SemaphoreType.DMA((11, PIECES)),
    ]


HALVES = 2
ORDER = (
    (0, 1, 0), (0, 1, 1), (1, 1, 0), (0, 0, 0), (1, 1, 1), (0, 0, 1),
    (1, 0, 0), (2, 1, 0), (1, 0, 1), (2, 1, 1), (2, 0, 0), (2, 0, 1),
)


def collect_scratch(rows, width, edges):
    return [
        pltpu.VMEM((edges, width), LOW),
        pltpu.VMEM((2, 3, 2, rows, width), WIDE),
        pltpu.VMEM((3, 2, rows, width), WIDE),
        pltpu.VMEM((2, rows, width), LOW),
        pltpu.VMEM((2, rows, width), LOW),
        pltpu.VMEM((2, rows, width), LOW),
        pltpu.VMEM((2, rows, width), LOW),
        pltpu.VMEM((rows, width), LOW),
        pltpu.VMEM((rows, width), LOW),
        pltpu.SemaphoreType.DMA,
        pltpu.SemaphoreType.DMA((3, 2, HALVES)),
        pltpu.SemaphoreType.DMA((3, 2, HALVES)),
        pltpu.SemaphoreType.DMA((5, PIECES)),
        pltpu.SemaphoreType.DMA((5, PIECES)),
    ]


def collect_moves(at, index, messages, out, refs):
    (
        held, parts, landed, far_out, far_in, near_out, near_in, pair_out, pair_in,
        load_sem, give_sems, take_sems, send_sems, recv_sems,
    ) = refs
    sub, partner, sibling = at["sub"], at["partner"], at["sibling"]
    rows = out.shape[0]
    size = rows // PIECES
    part_rows = rows // HALVES
    load = pltpu.make_async_copy(messages, held, load_sem)

    def piece_of(ref, piece):
        return ref.at[pl.ds(piece * size, size)]

    def give(role, side, half):
        span = pl.ds(pl.multiple_of(half * part_rows, part_rows), part_rows)
        return remote(
            parts.at[0, role, side, span], landed.at[role, side, span],
            give_sems.at[role, side, half], take_sems.at[role, side, half], at["to_sibling"],
        )

    def hop(kind, piece):
        source, target, device = {
            0: (far_out.at[0], far_in.at[0], at["to_source"]),
            1: (far_out.at[1], far_in.at[1], at["to_source"]),
            2: (near_out.at[0], near_in.at[0], at["to_beside"]),
            3: (near_out.at[1], near_in.at[1], at["to_beside"]),
            4: (pair_out, pair_in, at["to_partner"]),
        }[kind]
        return remote(
            piece_of(source, piece), piece_of(target, piece),
            send_sems.at[kind, piece], recv_sems.at[kind, piece], device,
        )

    def add_messages(step):
        def pick(column):
            return lax.rem(sum(int(item[column]) << (2 * i) for i, item in enumerate(ORDER)) >> (2 * step), 4)

        role, side, half = pick(0), pick(1), pick(2)
        relation = jnp.where(role == 0, at["far"], jnp.where(role == 1, at["near"], 1))
        span = pl.ds(pl.multiple_of(half * part_rows, part_rows), part_rows)

        def whose(w, carry):
            first = jnp.where(w == 0, sibling, sub)
            target = lax.rem(first + 2 * side, 4)
            base = (relation * 4 + target) * rows + half * part_rows
            node = lax.broadcasted_iota(jnp.int32, (part_rows, LANES), 0) + base
            chosen = jnp.concatenate(
                [jnp.where(node == index[j : j + 1, :], 1.0, 0.0).astype(LOW) for j in range(index.shape[0])], axis=1
            )
            parts[w, role, side, span, :] = dot(chosen, held[...])
            return carry

        lax.fori_loop(0, 2, whose, 0)
        give(role, side, half).start()

    def local(role, side, piece):
        span = pl.ds(piece * size, size)
        return parts[1, role, side, span, :] + landed[role, side, span, :]

    def arrived(kind, ref, piece):
        hop(kind, piece).wait_recv()
        return ref[pl.ds(piece * size, size), :].astype(WIDE)

    def pieces(half):
        return range(half * PIECES // HALVES, (half + 1) * PIECES // HALVES)

    def far_step(side, half):
        give(0, side, half).wait_recv()
        for piece in pieces(half):
            far_out[side, pl.ds(piece * size, size), :] = local(0, side, piece).astype(LOW)
            hop(side, piece).start()

    def near_step(side, half):
        give(1, side, half).wait_recv()
        for piece in pieces(half):
            value = local(1, side, piece) + arrived(side, far_in.at[side], piece)
            near_out[side, pl.ds(piece * size, size), :] = value.astype(LOW)
            hop(2 + side, piece).start()

    def pair_step(half):
        give(2, 1, half).wait_recv()
        for piece in pieces(half):
            value = local(2, 1, piece) + arrived(3, near_in.at[1], piece)
            pair_out[pl.ds(piece * size, size), :] = value.astype(LOW)
            hop(4, piece).start()

    def last_step(half):
        give(2, 0, half).wait_recv()
        for piece in pieces(half):
            value = local(2, 0, piece) + arrived(2, near_in.at[0], piece) + arrived(4, pair_in, piece)
            out[pl.ds(piece * size, size), :] = value

    def drain():
        for item in ORDER:
            give(*item).wait_send()
        for kind in range(5):
            for piece in range(PIECES):
                hop(kind, piece).wait_send()

    events = {
        1: [lambda: far_step(1, 0)],
        2: [lambda: far_step(1, 1)],
        3: [lambda: near_step(1, 0)],
        4: [lambda: far_step(0, 0)],
        5: [lambda: near_step(1, 1), lambda: far_step(0, 1)],
        7: [lambda: near_step(0, 0), lambda: pair_step(0)],
        9: [lambda: near_step(0, 1), lambda: pair_step(1)],
    }

    def run(more):
        def step(i, carry):
            add_messages(i)
            for k in sorted(set(events) | set(more)):
                @pl.when(i == k)
                def _():
                    for event in events.get(k, []) + more.get(k, []):
                        event()

            return carry

        lax.fori_loop(0, len(ORDER), step, 0)
        for half in range(HALVES):
            last_step(half)

    return load, run, drain


def exchange_scratch(rows, width, devices):
    slab = width // devices * (rows // LANES)
    return [
        pltpu.VMEM((devices * slab, LANES), WIDE),
        pltpu.VMEM((devices * slab, LANES), LOW),
        pltpu.VMEM((devices, slab, LANES), LOW),
        pltpu.VMEM((slab, LANES), WIDE),
        pltpu.SemaphoreType.DMA((devices - 1,)),
        pltpu.SemaphoreType.DMA((devices - 1,)),
    ]


def exchange_moves(residual, out, refs):
    flat, packed, landed, opened, send_sems, recv_sems = refs
    subs = lax.axis_size("sub")
    devices = lax.axis_size("blk") * subs
    here = lax.axis_index("blk") * subs + lax.axis_index("sub")
    slab = landed.shape[1]
    channels = out.shape[0]
    parts = slab // channels
    nodes = parts * LANES

    def move(k):
        there = lax.rem(here + k, devices)
        return remote(
            packed.at[pl.ds(pl.multiple_of(there * slab, slab), slab)], landed.at[here],
            send_sems.at[k - 1], recv_sems.at[k - 1], (there // subs, lax.rem(there, subs)),
        )

    def start(values):
        lay_rows(flat, 0, values.T)

        def cast(i, block):
            packed[pl.ds(i, block), :] = flat[pl.ds(i, block), :].astype(LOW)

        in_pieces(flat.shape[0], cast)

        def send(k, carry):
            move(k).start()
            return carry

        lax.fori_loop(1, devices, send, 0)

    def open_slab(source, device):
        opened[...] = source.astype(WIDE)
        for j in range(parts):
            columns = pl.ds(pl.multiple_of(device * nodes + j * LANES, LANES), LANES)
            out[:, columns] = residual[:, columns] + opened[pl.ds(j, channels, stride=parts), :]

    def last():
        open_slab(packed[pl.ds(pl.multiple_of(here * slab, slab), slab), :], here)

        def take(k, carry):
            move(k).wait_recv()
            device = lax.rem(here - k + devices, devices)
            open_slab(landed[device], device)
            return carry

        lax.fori_loop(1, devices, take, 0)

        def sent(k, carry):
            move(k).wait_send()
            return carry

        lax.fori_loop(1, devices, sent, 0)

    return start, last


def finish_kernel(
    index, messages, edge_grads, node_grads, vectors, node_part, weight, residual,
    node_grad, one_out, two_out, three_out, four_out, reduced_vectors, total, reduced, out_sems, *refs,
):
    at = places()
    count = len(collect_scratch(64, 128, 64))
    load, run, drain = collect_moves(at, index, messages, total, refs[:count])
    load.start()
    meet_all()
    steps, refs = reducers(at, (edge_grads, node_grads), reduced, refs[count:])
    vector_steps = vector_reducer(at, vectors, reduced_vectors, refs[:4])
    exchange, receive = exchange_moves(residual, node_grad, refs[4:])
    steps[0]()
    vector_steps[0]()
    load.wait()
    run({
        1: [steps[1], vector_steps[1]],
        4: [steps[2], vector_steps[2]],
        7: [steps[3], vector_steps[3]],
        10: [steps[4]],
    })
    steps[5]()
    high, rest = split_low(total[...])
    exchange(node_part[...] + dot_right(high, weight[...]) + dot_right(rest, weight[...]))
    steps[6]()
    steps[7]()
    receive()
    steps[8]()
    width = total.shape[1]
    nodes_at = edge_grads.shape[0]
    copies = [
        pltpu.make_async_copy(reduced.at[pl.ds(first, target.shape[0])], target, out_sems.at[i])
        for i, (first, target) in enumerate((
            (0, one_out), (3 * width, two_out), (nodes_at, three_out), (nodes_at + 2 * width, four_out)
        ))
    ]
    for copy in copies:
        copy.start()
    vector_steps[4]()
    drain()
    steps[9]()
    for copy in copies:
        copy.wait()


def finish(index, messages, edge_grads, node_grads, vectors, node_part, weight, residual, collective):
    rows, width = node_part.shape
    edges = messages.shape[0]
    sources = [edge_grads.shape[0], node_grads.shape[0]]
    along = lax.axis_size("blk") // 2
    devices = lax.axis_size("blk") * lax.axis_size("sub")
    hold = pl.BlockSpec(memory_space=pltpu.VMEM)
    across = pl.BlockSpec(memory_space=pl.ANY)
    return pl.pallas_call(
        finish_kernel,
        grid=(1,),
        in_specs=[
            hold, across, across, across, hold, hold, pl.BlockSpec((width, width), lambda i: (2, 0)), hold,
        ],
        out_specs=[hold] + [across] * 4 + [hold],
        out_shape=[
            jax.ShapeDtypeStruct(residual.shape, WIDE),
            jax.ShapeDtypeStruct((3 * width, width), LOW),
            jax.ShapeDtypeStruct((width, width), LOW),
            jax.ShapeDtypeStruct((2 * width, width), LOW),
            jax.ShapeDtypeStruct((width, width), LOW),
            jax.ShapeDtypeStruct(vectors.shape, WIDE),
        ],
        scratch_shapes=[
            pltpu.VMEM((rows, width), WIDE),
            pltpu.VMEM((sum(sources), width), LOW),
            pltpu.SemaphoreType.DMA((4,)),
            *collect_scratch(rows, width, edges),
            *reducers_scratch(sources, width, along),
            *vector_scratch(vectors.shape, along),
            *exchange_scratch(rows, width, devices),
        ],
        compiler_params=pltpu.CompilerParams(
            collective_id=collective, has_side_effects=True, vmem_limit_bytes=VMEM_BYTES
        ),
        name="finish_sums",
    )(index.reshape(edges // LANES, LANES), messages, edge_grads, node_grads, vectors, node_part, weight, residual)


def middle_kernel(
    index, messages, node_low, upstream, w_one, b_one, w_two, b_two, gain, shift, residual,
    table, node_part, node_out, grads, vectors, total, sent, *refs
):
    at = places()
    count = len(collect_scratch(64, 128, 64))
    load, run, drain = collect_moves(at, index, messages, total, refs[:count])
    load.start()
    meet_all()
    refs = refs[count:]
    start, one, two, three, end = spread_moves(at, sent, table, *refs[:3])
    exchange, receive = exchange_moves(residual, node_out, refs[3:])
    load.wait()
    run({})

    width = total.shape[1]
    low = total[...].astype(LOW)
    pre = dot(node_low[...], w_one[:width]) + dot(low, w_one[width:]) + b_one[...]
    logistic = jax.nn.sigmoid(pre)
    act = (pre * logistic).astype(LOW)
    normal, scale = row_normal(dot(act, w_two[...]) + b_two[...])
    given = upstream[...].T
    scaled = given * gain[...]
    slope = jnp.mean(scaled * normal, -1, keepdims=True)
    fourth = scale * (scaled - jnp.mean(scaled, -1, keepdims=True) - normal * slope)
    fourth_low = fourth.astype(LOW)
    third = dot_right(fourth_low, w_two[...]) * (logistic * (1.0 + pre * (1.0 - logistic)))
    third_low = third.astype(LOW)
    sent[...] = dot_right(third_low, w_one[width:]).astype(LOW)
    start()
    grads[:width] = dot_left(node_low[...], third_low)
    grads[width : 2 * width] = dot_left(low, third_low)
    grads[2 * width : 3 * width] = dot_left(act, fourth_low)
    vectors[...] = jnp.zeros_like(vectors)
    vectors[0:1] = jnp.sum(third_low.astype(WIDE), 0, keepdims=True)
    vectors[1:2] = jnp.sum(fourth_low.astype(WIDE), 0, keepdims=True)
    vectors[2:3] = jnp.sum(given * normal, 0, keepdims=True)
    vectors[3:4] = jnp.sum(given, 0, keepdims=True)
    node_part[...] = dot_right(third_low, w_one[:width])
    exchange(normal * gain[...] + shift[...])

    for stage in (one, two, three):
        for piece in range(PIECES):
            stage(piece)
    receive()
    end()
    drain()


def middle(index, messages, node_low, upstream, w_one, b_one, w_two, b_two, gain, shift, residual, collective):
    rows, width = node_low.shape
    edges = messages.shape[0]
    devices = lax.axis_size("blk") * lax.axis_size("sub")
    grad_rows = padded_rows(3 * width)
    hold = pl.BlockSpec(memory_space=pltpu.VMEM)
    across = pl.BlockSpec(memory_space=pl.ANY)
    table, node_part, node_out, grads, vectors = pl.pallas_call(
        middle_kernel,
        in_specs=[hold, across] + [hold] * 9,
        out_specs=[across] + [hold] * 4,
        out_shape=[
            jax.ShapeDtypeStruct((3, 4, rows, width), LOW),
            jax.ShapeDtypeStruct((rows, width), WIDE),
            jax.ShapeDtypeStruct(residual.shape, WIDE),
            jax.ShapeDtypeStruct((grad_rows, width), WIDE),
            jax.ShapeDtypeStruct((8, width), WIDE),
        ],
        scratch_shapes=[
            pltpu.VMEM((rows, width), WIDE),
            pltpu.VMEM((rows, width), LOW),
            *collect_scratch(rows, width, edges),
            *spread_scratch(),
            *exchange_scratch(rows, width, devices),
        ],
        compiler_params=pltpu.CompilerParams(
            collective_id=collective, has_side_effects=True, vmem_limit_bytes=VMEM_BYTES
        ),
        name="middle_nodes",
    )(
        index.reshape(edges // LANES, LANES), messages, node_low, upstream,
        w_one, b_one, w_two, b_two, gain, shift, residual,
    )
    return table.reshape(12 * rows, width), node_part, node_out, grads, vectors


def scatter_scratch(channels, nodes, devices):
    slab = channels * (nodes // LANES)
    return [
        pltpu.VMEM((devices * slab, LANES), WIDE),
        pltpu.VMEM((devices * slab, LANES), LOW),
        pltpu.VMEM((devices, slab, LANES), LOW),
        pltpu.VMEM((slab, LANES), WIDE),
        pltpu.VMEM((nodes // LANES * devices * channels, LANES), WIDE),
        pltpu.SemaphoreType.DMA((devices - 1,)),
        pltpu.SemaphoreType.DMA((devices - 1,)),
    ]


def scatter_moves(shard, refs):
    flat, packed, landed, opened, square, send_sems, recv_sems = refs
    subs = lax.axis_size("sub")
    devices = lax.axis_size("blk") * subs
    here = lax.axis_index("blk") * subs + lax.axis_index("sub")
    slab = landed.shape[1]
    channels = shard.shape[0]
    parts = slab // channels
    nodes = parts * LANES

    def move(k):
        there = lax.rem(here + k, devices)
        return remote(
            packed.at[pl.ds(pl.multiple_of(there * slab, slab), slab)], landed.at[here],
            send_sems.at[k - 1], recv_sems.at[k - 1], (there // subs, lax.rem(there, subs)),
        )

    def start():
        def pack(k, carry):
            device = lax.rem(here + k, devices)
            rows = pl.ds(pl.multiple_of(device * slab, slab), slab)
            for j in range(parts):
                columns = pl.ds(pl.multiple_of(device * nodes + j * LANES, LANES), LANES)
                flat[pl.ds(device * slab + j, channels, stride=parts), :] = shard[:, columns]
            packed[rows, :] = flat[rows, :].astype(LOW)
            return carry

        def send(k, carry):
            pack(k, carry)
            move(k).start()
            return carry

        lax.fori_loop(1, devices, send, 0)
        pack(0, 0)

    def open_slab(source, device):
        opened[...] = source.astype(WIDE)
        for j in range(parts):
            rows = pl.ds(pl.multiple_of((j * devices + device) * channels, channels), channels)
            square[rows, :] = opened[pl.ds(j, channels, stride=parts), :]

    def last(rows):
        open_slab(packed[pl.ds(pl.multiple_of(here * slab, slab), slab), :], here)

        def take(k, carry):
            move(k).wait_recv()
            device = lax.rem(here - k + devices, devices)
            open_slab(landed[device], device)
            return carry

        lax.fori_loop(1, devices, take, 0)
        width = devices * channels
        for j in range(parts):
            rows[j * LANES : (j + 1) * LANES, :] = square[j * width : (j + 1) * width, :].T.astype(LOW)

    def drain():
        def sent(k, carry):
            move(k).wait_send()
            return carry

        lax.fori_loop(1, devices, sent, 0)

    return start, last, drain


def begin_kernel(
    shard, later, senders, receivers, own, table, later_out, send_local, recv_wide, held, held_sem, slab_sems, *refs
):
    at = places()
    fetch = pltpu.make_async_copy(later, held, held_sem)
    fetch.start()
    meet_all()
    start, last, drain = scatter_moves(shard, refs[3:])
    start()
    last(own)
    begin, one, two, three, end = spread_moves(at, own, table, *refs[:3])
    begin()
    rows = own.shape[0]
    groups, subs = lax.axis_size("blk"), lax.axis_size("sub")
    send_local[...] = senders[...] - (at["group"] * subs + at["sub"]) * rows
    relative = lax.rem(receivers[...] // (rows * subs) - at["group"] + 1 + groups, groups)
    recv_wide[...] = relative * (rows * subs) + lax.rem(receivers[...], rows * subs)
    fetch.wait()
    devices, _, nodes = later_out.shape

    def slab(k):
        columns = pl.ds(pl.multiple_of(k * nodes, LANES), nodes)
        return pltpu.make_async_copy(held.at[:, columns], later_out.at[k], slab_sems.at[k])

    def give(k, carry):
        slab(k).start()
        return carry

    def given(k, carry):
        slab(k).wait()
        return carry

    lax.fori_loop(0, devices, give, 0)
    drain()
    for stage in (one, two, three):
        for piece in range(PIECES):
            stage(piece)
    lax.fori_loop(0, devices, given, 0)
    end()


def begin(shard, later, senders, receivers, rows, collective):
    channels, nodes = shard.shape
    devices = lax.axis_size("blk") * lax.axis_size("sub")
    width = channels * devices
    hold = pl.BlockSpec(memory_space=pltpu.VMEM)
    across = pl.BlockSpec(memory_space=pl.ANY)
    lines = (senders.shape[0] // LANES, LANES)
    own, table, later, send_local, recv_wide = pl.pallas_call(
        begin_kernel,
        in_specs=[hold, across, hold, hold],
        out_specs=[hold, across, across, hold, hold],
        out_shape=[
            jax.ShapeDtypeStruct((rows, width), LOW),
            jax.ShapeDtypeStruct((3, 4, rows, width), LOW),
            jax.ShapeDtypeStruct((devices, channels, rows), later.dtype),
            jax.ShapeDtypeStruct(lines, jnp.int32),
            jax.ShapeDtypeStruct(lines, jnp.int32),
        ],
        scratch_shapes=[
            pltpu.VMEM(later.shape, later.dtype),
            pltpu.SemaphoreType.DMA,
            pltpu.SemaphoreType.DMA((devices,)),
            *spread_scratch(),
            *scatter_scratch(channels, rows, devices),
        ],
        compiler_params=pltpu.CompilerParams(
            collective_id=collective, has_side_effects=True, vmem_limit_bytes=VMEM_BYTES
        ),
        name="begin_rows",
    )(shard, later, senders.reshape(lines), receivers.reshape(lines))
    return own, table.reshape(12 * rows, width), later, send_local, recv_wide


def shards(
    node_input,
    edge_input,
    senders,
    receivers,
    edge_count,
    edge_w_one,
    edge_b_one,
    edge_w_two,
    edge_b_two,
    edge_gain,
    edge_shift,
    node_w_one,
    node_b_one,
    node_w_two,
    node_b_two,
    node_gain,
    node_shift,
    node_cotangent,
    edge_cotangent,
):
    groups = lax.axis_size("blk")
    sub_count = lax.axis_size("sub")
    width = edge_input.shape[1]
    per_device = node_input.shape[1] // (groups * sub_count)
    node_low, wide_low, cotangent_later, send_local, recv_wide = begin(
        node_input, node_cotangent, senders, receivers, per_device, 0
    )
    node_upstream = lax.all_to_all(
        cotangent_later, ("blk", "sub"), split_axis=0, concat_axis=0, tiled=True
    ).reshape(width, per_device)
    recv_list = recv_wide.reshape(-1)
    edge_result, first_pre, second_pre, received, messages = edge_forward(
        edge_count, recv_list, send_local, edge_input, wide_low, node_low,
        edge_w_one, edge_b_one[None], edge_w_two, edge_b_two[None], edge_gain[None], edge_shift[None],
    )
    wide_grad, node_part, node_out, node_grads, node_vectors = middle(
        recv_list, messages, node_low, node_upstream, node_w_one, node_b_one[None], node_w_two, node_b_two[None],
        node_gain[None], node_shift[None], node_input, 1,
    )
    edge_grad, messages, edge_grads, vectors, node_part = edge_backward(
        edge_count, recv_list, send_local, edge_cotangent, edge_input, received, first_pre, second_pre,
        wide_grad, node_part, node_low, edge_w_one, edge_w_two, edge_gain[None],
    )
    node_grad, *summed, vectors = finish(
        recv_list, messages, edge_grads, node_grads, jnp.concatenate([vectors[:4], node_vectors[:4]]), node_part,
        edge_w_one, node_cotangent, 3,
    )
    summed = [item.astype(jnp.float32) for item in summed]
    return (
        node_out,
        edge_result,
        node_grad,
        edge_grad,
        summed[0],
        vectors[0],
        summed[1],
        vectors[1],
        vectors[2],
        vectors[3],
        summed[2],
        vectors[4],
        summed[3],
        vectors[5],
        vectors[6],
        vectors[7],
    )


def solution(mesh):
    placed = (
        P(("blk", "sub"), None),
        P(("blk", "sub"), None),
        P(("blk", "sub")),
        P(("blk", "sub")),
        P(("blk", "sub")),
        P(),
        P(),
        P(),
        P(),
        P(),
        P(),
        P(),
        P(),
        P(),
        P(),
        P(),
        P(),
        P(("blk", "sub"), None),
        P(("blk", "sub"), None),
    )
    return jax.shard_map(
        shards,
        mesh=mesh,
        in_specs=placed,
        out_specs=(
            P(("blk", "sub"), None),
            P(("blk", "sub"), None),
            P(("blk", "sub"), None),
            P(("blk", "sub"), None),
            P(),
            P(),
            P(),
            P(),
            P(),
            P(),
            P(),
            P(),
            P(),
            P(),
            P(),
            P(),
        ),
        check_vma=False,
    )
```

```python
import functools
import math

import jax
import jax.numpy as jnp
from jax import lax
from jax.experimental import pallas as pl
from jax.experimental.pallas import tpu as pltpu
from jax.sharding import PartitionSpec as P

EPSILON = 1e-05


TILE = 512
CHUNK = 512
LANES = 128
VMEM_BYTES = 60 * 2**20


def dot(left, right):
    return jnp.dot(left, right, preferred_element_type=jnp.float32)


def dot_left(left, right):
    return lax.dot_general(
        left, right, (((0,), (0,)), ((), ())), preferred_element_type=jnp.float32
    )


def dot_right(left, right):
    return lax.dot_general(
        left, right, (((1,), (1,)), ((), ())), preferred_element_type=jnp.float32
    )


def split_low(values):
    high = values.astype(jnp.bfloat16)
    return high, (values - high.astype(jnp.float32)).astype(jnp.bfloat16)


def lay_rows(target, start, values):
    count, width = values.shape
    parts = width // LANES
    for j in range(parts):
        target[pl.ds(start * parts + j, count, stride=parts), :] = values[:, j * LANES : (j + 1) * LANES]


def read_rows(source, start, count, parts):
    return jnp.concatenate(
        [source[pl.ds(start * parts + j, count, stride=parts), :] for j in range(parts)], axis=1
    )


def load_table(wide, table, stage, sems):
    steps = wide.shape[0] // CHUNK

    def fetch(i, slot):
        return pltpu.make_async_copy(wide.at[pl.ds(i * CHUNK, CHUNK)], stage.at[slot], sems.at[slot])

    for i in range(3):
        fetch(i, i).start()

    def body(i, carry):
        slot = lax.rem(i, 4)

        @pl.when(i + 3 < steps)
        def _():
            fetch(i + 3, lax.rem(i + 3, 4)).start()

        fetch(i, slot).wait()

        def piece(k, carry):
            values = stage[slot, pl.ds(k * 64, 64), :].astype(jnp.float32)
            lay_rows(table, i * CHUNK + k * 64, values)
            return carry

        return lax.fori_loop(0, CHUNK // 64, piece, carry)

    lax.fori_loop(0, steps, body, 0)


def gather_rows(index, base, table, rows, parts):
    count = rows.shape[0] // parts

    def body(i, carry):
        for u in range(16):
            slot = i * 16 + u
            place = index[base + slot]
            rows[pl.ds(pl.multiple_of(slot * parts, parts), parts), :] = table[
                pl.ds(pl.multiple_of(place * parts, parts), parts), :
            ]
        return carry

    lax.fori_loop(0, count // 16, body, 0)


def gather_inline(index, base, table, rows, parts):
    for slot in range(rows.shape[0] // parts):
        place = index[base + slot]
        rows[slot * parts : (slot + 1) * parts, :] = table[pl.ds(pl.multiple_of(place * parts, parts), parts), :]


def row_normal(values):
    average = jnp.mean(values, -1, keepdims=True)
    centred = values - average
    variance = jnp.mean(centred * centred, -1, keepdims=True)
    scale = lax.rsqrt(variance + EPSILON)
    return centred * scale, scale


def forward_kernel(
    count, recv, send, edge, wide, nodes, w_one, b_one, w_two, b_two, gain, shift,
    result, first, second, received, message,
    table, rows, stage, sems,
):
    step = pl.program_id(0)
    base = step * TILE
    width = nodes.shape[1]
    parts = width // LANES

    @pl.when(step == 0)
    def _():
        load_table(wide, table, stage, sems)
        gather_rows(recv, base, table, rows, parts)

    later = jnp.where(step + 1 < pl.num_programs(0), base + TILE, 0)
    received[...] = read_rows(rows, 0, TILE, parts).astype(jnp.bfloat16)
    gather_inline(recv, later, table, rows, parts)
    from_recv = received[...]
    lane = lax.broadcasted_iota(jnp.int32, (LANES, LANES), 1)
    chosen = []
    for i in range(TILE // LANES):
        column = jnp.broadcast_to(send[pl.ds(step * (TILE // LANES) + i, 1), :], (LANES, LANES)).T
        chosen.append(
            jnp.concatenate(
                [
                    jnp.where(column == lane + j * LANES, 1.0, 0.0).astype(jnp.bfloat16)
                    for j in range(nodes.shape[0] // LANES)
                ],
                axis=1,
            )
        )
    chosen = jnp.concatenate(chosen, axis=0)
    from_send = dot(chosen, nodes[...]).astype(jnp.bfloat16)
    pre = (
        dot(edge[...], w_one[:width])
        + dot(from_send, w_one[width : 2 * width])
        + dot(from_recv, w_one[2 * width :])
        + b_one[...]
    )
    first[...] = pre
    act = (pre * jax.nn.sigmoid(pre)).astype(jnp.bfloat16)
    post = dot(act, w_two[...]) + b_two[...]
    second[...] = post
    normal, _ = row_normal(post)
    branch = normal * gain[...] + shift[...]
    live = base + lax.broadcasted_iota(jnp.int32, (TILE, 1), 0) < count[0]
    outcome = edge[...].astype(jnp.float32) + jnp.where(live, branch, 0.0)
    result[...] = outcome
    message[...] = jnp.where(live, outcome, 0.0).astype(jnp.bfloat16)


def edge_forward(count, recv, send, edge, wide, nodes, w_one, b_one, w_two, b_two, gain, shift):
    edges, width = edge.shape
    steps = edges // TILE
    parts = width // LANES
    hold = pl.BlockSpec(memory_space=pltpu.VMEM)
    scalar = pl.BlockSpec(memory_space=pltpu.SMEM)
    tile = pl.BlockSpec((TILE, width), lambda i: (i, 0))
    return pl.pallas_call(
        forward_kernel,
        grid=(steps,),
        in_specs=[
            scalar, scalar, hold, tile,
            pl.BlockSpec(memory_space=pl.ANY), hold, hold, hold, hold, hold, hold, hold,
        ],
        out_specs=[tile] * 5,
        out_shape=[
            jax.ShapeDtypeStruct((edges, width), jnp.float32),
            jax.ShapeDtypeStruct((edges, width), jnp.float32),
            jax.ShapeDtypeStruct((edges, width), jnp.float32),
            jax.ShapeDtypeStruct((edges, width), jnp.bfloat16),
            jax.ShapeDtypeStruct((edges, width), jnp.bfloat16),
        ],
        scratch_shapes=[
            pltpu.VMEM((wide.shape[0] * parts, LANES), jnp.float32),
            pltpu.VMEM((TILE * parts, LANES), jnp.float32),
            pltpu.VMEM((4, CHUNK, width), jnp.bfloat16),
            pltpu.SemaphoreType.DMA((4,)),
        ],
        compiler_params=pltpu.CompilerParams(vmem_limit_bytes=VMEM_BYTES),
        cost_estimate=pl.CostEstimate(
            flops=20 * edges * width * width, bytes_accessed=40 * edges * width, transcendentals=2 * edges * width
        ),
        name="edge_forward",
    )(count, recv, send, edge, wide, nodes, w_one, b_one, w_two, b_two, gain, shift)


def backward_kernel(
    count, recv, send, cotangent, edge, received, first, second, wide, node_part, node_vectors, nodes, w_one, w_two, gain,
    grad, message, all_grads, vectors, sender_grad,
    table, rows, stage, sems, by_sender, grads, give_sem,
):
    step = pl.program_id(0)
    base = step * TILE
    width = nodes.shape[1]
    parts = width // LANES

    @pl.when(step == 0)
    def _():
        load_table(wide, table, stage, sems)
        grads[...] = jnp.zeros_like(grads)
        vectors[...] = node_vectors[...]
        by_sender[...] = jnp.zeros_like(by_sender)
        gather_rows(recv, base, table, rows, parts)

    live = base + lax.broadcasted_iota(jnp.int32, (TILE, 1), 0) < count[0]
    upstream = cotangent[...].astype(jnp.float32) + jnp.where(live, read_rows(rows, 0, TILE, parts), 0.0)
    grad[...] = upstream
    later = jnp.where(step + 1 < pl.num_programs(0), base + TILE, 0)
    gather_inline(recv, later, table, rows, parts)
    masked = jnp.where(live, upstream, 0.0)
    normal, scale = row_normal(second[...])
    vectors[2:3, :] += jnp.sum(masked * normal, 0, keepdims=True)
    vectors[3:4, :] += jnp.sum(masked, 0, keepdims=True)
    scaled = masked * gain[...]
    slope = jnp.mean(scaled * normal, -1, keepdims=True)
    grad_second = scale * (scaled - jnp.mean(scaled, -1, keepdims=True) - normal * slope)
    second_low = grad_second.astype(jnp.bfloat16)
    vectors[1:2, :] += jnp.sum(second_low.astype(jnp.float32), 0, keepdims=True)
    pre = first[...]
    logistic = jax.nn.sigmoid(pre)
    act = (pre * logistic).astype(jnp.bfloat16)
    grads[3 * width : 4 * width] += dot_left(act, second_low)
    grad_first = dot_right(second_low, w_two[...]) * (logistic * (1.0 + pre * (1.0 - logistic)))
    first_low = grad_first.astype(jnp.bfloat16)
    message[...] = first_low
    vectors[0:1, :] += jnp.sum(first_low.astype(jnp.float32), 0, keepdims=True)
    grads[:width] += dot_left(edge[...], first_low)
    grads[2 * width : 3 * width] += dot_left(received[...], first_low)
    node = lax.broadcasted_iota(jnp.int32, (nodes.shape[0], LANES), 0)
    chosen = jnp.concatenate(
        [
            jnp.where(node == send[pl.ds(step * (TILE // LANES) + i, 1), :], 1.0, 0.0).astype(jnp.bfloat16)
            for i in range(TILE // LANES)
        ],
        axis=1,
    )
    by_sender[...] += dot(chosen, first_low)
    grad[...] += dot_right(first_low, w_one[:width])

    @pl.when(step == pl.num_programs(0) - 1)
    def _():
        high, rest = split_low(by_sender[...])
        grads[width : 2 * width] = dot_left(nodes[...], high) + dot_left(nodes[...], rest)
        give = pltpu.make_async_copy(grads, all_grads, give_sem)
        give.start()
        middle = w_one[width : 2 * width]
        sender_grad[...] = node_part[...] + dot_right(high, middle) + dot_right(rest, middle)
        give.wait()


def edge_backward(
    count, recv, send, cotangent, edge, received, first, second, wide, node_part, node_vectors, nodes,
    w_one, w_two, gain,
):
    edges, width = edge.shape
    steps = edges // TILE
    parts = width // LANES
    per_device = nodes.shape[0]
    hold = pl.BlockSpec(memory_space=pltpu.VMEM)
    scalar = pl.BlockSpec(memory_space=pltpu.SMEM)
    tile = pl.BlockSpec((TILE, width), lambda i: (i, 0))

    across = pl.BlockSpec(memory_space=pl.ANY)

    def whole(rows):
        return pl.BlockSpec((rows, width), lambda i: (0, 0))

    return pl.pallas_call(
        backward_kernel,
        grid=(steps,),
        in_specs=[
            scalar, scalar, hold, tile, tile, tile, tile, tile,
            across, hold, hold, hold, hold, hold, hold,
        ],
        out_specs=[
            tile, tile, across, whole(8), whole(per_device),
        ],
        out_shape=[
            jax.ShapeDtypeStruct((edges, width), jnp.float32),
            jax.ShapeDtypeStruct((edges, width), jnp.bfloat16),
            jax.ShapeDtypeStruct((4 * width, width), jnp.float32),
            jax.ShapeDtypeStruct((8, width), jnp.float32),
            jax.ShapeDtypeStruct((per_device, width), jnp.float32),
        ],
        scratch_shapes=[
            pltpu.VMEM((wide.shape[0] * parts, LANES), jnp.float32),
            pltpu.VMEM((TILE * parts, LANES), jnp.float32),
            pltpu.VMEM((4, CHUNK, width), jnp.bfloat16),
            pltpu.SemaphoreType.DMA((4,)),
            pltpu.VMEM((per_device, width), jnp.float32),
            pltpu.VMEM((4 * width, width), jnp.float32),
            pltpu.SemaphoreType.DMA,
        ],
        compiler_params=pltpu.CompilerParams(vmem_limit_bytes=VMEM_BYTES),
        cost_estimate=pl.CostEstimate(
            flops=24 * edges * width * width, bytes_accessed=40 * edges * width, transcendentals=2 * edges * width
        ),
        name="edge_backward",
    )(
        count, recv, send, cotangent, edge, received, first, second, wide,
        node_part, node_vectors, nodes, w_one, w_two, gain,
    )


MESH = pl.DeviceIdType.MESH
PIECES = 4
SPLIT = True
LOW = jnp.bfloat16
WIDE = jnp.float32


def places():
    groups = lax.axis_size("blk")
    group, sub = lax.axis_index("blk"), lax.axis_index("sub")
    odd = lax.rem(group, 2)
    along = groups // 2
    spot = group // 2
    beside = group + 1 - 2 * odd
    return dict(
        group=group,
        sub=sub,
        core=lax.rem(sub, 2),
        chip=sub // 2,
        odd=odd,
        spot=spot,
        along=along,
        sibling=sub + 1 - 2 * lax.rem(sub, 2),
        partner=lax.rem(sub + 2, 4),
        to_sibling=(group, sub + 1 - 2 * lax.rem(sub, 2)),
        to_partner=(group, lax.rem(sub + 2, 4)),
        to_beside=(beside, sub),
        to_onward=(lax.rem(group + 2 - 4 * odd + groups, groups), sub),
        to_source=(lax.rem(group - 2 + 4 * odd + groups, groups), sub),
        peers=[(2 * lax.rem(spot + k, along) + odd, sub) for k in range(1, along)],
        near=2 - 2 * odd,
        far=2 * odd,
    )


def meet(senders):
    barrier = pltpu.get_barrier_semaphore()
    for device in senders:
        pl.semaphore_signal(barrier, inc=1, device_id=device, device_id_type=MESH)
    pl.semaphore_wait(barrier, len(senders))


def meet_all():
    barrier = pltpu.get_barrier_semaphore()
    subs = lax.axis_size("sub")
    devices = lax.axis_size("blk") * subs
    here = lax.axis_index("blk") * subs + lax.axis_index("sub")

    def greet(k, carry):
        there = lax.rem(here + k, devices)
        pl.semaphore_signal(barrier, inc=1, device_id=(there // subs, lax.rem(there, subs)), device_id_type=MESH)
        return carry

    lax.fori_loop(1, devices, greet, 0)
    pl.semaphore_wait(barrier, devices - 1)


def remote(source, target, send, recv, device):
    return pltpu.make_async_remote_copy(
        src_ref=source, dst_ref=target, send_sem=send, recv_sem=recv, device_id=device, device_id_type=MESH
    )


def in_pieces(count, body):
    block = math.gcd(count, 128)

    def run(i, carry):
        body(pl.multiple_of(i * block, block), block)
        return carry

    lax.fori_loop(0, count // block, run, 0)


def padded_rows(rows):
    unit = 64 * lax.axis_size("blk")
    return -(-rows // unit) * unit


def streams_of(sources):
    unit = 64 * lax.axis_size("blk")
    streams = []
    for i, rows in enumerate(sources):
        first = -(-(rows // unit) // 2) * unit if SPLIT else rows
        streams.append((i, 0, first))
        if first < rows:
            streams.append((i, first, rows - first))
    return streams


def reducers_scratch(sources, width, along):
    return [ref for _, _, rows in streams_of(sources) for ref in reducer_scratch(rows, width, along)]


def reducers(at, sources, reduced, refs):
    made = []
    for i, (which, start, rows) in enumerate(streams_of([source.shape[0] for source in sources])):
        first = start + sum(source.shape[0] for source in sources[:which])
        made.append(reducer(at, sources[which], start, reduced, first, rows, i % 2 > 0, refs[i * 13 : i * 13 + 13]))
    return both(made), refs[len(made) * 13 :]


def reducer_scratch(rows, width, along):
    return [
        pltpu.VMEM((rows // 2, width), WIDE),
        pltpu.VMEM((rows // 2, width), WIDE),
        pltpu.VMEM((rows // 4, width), LOW),
        pltpu.VMEM((rows // 4, width), LOW),
        pltpu.VMEM((rows // 8, width), LOW),
        pltpu.VMEM((rows // 8, width), LOW),
        pltpu.VMEM((rows // 8, width), LOW),
        pltpu.VMEM((along - 1, rows // 8 // along, width), LOW),
        pltpu.SemaphoreType.DMA,
        pltpu.SemaphoreType.DMA((6,)),
        pltpu.SemaphoreType.DMA((6,)),
        pltpu.SemaphoreType.DMA((2, along - 1)),
        pltpu.SemaphoreType.DMA((2, along - 1)),
    ]


def reducer(at, grads, source_first, reduced, first, rows, swap, refs):
    (
        half, half_in, cross_out, cross_in, side_out, side_in, ring_out, ring_in,
        load_sem, step_send, step_recv, ring_send, ring_recv,
    ) = refs
    along, peers = at["along"], at["peers"]
    turns = [(at["chip"], at["to_partner"]), (at["odd"], at["to_beside"])]
    (bit_one, device_one), (bit_two, device_two) = turns[::-1] if swap else turns
    core, spot = at["core"], at["spot"]
    n_half, n_cross, n_side, n_ring = rows // 2, rows // 4, rows // 8, rows // 8 // along
    at_half = first + core * n_half
    at_cross = at_half + bit_one * n_cross
    at_side = at_cross + bit_two * n_side
    at_ring = at_side + spot * n_ring

    def span(start, count):
        return pl.ds(pl.multiple_of(start, 16), count)

    def step(kind):
        if kind == 0:
            other = span(source_first + (1 - core) * n_half, n_half)
            source, target, device = grads.at[other], half_in, at["to_sibling"]
        elif kind == 1:
            source, target, device = cross_out, cross_in, device_one
        elif kind == 2:
            source, target, device = side_out, side_in, device_two
        else:
            start, count, device = {
                3: (at_side, n_side, device_two),
                4: (at_cross, n_cross, device_one),
                5: (at_half, n_half, at["to_sibling"]),
            }[kind]
            source = target = reduced.at[span(start, count)]
        return remote(source, target, step_send.at[kind], step_recv.at[kind], device)

    def ring(kind, k):
        if kind == 0:
            source = ring_out.at[span(lax.rem(spot + k, along) * n_ring, n_ring)]
            target = ring_in.at[k - 1]
        else:
            source = target = reduced.at[span(at_ring, n_ring)]
        return remote(source, target, ring_send.at[kind, k - 1], ring_recv.at[kind, k - 1], peers[k - 1])

    load = pltpu.make_async_copy(grads.at[span(source_first + core * n_half, n_half)], half, load_sem)

    def start():
        step(0).start()
        load.start()

    def add_half():
        load.wait()
        step(0).wait_recv()
        other = (1 - bit_one) * n_cross

        def part(i, block):
            here = pl.ds(pl.multiple_of(other + i, block), block)
            cross_out[pl.ds(i, block), :] = (half[here, :] + half_in[here, :]).astype(LOW)

        in_pieces(n_cross, part)
        step(1).start()

    def add_cross():
        mine, other = bit_one * n_cross, (1 - bit_two) * n_side
        step(1).wait_recv()

        def part(i, block):
            there = pl.ds(pl.multiple_of(other + i, block), block)
            here = pl.ds(pl.multiple_of(mine + other + i, block), block)
            side_out[pl.ds(i, block), :] = (half[here, :] + half_in[here, :] + cross_in[there, :].astype(WIDE)).astype(LOW)

        in_pieces(n_side, part)
        step(2).start()

    def add_side():
        mine, kept = bit_one * n_cross, bit_two * n_side
        step(2).wait_recv()

        def part(i, block):
            there = pl.ds(pl.multiple_of(kept + i, block), block)
            here = pl.ds(pl.multiple_of(mine + kept + i, block), block)
            flat = pl.ds(i, block)
            value = half[here, :] + half_in[here, :] + cross_in[there, :].astype(WIDE) + side_in[flat, :].astype(WIDE)
            half[here, :] = value
            ring_out[flat, :] = value.astype(LOW)

        in_pieces(n_side, part)
        for k in range(1, along):
            ring(0, k).start()

    def add_ring():
        value = half[span(bit_one * n_cross + bit_two * n_side + spot * n_ring, n_ring), :]
        for k in range(1, along):
            ring(0, k).wait_recv()
            value = value + ring_in[k - 1].astype(WIDE)
        reduced[span(at_ring, n_ring), :] = value.astype(LOW)
        for k in range(1, along):
            ring(1, k).start()

    def share_side():
        for k in range(1, along):
            ring(1, k).wait_recv()
        step(3).start()

    def share_cross():
        step(3).wait_recv()
        step(4).start()

    def share_half():
        step(4).wait_recv()
        step(5).start()

    def last():
        step(5).wait_recv()

    def drain():
        for kind in range(6):
            step(kind).wait_send()
        for k in range(1, along):
            ring(0, k).wait_send()
            ring(1, k).wait_send()

    return [start, add_half, add_cross, add_side, add_ring, share_side, share_cross, share_half, last, drain]


def vector_scratch(shape, along):
    return [
        pltpu.VMEM((4, *shape), WIDE),
        pltpu.VMEM((2 + along, *shape), WIDE),
        pltpu.SemaphoreType.DMA((2 + along,)),
        pltpu.SemaphoreType.DMA((2 + along,)),
    ]


def vector_reducer(at, vectors, reduced, refs):
    held, held_in, send_sems, recv_sems = refs
    along = at["along"]
    devices = (at["to_sibling"], at["to_partner"], at["to_beside"], *at["peers"])

    def move(kind):
        return remote(held.at[min(kind, 3)], held_in.at[kind], send_sems.at[kind], recv_sems.at[kind], devices[kind])

    def start():
        held[0] = vectors[...]
        move(0).start()

    def turn(kind):
        def run():
            move(kind).wait_recv()
            held[kind + 1] = held[kind] + held_in[kind]
            for k in range(kind + 1, kind + 2 if kind < 2 else 2 + along):
                move(k).start()

        return run

    def last():
        value = held[3]
        for k in range(3, 2 + along):
            move(k).wait_recv()
            value = value + held_in[k]
        reduced[...] = value
        for k in range(2 + along):
            move(k).wait_send()

    return [start, turn(0), turn(1), turn(2), last]


def both(streams):
    return [lambda steps=steps: [step() for step in steps] for steps in zip(*streams)]


def spread_moves(at, own, table, keep_sem, send_sems, recv_sems):
    sub, partner, near, far = at["sub"], at["partner"], at["near"], at["far"]
    to_sibling, to_partner, to_beside, to_onward = (
        at["to_sibling"], at["to_partner"], at["to_beside"], at["to_onward"]
    )
    size = own.shape[0] // PIECES

    def move(kind, piece):
        source, slot, device = {
            0: (None, (1, sub), to_partner),
            1: (None, (far, sub), to_beside),
            2: (None, (1, sub), to_sibling),
            3: ((1, partner), (far, partner), to_beside),
            4: ((1, partner), (1, partner), to_sibling),
            5: ((near, sub), (far, sub), to_onward),
            6: ((near, sub), (near, sub), to_sibling),
            7: ((near, partner), (far, partner), to_onward),
            8: ((near, partner), (near, partner), to_sibling),
            9: ((far, sub), (far, sub), to_sibling),
            10: ((far, partner), (far, partner), to_sibling),
            11: ((near, sub), (near, sub), to_partner),
            12: ((far, sub), (far, sub), to_partner),
        }[kind]
        source = own if source is None else table.at[source[0], source[1]]
        rows = pl.ds(piece * size, size)
        return remote(
            source.at[rows], table.at[slot[0], slot[1], rows],
            send_sems.at[kind, piece], recv_sems.at[kind, piece], device,
        )

    keep = pltpu.make_async_copy(own, table.at[1, sub], keep_sem)

    def start():
        for piece in range(PIECES):
            for kind in (0, 1, 2):
                move(kind, piece).start()
        keep.start()

    def relay(arrived, kinds, piece):
        move(arrived, piece).wait_recv()
        for kind in kinds:
            move(kind, piece).start()

    straight = range(PIECES - 1)

    def one(piece):
        relay(0, (3, 4) if piece in straight else (4,), piece)
        relay(1, (5, 6) if piece in straight else (5, 6, 11), piece)

    def two(piece):
        if piece in straight:
            relay(3, (7, 8), piece)
            relay(5, (9,), piece)
        else:
            relay(5, (9, 12), piece)
            relay(11, (8,), piece)

    def three(piece):
        if piece in straight:
            relay(7, (10,), piece)
        else:
            relay(12, (10,), piece)

    def drain():
        for kind in range(13):
            for piece in range(PIECES):
                if kind in ((11, 12) if piece in straight else (3, 7)):
                    continue
                if kind in (2, 4, 6, 8, 9, 10):
                    move(kind, piece).wait_recv()
                move(kind, piece).wait_send()
        keep.wait()

    return start, one, two, three, drain


def spread_scratch():
    return [
        pltpu.SemaphoreType.DMA,
        pltpu.SemaphoreType.DMA((13, PIECES)),
        pltpu.SemaphoreType.DMA((13, PIECES)),
    ]


HALVES = 2
ORDER = (
    (0, 1, 0), (0, 1, 1), (1, 1, 0), (0, 0, 0), (1, 1, 1), (0, 0, 1),
    (1, 0, 0), (2, 1, 0), (1, 0, 1), (2, 1, 1), (2, 0, 0), (2, 0, 1),
)


def collect_scratch(rows, width, edges):
    return [
        pltpu.VMEM((edges, width), LOW),
        pltpu.VMEM((2, 3, 2, rows, width), WIDE),
        pltpu.VMEM((3, 2, rows, width), WIDE),
        pltpu.VMEM((2, rows, width), LOW),
        pltpu.VMEM((2, rows, width), LOW),
        pltpu.VMEM((2, rows, width), LOW),
        pltpu.VMEM((2, rows, width), LOW),
        pltpu.VMEM((rows, width), LOW),
        pltpu.VMEM((rows, width), LOW),
        pltpu.SemaphoreType.DMA,
        pltpu.SemaphoreType.DMA((3, 2, HALVES)),
        pltpu.SemaphoreType.DMA((3, 2, HALVES)),
        pltpu.SemaphoreType.DMA((5, PIECES)),
        pltpu.SemaphoreType.DMA((5, PIECES)),
    ]


def collect_moves(at, index, messages, out, refs):
    (
        held, parts, landed, far_out, far_in, near_out, near_in, pair_out, pair_in,
        load_sem, give_sems, take_sems, send_sems, recv_sems,
    ) = refs
    sub, partner, sibling = at["sub"], at["partner"], at["sibling"]
    rows = out.shape[0]
    size = rows // PIECES
    part_rows = rows // HALVES
    load = pltpu.make_async_copy(messages, held, load_sem)

    def piece_of(ref, piece):
        return ref.at[pl.ds(piece * size, size)]

    def give(role, side, half):
        span = pl.ds(pl.multiple_of(half * part_rows, part_rows), part_rows)
        return remote(
            parts.at[0, role, side, span], landed.at[role, side, span],
            give_sems.at[role, side, half], take_sems.at[role, side, half], at["to_sibling"],
        )

    def hop(kind, piece):
        source, target, device = {
            0: (far_out.at[0], far_in.at[0], at["to_source"]),
            1: (far_out.at[1], far_in.at[1], at["to_source"]),
            2: (near_out.at[0], near_in.at[0], at["to_beside"]),
            3: (near_out.at[1], near_in.at[1], at["to_beside"]),
            4: (pair_out, pair_in, at["to_partner"]),
        }[kind]
        return remote(
            piece_of(source, piece), piece_of(target, piece),
            send_sems.at[kind, piece], recv_sems.at[kind, piece], device,
        )

    def add_messages(step):
        def pick(column):
            return lax.rem(sum(int(item[column]) << (2 * i) for i, item in enumerate(ORDER)) >> (2 * step), 4)

        role, side, half = pick(0), pick(1), pick(2)
        relation = jnp.where(role == 0, at["far"], jnp.where(role == 1, at["near"], 1))
        span = pl.ds(pl.multiple_of(half * part_rows, part_rows), part_rows)

        def whose(w, carry):
            first = jnp.where(w == 0, sibling, sub)
            target = lax.rem(first + 2 * side, 4)
            base = (relation * 4 + target) * rows + half * part_rows
            node = lax.broadcasted_iota(jnp.int32, (part_rows, LANES), 0) + base
            chosen = jnp.concatenate(
                [jnp.where(node == index[j : j + 1, :], 1.0, 0.0).astype(LOW) for j in range(index.shape[0])], axis=1
            )
            parts[w, role, side, span, :] = dot(chosen, held[...])
            return carry

        lax.fori_loop(0, 2, whose, 0)
        give(role, side, half).start()

    def local(role, side, piece):
        span = pl.ds(piece * size, size)
        return parts[1, role, side, span, :] + landed[role, side, span, :]

    def arrived(kind, ref, piece):
        hop(kind, piece).wait_recv()
        return ref[pl.ds(piece * size, size), :].astype(WIDE)

    def pieces(half):
        return range(half * PIECES // HALVES, (half + 1) * PIECES // HALVES)

    def far_step(side, half):
        give(0, side, half).wait_recv()
        for piece in pieces(half):
            far_out[side, pl.ds(piece * size, size), :] = local(0, side, piece).astype(LOW)
            hop(side, piece).start()

    def near_step(side, half):
        give(1, side, half).wait_recv()
        for piece in pieces(half):
            value = local(1, side, piece) + arrived(side, far_in.at[side], piece)
            near_out[side, pl.ds(piece * size, size), :] = value.astype(LOW)
            hop(2 + side, piece).start()

    def pair_step(half):
        give(2, 1, half).wait_recv()
        for piece in pieces(half):
            value = local(2, 1, piece) + arrived(3, near_in.at[1], piece)
            pair_out[pl.ds(piece * size, size), :] = value.astype(LOW)
            hop(4, piece).start()

    def last_step(half):
        give(2, 0, half).wait_recv()
        for piece in pieces(half):
            value = local(2, 0, piece) + arrived(2, near_in.at[0], piece) + arrived(4, pair_in, piece)
            out[pl.ds(piece * size, size), :] = value

    def drain():
        for item in ORDER:
            give(*item).wait_send()
        for kind in range(5):
            for piece in range(PIECES):
                hop(kind, piece).wait_send()

    events = {
        1: [lambda: far_step(1, 0)],
        2: [lambda: far_step(1, 1)],
        3: [lambda: near_step(1, 0)],
        4: [lambda: far_step(0, 0)],
        5: [lambda: near_step(1, 1), lambda: far_step(0, 1)],
        7: [lambda: near_step(0, 0), lambda: pair_step(0)],
        9: [lambda: near_step(0, 1), lambda: pair_step(1)],
    }

    def run(more):
        def step(i, carry):
            add_messages(i)
            for k in sorted(set(events) | set(more)):
                @pl.when(i == k)
                def _():
                    for event in events.get(k, []) + more.get(k, []):
                        event()

            return carry

        lax.fori_loop(0, len(ORDER), step, 0)
        for half in range(HALVES):
            last_step(half)

    return load, run, drain


def exchange_scratch(rows, width, devices):
    slab = width // devices * (rows // LANES)
    return [
        pltpu.VMEM((devices * slab, LANES), WIDE),
        pltpu.VMEM((devices * slab, LANES), LOW),
        pltpu.VMEM((devices, slab, LANES), LOW),
        pltpu.VMEM((slab, LANES), WIDE),
        pltpu.SemaphoreType.DMA((devices - 1,)),
        pltpu.SemaphoreType.DMA((devices - 1,)),
    ]


def exchange_moves(residual, out, refs):
    flat, packed, landed, opened, send_sems, recv_sems = refs
    subs = lax.axis_size("sub")
    devices = lax.axis_size("blk") * subs
    here = lax.axis_index("blk") * subs + lax.axis_index("sub")
    slab = landed.shape[1]
    channels = out.shape[0]
    parts = slab // channels
    nodes = parts * LANES

    def move(k):
        there = lax.rem(here + k, devices)
        return remote(
            packed.at[pl.ds(pl.multiple_of(there * slab, slab), slab)], landed.at[here],
            send_sems.at[k - 1], recv_sems.at[k - 1], (there // subs, lax.rem(there, subs)),
        )

    def start(values):
        lay_rows(flat, 0, values.T)

        def cast(i, block):
            packed[pl.ds(i, block), :] = flat[pl.ds(i, block), :].astype(LOW)

        in_pieces(flat.shape[0], cast)

        def send(k, carry):
            move(k).start()
            return carry

        lax.fori_loop(1, devices, send, 0)

    def open_slab(source, device):
        opened[...] = source.astype(WIDE)
        for j in range(parts):
            columns = pl.ds(pl.multiple_of(device * nodes + j * LANES, LANES), LANES)
            out[:, columns] = residual[:, columns] + opened[pl.ds(j, channels, stride=parts), :]

    def last():
        open_slab(packed[pl.ds(pl.multiple_of(here * slab, slab), slab), :], here)

        def take(k, carry):
            move(k).wait_recv()
            device = lax.rem(here - k + devices, devices)
            open_slab(landed[device], device)
            return carry

        lax.fori_loop(1, devices, take, 0)

        def sent(k, carry):
            move(k).wait_send()
            return carry

        lax.fori_loop(1, devices, sent, 0)

    return start, last


def finish_kernel(
    index, messages, edge_grads, node_grads, vectors, node_part, weight, residual,
    node_grad, one_out, two_out, three_out, four_out, reduced_vectors, total, reduced, out_sems, *refs,
):
    at = places()
    count = len(collect_scratch(64, 128, 64))
    load, run, drain = collect_moves(at, index, messages, total, refs[:count])
    load.start()
    meet_all()
    steps, refs = reducers(at, (edge_grads, node_grads), reduced, refs[count:])
    vector_steps = vector_reducer(at, vectors, reduced_vectors, refs[:4])
    exchange, receive = exchange_moves(residual, node_grad, refs[4:])
    steps[0]()
    vector_steps[0]()
    load.wait()
    run({
        1: [steps[1], vector_steps[1]],
        4: [steps[2], vector_steps[2]],
        7: [steps[3], vector_steps[3]],
        10: [steps[4]],
    })
    steps[5]()
    high, rest = split_low(total[...])
    exchange(node_part[...] + dot_right(high, weight[...]) + dot_right(rest, weight[...]))
    steps[6]()
    steps[7]()
    receive()
    steps[8]()
    width = total.shape[1]
    nodes_at = edge_grads.shape[0]
    copies = [
        pltpu.make_async_copy(reduced.at[pl.ds(first, target.shape[0])], target, out_sems.at[i])
        for i, (first, target) in enumerate((
            (0, one_out), (3 * width, two_out), (nodes_at, three_out), (nodes_at + 2 * width, four_out)
        ))
    ]
    for copy in copies:
        copy.start()
    vector_steps[4]()
    drain()
    steps[9]()
    for copy in copies:
        copy.wait()


def finish(index, messages, edge_grads, node_grads, vectors, node_part, weight, residual, collective):
    rows, width = node_part.shape
    edges = messages.shape[0]
    sources = [edge_grads.shape[0], node_grads.shape[0]]
    along = lax.axis_size("blk") // 2
    devices = lax.axis_size("blk") * lax.axis_size("sub")
    hold = pl.BlockSpec(memory_space=pltpu.VMEM)
    across = pl.BlockSpec(memory_space=pl.ANY)
    return pl.pallas_call(
        finish_kernel,
        grid=(1,),
        in_specs=[
            hold, across, across, across, hold, hold, pl.BlockSpec((width, width), lambda i: (2, 0)), hold,
        ],
        out_specs=[hold] + [across] * 4 + [hold],
        out_shape=[
            jax.ShapeDtypeStruct(residual.shape, WIDE),
            jax.ShapeDtypeStruct((3 * width, width), LOW),
            jax.ShapeDtypeStruct((width, width), LOW),
            jax.ShapeDtypeStruct((2 * width, width), LOW),
            jax.ShapeDtypeStruct((width, width), LOW),
            jax.ShapeDtypeStruct(vectors.shape, WIDE),
        ],
        scratch_shapes=[
            pltpu.VMEM((rows, width), WIDE),
            pltpu.VMEM((sum(sources), width), LOW),
            pltpu.SemaphoreType.DMA((4,)),
            *collect_scratch(rows, width, edges),
            *reducers_scratch(sources, width, along),
            *vector_scratch(vectors.shape, along),
            *exchange_scratch(rows, width, devices),
        ],
        compiler_params=pltpu.CompilerParams(
            collective_id=collective, has_side_effects=True, vmem_limit_bytes=VMEM_BYTES
        ),
        name="finish_sums",
    )(index.reshape(edges // LANES, LANES), messages, edge_grads, node_grads, vectors, node_part, weight, residual)


def middle_kernel(
    index, messages, node_low, upstream, w_one, b_one, w_two, b_two, gain, shift, residual,
    table, node_part, node_out, grads, vectors, total, sent, *refs
):
    at = places()
    count = len(collect_scratch(64, 128, 64))
    load, run, drain = collect_moves(at, index, messages, total, refs[:count])
    load.start()
    meet_all()
    refs = refs[count:]
    start, one, two, three, end = spread_moves(at, sent, table, *refs[:3])
    exchange, receive = exchange_moves(residual, node_out, refs[3:])
    load.wait()
    run({})

    width = total.shape[1]
    low = total[...].astype(LOW)
    pre = dot(node_low[...], w_one[:width]) + dot(low, w_one[width:]) + b_one[...]
    logistic = jax.nn.sigmoid(pre)
    act = (pre * logistic).astype(LOW)
    normal, scale = row_normal(dot(act, w_two[...]) + b_two[...])
    given = upstream[...].T
    scaled = given * gain[...]
    slope = jnp.mean(scaled * normal, -1, keepdims=True)
    fourth = scale * (scaled - jnp.mean(scaled, -1, keepdims=True) - normal * slope)
    fourth_low = fourth.astype(LOW)
    third = dot_right(fourth_low, w_two[...]) * (logistic * (1.0 + pre * (1.0 - logistic)))
    third_low = third.astype(LOW)
    sent[...] = dot_right(third_low, w_one[width:]).astype(LOW)
    start()
    grads[:width] = dot_left(node_low[...], third_low)
    grads[width : 2 * width] = dot_left(low, third_low)
    grads[2 * width : 3 * width] = dot_left(act, fourth_low)
    vectors[...] = jnp.zeros_like(vectors)
    vectors[4:5] = jnp.sum(third_low.astype(WIDE), 0, keepdims=True)
    vectors[5:6] = jnp.sum(fourth_low.astype(WIDE), 0, keepdims=True)
    vectors[6:7] = jnp.sum(given * normal, 0, keepdims=True)
    vectors[7:8] = jnp.sum(given, 0, keepdims=True)
    node_part[...] = dot_right(third_low, w_one[:width])
    exchange(normal * gain[...] + shift[...])

    for stage in (one, two, three):
        for piece in range(PIECES):
            stage(piece)
    receive()
    end()
    drain()


def middle(index, messages, node_low, upstream, w_one, b_one, w_two, b_two, gain, shift, residual, collective):
    rows, width = node_low.shape
    edges = messages.shape[0]
    devices = lax.axis_size("blk") * lax.axis_size("sub")
    grad_rows = padded_rows(3 * width)
    hold = pl.BlockSpec(memory_space=pltpu.VMEM)
    across = pl.BlockSpec(memory_space=pl.ANY)
    table, node_part, node_out, grads, vectors = pl.pallas_call(
        middle_kernel,
        in_specs=[hold, across] + [hold] * 9,
        out_specs=[across] + [hold] * 4,
        out_shape=[
            jax.ShapeDtypeStruct((3, 4, rows, width), LOW),
            jax.ShapeDtypeStruct((rows, width), WIDE),
            jax.ShapeDtypeStruct(residual.shape, WIDE),
            jax.ShapeDtypeStruct((grad_rows, width), WIDE),
            jax.ShapeDtypeStruct((8, width), WIDE),
        ],
        scratch_shapes=[
            pltpu.VMEM((rows, width), WIDE),
            pltpu.VMEM((rows, width), LOW),
            *collect_scratch(rows, width, edges),
            *spread_scratch(),
            *exchange_scratch(rows, width, devices),
        ],
        compiler_params=pltpu.CompilerParams(
            collective_id=collective, has_side_effects=True, vmem_limit_bytes=VMEM_BYTES
        ),
        name="middle_nodes",
    )(
        index.reshape(edges // LANES, LANES), messages, node_low, upstream,
        w_one, b_one, w_two, b_two, gain, shift, residual,
    )
    return table.reshape(12 * rows, width), node_part, node_out, grads, vectors


def scatter_scratch(channels, nodes, devices):
    slab = channels * (nodes // LANES)
    return [
        pltpu.VMEM((devices * slab, LANES), WIDE),
        pltpu.VMEM((devices * slab, LANES), LOW),
        pltpu.VMEM((devices, slab, LANES), LOW),
        pltpu.VMEM((slab, LANES), WIDE),
        pltpu.VMEM((nodes // LANES * devices * channels, LANES), WIDE),
        pltpu.SemaphoreType.DMA((devices - 1,)),
        pltpu.SemaphoreType.DMA((devices - 1,)),
    ]


def scatter_moves(shard, refs):
    flat, packed, landed, opened, square, send_sems, recv_sems = refs
    subs = lax.axis_size("sub")
    devices = lax.axis_size("blk") * subs
    here = lax.axis_index("blk") * subs + lax.axis_index("sub")
    slab = landed.shape[1]
    channels = shard.shape[0]
    parts = slab // channels
    nodes = parts * LANES

    def move(k):
        there = lax.rem(here + k, devices)
        return remote(
            packed.at[pl.ds(pl.multiple_of(there * slab, slab), slab)], landed.at[here],
            send_sems.at[k - 1], recv_sems.at[k - 1], (there // subs, lax.rem(there, subs)),
        )

    def start():
        def pack(k, carry):
            device = lax.rem(here + k, devices)
            rows = pl.ds(pl.multiple_of(device * slab, slab), slab)
            for j in range(parts):
                columns = pl.ds(pl.multiple_of(device * nodes + j * LANES, LANES), LANES)
                flat[pl.ds(device * slab + j, channels, stride=parts), :] = shard[:, columns]
            packed[rows, :] = flat[rows, :].astype(LOW)
            return carry

        def send(k, carry):
            pack(k, carry)
            move(k).start()
            return carry

        lax.fori_loop(1, devices, send, 0)
        pack(0, 0)

    def open_slab(source, device):
        opened[...] = source.astype(WIDE)
        for j in range(parts):
            rows = pl.ds(pl.multiple_of((j * devices + device) * channels, channels), channels)
            square[rows, :] = opened[pl.ds(j, channels, stride=parts), :]

    def last(rows):
        open_slab(packed[pl.ds(pl.multiple_of(here * slab, slab), slab), :], here)

        def take(k, carry):
            move(k).wait_recv()
            device = lax.rem(here - k + devices, devices)
            open_slab(landed[device], device)
            return carry

        lax.fori_loop(1, devices, take, 0)
        width = devices * channels
        for j in range(parts):
            rows[j * LANES : (j + 1) * LANES, :] = square[j * width : (j + 1) * width, :].T.astype(LOW)

    def drain():
        def sent(k, carry):
            move(k).wait_send()
            return carry

        lax.fori_loop(1, devices, sent, 0)

    return start, last, drain


def begin_kernel(
    shard, later, senders, receivers, own, table, later_out, send_local, recv_wide, held, held_sem, slab_sems, *refs
):
    at = places()
    fetch = pltpu.make_async_copy(later, held, held_sem)
    fetch.start()
    meet_all()
    start, last, drain = scatter_moves(shard, refs[3:])
    start()
    last(own)
    begin, one, two, three, end = spread_moves(at, own, table, *refs[:3])
    begin()
    rows = own.shape[0]
    groups, subs = lax.axis_size("blk"), lax.axis_size("sub")
    send_local[...] = senders[...] - (at["group"] * subs + at["sub"]) * rows
    relative = lax.rem(receivers[...] // (rows * subs) - at["group"] + 1 + groups, groups)
    recv_wide[...] = relative * (rows * subs) + lax.rem(receivers[...], rows * subs)
    fetch.wait()
    devices, _, nodes = later_out.shape

    def slab(k):
        columns = pl.ds(pl.multiple_of(k * nodes, LANES), nodes)
        return pltpu.make_async_copy(held.at[:, columns], later_out.at[k], slab_sems.at[k])

    def give(k, carry):
        slab(k).start()
        return carry

    def given(k, carry):
        slab(k).wait()
        return carry

    lax.fori_loop(0, devices, give, 0)
    drain()
    for stage in (one, two, three):
        for piece in range(PIECES):
            stage(piece)
    lax.fori_loop(0, devices, given, 0)
    end()


def begin(shard, later, senders, receivers, rows, collective):
    channels, nodes = shard.shape
    devices = lax.axis_size("blk") * lax.axis_size("sub")
    width = channels * devices
    hold = pl.BlockSpec(memory_space=pltpu.VMEM)
    across = pl.BlockSpec(memory_space=pl.ANY)
    lines = (senders.shape[0] // LANES, LANES)
    own, table, later, send_local, recv_wide = pl.pallas_call(
        begin_kernel,
        in_specs=[hold, across, hold, hold],
        out_specs=[hold, across, across, hold, hold],
        out_shape=[
            jax.ShapeDtypeStruct((rows, width), LOW),
            jax.ShapeDtypeStruct((3, 4, rows, width), LOW),
            jax.ShapeDtypeStruct((devices, channels, rows), later.dtype),
            jax.ShapeDtypeStruct(lines, jnp.int32),
            jax.ShapeDtypeStruct(lines, jnp.int32),
        ],
        scratch_shapes=[
            pltpu.VMEM(later.shape, later.dtype),
            pltpu.SemaphoreType.DMA,
            pltpu.SemaphoreType.DMA((devices,)),
            *spread_scratch(),
            *scatter_scratch(channels, rows, devices),
        ],
        compiler_params=pltpu.CompilerParams(
            collective_id=collective, has_side_effects=True, vmem_limit_bytes=VMEM_BYTES
        ),
        name="begin_rows",
    )(shard, later, senders.reshape(lines), receivers.reshape(lines))
    return own, table.reshape(12 * rows, width), later, send_local, recv_wide


def release_kernel(count, *refs):
    for source, target in zip(refs[:count], refs[count:]):
        target[...] = source[...].astype(target.dtype)


def release(whole, reduced):
    arrays = [*whole, *reduced]
    steps = 4

    def spec(item, kept):
        rows, columns = item.shape
        if kept:
            return pl.BlockSpec((rows, columns // steps), lambda i: (0, i))
        return pl.BlockSpec((rows // steps, columns), lambda i: (i, 0))

    specs = [spec(item, i < len(whole)) for i, item in enumerate(arrays)]
    return pl.pallas_call(
        functools.partial(release_kernel, len(arrays)),
        grid=(steps,),
        in_specs=specs,
        out_specs=specs,
        out_shape=[jax.ShapeDtypeStruct(item.shape, WIDE) for item in arrays],
        compiler_params=pltpu.CompilerParams(vmem_limit_bytes=VMEM_BYTES),
        name="release_results",
    )(*arrays)


def shards(
    node_input,
    edge_input,
    senders,
    receivers,
    edge_count,
    edge_w_one,
    edge_b_one,
    edge_w_two,
    edge_b_two,
    edge_gain,
    edge_shift,
    node_w_one,
    node_b_one,
    node_w_two,
    node_b_two,
    node_gain,
    node_shift,
    node_cotangent,
    edge_cotangent,
):
    groups = lax.axis_size("blk")
    sub_count = lax.axis_size("sub")
    width = edge_input.shape[1]
    per_device = node_input.shape[1] // (groups * sub_count)
    node_low, wide_low, cotangent_later, send_local, recv_wide = begin(
        node_input, node_cotangent, senders, receivers, per_device, 0
    )
    node_upstream = lax.all_to_all(
        cotangent_later, ("blk", "sub"), split_axis=0, concat_axis=0, tiled=True
    ).reshape(width, per_device)
    recv_list = recv_wide.reshape(-1)
    edge_result, first_pre, second_pre, received, messages = edge_forward(
        edge_count, recv_list, send_local, edge_input, wide_low, node_low,
        edge_w_one, edge_b_one[None], edge_w_two, edge_b_two[None], edge_gain[None], edge_shift[None],
    )
    wide_grad, node_part, node_out, node_grads, node_vectors = middle(
        recv_list, messages, node_low, node_upstream, node_w_one, node_b_one[None], node_w_two, node_b_two[None],
        node_gain[None], node_shift[None], node_input, 1,
    )
    edge_grad, messages, edge_grads, vectors, node_part = edge_backward(
        edge_count, recv_list, send_local, edge_cotangent, edge_input, received, first_pre, second_pre,
        wide_grad, node_part, node_vectors, node_low, edge_w_one, edge_w_two, edge_gain[None],
    )
    node_grad, *summed, vectors = finish(
        recv_list, messages, edge_grads, node_grads, vectors, node_part, edge_w_one, node_cotangent, 3
    )
    node_out, node_grad, *summed = release((node_out, node_grad), summed)
    return (
        node_out,
        edge_result,
        node_grad,
        edge_grad,
        summed[0],
        vectors[0],
        summed[1],
        vectors[1],
        vectors[2],
        vectors[3],
        summed[2],
        vectors[4],
        summed[3],
        vectors[5],
        vectors[6],
        vectors[7],
    )


def solution(mesh):
    placed = (
        P(("blk", "sub"), None),
        P(("blk", "sub"), None),
        P(("blk", "sub")),
        P(("blk", "sub")),
        P(("blk", "sub")),
        P(),
        P(),
        P(),
        P(),
        P(),
        P(),
        P(),
        P(),
        P(),
        P(),
        P(),
        P(),
        P(("blk", "sub"), None),
        P(("blk", "sub"), None),
    )
    return jax.shard_map(
        shards,
        mesh=mesh,
        in_specs=placed,
        out_specs=(
            P(("blk", "sub"), None),
            P(("blk", "sub"), None),
            P(("blk", "sub"), None),
            P(("blk", "sub"), None),
            P(),
            P(),
            P(),
            P(),
            P(),
            P(),
            P(),
            P(),
            P(),
            P(),
            P(),
            P(),
        ),
        check_vma=False,
    )
```

```python
import functools
import math

import jax
import jax.numpy as jnp
from jax import lax
from jax.experimental import pallas as pl
from jax.experimental.pallas import tpu as pltpu
from jax.sharding import PartitionSpec as P

EPSILON = 1e-05


TILE = 512
CHUNK = 512
LANES = 128
VMEM_BYTES = 60 * 2**20


def dot(left, right):
    return jnp.dot(left, right, preferred_element_type=jnp.float32)


def dot_left(left, right):
    return lax.dot_general(
        left, right, (((0,), (0,)), ((), ())), preferred_element_type=jnp.float32
    )


def dot_right(left, right):
    return lax.dot_general(
        left, right, (((1,), (1,)), ((), ())), preferred_element_type=jnp.float32
    )


def split_low(values):
    high = values.astype(jnp.bfloat16)
    return high, (values - high.astype(jnp.float32)).astype(jnp.bfloat16)


def lay_rows(target, start, values):
    count, width = values.shape
    parts = width // LANES
    for j in range(parts):
        target[pl.ds(start * parts + j, count, stride=parts), :] = values[:, j * LANES : (j + 1) * LANES]


def read_rows(source, start, count, parts):
    return jnp.concatenate(
        [source[pl.ds(start * parts + j, count, stride=parts), :] for j in range(parts)], axis=1
    )


def load_table(wide, table, stage, sems):
    steps = wide.shape[0] // CHUNK

    def fetch(i, slot):
        return pltpu.make_async_copy(wide.at[pl.ds(i * CHUNK, CHUNK)], stage.at[slot], sems.at[slot])

    for i in range(3):
        fetch(i, i).start()

    def body(i, carry):
        slot = lax.rem(i, 4)

        @pl.when(i + 3 < steps)
        def _():
            fetch(i + 3, lax.rem(i + 3, 4)).start()

        fetch(i, slot).wait()

        def piece(k, carry):
            values = stage[slot, pl.ds(k * 64, 64), :].astype(jnp.float32)
            lay_rows(table, i * CHUNK + k * 64, values)
            return carry

        return lax.fori_loop(0, CHUNK // 64, piece, carry)

    lax.fori_loop(0, steps, body, 0)


def gather_rows(index, base, table, rows, parts):
    count = rows.shape[0] // parts

    def body(i, carry):
        for u in range(16):
            slot = i * 16 + u
            place = index[base + slot]
            rows[pl.ds(pl.multiple_of(slot * parts, parts), parts), :] = table[
                pl.ds(pl.multiple_of(place * parts, parts), parts), :
            ]
        return carry

    lax.fori_loop(0, count // 16, body, 0)


def gather_inline(index, base, table, rows, parts):
    for slot in range(rows.shape[0] // parts):
        place = index[base + slot]
        rows[slot * parts : (slot + 1) * parts, :] = table[pl.ds(pl.multiple_of(place * parts, parts), parts), :]


def row_normal(values):
    average = jnp.mean(values, -1, keepdims=True)
    centred = values - average
    variance = jnp.mean(centred * centred, -1, keepdims=True)
    scale = lax.rsqrt(variance + EPSILON)
    return centred * scale, scale


def forward_kernel(
    count, recv, send, edge, wide, nodes, w_one, b_one, w_two, b_two, gain, shift,
    result, first, second, received, message,
    table, rows, stage, sems,
):
    step = pl.program_id(0)
    base = step * TILE
    width = nodes.shape[1]
    parts = width // LANES

    @pl.when(step == 0)
    def _():
        load_table(wide, table, stage, sems)
        gather_rows(recv, base, table, rows, parts)

    later = jnp.where(step + 1 < pl.num_programs(0), base + TILE, 0)
    received[...] = read_rows(rows, 0, TILE, parts).astype(jnp.bfloat16)
    gather_inline(recv, later, table, rows, parts)
    from_recv = received[...]
    lane = lax.broadcasted_iota(jnp.int32, (LANES, LANES), 1)
    chosen = []
    for i in range(TILE // LANES):
        column = jnp.broadcast_to(send[pl.ds(step * (TILE // LANES) + i, 1), :], (LANES, LANES)).T
        chosen.append(
            jnp.concatenate(
                [
                    jnp.where(column == lane + j * LANES, 1.0, 0.0).astype(jnp.bfloat16)
                    for j in range(nodes.shape[0] // LANES)
                ],
                axis=1,
            )
        )
    chosen = jnp.concatenate(chosen, axis=0)
    from_send = dot(chosen, nodes[...]).astype(jnp.bfloat16)
    pre = (
        dot(edge[...], w_one[:width])
        + dot(from_send, w_one[width : 2 * width])
        + dot(from_recv, w_one[2 * width :])
        + b_one[...]
    )
    first[...] = pre
    act = (pre * jax.nn.sigmoid(pre)).astype(jnp.bfloat16)
    post = dot(act, w_two[...]) + b_two[...]
    second[...] = post
    normal, _ = row_normal(post)
    branch = normal * gain[...] + shift[...]
    live = base + lax.broadcasted_iota(jnp.int32, (TILE, 1), 0) < count[0]
    outcome = edge[...].astype(jnp.float32) + jnp.where(live, branch, 0.0)
    result[...] = outcome
    message[...] = jnp.where(live, outcome, 0.0).astype(jnp.bfloat16)


def edge_forward(count, recv, send, edge, wide, nodes, w_one, b_one, w_two, b_two, gain, shift):
    edges, width = edge.shape
    steps = edges // TILE
    parts = width // LANES
    hold = pl.BlockSpec(memory_space=pltpu.VMEM)
    scalar = pl.BlockSpec(memory_space=pltpu.SMEM)
    tile = pl.BlockSpec((TILE, width), lambda i: (i, 0))
    return pl.pallas_call(
        forward_kernel,
        grid=(steps,),
        in_specs=[
            scalar, scalar, hold, tile,
            pl.BlockSpec(memory_space=pl.ANY), hold, hold, hold, hold, hold, hold, hold,
        ],
        out_specs=[tile] * 5,
        out_shape=[
            jax.ShapeDtypeStruct((edges, width), jnp.float32),
            jax.ShapeDtypeStruct((edges, width), jnp.float32),
            jax.ShapeDtypeStruct((edges, width), jnp.float32),
            jax.ShapeDtypeStruct((edges, width), jnp.bfloat16),
            jax.ShapeDtypeStruct((edges, width), jnp.bfloat16),
        ],
        scratch_shapes=[
            pltpu.VMEM((wide.shape[0] * parts, LANES), jnp.float32),
            pltpu.VMEM((TILE * parts, LANES), jnp.float32),
            pltpu.VMEM((4, CHUNK, width), jnp.bfloat16),
            pltpu.SemaphoreType.DMA((4,)),
        ],
        compiler_params=pltpu.CompilerParams(vmem_limit_bytes=VMEM_BYTES),
        cost_estimate=pl.CostEstimate(
            flops=20 * edges * width * width, bytes_accessed=40 * edges * width, transcendentals=2 * edges * width
        ),
        name="edge_forward",
    )(count, recv, send, edge, wide, nodes, w_one, b_one, w_two, b_two, gain, shift)


def backward_kernel(
    count, recv, send, cotangent, edge, received, first, second, wide, node_part, node_vectors, nodes, w_one, w_two, gain,
    grad, message, all_grads, vectors, sender_grad,
    table, rows, stage, sems, by_sender, grads, give_sem,
):
    step = pl.program_id(0)
    base = step * TILE
    width = nodes.shape[1]
    parts = width // LANES

    @pl.when(step == 0)
    def _():
        load_table(wide, table, stage, sems)
        grads[...] = jnp.zeros_like(grads)
        vectors[...] = node_vectors[...]
        by_sender[...] = jnp.zeros_like(by_sender)
        gather_rows(recv, base, table, rows, parts)

    live = base + lax.broadcasted_iota(jnp.int32, (TILE, 1), 0) < count[0]
    upstream = cotangent[...].astype(jnp.float32) + jnp.where(live, read_rows(rows, 0, TILE, parts), 0.0)
    grad[...] = upstream
    later = jnp.where(step + 1 < pl.num_programs(0), base + TILE, 0)
    gather_inline(recv, later, table, rows, parts)
    masked = jnp.where(live, upstream, 0.0)
    normal, scale = row_normal(second[...])
    vectors[2:3, :] += jnp.sum(masked * normal, 0, keepdims=True)
    vectors[3:4, :] += jnp.sum(masked, 0, keepdims=True)
    scaled = masked * gain[...]
    slope = jnp.mean(scaled * normal, -1, keepdims=True)
    grad_second = scale * (scaled - jnp.mean(scaled, -1, keepdims=True) - normal * slope)
    second_low = grad_second.astype(jnp.bfloat16)
    vectors[1:2, :] += jnp.sum(second_low.astype(jnp.float32), 0, keepdims=True)
    pre = first[...]
    logistic = jax.nn.sigmoid(pre)
    act = (pre * logistic).astype(jnp.bfloat16)
    grads[3 * width : 4 * width] += dot_left(act, second_low)
    grad_first = dot_right(second_low, w_two[...]) * (logistic * (1.0 + pre * (1.0 - logistic)))
    first_low = grad_first.astype(jnp.bfloat16)
    message[...] = first_low
    vectors[0:1, :] += jnp.sum(first_low.astype(jnp.float32), 0, keepdims=True)
    grads[:width] += dot_left(edge[...], first_low)
    grads[2 * width : 3 * width] += dot_left(received[...], first_low)
    node = lax.broadcasted_iota(jnp.int32, (nodes.shape[0], LANES), 0)
    chosen = jnp.concatenate(
        [
            jnp.where(node == send[pl.ds(step * (TILE // LANES) + i, 1), :], 1.0, 0.0).astype(jnp.bfloat16)
            for i in range(TILE // LANES)
        ],
        axis=1,
    )
    by_sender[...] += dot(chosen, first_low)
    grad[...] += dot_right(first_low, w_one[:width])

    @pl.when(step == pl.num_programs(0) - 1)
    def _():
        high, rest = split_low(by_sender[...])
        grads[width : 2 * width] = dot_left(nodes[...], high) + dot_left(nodes[...], rest)
        give = pltpu.make_async_copy(grads, all_grads, give_sem)
        give.start()
        middle = w_one[width : 2 * width]
        sender_grad[...] = node_part[...] + dot_right(high, middle) + dot_right(rest, middle)
        give.wait()


def edge_backward(
    count, recv, send, cotangent, edge, received, first, second, wide, node_part, node_vectors, nodes,
    w_one, w_two, gain,
):
    edges, width = edge.shape
    steps = edges // TILE
    parts = width // LANES
    per_device = nodes.shape[0]
    hold = pl.BlockSpec(memory_space=pltpu.VMEM)
    scalar = pl.BlockSpec(memory_space=pltpu.SMEM)
    tile = pl.BlockSpec((TILE, width), lambda i: (i, 0))

    across = pl.BlockSpec(memory_space=pl.ANY)

    def whole(rows):
        return pl.BlockSpec((rows, width), lambda i: (0, 0))

    return pl.pallas_call(
        backward_kernel,
        grid=(steps,),
        in_specs=[
            scalar, scalar, hold, tile, tile, tile, tile, tile,
            across, hold, hold, hold, hold, hold, hold,
        ],
        out_specs=[
            tile, tile, across, whole(8), whole(per_device),
        ],
        out_shape=[
            jax.ShapeDtypeStruct((edges, width), jnp.float32),
            jax.ShapeDtypeStruct((edges, width), jnp.bfloat16),
            jax.ShapeDtypeStruct((4 * width, width), jnp.float32),
            jax.ShapeDtypeStruct((8, width), jnp.float32),
            jax.ShapeDtypeStruct((per_device, width), jnp.float32),
        ],
        scratch_shapes=[
            pltpu.VMEM((wide.shape[0] * parts, LANES), jnp.float32),
            pltpu.VMEM((TILE * parts, LANES), jnp.float32),
            pltpu.VMEM((4, CHUNK, width), jnp.bfloat16),
            pltpu.SemaphoreType.DMA((4,)),
            pltpu.VMEM((per_device, width), jnp.float32),
            pltpu.VMEM((4 * width, width), jnp.float32),
            pltpu.SemaphoreType.DMA,
        ],
        compiler_params=pltpu.CompilerParams(vmem_limit_bytes=VMEM_BYTES),
        cost_estimate=pl.CostEstimate(
            flops=24 * edges * width * width, bytes_accessed=40 * edges * width, transcendentals=2 * edges * width
        ),
        name="edge_backward",
    )(
        count, recv, send, cotangent, edge, received, first, second, wide,
        node_part, node_vectors, nodes, w_one, w_two, gain,
    )


MESH = pl.DeviceIdType.MESH
PIECES = 4
SPLIT = True
LOW = jnp.bfloat16
WIDE = jnp.float32


def places():
    groups = lax.axis_size("blk")
    group, sub = lax.axis_index("blk"), lax.axis_index("sub")
    odd = lax.rem(group, 2)
    along = groups // 2
    spot = group // 2
    beside = group + 1 - 2 * odd
    return dict(
        group=group,
        sub=sub,
        core=lax.rem(sub, 2),
        chip=sub // 2,
        odd=odd,
        spot=spot,
        along=along,
        sibling=sub + 1 - 2 * lax.rem(sub, 2),
        partner=lax.rem(sub + 2, 4),
        to_sibling=(group, sub + 1 - 2 * lax.rem(sub, 2)),
        to_partner=(group, lax.rem(sub + 2, 4)),
        to_beside=(beside, sub),
        to_onward=(lax.rem(group + 2 - 4 * odd + groups, groups), sub),
        to_source=(lax.rem(group - 2 + 4 * odd + groups, groups), sub),
        peers=[(2 * lax.rem(spot + k, along) + odd, sub) for k in range(1, along)],
        near=2 - 2 * odd,
        far=2 * odd,
    )


def meet(senders):
    barrier = pltpu.get_barrier_semaphore()
    for device in senders:
        pl.semaphore_signal(barrier, inc=1, device_id=device, device_id_type=MESH)
    pl.semaphore_wait(barrier, len(senders))


def meet_all():
    barrier = pltpu.get_barrier_semaphore()
    subs = lax.axis_size("sub")
    devices = lax.axis_size("blk") * subs
    here = lax.axis_index("blk") * subs + lax.axis_index("sub")

    def greet(k, carry):
        there = lax.rem(here + k, devices)
        pl.semaphore_signal(barrier, inc=1, device_id=(there // subs, lax.rem(there, subs)), device_id_type=MESH)
        return carry

    lax.fori_loop(1, devices, greet, 0)
    pl.semaphore_wait(barrier, devices - 1)


def remote(source, target, send, recv, device):
    return pltpu.make_async_remote_copy(
        src_ref=source, dst_ref=target, send_sem=send, recv_sem=recv, device_id=device, device_id_type=MESH
    )


def in_pieces(count, body):
    block = math.gcd(count, 128)

    def run(i, carry):
        body(pl.multiple_of(i * block, block), block)
        return carry

    lax.fori_loop(0, count // block, run, 0)


def padded_rows(rows):
    unit = 64 * lax.axis_size("blk")
    return -(-rows // unit) * unit


def streams_of(sources):
    unit = 64 * lax.axis_size("blk")
    streams = []
    for i, rows in enumerate(sources):
        first = -(-(rows // unit) // 2) * unit if SPLIT else rows
        streams.append((i, 0, first))
        if first < rows:
            streams.append((i, first, rows - first))
    return streams


def reducers_scratch(sources, width, along):
    return [ref for _, _, rows in streams_of(sources) for ref in reducer_scratch(rows, width, along)]


def reducers(at, sources, reduced, refs):
    made = []
    for i, (which, start, rows) in enumerate(streams_of([source.shape[0] for source in sources])):
        first = start + sum(source.shape[0] for source in sources[:which])
        made.append(reducer(at, sources[which], start, reduced, first, rows, i % 2 > 0, refs[i * 13 : i * 13 + 13]))
    return made, refs[len(made) * 13 :]


def reducer_scratch(rows, width, along):
    return [
        pltpu.VMEM((rows // 2, width), WIDE),
        pltpu.VMEM((rows // 2, width), WIDE),
        pltpu.VMEM((rows // 4, width), LOW),
        pltpu.VMEM((rows // 4, width), LOW),
        pltpu.VMEM((rows // 8, width), LOW),
        pltpu.VMEM((rows // 8, width), LOW),
        pltpu.VMEM((rows // 8, width), LOW),
        pltpu.VMEM((along - 1, rows // 8 // along, width), LOW),
        pltpu.SemaphoreType.DMA,
        pltpu.SemaphoreType.DMA((6,)),
        pltpu.SemaphoreType.DMA((6,)),
        pltpu.SemaphoreType.DMA((2, along - 1)),
        pltpu.SemaphoreType.DMA((2, along - 1)),
    ]


def reducer(at, grads, source_first, reduced, first, rows, swap, refs):
    (
        half, half_in, cross_out, cross_in, side_out, side_in, ring_out, ring_in,
        load_sem, step_send, step_recv, ring_send, ring_recv,
    ) = refs
    along, peers = at["along"], at["peers"]
    turns = [(at["chip"], at["to_partner"]), (at["odd"], at["to_beside"])]
    (bit_one, device_one), (bit_two, device_two) = turns[::-1] if swap else turns
    core, spot = at["core"], at["spot"]
    n_half, n_cross, n_side, n_ring = rows // 2, rows // 4, rows // 8, rows // 8 // along
    at_half = first + core * n_half
    at_cross = at_half + bit_one * n_cross
    at_side = at_cross + bit_two * n_side
    at_ring = at_side + spot * n_ring

    def span(start, count):
        return pl.ds(pl.multiple_of(start, 16), count)

    def step(kind):
        if kind == 0:
            other = span(source_first + (1 - core) * n_half, n_half)
            source, target, device = grads.at[other], half_in, at["to_sibling"]
        elif kind == 1:
            source, target, device = cross_out, cross_in, device_one
        elif kind == 2:
            source, target, device = side_out, side_in, device_two
        else:
            start, count, device = {
                3: (at_side, n_side, device_two),
                4: (at_cross, n_cross, device_one),
                5: (at_half, n_half, at["to_sibling"]),
            }[kind]
            source = target = reduced.at[span(start, count)]
        return remote(source, target, step_send.at[kind], step_recv.at[kind], device)

    def ring(kind, k):
        if kind == 0:
            source = ring_out.at[span(lax.rem(spot + k, along) * n_ring, n_ring)]
            target = ring_in.at[k - 1]
        else:
            source = target = reduced.at[span(at_ring, n_ring)]
        return remote(source, target, ring_send.at[kind, k - 1], ring_recv.at[kind, k - 1], peers[k - 1])

    load = pltpu.make_async_copy(grads.at[span(source_first + core * n_half, n_half)], half, load_sem)

    def start():
        step(0).start()
        load.start()

    def add_half():
        load.wait()
        step(0).wait_recv()
        other = (1 - bit_one) * n_cross

        def part(i, block):
            here = pl.ds(pl.multiple_of(other + i, block), block)
            cross_out[pl.ds(i, block), :] = (half[here, :] + half_in[here, :]).astype(LOW)

        in_pieces(n_cross, part)
        step(1).start()

    def add_cross():
        mine, other = bit_one * n_cross, (1 - bit_two) * n_side
        step(1).wait_recv()

        def part(i, block):
            there = pl.ds(pl.multiple_of(other + i, block), block)
            here = pl.ds(pl.multiple_of(mine + other + i, block), block)
            side_out[pl.ds(i, block), :] = (half[here, :] + half_in[here, :] + cross_in[there, :].astype(WIDE)).astype(LOW)

        in_pieces(n_side, part)
        step(2).start()

    def add_side():
        mine, kept = bit_one * n_cross, bit_two * n_side
        step(2).wait_recv()

        def part(i, block):
            there = pl.ds(pl.multiple_of(kept + i, block), block)
            here = pl.ds(pl.multiple_of(mine + kept + i, block), block)
            flat = pl.ds(i, block)
            value = half[here, :] + half_in[here, :] + cross_in[there, :].astype(WIDE) + side_in[flat, :].astype(WIDE)
            half[here, :] = value
            ring_out[flat, :] = value.astype(LOW)

        in_pieces(n_side, part)
        for k in range(1, along):
            ring(0, k).start()

    def add_ring():
        value = half[span(bit_one * n_cross + bit_two * n_side + spot * n_ring, n_ring), :]
        for k in range(1, along):
            ring(0, k).wait_recv()
            value = value + ring_in[k - 1].astype(WIDE)
        reduced[span(at_ring, n_ring), :] = value.astype(LOW)
        for k in range(1, along):
            ring(1, k).start()

    def share_side():
        for k in range(1, along):
            ring(1, k).wait_recv()
        step(3).start()

    def share_cross():
        step(3).wait_recv()
        step(4).start()

    def share_half():
        step(4).wait_recv()
        step(5).start()

    def last():
        step(5).wait_recv()

    def drain():
        for kind in range(6):
            step(kind).wait_send()
        for k in range(1, along):
            ring(0, k).wait_send()
            ring(1, k).wait_send()

    return [start, add_half, add_cross, add_side, add_ring, share_side, share_cross, share_half, last, drain]


def vector_scratch(shape, along):
    return [
        pltpu.VMEM((4, *shape), WIDE),
        pltpu.VMEM((2 + along, *shape), WIDE),
        pltpu.SemaphoreType.DMA((2 + along,)),
        pltpu.SemaphoreType.DMA((2 + along,)),
    ]


def vector_reducer(at, vectors, reduced, refs):
    held, held_in, send_sems, recv_sems = refs
    along = at["along"]
    devices = (at["to_sibling"], at["to_partner"], at["to_beside"], *at["peers"])

    def move(kind):
        return remote(held.at[min(kind, 3)], held_in.at[kind], send_sems.at[kind], recv_sems.at[kind], devices[kind])

    def start():
        held[0] = vectors[...]
        move(0).start()

    def turn(kind):
        def run():
            move(kind).wait_recv()
            held[kind + 1] = held[kind] + held_in[kind]
            for k in range(kind + 1, kind + 2 if kind < 2 else 2 + along):
                move(k).start()

        return run

    def last():
        value = held[3]
        for k in range(3, 2 + along):
            move(k).wait_recv()
            value = value + held_in[k]
        reduced[...] = value
        for k in range(2 + along):
            move(k).wait_send()

    return [start, turn(0), turn(1), turn(2), last]


def spread_moves(at, own, table, keep_sem, send_sems, recv_sems):
    sub, partner, near, far = at["sub"], at["partner"], at["near"], at["far"]
    to_sibling, to_partner, to_beside, to_onward = (
        at["to_sibling"], at["to_partner"], at["to_beside"], at["to_onward"]
    )
    size = own.shape[0] // PIECES

    def move(kind, piece):
        source, slot, device = {
            0: (None, (1, sub), to_partner),
            1: (None, (far, sub), to_beside),
            2: (None, (1, sub), to_sibling),
            3: ((1, partner), (far, partner), to_beside),
            4: ((1, partner), (1, partner), to_sibling),
            5: ((near, sub), (far, sub), to_onward),
            6: ((near, sub), (near, sub), to_sibling),
            7: ((near, partner), (far, partner), to_onward),
            8: ((near, partner), (near, partner), to_sibling),
            9: ((far, sub), (far, sub), to_sibling),
            10: ((far, partner), (far, partner), to_sibling),
            11: ((near, sub), (near, sub), to_partner),
            12: ((far, sub), (far, sub), to_partner),
        }[kind]
        source = own if source is None else table.at[source[0], source[1]]
        rows = pl.ds(piece * size, size)
        return remote(
            source.at[rows], table.at[slot[0], slot[1], rows],
            send_sems.at[kind, piece], recv_sems.at[kind, piece], device,
        )

    keep = pltpu.make_async_copy(own, table.at[1, sub], keep_sem)

    def start():
        for piece in range(PIECES):
            for kind in (0, 1, 2):
                move(kind, piece).start()
        keep.start()

    def relay(arrived, kinds, piece):
        move(arrived, piece).wait_recv()
        for kind in kinds:
            move(kind, piece).start()

    straight = range(PIECES - 1)

    def one(piece):
        relay(0, (3, 4) if piece in straight else (4,), piece)
        relay(1, (5, 6) if piece in straight else (5, 6, 11), piece)

    def two(piece):
        if piece in straight:
            relay(3, (7, 8), piece)
            relay(5, (9,), piece)
        else:
            relay(5, (9, 12), piece)
            relay(11, (8,), piece)

    def three(piece):
        if piece in straight:
            relay(7, (10,), piece)
        else:
            relay(12, (10,), piece)

    def drain():
        for kind in range(13):
            for piece in range(PIECES):
                if kind in ((11, 12) if piece in straight else (3, 7)):
                    continue
                if kind in (2, 4, 6, 8, 9, 10):
                    move(kind, piece).wait_recv()
                move(kind, piece).wait_send()
        keep.wait()

    return start, one, two, three, drain


def spread_scratch():
    return [
        pltpu.SemaphoreType.DMA,
        pltpu.SemaphoreType.DMA((13, PIECES)),
        pltpu.SemaphoreType.DMA((13, PIECES)),
    ]


HALVES = 2
ORDER = (
    (0, 1, 0), (0, 1, 1), (1, 1, 0), (0, 0, 0), (1, 1, 1), (0, 0, 1),
    (1, 0, 0), (2, 1, 0), (1, 0, 1), (2, 1, 1), (2, 0, 0), (2, 0, 1),
)


def collect_scratch(rows, width, edges):
    return [
        pltpu.VMEM((edges, width), LOW),
        pltpu.VMEM((2, 3, 2, rows, width), WIDE),
        pltpu.VMEM((3, 2, rows, width), WIDE),
        pltpu.VMEM((2, rows, width), LOW),
        pltpu.VMEM((2, rows, width), LOW),
        pltpu.VMEM((2, rows, width), LOW),
        pltpu.VMEM((2, rows, width), LOW),
        pltpu.VMEM((rows, width), LOW),
        pltpu.VMEM((rows, width), LOW),
        pltpu.SemaphoreType.DMA,
        pltpu.SemaphoreType.DMA((3, 2, HALVES)),
        pltpu.SemaphoreType.DMA((3, 2, HALVES)),
        pltpu.SemaphoreType.DMA((5, PIECES)),
        pltpu.SemaphoreType.DMA((5, PIECES)),
    ]


def collect_moves(at, index, messages, out, refs):
    (
        held, parts, landed, far_out, far_in, near_out, near_in, pair_out, pair_in,
        load_sem, give_sems, take_sems, send_sems, recv_sems,
    ) = refs
    sub, partner, sibling = at["sub"], at["partner"], at["sibling"]
    rows = out.shape[0]
    size = rows // PIECES
    part_rows = rows // HALVES
    load = pltpu.make_async_copy(messages, held, load_sem)

    def piece_of(ref, piece):
        return ref.at[pl.ds(piece * size, size)]

    def give(role, side, half):
        span = pl.ds(pl.multiple_of(half * part_rows, part_rows), part_rows)
        return remote(
            parts.at[0, role, side, span], landed.at[role, side, span],
            give_sems.at[role, side, half], take_sems.at[role, side, half], at["to_sibling"],
        )

    def hop(kind, piece):
        source, target, device = {
            0: (far_out.at[0], far_in.at[0], at["to_source"]),
            1: (far_out.at[1], far_in.at[1], at["to_source"]),
            2: (near_out.at[0], near_in.at[0], at["to_beside"]),
            3: (near_out.at[1], near_in.at[1], at["to_beside"]),
            4: (pair_out, pair_in, at["to_partner"]),
        }[kind]
        return remote(
            piece_of(source, piece), piece_of(target, piece),
            send_sems.at[kind, piece], recv_sems.at[kind, piece], device,
        )

    def add_messages(step):
        def pick(column):
            return lax.rem(sum(int(item[column]) << (2 * i) for i, item in enumerate(ORDER)) >> (2 * step), 4)

        role, side, half = pick(0), pick(1), pick(2)
        relation = jnp.where(role == 0, at["far"], jnp.where(role == 1, at["near"], 1))
        span = pl.ds(pl.multiple_of(half * part_rows, part_rows), part_rows)

        def whose(w, carry):
            first = jnp.where(w == 0, sibling, sub)
            target = lax.rem(first + 2 * side, 4)
            base = (relation * 4 + target) * rows + half * part_rows
            node = lax.broadcasted_iota(jnp.int32, (part_rows, LANES), 0) + base
            chosen = jnp.concatenate(
                [jnp.where(node == index[j : j + 1, :], 1.0, 0.0).astype(LOW) for j in range(index.shape[0])], axis=1
            )
            parts[w, role, side, span, :] = dot(chosen, held[...])
            return carry

        lax.fori_loop(0, 2, whose, 0)
        give(role, side, half).start()

    def local(role, side, piece):
        span = pl.ds(piece * size, size)
        return parts[1, role, side, span, :] + landed[role, side, span, :]

    def arrived(kind, ref, piece):
        hop(kind, piece).wait_recv()
        return ref[pl.ds(piece * size, size), :].astype(WIDE)

    def pieces(half):
        return range(half * PIECES // HALVES, (half + 1) * PIECES // HALVES)

    def far_step(side, half):
        give(0, side, half).wait_recv()
        for piece in pieces(half):
            far_out[side, pl.ds(piece * size, size), :] = local(0, side, piece).astype(LOW)
            hop(side, piece).start()

    def near_step(side, half):
        give(1, side, half).wait_recv()
        for piece in pieces(half):
            value = local(1, side, piece) + arrived(side, far_in.at[side], piece)
            near_out[side, pl.ds(piece * size, size), :] = value.astype(LOW)
            hop(2 + side, piece).start()

    def pair_step(half):
        give(2, 1, half).wait_recv()
        for piece in pieces(half):
            value = local(2, 1, piece) + arrived(3, near_in.at[1], piece)
            pair_out[pl.ds(piece * size, size), :] = value.astype(LOW)
            hop(4, piece).start()

    def last_step(half):
        give(2, 0, half).wait_recv()
        for piece in pieces(half):
            value = local(2, 0, piece) + arrived(2, near_in.at[0], piece) + arrived(4, pair_in, piece)
            out[pl.ds(piece * size, size), :] = value

    def drain():
        for item in ORDER:
            give(*item).wait_send()
        for kind in range(5):
            for piece in range(PIECES):
                hop(kind, piece).wait_send()

    events = {
        1: [lambda: far_step(1, 0)],
        2: [lambda: far_step(1, 1)],
        3: [lambda: near_step(1, 0)],
        4: [lambda: far_step(0, 0)],
        5: [lambda: near_step(1, 1), lambda: far_step(0, 1)],
        7: [lambda: near_step(0, 0), lambda: pair_step(0)],
        9: [lambda: near_step(0, 1), lambda: pair_step(1)],
    }

    def run(more):
        def step(i, carry):
            add_messages(i)
            for k in sorted(set(events) | set(more)):
                @pl.when(i == k)
                def _():
                    for event in events.get(k, []) + more.get(k, []):
                        event()

            return carry

        lax.fori_loop(0, len(ORDER), step, 0)
        for half in range(HALVES):
            last_step(half)

    return load, run, drain


def exchange_scratch(rows, width, devices):
    slab = width // devices * (rows // LANES)
    return [
        pltpu.VMEM((devices * slab, LANES), WIDE),
        pltpu.VMEM((devices * slab, LANES), LOW),
        pltpu.VMEM((devices, slab, LANES), LOW),
        pltpu.VMEM((slab, LANES), WIDE),
        pltpu.SemaphoreType.DMA((devices - 1,)),
        pltpu.SemaphoreType.DMA((devices - 1,)),
    ]


def exchange_moves(residual, out, refs):
    flat, packed, landed, opened, send_sems, recv_sems = refs
    subs = lax.axis_size("sub")
    devices = lax.axis_size("blk") * subs
    here = lax.axis_index("blk") * subs + lax.axis_index("sub")
    slab = landed.shape[1]
    channels = out.shape[0]
    parts = slab // channels
    nodes = parts * LANES

    def move(k):
        there = lax.rem(here + k, devices)
        return remote(
            packed.at[pl.ds(pl.multiple_of(there * slab, slab), slab)], landed.at[here],
            send_sems.at[k - 1], recv_sems.at[k - 1], (there // subs, lax.rem(there, subs)),
        )

    def start(values):
        lay_rows(flat, 0, values.T)

        def cast(i, block):
            packed[pl.ds(i, block), :] = flat[pl.ds(i, block), :].astype(LOW)

        in_pieces(flat.shape[0], cast)

        def send(k, carry):
            move(k).start()
            return carry

        lax.fori_loop(1, devices, send, 0)

    def open_slab(source, device):
        opened[...] = source.astype(WIDE)
        for j in range(parts):
            columns = pl.ds(pl.multiple_of(device * nodes + j * LANES, LANES), LANES)
            out[:, columns] = residual[:, columns] + opened[pl.ds(j, channels, stride=parts), :]

    def last():
        open_slab(packed[pl.ds(pl.multiple_of(here * slab, slab), slab), :], here)

        def take(k, carry):
            move(k).wait_recv()
            device = lax.rem(here - k + devices, devices)
            open_slab(landed[device], device)
            return carry

        lax.fori_loop(1, devices, take, 0)

        def sent(k, carry):
            move(k).wait_send()
            return carry

        lax.fori_loop(1, devices, sent, 0)

    return start, last


def finish_kernel(
    index, messages, edge_grads, node_grads, vectors, node_part, weight, residual,
    node_grad, one_out, two_out, three_out, four_out, reduced_vectors, total, reduced, out_sems, *refs,
):
    at = places()
    count = len(collect_scratch(64, 128, 64))
    load, run, drain = collect_moves(at, index, messages, total, refs[:count])
    load.start()
    meet_all()
    streams, refs = reducers(at, (edge_grads, node_grads), reduced, refs[count:])
    vector_steps = vector_reducer(at, vectors, reduced_vectors, refs[:4])
    exchange, receive = exchange_moves(residual, node_grad, refs[4:])
    for stream in streams:
        stream[0]()
    vector_steps[0]()
    load.wait()
    timetable = (
        (0, 1, (0,)), (1, 1, (1, 2, 3)), (4, 2, (0, 1)), (6, 2, (3, 2)), (6, 3, (1,)), (7, 3, (0,)), (8, 3, (3, 2)),
        (10, 4, (1, 0)), (11, 4, (3, 2)),
    )
    later = {1: [vector_steps[1]], 4: [vector_steps[2]], 7: [vector_steps[3]]}
    for when, hop, which in timetable:
        later.setdefault(when, []).extend(streams[i][hop] for i in which if i < len(streams))
    run(later)

    def hops(hop, which):
        for i in which:
            if i < len(streams):
                streams[i][hop]()

    hops(5, (1, 0))
    high, rest = split_low(total[...])
    exchange(node_part[...] + dot_right(high, weight[...]) + dot_right(rest, weight[...]))
    hops(5, (3, 2))
    hops(6, (1, 0, 3, 2))
    hops(7, range(4))
    receive()
    hops(8, range(4))
    width = total.shape[1]
    nodes_at = edge_grads.shape[0]
    copies = [
        pltpu.make_async_copy(reduced.at[pl.ds(first, target.shape[0])], target, out_sems.at[i])
        for i, (first, target) in enumerate((
            (0, one_out), (3 * width, two_out), (nodes_at, three_out), (nodes_at + 2 * width, four_out)
        ))
    ]
    for copy in copies:
        copy.start()
    vector_steps[4]()
    drain()
    for stream in streams:
        stream[9]()
    for copy in copies:
        copy.wait()


def finish(index, messages, edge_grads, node_grads, vectors, node_part, weight, residual, collective):
    rows, width = node_part.shape
    edges = messages.shape[0]
    sources = [edge_grads.shape[0], node_grads.shape[0]]
    along = lax.axis_size("blk") // 2
    devices = lax.axis_size("blk") * lax.axis_size("sub")
    hold = pl.BlockSpec(memory_space=pltpu.VMEM)
    across = pl.BlockSpec(memory_space=pl.ANY)
    return pl.pallas_call(
        finish_kernel,
        grid=(1,),
        in_specs=[
            hold, across, across, across, hold, hold, pl.BlockSpec((width, width), lambda i: (2, 0)), hold,
        ],
        out_specs=[hold] + [across] * 4 + [hold],
        out_shape=[
            jax.ShapeDtypeStruct(residual.shape, WIDE),
            jax.ShapeDtypeStruct((3 * width, width), LOW),
            jax.ShapeDtypeStruct((width, width), LOW),
            jax.ShapeDtypeStruct((2 * width, width), LOW),
            jax.ShapeDtypeStruct((width, width), LOW),
            jax.ShapeDtypeStruct(vectors.shape, WIDE),
        ],
        scratch_shapes=[
            pltpu.VMEM((rows, width), WIDE),
            pltpu.VMEM((sum(sources), width), LOW),
            pltpu.SemaphoreType.DMA((4,)),
            *collect_scratch(rows, width, edges),
            *reducers_scratch(sources, width, along),
            *vector_scratch(vectors.shape, along),
            *exchange_scratch(rows, width, devices),
        ],
        compiler_params=pltpu.CompilerParams(
            collective_id=collective, has_side_effects=True, vmem_limit_bytes=VMEM_BYTES
        ),
        name="finish_sums",
    )(index.reshape(edges // LANES, LANES), messages, edge_grads, node_grads, vectors, node_part, weight, residual)


def middle_kernel(
    index, messages, node_low, upstream, w_one, b_one, w_two, b_two, gain, shift, residual,
    table, node_part, node_out, grads, vectors, total, sent, *refs
):
    at = places()
    count = len(collect_scratch(64, 128, 64))
    load, run, drain = collect_moves(at, index, messages, total, refs[:count])
    load.start()
    meet_all()
    refs = refs[count:]
    start, one, two, three, end = spread_moves(at, sent, table, *refs[:3])
    exchange, receive = exchange_moves(residual, node_out, refs[3:])
    load.wait()
    run({})

    width = total.shape[1]
    low = total[...].astype(LOW)
    pre = dot(node_low[...], w_one[:width]) + dot(low, w_one[width:]) + b_one[...]
    logistic = jax.nn.sigmoid(pre)
    act = (pre * logistic).astype(LOW)
    normal, scale = row_normal(dot(act, w_two[...]) + b_two[...])
    given = upstream[...].T
    scaled = given * gain[...]
    slope = jnp.mean(scaled * normal, -1, keepdims=True)
    fourth = scale * (scaled - jnp.mean(scaled, -1, keepdims=True) - normal * slope)
    fourth_low = fourth.astype(LOW)
    third = dot_right(fourth_low, w_two[...]) * (logistic * (1.0 + pre * (1.0 - logistic)))
    third_low = third.astype(LOW)
    sent[...] = dot_right(third_low, w_one[width:]).astype(LOW)
    start()
    grads[:width] = dot_left(node_low[...], third_low)
    grads[width : 2 * width] = dot_left(low, third_low)
    grads[2 * width : 3 * width] = dot_left(act, fourth_low)
    vectors[...] = jnp.zeros_like(vectors)
    vectors[4:5] = jnp.sum(third_low.astype(WIDE), 0, keepdims=True)
    vectors[5:6] = jnp.sum(fourth_low.astype(WIDE), 0, keepdims=True)
    vectors[6:7] = jnp.sum(given * normal, 0, keepdims=True)
    vectors[7:8] = jnp.sum(given, 0, keepdims=True)
    node_part[...] = dot_right(third_low, w_one[:width])
    exchange(normal * gain[...] + shift[...])

    for stage in (one, two, three):
        for piece in range(PIECES):
            stage(piece)
    receive()
    end()
    drain()


def middle(index, messages, node_low, upstream, w_one, b_one, w_two, b_two, gain, shift, residual, collective):
    rows, width = node_low.shape
    edges = messages.shape[0]
    devices = lax.axis_size("blk") * lax.axis_size("sub")
    grad_rows = padded_rows(3 * width)
    hold = pl.BlockSpec(memory_space=pltpu.VMEM)
    across = pl.BlockSpec(memory_space=pl.ANY)
    table, node_part, node_out, grads, vectors = pl.pallas_call(
        middle_kernel,
        in_specs=[hold, across] + [hold] * 9,
        out_specs=[across] + [hold] * 4,
        out_shape=[
            jax.ShapeDtypeStruct((3, 4, rows, width), LOW),
            jax.ShapeDtypeStruct((rows, width), WIDE),
            jax.ShapeDtypeStruct(residual.shape, WIDE),
            jax.ShapeDtypeStruct((grad_rows, width), WIDE),
            jax.ShapeDtypeStruct((8, width), WIDE),
        ],
        scratch_shapes=[
            pltpu.VMEM((rows, width), WIDE),
            pltpu.VMEM((rows, width), LOW),
            *collect_scratch(rows, width, edges),
            *spread_scratch(),
            *exchange_scratch(rows, width, devices),
        ],
        compiler_params=pltpu.CompilerParams(
            collective_id=collective, has_side_effects=True, vmem_limit_bytes=VMEM_BYTES
        ),
        name="middle_nodes",
    )(
        index.reshape(edges // LANES, LANES), messages, node_low, upstream,
        w_one, b_one, w_two, b_two, gain, shift, residual,
    )
    return table.reshape(12 * rows, width), node_part, node_out, grads, vectors


def scatter_scratch(channels, nodes, devices):
    slab = channels * (nodes // LANES)
    return [
        pltpu.VMEM((devices * slab, LANES), WIDE),
        pltpu.VMEM((devices * slab, LANES), LOW),
        pltpu.VMEM((devices, slab, LANES), LOW),
        pltpu.VMEM((slab, LANES), WIDE),
        pltpu.VMEM((nodes // LANES * devices * channels, LANES), WIDE),
        pltpu.SemaphoreType.DMA((devices - 1,)),
        pltpu.SemaphoreType.DMA((devices - 1,)),
    ]


def scatter_moves(shard, refs):
    flat, packed, landed, opened, square, send_sems, recv_sems = refs
    subs = lax.axis_size("sub")
    devices = lax.axis_size("blk") * subs
    here = lax.axis_index("blk") * subs + lax.axis_index("sub")
    slab = landed.shape[1]
    channels = shard.shape[0]
    parts = slab // channels
    nodes = parts * LANES

    def move(k):
        there = lax.rem(here + k, devices)
        return remote(
            packed.at[pl.ds(pl.multiple_of(there * slab, slab), slab)], landed.at[here],
            send_sems.at[k - 1], recv_sems.at[k - 1], (there // subs, lax.rem(there, subs)),
        )

    def start():
        def pack(k, carry):
            device = lax.rem(here + k, devices)
            rows = pl.ds(pl.multiple_of(device * slab, slab), slab)
            for j in range(parts):
                columns = pl.ds(pl.multiple_of(device * nodes + j * LANES, LANES), LANES)
                flat[pl.ds(device * slab + j, channels, stride=parts), :] = shard[:, columns]
            packed[rows, :] = flat[rows, :].astype(LOW)
            return carry

        def send(k, carry):
            pack(k, carry)
            move(k).start()
            return carry

        lax.fori_loop(1, devices, send, 0)
        pack(0, 0)

    def open_slab(source, device):
        opened[...] = source.astype(WIDE)
        for j in range(parts):
            rows = pl.ds(pl.multiple_of((j * devices + device) * channels, channels), channels)
            square[rows, :] = opened[pl.ds(j, channels, stride=parts), :]

    def last(rows):
        open_slab(packed[pl.ds(pl.multiple_of(here * slab, slab), slab), :], here)

        def take(k, carry):
            move(k).wait_recv()
            device = lax.rem(here - k + devices, devices)
            open_slab(landed[device], device)
            return carry

        lax.fori_loop(1, devices, take, 0)
        width = devices * channels
        for j in range(parts):
            rows[j * LANES : (j + 1) * LANES, :] = square[j * width : (j + 1) * width, :].T.astype(LOW)

    def drain():
        def sent(k, carry):
            move(k).wait_send()
            return carry

        lax.fori_loop(1, devices, sent, 0)

    return start, last, drain


def begin_kernel(
    shard, later, senders, receivers, own, table, later_out, send_local, recv_wide, held, held_sem, slab_sems, *refs
):
    at = places()
    fetch = pltpu.make_async_copy(later, held, held_sem)
    fetch.start()
    meet_all()
    start, last, drain = scatter_moves(shard, refs[3:])
    start()
    last(own)
    begin, one, two, three, end = spread_moves(at, own, table, *refs[:3])
    begin()
    rows = own.shape[0]
    groups, subs = lax.axis_size("blk"), lax.axis_size("sub")
    send_local[...] = senders[...] - (at["group"] * subs + at["sub"]) * rows
    relative = lax.rem(receivers[...] // (rows * subs) - at["group"] + 1 + groups, groups)
    recv_wide[...] = relative * (rows * subs) + lax.rem(receivers[...], rows * subs)
    fetch.wait()
    devices, _, nodes = later_out.shape

    def slab(k):
        columns = pl.ds(pl.multiple_of(k * nodes, LANES), nodes)
        return pltpu.make_async_copy(held.at[:, columns], later_out.at[k], slab_sems.at[k])

    def give(k, carry):
        slab(k).start()
        return carry

    def given(k, carry):
        slab(k).wait()
        return carry

    lax.fori_loop(0, devices, give, 0)
    drain()
    for stage in (one, two, three):
        for piece in range(PIECES):
            stage(piece)
    lax.fori_loop(0, devices, given, 0)
    end()


def begin(shard, later, senders, receivers, rows, collective):
    channels, nodes = shard.shape
    devices = lax.axis_size("blk") * lax.axis_size("sub")
    width = channels * devices
    hold = pl.BlockSpec(memory_space=pltpu.VMEM)
    across = pl.BlockSpec(memory_space=pl.ANY)
    lines = (senders.shape[0] // LANES, LANES)
    own, table, later, send_local, recv_wide = pl.pallas_call(
        begin_kernel,
        in_specs=[hold, across, hold, hold],
        out_specs=[hold, across, across, hold, hold],
        out_shape=[
            jax.ShapeDtypeStruct((rows, width), LOW),
            jax.ShapeDtypeStruct((3, 4, rows, width), LOW),
            jax.ShapeDtypeStruct((devices, channels, rows), later.dtype),
            jax.ShapeDtypeStruct(lines, jnp.int32),
            jax.ShapeDtypeStruct(lines, jnp.int32),
        ],
        scratch_shapes=[
            pltpu.VMEM(later.shape, later.dtype),
            pltpu.SemaphoreType.DMA,
            pltpu.SemaphoreType.DMA((devices,)),
            *spread_scratch(),
            *scatter_scratch(channels, rows, devices),
        ],
        compiler_params=pltpu.CompilerParams(
            collective_id=collective, has_side_effects=True, vmem_limit_bytes=VMEM_BYTES
        ),
        name="begin_rows",
    )(shard, later, senders.reshape(lines), receivers.reshape(lines))
    return own, table.reshape(12 * rows, width), later, send_local, recv_wide


def release_kernel(count, *refs):
    for source, target in zip(refs[:count], refs[count:]):
        target[...] = source[...].astype(target.dtype)


def release(whole, reduced):
    arrays = [*whole, *reduced]
    steps = 8

    def spec(item, kept):
        rows, columns = item.shape
        if kept:
            return pl.BlockSpec((rows, columns // steps), lambda i: (0, i))
        return pl.BlockSpec((rows // steps, columns), lambda i: (i, 0))

    specs = [spec(item, i < len(whole)) for i, item in enumerate(arrays)]
    return pl.pallas_call(
        functools.partial(release_kernel, len(arrays)),
        grid=(steps,),
        in_specs=specs,
        out_specs=specs,
        out_shape=[jax.ShapeDtypeStruct(item.shape, WIDE) for item in arrays],
        compiler_params=pltpu.CompilerParams(vmem_limit_bytes=VMEM_BYTES),
        name="release_results",
    )(*arrays)


def shards(
    node_input,
    edge_input,
    senders,
    receivers,
    edge_count,
    edge_w_one,
    edge_b_one,
    edge_w_two,
    edge_b_two,
    edge_gain,
    edge_shift,
    node_w_one,
    node_b_one,
    node_w_two,
    node_b_two,
    node_gain,
    node_shift,
    node_cotangent,
    edge_cotangent,
):
    groups = lax.axis_size("blk")
    sub_count = lax.axis_size("sub")
    width = edge_input.shape[1]
    per_device = node_input.shape[1] // (groups * sub_count)
    node_low, wide_low, cotangent_later, send_local, recv_wide = begin(
        node_input, node_cotangent, senders, receivers, per_device, 0
    )
    node_upstream = lax.all_to_all(
        cotangent_later, ("blk", "sub"), split_axis=0, concat_axis=0, tiled=True
    ).reshape(width, per_device)
    recv_list = recv_wide.reshape(-1)
    edge_result, first_pre, second_pre, received, messages = edge_forward(
        edge_count, recv_list, send_local, edge_input, wide_low, node_low,
        edge_w_one, edge_b_one[None], edge_w_two, edge_b_two[None], edge_gain[None], edge_shift[None],
    )
    wide_grad, node_part, node_out, node_grads, node_vectors = middle(
        recv_list, messages, node_low, node_upstream, node_w_one, node_b_one[None], node_w_two, node_b_two[None],
        node_gain[None], node_shift[None], node_input, 1,
    )
    edge_grad, messages, edge_grads, vectors, node_part = edge_backward(
        edge_count, recv_list, send_local, edge_cotangent, edge_input, received, first_pre, second_pre,
        wide_grad, node_part, node_vectors, node_low, edge_w_one, edge_w_two, edge_gain[None],
    )
    node_grad, *summed, vectors = finish(
        recv_list, messages, edge_grads, node_grads, vectors, node_part, edge_w_one, node_cotangent, 3
    )
    node_out, node_grad, *summed = release((node_out, node_grad), summed)
    return (
        node_out,
        edge_result,
        node_grad,
        edge_grad,
        summed[0],
        vectors[0],
        summed[1],
        vectors[1],
        vectors[2],
        vectors[3],
        summed[2],
        vectors[4],
        summed[3],
        vectors[5],
        vectors[6],
        vectors[7],
    )


def solution(mesh):
    placed = (
        P(("blk", "sub"), None),
        P(("blk", "sub"), None),
        P(("blk", "sub")),
        P(("blk", "sub")),
        P(("blk", "sub")),
        P(),
        P(),
        P(),
        P(),
        P(),
        P(),
        P(),
        P(),
        P(),
        P(),
        P(),
        P(),
        P(("blk", "sub"), None),
        P(("blk", "sub"), None),
    )
    return jax.shard_map(
        shards,
        mesh=mesh,
        in_specs=placed,
        out_specs=(
            P(("blk", "sub"), None),
            P(("blk", "sub"), None),
            P(("blk", "sub"), None),
            P(("blk", "sub"), None),
            P(),
            P(),
            P(),
            P(),
            P(),
            P(),
            P(),
            P(),
            P(),
            P(),
            P(),
            P(),
        ),
        check_vma=False,
    )
```

```python
import functools
import math

import jax
import jax.numpy as jnp
from jax import lax
from jax.experimental import pallas as pl
from jax.experimental.pallas import tpu as pltpu
from jax.sharding import PartitionSpec as P

EPSILON = 1e-05


TILE = 512
CHUNK = 512
LANES = 128
VMEM_BYTES = 60 * 2**20


def dot(left, right):
    return jnp.dot(left, right, preferred_element_type=jnp.float32)


def dot_left(left, right):
    return lax.dot_general(
        left, right, (((0,), (0,)), ((), ())), preferred_element_type=jnp.float32
    )


def dot_right(left, right):
    return lax.dot_general(
        left, right, (((1,), (1,)), ((), ())), preferred_element_type=jnp.float32
    )


def split_low(values):
    high = values.astype(jnp.bfloat16)
    return high, (values - high.astype(jnp.float32)).astype(jnp.bfloat16)


def lay_rows(target, start, values):
    count, width = values.shape
    parts = width // LANES
    for j in range(parts):
        target[pl.ds(start * parts + j, count, stride=parts), :] = values[:, j * LANES : (j + 1) * LANES]


def read_rows(source, start, count, parts):
    return jnp.concatenate(
        [source[pl.ds(start * parts + j, count, stride=parts), :] for j in range(parts)], axis=1
    )


def load_table(wide, table, stage, sems):
    steps = wide.shape[0] // CHUNK

    def fetch(i, slot):
        return pltpu.make_async_copy(wide.at[pl.ds(i * CHUNK, CHUNK)], stage.at[slot], sems.at[slot])

    for i in range(3):
        fetch(i, i).start()

    def body(i, carry):
        slot = lax.rem(i, 4)

        @pl.when(i + 3 < steps)
        def _():
            fetch(i + 3, lax.rem(i + 3, 4)).start()

        fetch(i, slot).wait()

        def piece(k, carry):
            values = stage[slot, pl.ds(k * 64, 64), :].astype(jnp.float32)
            lay_rows(table, i * CHUNK + k * 64, values)
            return carry

        return lax.fori_loop(0, CHUNK // 64, piece, carry)

    lax.fori_loop(0, steps, body, 0)


def gather_rows(index, base, table, rows, parts):
    count = rows.shape[0] // parts

    def body(i, carry):
        for u in range(16):
            slot = i * 16 + u
            place = index[base + slot]
            rows[pl.ds(pl.multiple_of(slot * parts, parts), parts), :] = table[
                pl.ds(pl.multiple_of(place * parts, parts), parts), :
            ]
        return carry

    lax.fori_loop(0, count // 16, body, 0)


def gather_inline(index, base, table, rows, parts):
    for slot in range(rows.shape[0] // parts):
        place = index[base + slot]
        rows[slot * parts : (slot + 1) * parts, :] = table[pl.ds(pl.multiple_of(place * parts, parts), parts), :]


def row_normal(values):
    average = jnp.mean(values, -1, keepdims=True)
    centred = values - average
    variance = jnp.mean(centred * centred, -1, keepdims=True)
    scale = lax.rsqrt(variance + EPSILON)
    return centred * scale, scale


def forward_kernel(
    count, recv, send, edge, wide, nodes, w_one, b_one, w_two, b_two, gain, shift,
    result, first, second, received, message,
    table, rows, stage, sems,
):
    step = pl.program_id(0)
    base = step * TILE
    width = nodes.shape[1]
    parts = width // LANES

    @pl.when(step == 0)
    def _():
        load_table(wide, table, stage, sems)
        gather_rows(recv, base, table, rows, parts)

    later = jnp.where(step + 1 < pl.num_programs(0), base + TILE, 0)
    received[...] = read_rows(rows, 0, TILE, parts).astype(jnp.bfloat16)
    gather_inline(recv, later, table, rows, parts)
    from_recv = received[...]
    lane = lax.broadcasted_iota(jnp.int32, (LANES, LANES), 1)
    chosen = []
    for i in range(TILE // LANES):
        column = jnp.broadcast_to(send[pl.ds(step * (TILE // LANES) + i, 1), :], (LANES, LANES)).T
        chosen.append(
            jnp.concatenate(
                [
                    jnp.where(column == lane + j * LANES, 1.0, 0.0).astype(jnp.bfloat16)
                    for j in range(nodes.shape[0] // LANES)
                ],
                axis=1,
            )
        )
    chosen = jnp.concatenate(chosen, axis=0)
    from_send = dot(chosen, nodes[...]).astype(jnp.bfloat16)
    pre = (
        dot(edge[...], w_one[:width])
        + dot(from_send, w_one[width : 2 * width])
        + dot(from_recv, w_one[2 * width :])
        + b_one[...]
    )
    first[...] = pre
    act = (pre * jax.nn.sigmoid(pre)).astype(jnp.bfloat16)
    post = dot(act, w_two[...]) + b_two[...]
    second[...] = post
    normal, _ = row_normal(post)
    branch = normal * gain[...] + shift[...]
    live = base + lax.broadcasted_iota(jnp.int32, (TILE, 1), 0) < count[0]
    outcome = edge[...].astype(jnp.float32) + jnp.where(live, branch, 0.0)
    result[...] = outcome
    message[...] = jnp.where(live, outcome, 0.0).astype(jnp.bfloat16)


def edge_forward(count, recv, send, edge, wide, nodes, w_one, b_one, w_two, b_two, gain, shift):
    edges, width = edge.shape
    steps = edges // TILE
    parts = width // LANES
    hold = pl.BlockSpec(memory_space=pltpu.VMEM)
    scalar = pl.BlockSpec(memory_space=pltpu.SMEM)
    tile = pl.BlockSpec((TILE, width), lambda i: (i, 0))
    return pl.pallas_call(
        forward_kernel,
        grid=(steps,),
        in_specs=[
            scalar, scalar, hold, tile,
            pl.BlockSpec(memory_space=pl.ANY), hold, hold, hold, hold, hold, hold, hold,
        ],
        out_specs=[tile] * 5,
        out_shape=[
            jax.ShapeDtypeStruct((edges, width), jnp.float32),
            jax.ShapeDtypeStruct((edges, width), jnp.float32),
            jax.ShapeDtypeStruct((edges, width), jnp.float32),
            jax.ShapeDtypeStruct((edges, width), jnp.bfloat16),
            jax.ShapeDtypeStruct((edges, width), jnp.bfloat16),
        ],
        scratch_shapes=[
            pltpu.VMEM((wide.shape[0] * parts, LANES), jnp.float32),
            pltpu.VMEM((TILE * parts, LANES), jnp.float32),
            pltpu.VMEM((4, CHUNK, width), jnp.bfloat16),
            pltpu.SemaphoreType.DMA((4,)),
        ],
        compiler_params=pltpu.CompilerParams(vmem_limit_bytes=VMEM_BYTES),
        cost_estimate=pl.CostEstimate(
            flops=20 * edges * width * width, bytes_accessed=40 * edges * width, transcendentals=2 * edges * width
        ),
        name="edge_forward",
    )(count, recv, send, edge, wide, nodes, w_one, b_one, w_two, b_two, gain, shift)


def backward_kernel(
    count, recv, send, cotangent, edge, received, first, second, wide, node_part, node_vectors, nodes, w_one, w_two, gain,
    grad, message, all_grads, vectors, sender_grad,
    table, rows, stage, sems, by_sender, grads, give_sem,
):
    step = pl.program_id(0)
    base = step * TILE
    width = nodes.shape[1]
    parts = width // LANES

    @pl.when(step == 0)
    def _():
        load_table(wide, table, stage, sems)
        grads[...] = jnp.zeros_like(grads)
        vectors[...] = node_vectors[...]
        by_sender[...] = jnp.zeros_like(by_sender)
        gather_rows(recv, base, table, rows, parts)

    live = base + lax.broadcasted_iota(jnp.int32, (TILE, 1), 0) < count[0]
    upstream = cotangent[...].astype(jnp.float32) + jnp.where(live, read_rows(rows, 0, TILE, parts), 0.0)
    grad[...] = upstream
    later = jnp.where(step + 1 < pl.num_programs(0), base + TILE, 0)
    gather_inline(recv, later, table, rows, parts)
    masked = jnp.where(live, upstream, 0.0)
    normal, scale = row_normal(second[...])
    vectors[2:3, :] += jnp.sum(masked * normal, 0, keepdims=True)
    vectors[3:4, :] += jnp.sum(masked, 0, keepdims=True)
    scaled = masked * gain[...]
    slope = jnp.mean(scaled * normal, -1, keepdims=True)
    grad_second = scale * (scaled - jnp.mean(scaled, -1, keepdims=True) - normal * slope)
    second_low = grad_second.astype(jnp.bfloat16)
    vectors[1:2, :] += jnp.sum(second_low.astype(jnp.float32), 0, keepdims=True)
    pre = first[...]
    logistic = jax.nn.sigmoid(pre)
    act = (pre * logistic).astype(jnp.bfloat16)
    grads[3 * width : 4 * width] += dot_left(act, second_low)
    grad_first = dot_right(second_low, w_two[...]) * (logistic * (1.0 + pre * (1.0 - logistic)))
    first_low = grad_first.astype(jnp.bfloat16)
    message[...] = first_low
    vectors[0:1, :] += jnp.sum(first_low.astype(jnp.float32), 0, keepdims=True)
    grads[:width] += dot_left(edge[...], first_low)
    grads[2 * width : 3 * width] += dot_left(received[...], first_low)
    node = lax.broadcasted_iota(jnp.int32, (nodes.shape[0], LANES), 0)
    chosen = jnp.concatenate(
        [
            jnp.where(node == send[pl.ds(step * (TILE // LANES) + i, 1), :], 1.0, 0.0).astype(jnp.bfloat16)
            for i in range(TILE // LANES)
        ],
        axis=1,
    )
    by_sender[...] += dot(chosen, first_low)
    grad[...] += dot_right(first_low, w_one[:width])

    @pl.when(step == pl.num_programs(0) - 1)
    def _():
        high, rest = split_low(by_sender[...])
        grads[width : 2 * width] = dot_left(nodes[...], high) + dot_left(nodes[...], rest)
        give = pltpu.make_async_copy(grads, all_grads, give_sem)
        give.start()
        middle = w_one[width : 2 * width]
        sender_grad[...] = node_part[...] + dot_right(high, middle) + dot_right(rest, middle)
        give.wait()


def edge_backward(
    count, recv, send, cotangent, edge, received, first, second, wide, node_part, node_vectors, nodes,
    w_one, w_two, gain,
):
    edges, width = edge.shape
    steps = edges // TILE
    parts = width // LANES
    per_device = nodes.shape[0]
    hold = pl.BlockSpec(memory_space=pltpu.VMEM)
    scalar = pl.BlockSpec(memory_space=pltpu.SMEM)
    tile = pl.BlockSpec((TILE, width), lambda i: (i, 0))

    across = pl.BlockSpec(memory_space=pl.ANY)

    def whole(rows):
        return pl.BlockSpec((rows, width), lambda i: (0, 0))

    return pl.pallas_call(
        backward_kernel,
        grid=(steps,),
        in_specs=[
            scalar, scalar, hold, tile, tile, tile, tile, tile,
            across, hold, hold, hold, hold, hold, hold,
        ],
        out_specs=[
            tile, tile, across, whole(8), whole(per_device),
        ],
        out_shape=[
            jax.ShapeDtypeStruct((edges, width), jnp.float32),
            jax.ShapeDtypeStruct((edges, width), jnp.bfloat16),
            jax.ShapeDtypeStruct((4 * width, width), jnp.float32),
            jax.ShapeDtypeStruct((8, width), jnp.float32),
            jax.ShapeDtypeStruct((per_device, width), jnp.float32),
        ],
        scratch_shapes=[
            pltpu.VMEM((wide.shape[0] * parts, LANES), jnp.float32),
            pltpu.VMEM((TILE * parts, LANES), jnp.float32),
            pltpu.VMEM((4, CHUNK, width), jnp.bfloat16),
            pltpu.SemaphoreType.DMA((4,)),
            pltpu.VMEM((per_device, width), jnp.float32),
            pltpu.VMEM((4 * width, width), jnp.float32),
            pltpu.SemaphoreType.DMA,
        ],
        compiler_params=pltpu.CompilerParams(vmem_limit_bytes=VMEM_BYTES),
        cost_estimate=pl.CostEstimate(
            flops=24 * edges * width * width, bytes_accessed=40 * edges * width, transcendentals=2 * edges * width
        ),
        name="edge_backward",
    )(
        count, recv, send, cotangent, edge, received, first, second, wide,
        node_part, node_vectors, nodes, w_one, w_two, gain,
    )


MESH = pl.DeviceIdType.MESH
PIECES = 4
SPLIT = True
LOW = jnp.bfloat16
WIDE = jnp.float32


def places():
    groups = lax.axis_size("blk")
    group, sub = lax.axis_index("blk"), lax.axis_index("sub")
    odd = lax.rem(group, 2)
    along = groups // 2
    spot = group // 2
    beside = group + 1 - 2 * odd
    return dict(
        group=group,
        sub=sub,
        core=lax.rem(sub, 2),
        chip=sub // 2,
        odd=odd,
        spot=spot,
        along=along,
        sibling=sub + 1 - 2 * lax.rem(sub, 2),
        partner=lax.rem(sub + 2, 4),
        to_sibling=(group, sub + 1 - 2 * lax.rem(sub, 2)),
        to_partner=(group, lax.rem(sub + 2, 4)),
        to_beside=(beside, sub),
        to_onward=(lax.rem(group + 2 - 4 * odd + groups, groups), sub),
        to_source=(lax.rem(group - 2 + 4 * odd + groups, groups), sub),
        peers=[(2 * lax.rem(spot + k, along) + odd, sub) for k in range(1, along)],
        near=2 - 2 * odd,
        far=2 * odd,
    )


def meet(senders):
    barrier = pltpu.get_barrier_semaphore()
    for device in senders:
        pl.semaphore_signal(barrier, inc=1, device_id=device, device_id_type=MESH)
    pl.semaphore_wait(barrier, len(senders))


def meet_all():
    barrier = pltpu.get_barrier_semaphore()
    subs = lax.axis_size("sub")
    devices = lax.axis_size("blk") * subs
    here = lax.axis_index("blk") * subs + lax.axis_index("sub")

    def greet(k, carry):
        there = lax.rem(here + k, devices)
        pl.semaphore_signal(barrier, inc=1, device_id=(there // subs, lax.rem(there, subs)), device_id_type=MESH)
        return carry

    lax.fori_loop(1, devices, greet, 0)
    pl.semaphore_wait(barrier, devices - 1)


def remote(source, target, send, recv, device):
    return pltpu.make_async_remote_copy(
        src_ref=source, dst_ref=target, send_sem=send, recv_sem=recv, device_id=device, device_id_type=MESH
    )


def in_pieces(count, body):
    block = math.gcd(count, 128)

    def run(i, carry):
        body(pl.multiple_of(i * block, block), block)
        return carry

    lax.fori_loop(0, count // block, run, 0)


def padded_rows(rows):
    unit = 64 * lax.axis_size("blk")
    return -(-rows // unit) * unit


def streams_of(sources):
    unit = 64 * lax.axis_size("blk")
    streams = []
    for i, rows in enumerate(sources):
        first = -(-(rows // unit) // 2) * unit if SPLIT else rows
        streams.append((i, 0, first))
        if first < rows:
            streams.append((i, first, rows - first))
    return streams


def reducers_scratch(sources, width, along):
    return [ref for _, _, rows in streams_of(sources) for ref in reducer_scratch(rows, width, along)]


def reducers(at, sources, reduced, refs):
    made = []
    for i, (which, start, rows) in enumerate(streams_of([source.shape[0] for source in sources])):
        first = start + sum(source.shape[0] for source in sources[:which])
        made.append(reducer(at, sources[which], start, reduced, first, rows, i % 2 > 0, refs[i * 13 : i * 13 + 13]))
    return made, refs[len(made) * 13 :]


def reducer_scratch(rows, width, along):
    return [
        pltpu.VMEM((rows // 2, width), WIDE),
        pltpu.VMEM((rows // 2, width), WIDE),
        pltpu.VMEM((rows // 4, width), LOW),
        pltpu.VMEM((rows // 4, width), LOW),
        pltpu.VMEM((rows // 8, width), LOW),
        pltpu.VMEM((rows // 8, width), LOW),
        pltpu.VMEM((rows // 8, width), LOW),
        pltpu.VMEM((along - 1, rows // 8 // along, width), LOW),
        pltpu.SemaphoreType.DMA,
        pltpu.SemaphoreType.DMA((6,)),
        pltpu.SemaphoreType.DMA((6,)),
        pltpu.SemaphoreType.DMA((2, along - 1)),
        pltpu.SemaphoreType.DMA((2, along - 1)),
    ]


def reducer(at, grads, source_first, reduced, first, rows, swap, refs):
    (
        half, half_in, cross_out, cross_in, side_out, side_in, ring_out, ring_in,
        load_sem, step_send, step_recv, ring_send, ring_recv,
    ) = refs
    along, peers = at["along"], at["peers"]
    turns = [(at["chip"], at["to_partner"]), (at["odd"], at["to_beside"])]
    (bit_one, device_one), (bit_two, device_two) = turns[::-1] if swap else turns
    core, spot = at["core"], at["spot"]
    n_half, n_cross, n_side, n_ring = rows // 2, rows // 4, rows // 8, rows // 8 // along
    at_half = first + core * n_half
    at_cross = at_half + bit_one * n_cross
    at_side = at_cross + bit_two * n_side
    at_ring = at_side + spot * n_ring

    def span(start, count):
        return pl.ds(pl.multiple_of(start, 16), count)

    def step(kind):
        if kind == 0:
            other = span(source_first + (1 - core) * n_half, n_half)
            source, target, device = grads.at[other], half_in, at["to_sibling"]
        elif kind == 1:
            source, target, device = cross_out, cross_in, device_one
        elif kind == 2:
            source, target, device = side_out, side_in, device_two
        else:
            start, count, device = {
                3: (at_side, n_side, device_two),
                4: (at_cross, n_cross, device_one),
                5: (at_half, n_half, at["to_sibling"]),
            }[kind]
            source = target = reduced.at[span(start, count)]
        return remote(source, target, step_send.at[kind], step_recv.at[kind], device)

    def ring(kind, k):
        if kind == 0:
            source = ring_out.at[span(lax.rem(spot + k, along) * n_ring, n_ring)]
            target = ring_in.at[k - 1]
        else:
            source = target = reduced.at[span(at_ring, n_ring)]
        return remote(source, target, ring_send.at[kind, k - 1], ring_recv.at[kind, k - 1], peers[k - 1])

    load = pltpu.make_async_copy(grads.at[span(source_first + core * n_half, n_half)], half, load_sem)

    def start():
        step(0).start()
        load.start()

    def add_half():
        load.wait()
        step(0).wait_recv()
        other = (1 - bit_one) * n_cross

        def part(i, block):
            here = pl.ds(pl.multiple_of(other + i, block), block)
            cross_out[pl.ds(i, block), :] = (half[here, :] + half_in[here, :]).astype(LOW)

        in_pieces(n_cross, part)
        step(1).start()

    def add_cross():
        mine, other = bit_one * n_cross, (1 - bit_two) * n_side
        step(1).wait_recv()

        def part(i, block):
            there = pl.ds(pl.multiple_of(other + i, block), block)
            here = pl.ds(pl.multiple_of(mine + other + i, block), block)
            side_out[pl.ds(i, block), :] = (half[here, :] + half_in[here, :] + cross_in[there, :].astype(WIDE)).astype(LOW)

        in_pieces(n_side, part)
        step(2).start()

    def add_side():
        mine, kept = bit_one * n_cross, bit_two * n_side
        step(2).wait_recv()

        def part(i, block):
            there = pl.ds(pl.multiple_of(kept + i, block), block)
            here = pl.ds(pl.multiple_of(mine + kept + i, block), block)
            flat = pl.ds(i, block)
            value = half[here, :] + half_in[here, :] + cross_in[there, :].astype(WIDE) + side_in[flat, :].astype(WIDE)
            half[here, :] = value
            ring_out[flat, :] = value.astype(LOW)

        in_pieces(n_side, part)
        for k in range(1, along):
            ring(0, k).start()

    def add_ring():
        value = half[span(bit_one * n_cross + bit_two * n_side + spot * n_ring, n_ring), :]
        for k in range(1, along):
            ring(0, k).wait_recv()
            value = value + ring_in[k - 1].astype(WIDE)
        reduced[span(at_ring, n_ring), :] = value.astype(LOW)
        for k in range(1, along):
            ring(1, k).start()

    def share_side():
        for k in range(1, along):
            ring(1, k).wait_recv()
        step(3).start()

    def share_cross():
        step(3).wait_recv()
        step(4).start()

    def share_half():
        step(4).wait_recv()
        step(5).start()

    def last():
        step(5).wait_recv()

    def drain():
        for kind in range(6):
            step(kind).wait_send()
        for k in range(1, along):
            ring(0, k).wait_send()
            ring(1, k).wait_send()

    return [start, add_half, add_cross, add_side, add_ring, share_side, share_cross, share_half, last, drain]


def vector_scratch(shape, along):
    return [
        pltpu.VMEM((4, *shape), WIDE),
        pltpu.VMEM((2 + along, *shape), WIDE),
        pltpu.SemaphoreType.DMA((2 + along,)),
        pltpu.SemaphoreType.DMA((2 + along,)),
    ]


def vector_reducer(at, vectors, reduced, refs):
    held, held_in, send_sems, recv_sems = refs
    along = at["along"]
    devices = (at["to_sibling"], at["to_partner"], at["to_beside"], *at["peers"])

    def move(kind):
        return remote(held.at[min(kind, 3)], held_in.at[kind], send_sems.at[kind], recv_sems.at[kind], devices[kind])

    def start():
        held[0] = vectors[...]
        move(0).start()

    def turn(kind):
        def run():
            move(kind).wait_recv()
            held[kind + 1] = held[kind] + held_in[kind]
            for k in range(kind + 1, kind + 2 if kind < 2 else 2 + along):
                move(k).start()

        return run

    def last():
        value = held[3]
        for k in range(3, 2 + along):
            move(k).wait_recv()
            value = value + held_in[k]
        reduced[...] = value
        for k in range(2 + along):
            move(k).wait_send()

    return [start, turn(0), turn(1), turn(2), last]


def spread_moves(at, own, table, keep_sem, send_sems, recv_sems):
    sub, partner, near, far = at["sub"], at["partner"], at["near"], at["far"]
    to_sibling, to_partner, to_beside, to_onward = (
        at["to_sibling"], at["to_partner"], at["to_beside"], at["to_onward"]
    )
    size = own.shape[0] // PIECES

    def move(kind, piece):
        source, slot, device = {
            0: (None, (1, sub), to_partner),
            1: (None, (far, sub), to_beside),
            2: (None, (1, sub), to_sibling),
            3: ((1, partner), (far, partner), to_beside),
            4: ((1, partner), (1, partner), to_sibling),
            5: ((near, sub), (far, sub), to_onward),
            6: ((near, sub), (near, sub), to_sibling),
            7: ((near, partner), (far, partner), to_onward),
            8: ((near, partner), (near, partner), to_sibling),
            9: ((far, sub), (far, sub), to_sibling),
            10: ((far, partner), (far, partner), to_sibling),
            11: ((near, sub), (near, sub), to_partner),
            12: ((far, sub), (far, sub), to_partner),
        }[kind]
        source = own if source is None else table.at[source[0], source[1]]
        rows = pl.ds(piece * size, size)
        return remote(
            source.at[rows], table.at[slot[0], slot[1], rows],
            send_sems.at[kind, piece], recv_sems.at[kind, piece], device,
        )

    keep = pltpu.make_async_copy(own, table.at[1, sub], keep_sem)

    def start():
        for piece in range(PIECES):
            for kind in (0, 1, 2):
                move(kind, piece).start()
        keep.start()

    def relay(arrived, kinds, piece):
        move(arrived, piece).wait_recv()
        for kind in kinds:
            move(kind, piece).start()

    straight = range(PIECES - 2)

    def one(piece):
        relay(0, (3, 4) if piece in straight else (4,), piece)
        relay(1, (5, 6) if piece in straight else (5, 6, 11), piece)

    def two(piece):
        if piece in straight:
            relay(3, (7, 8), piece)
            relay(5, (9,), piece)
        else:
            relay(5, (9, 12), piece)
            relay(11, (8,), piece)

    def three(piece):
        if piece in straight:
            relay(7, (10,), piece)
        else:
            relay(12, (10,), piece)

    def drain():
        for kind in range(13):
            for piece in range(PIECES):
                if kind in ((11, 12) if piece in straight else (3, 7)):
                    continue
                if kind in (2, 4, 6, 8, 9, 10):
                    move(kind, piece).wait_recv()
                move(kind, piece).wait_send()
        keep.wait()

    return start, one, two, three, drain


def spread_scratch():
    return [
        pltpu.SemaphoreType.DMA,
        pltpu.SemaphoreType.DMA((13, PIECES)),
        pltpu.SemaphoreType.DMA((13, PIECES)),
    ]


HALVES = 2
ORDER = (
    (0, 1, 0), (0, 1, 1), (1, 1, 0), (0, 0, 0), (1, 1, 1), (0, 0, 1),
    (1, 0, 0), (2, 1, 0), (1, 0, 1), (2, 1, 1), (2, 0, 0), (2, 0, 1),
)


def collect_scratch(rows, width, edges):
    return [
        pltpu.VMEM((edges, width), LOW),
        pltpu.VMEM((2, 3, 2, rows, width), WIDE),
        pltpu.VMEM((3, 2, rows, width), WIDE),
        pltpu.VMEM((2, rows, width), LOW),
        pltpu.VMEM((2, rows, width), LOW),
        pltpu.VMEM((2, rows, width), LOW),
        pltpu.VMEM((2, rows, width), LOW),
        pltpu.VMEM((rows, width), LOW),
        pltpu.VMEM((rows, width), LOW),
        pltpu.SemaphoreType.DMA,
        pltpu.SemaphoreType.DMA((3, 2, HALVES)),
        pltpu.SemaphoreType.DMA((3, 2, HALVES)),
        pltpu.SemaphoreType.DMA((5, PIECES)),
        pltpu.SemaphoreType.DMA((5, PIECES)),
    ]


def collect_moves(at, index, messages, out, refs):
    (
        held, parts, landed, far_out, far_in, near_out, near_in, pair_out, pair_in,
        load_sem, give_sems, take_sems, send_sems, recv_sems,
    ) = refs
    sub, partner, sibling = at["sub"], at["partner"], at["sibling"]
    rows = out.shape[0]
    size = rows // PIECES
    part_rows = rows // HALVES
    load = pltpu.make_async_copy(messages, held, load_sem)

    def piece_of(ref, piece):
        return ref.at[pl.ds(piece * size, size)]

    def give(role, side, half):
        span = pl.ds(pl.multiple_of(half * part_rows, part_rows), part_rows)
        return remote(
            parts.at[0, role, side, span], landed.at[role, side, span],
            give_sems.at[role, side, half], take_sems.at[role, side, half], at["to_sibling"],
        )

    def hop(kind, piece):
        source, target, device = {
            0: (far_out.at[0], far_in.at[0], at["to_source"]),
            1: (far_out.at[1], far_in.at[1], at["to_source"]),
            2: (near_out.at[0], near_in.at[0], at["to_beside"]),
            3: (near_out.at[1], near_in.at[1], at["to_beside"]),
            4: (pair_out, pair_in, at["to_partner"]),
        }[kind]
        return remote(
            piece_of(source, piece), piece_of(target, piece),
            send_sems.at[kind, piece], recv_sems.at[kind, piece], device,
        )

    def add_messages(step):
        def pick(column):
            return lax.rem(sum(int(item[column]) << (2 * i) for i, item in enumerate(ORDER)) >> (2 * step), 4)

        role, side, half = pick(0), pick(1), pick(2)
        relation = jnp.where(role == 0, at["far"], jnp.where(role == 1, at["near"], 1))
        span = pl.ds(pl.multiple_of(half * part_rows, part_rows), part_rows)

        def whose(w, carry):
            first = jnp.where(w == 0, sibling, sub)
            target = lax.rem(first + 2 * side, 4)
            base = (relation * 4 + target) * rows + half * part_rows
            node = lax.broadcasted_iota(jnp.int32, (part_rows, LANES), 0) + base
            chosen = jnp.concatenate(
                [jnp.where(node == index[j : j + 1, :], 1.0, 0.0).astype(LOW) for j in range(index.shape[0])], axis=1
            )
            parts[w, role, side, span, :] = dot(chosen, held[...])
            return carry

        lax.fori_loop(0, 2, whose, 0)
        give(role, side, half).start()

    def local(role, side, piece):
        span = pl.ds(piece * size, size)
        return parts[1, role, side, span, :] + landed[role, side, span, :]

    def arrived(kind, ref, piece):
        hop(kind, piece).wait_recv()
        return ref[pl.ds(piece * size, size), :].astype(WIDE)

    def pieces(half):
        return range(half * PIECES // HALVES, (half + 1) * PIECES // HALVES)

    def far_step(side, half):
        give(0, side, half).wait_recv()
        for piece in pieces(half):
            far_out[side, pl.ds(piece * size, size), :] = local(0, side, piece).astype(LOW)
            hop(side, piece).start()

    def near_step(side, half):
        give(1, side, half).wait_recv()
        for piece in pieces(half):
            value = local(1, side, piece) + arrived(side, far_in.at[side], piece)
            near_out[side, pl.ds(piece * size, size), :] = value.astype(LOW)
            hop(2 + side, piece).start()

    def pair_step(half):
        give(2, 1, half).wait_recv()
        for piece in pieces(half):
            value = local(2, 1, piece) + arrived(3, near_in.at[1], piece)
            pair_out[pl.ds(piece * size, size), :] = value.astype(LOW)
            hop(4, piece).start()

    def last_step(half):
        give(2, 0, half).wait_recv()
        for piece in pieces(half):
            value = local(2, 0, piece) + arrived(2, near_in.at[0], piece) + arrived(4, pair_in, piece)
            out[pl.ds(piece * size, size), :] = value

    def drain():
        for item in ORDER:
            give(*item).wait_send()
        for kind in range(5):
            for piece in range(PIECES):
                hop(kind, piece).wait_send()

    events = {
        1: [lambda: far_step(1, 0)],
        2: [lambda: far_step(1, 1)],
        3: [lambda: near_step(1, 0)],
        4: [lambda: far_step(0, 0)],
        5: [lambda: near_step(1, 1), lambda: far_step(0, 1)],
        7: [lambda: near_step(0, 0), lambda: pair_step(0)],
        9: [lambda: near_step(0, 1), lambda: pair_step(1)],
    }

    def run(more):
        def step(i, carry):
            add_messages(i)
            for k in sorted(set(events) | set(more)):
                @pl.when(i == k)
                def _():
                    for event in events.get(k, []) + more.get(k, []):
                        event()

            return carry

        lax.fori_loop(0, len(ORDER), step, 0)
        for half in range(HALVES):
            last_step(half)

    return load, run, drain


def exchange_scratch(rows, width, devices):
    slab = width // devices * (rows // LANES)
    return [
        pltpu.VMEM((devices * slab, LANES), WIDE),
        pltpu.VMEM((devices * slab, LANES), LOW),
        pltpu.VMEM((devices, slab, LANES), LOW),
        pltpu.VMEM((slab, LANES), WIDE),
        pltpu.SemaphoreType.DMA((devices - 1,)),
        pltpu.SemaphoreType.DMA((devices - 1,)),
    ]


def exchange_moves(residual, out, refs):
    flat, packed, landed, opened, send_sems, recv_sems = refs
    subs = lax.axis_size("sub")
    devices = lax.axis_size("blk") * subs
    here = lax.axis_index("blk") * subs + lax.axis_index("sub")
    slab = landed.shape[1]
    channels = out.shape[0]
    parts = slab // channels
    nodes = parts * LANES

    def move(k):
        there = lax.rem(here + k, devices)
        return remote(
            packed.at[pl.ds(pl.multiple_of(there * slab, slab), slab)], landed.at[here],
            send_sems.at[k - 1], recv_sems.at[k - 1], (there // subs, lax.rem(there, subs)),
        )

    def start(values):
        lay_rows(flat, 0, values.T)

        def cast(i, block):
            packed[pl.ds(i, block), :] = flat[pl.ds(i, block), :].astype(LOW)

        in_pieces(flat.shape[0], cast)

        def send(k, carry):
            move(k).start()
            return carry

        lax.fori_loop(1, devices, send, 0)

    def open_slab(source, device):
        opened[...] = source.astype(WIDE)
        for j in range(parts):
            columns = pl.ds(pl.multiple_of(device * nodes + j * LANES, LANES), LANES)
            out[:, columns] = residual[:, columns] + opened[pl.ds(j, channels, stride=parts), :]

    def last():
        open_slab(packed[pl.ds(pl.multiple_of(here * slab, slab), slab), :], here)

        def take(k, carry):
            move(k).wait_recv()
            device = lax.rem(here - k + devices, devices)
            open_slab(landed[device], device)
            return carry

        lax.fori_loop(1, devices, take, 0)

        def sent(k, carry):
            move(k).wait_send()
            return carry

        lax.fori_loop(1, devices, sent, 0)

    return start, last


def finish_kernel(
    index, messages, edge_grads, node_grads, vectors, node_part, weight, residual,
    node_grad, one_out, two_out, three_out, four_out, reduced_vectors, total, reduced, out_sems, *refs,
):
    at = places()
    count = len(collect_scratch(64, 128, 64))
    load, run, drain = collect_moves(at, index, messages, total, refs[:count])
    load.start()
    meet_all()
    streams, refs = reducers(at, (edge_grads, node_grads), reduced, refs[count:])
    vector_steps = vector_reducer(at, vectors, reduced_vectors, refs[:4])
    exchange, receive = exchange_moves(residual, node_grad, refs[4:])
    for stream in streams:
        stream[0]()
    vector_steps[0]()
    load.wait()
    timetable = (
        (0, 1, (0,)), (1, 1, (1, 2, 3)), (4, 2, (0, 1)), (6, 2, (3, 2)), (6, 3, (1,)), (7, 3, (0,)), (8, 3, (3, 2)),
        (10, 4, (1, 0)), (11, 4, (3, 2)),
    )
    later = {1: [vector_steps[1]], 4: [vector_steps[2]], 7: [vector_steps[3]]}
    for when, hop, which in timetable:
        later.setdefault(when, []).extend(streams[i][hop] for i in which if i < len(streams))
    run(later)

    def hops(hop, which):
        for i in which:
            if i < len(streams):
                streams[i][hop]()

    hops(5, (1, 0))
    high, rest = split_low(total[...])
    exchange(node_part[...] + dot_right(high, weight[...]) + dot_right(rest, weight[...]))
    hops(5, (3, 2))
    hops(6, (1, 0, 3, 2))
    hops(7, range(4))
    receive()
    hops(8, range(4))
    width = total.shape[1]
    nodes_at = edge_grads.shape[0]
    copies = [
        pltpu.make_async_copy(reduced.at[pl.ds(first, target.shape[0])], target, out_sems.at[i])
        for i, (first, target) in enumerate((
            (0, one_out), (3 * width, two_out), (nodes_at, three_out), (nodes_at + 2 * width, four_out)
        ))
    ]
    for copy in copies:
        copy.start()
    vector_steps[4]()
    drain()
    for stream in streams:
        stream[9]()
    for copy in copies:
        copy.wait()


def finish(index, messages, edge_grads, node_grads, vectors, node_part, weight, residual, collective):
    rows, width = node_part.shape
    edges = messages.shape[0]
    sources = [edge_grads.shape[0], node_grads.shape[0]]
    along = lax.axis_size("blk") // 2
    devices = lax.axis_size("blk") * lax.axis_size("sub")
    hold = pl.BlockSpec(memory_space=pltpu.VMEM)
    across = pl.BlockSpec(memory_space=pl.ANY)
    return pl.pallas_call(
        finish_kernel,
        grid=(1,),
        in_specs=[
            hold, across, across, across, hold, hold, pl.BlockSpec((width, width), lambda i: (2, 0)), hold,
        ],
        out_specs=[hold] + [across] * 4 + [hold],
        out_shape=[
            jax.ShapeDtypeStruct(residual.shape, WIDE),
            jax.ShapeDtypeStruct((3 * width, width), LOW),
            jax.ShapeDtypeStruct((width, width), LOW),
            jax.ShapeDtypeStruct((2 * width, width), LOW),
            jax.ShapeDtypeStruct((width, width), LOW),
            jax.ShapeDtypeStruct(vectors.shape, WIDE),
        ],
        scratch_shapes=[
            pltpu.VMEM((rows, width), WIDE),
            pltpu.VMEM((sum(sources), width), LOW),
            pltpu.SemaphoreType.DMA((4,)),
            *collect_scratch(rows, width, edges),
            *reducers_scratch(sources, width, along),
            *vector_scratch(vectors.shape, along),
            *exchange_scratch(rows, width, devices),
        ],
        compiler_params=pltpu.CompilerParams(
            collective_id=collective, has_side_effects=True, vmem_limit_bytes=VMEM_BYTES
        ),
        name="finish_sums",
    )(index.reshape(edges // LANES, LANES), messages, edge_grads, node_grads, vectors, node_part, weight, residual)


def middle_kernel(
    index, messages, node_low, upstream, w_one, b_one, w_two, b_two, gain, shift, residual,
    table, node_part, node_out, grads, vectors, total, sent, *refs
):
    at = places()
    count = len(collect_scratch(64, 128, 64))
    load, run, drain = collect_moves(at, index, messages, total, refs[:count])
    load.start()
    meet_all()
    refs = refs[count:]
    start, one, two, three, end = spread_moves(at, sent, table, *refs[:3])
    exchange, receive = exchange_moves(residual, node_out, refs[3:])
    load.wait()
    run({})

    width = total.shape[1]
    low = total[...].astype(LOW)
    pre = dot(node_low[...], w_one[:width]) + dot(low, w_one[width:]) + b_one[...]
    logistic = jax.nn.sigmoid(pre)
    act = (pre * logistic).astype(LOW)
    normal, scale = row_normal(dot(act, w_two[...]) + b_two[...])
    given = upstream[...].T
    scaled = given * gain[...]
    slope = jnp.mean(scaled * normal, -1, keepdims=True)
    fourth = scale * (scaled - jnp.mean(scaled, -1, keepdims=True) - normal * slope)
    fourth_low = fourth.astype(LOW)
    third = dot_right(fourth_low, w_two[...]) * (logistic * (1.0 + pre * (1.0 - logistic)))
    third_low = third.astype(LOW)
    sent[...] = dot_right(third_low, w_one[width:]).astype(LOW)
    start()
    grads[:width] = dot_left(node_low[...], third_low)
    grads[width : 2 * width] = dot_left(low, third_low)
    grads[2 * width : 3 * width] = dot_left(act, fourth_low)
    vectors[...] = jnp.zeros_like(vectors)
    vectors[4:5] = jnp.sum(third_low.astype(WIDE), 0, keepdims=True)
    vectors[5:6] = jnp.sum(fourth_low.astype(WIDE), 0, keepdims=True)
    vectors[6:7] = jnp.sum(given * normal, 0, keepdims=True)
    vectors[7:8] = jnp.sum(given, 0, keepdims=True)
    node_part[...] = dot_right(third_low, w_one[:width])
    exchange(normal * gain[...] + shift[...])

    for stage in (one, two, three):
        for piece in range(PIECES):
            stage(piece)
    receive()
    end()
    drain()


def middle(index, messages, node_low, upstream, w_one, b_one, w_two, b_two, gain, shift, residual, collective):
    rows, width = node_low.shape
    edges = messages.shape[0]
    devices = lax.axis_size("blk") * lax.axis_size("sub")
    grad_rows = padded_rows(3 * width)
    hold = pl.BlockSpec(memory_space=pltpu.VMEM)
    across = pl.BlockSpec(memory_space=pl.ANY)
    table, node_part, node_out, grads, vectors = pl.pallas_call(
        middle_kernel,
        in_specs=[hold, across] + [hold] * 9,
        out_specs=[across] + [hold] * 4,
        out_shape=[
            jax.ShapeDtypeStruct((3, 4, rows, width), LOW),
            jax.ShapeDtypeStruct((rows, width), WIDE),
            jax.ShapeDtypeStruct(residual.shape, WIDE),
            jax.ShapeDtypeStruct((grad_rows, width), WIDE),
            jax.ShapeDtypeStruct((8, width), WIDE),
        ],
        scratch_shapes=[
            pltpu.VMEM((rows, width), WIDE),
            pltpu.VMEM((rows, width), LOW),
            *collect_scratch(rows, width, edges),
            *spread_scratch(),
            *exchange_scratch(rows, width, devices),
        ],
        compiler_params=pltpu.CompilerParams(
            collective_id=collective, has_side_effects=True, vmem_limit_bytes=VMEM_BYTES
        ),
        name="middle_nodes",
    )(
        index.reshape(edges // LANES, LANES), messages, node_low, upstream,
        w_one, b_one, w_two, b_two, gain, shift, residual,
    )
    return table.reshape(12 * rows, width), node_part, node_out, grads, vectors


def scatter_scratch(channels, nodes, devices):
    slab = channels * (nodes // LANES)
    return [
        pltpu.VMEM((devices * slab, LANES), WIDE),
        pltpu.VMEM((devices * slab, LANES), LOW),
        pltpu.VMEM((devices, slab, LANES), LOW),
        pltpu.VMEM((slab, LANES), WIDE),
        pltpu.VMEM((nodes // LANES * devices * channels, LANES), WIDE),
        pltpu.SemaphoreType.DMA((devices - 1,)),
        pltpu.SemaphoreType.DMA((devices - 1,)),
    ]


def scatter_moves(shard, refs):
    flat, packed, landed, opened, square, send_sems, recv_sems = refs
    subs = lax.axis_size("sub")
    devices = lax.axis_size("blk") * subs
    here = lax.axis_index("blk") * subs + lax.axis_index("sub")
    slab = landed.shape[1]
    channels = shard.shape[0]
    parts = slab // channels
    nodes = parts * LANES

    def move(k):
        there = lax.rem(here + k, devices)
        return remote(
            packed.at[pl.ds(pl.multiple_of(there * slab, slab), slab)], landed.at[here],
            send_sems.at[k - 1], recv_sems.at[k - 1], (there // subs, lax.rem(there, subs)),
        )

    def start():
        def pack(k, carry):
            device = lax.rem(here + k, devices)
            rows = pl.ds(pl.multiple_of(device * slab, slab), slab)
            for j in range(parts):
                columns = pl.ds(pl.multiple_of(device * nodes + j * LANES, LANES), LANES)
                flat[pl.ds(device * slab + j, channels, stride=parts), :] = shard[:, columns]
            packed[rows, :] = flat[rows, :].astype(LOW)
            return carry

        def send(k, carry):
            pack(k, carry)
            move(k).start()
            return carry

        lax.fori_loop(1, devices, send, 0)
        pack(0, 0)

    def open_slab(source, device):
        opened[...] = source.astype(WIDE)
        for j in range(parts):
            rows = pl.ds(pl.multiple_of((j * devices + device) * channels, channels), channels)
            square[rows, :] = opened[pl.ds(j, channels, stride=parts), :]

    def last(rows):
        open_slab(packed[pl.ds(pl.multiple_of(here * slab, slab), slab), :], here)

        def take(k, carry):
            move(k).wait_recv()
            device = lax.rem(here - k + devices, devices)
            open_slab(landed[device], device)
            return carry

        lax.fori_loop(1, devices, take, 0)
        width = devices * channels
        for j in range(parts):
            rows[j * LANES : (j + 1) * LANES, :] = square[j * width : (j + 1) * width, :].T.astype(LOW)

    def drain():
        def sent(k, carry):
            move(k).wait_send()
            return carry

        lax.fori_loop(1, devices, sent, 0)

    return start, last, drain


def begin_kernel(
    shard, later, senders, receivers, own, table, later_out, send_local, recv_wide, held, held_sem, slab_sems, *refs
):
    at = places()
    fetch = pltpu.make_async_copy(later, held, held_sem)
    fetch.start()
    meet_all()
    start, last, drain = scatter_moves(shard, refs[3:])
    start()
    last(own)
    begin, one, two, three, end = spread_moves(at, own, table, *refs[:3])
    begin()
    rows = own.shape[0]
    groups, subs = lax.axis_size("blk"), lax.axis_size("sub")
    send_local[...] = senders[...] - (at["group"] * subs + at["sub"]) * rows
    relative = lax.rem(receivers[...] // (rows * subs) - at["group"] + 1 + groups, groups)
    recv_wide[...] = relative * (rows * subs) + lax.rem(receivers[...], rows * subs)
    fetch.wait()
    devices, _, nodes = later_out.shape

    def slab(k):
        columns = pl.ds(pl.multiple_of(k * nodes, LANES), nodes)
        return pltpu.make_async_copy(held.at[:, columns], later_out.at[k], slab_sems.at[k])

    def give(k, carry):
        slab(k).start()
        return carry

    def given(k, carry):
        slab(k).wait()
        return carry

    lax.fori_loop(0, devices, give, 0)
    drain()
    for stage in (one, two, three):
        for piece in range(PIECES):
            stage(piece)
    lax.fori_loop(0, devices, given, 0)
    end()


def begin(shard, later, senders, receivers, rows, collective):
    channels, nodes = shard.shape
    devices = lax.axis_size("blk") * lax.axis_size("sub")
    width = channels * devices
    hold = pl.BlockSpec(memory_space=pltpu.VMEM)
    across = pl.BlockSpec(memory_space=pl.ANY)
    lines = (senders.shape[0] // LANES, LANES)
    own, table, later, send_local, recv_wide = pl.pallas_call(
        begin_kernel,
        in_specs=[hold, across, hold, hold],
        out_specs=[hold, across, across, hold, hold],
        out_shape=[
            jax.ShapeDtypeStruct((rows, width), LOW),
            jax.ShapeDtypeStruct((3, 4, rows, width), LOW),
            jax.ShapeDtypeStruct((devices, channels, rows), later.dtype),
            jax.ShapeDtypeStruct(lines, jnp.int32),
            jax.ShapeDtypeStruct(lines, jnp.int32),
        ],
        scratch_shapes=[
            pltpu.VMEM(later.shape, later.dtype),
            pltpu.SemaphoreType.DMA,
            pltpu.SemaphoreType.DMA((devices,)),
            *spread_scratch(),
            *scatter_scratch(channels, rows, devices),
        ],
        compiler_params=pltpu.CompilerParams(
            collective_id=collective, has_side_effects=True, vmem_limit_bytes=VMEM_BYTES
        ),
        name="begin_rows",
    )(shard, later, senders.reshape(lines), receivers.reshape(lines))
    return own, table.reshape(12 * rows, width), later, send_local, recv_wide


def release_kernel(count, *refs):
    for source, target in zip(refs[:count], refs[count:]):
        target[...] = source[...].astype(target.dtype)


def release(whole, reduced):
    arrays = [*whole, *reduced]
    steps = 2

    def spec(item, kept):
        rows, columns = item.shape
        if kept:
            return pl.BlockSpec((rows, columns // steps), lambda i: (0, i))
        return pl.BlockSpec((rows // steps, columns), lambda i: (i, 0))

    specs = [spec(item, i < len(whole)) for i, item in enumerate(arrays)]
    return pl.pallas_call(
        functools.partial(release_kernel, len(arrays)),
        grid=(steps,),
        in_specs=specs,
        out_specs=specs,
        out_shape=[jax.ShapeDtypeStruct(item.shape, WIDE) for item in arrays],
        compiler_params=pltpu.CompilerParams(vmem_limit_bytes=VMEM_BYTES),
        name="release_results",
    )(*arrays)


def shards(
    node_input,
    edge_input,
    senders,
    receivers,
    edge_count,
    edge_w_one,
    edge_b_one,
    edge_w_two,
    edge_b_two,
    edge_gain,
    edge_shift,
    node_w_one,
    node_b_one,
    node_w_two,
    node_b_two,
    node_gain,
    node_shift,
    node_cotangent,
    edge_cotangent,
):
    groups = lax.axis_size("blk")
    sub_count = lax.axis_size("sub")
    width = edge_input.shape[1]
    per_device = node_input.shape[1] // (groups * sub_count)
    node_low, wide_low, cotangent_later, send_local, recv_wide = begin(
        node_input, node_cotangent, senders, receivers, per_device, 0
    )
    node_upstream = lax.all_to_all(
        cotangent_later, ("blk", "sub"), split_axis=0, concat_axis=0, tiled=True
    ).reshape(width, per_device)
    recv_list = recv_wide.reshape(-1)
    edge_result, first_pre, second_pre, received, messages = edge_forward(
        edge_count, recv_list, send_local, edge_input, wide_low, node_low,
        edge_w_one, edge_b_one[None], edge_w_two, edge_b_two[None], edge_gain[None], edge_shift[None],
    )
    wide_grad, node_part, node_out, node_grads, node_vectors = middle(
        recv_list, messages, node_low, node_upstream, node_w_one, node_b_one[None], node_w_two, node_b_two[None],
        node_gain[None], node_shift[None], node_input, 1,
    )
    edge_grad, messages, edge_grads, vectors, node_part = edge_backward(
        edge_count, recv_list, send_local, edge_cotangent, edge_input, received, first_pre, second_pre,
        wide_grad, node_part, node_vectors, node_low, edge_w_one, edge_w_two, edge_gain[None],
    )
    node_grad, *summed, vectors = finish(
        recv_list, messages, edge_grads, node_grads, vectors, node_part, edge_w_one, node_cotangent, 3
    )
    node_out, node_grad, *summed = release((node_out, node_grad), summed)
    return (
        node_out,
        edge_result,
        node_grad,
        edge_grad,
        summed[0],
        vectors[0],
        summed[1],
        vectors[1],
        vectors[2],
        vectors[3],
        summed[2],
        vectors[4],
        summed[3],
        vectors[5],
        vectors[6],
        vectors[7],
    )


def solution(mesh):
    placed = (
        P(("blk", "sub"), None),
        P(("blk", "sub"), None),
        P(("blk", "sub")),
        P(("blk", "sub")),
        P(("blk", "sub")),
        P(),
        P(),
        P(),
        P(),
        P(),
        P(),
        P(),
        P(),
        P(),
        P(),
        P(),
        P(),
        P(("blk", "sub"), None),
        P(("blk", "sub"), None),
    )
    return jax.shard_map(
        shards,
        mesh=mesh,
        in_specs=placed,
        out_specs=(
            P(("blk", "sub"), None),
            P(("blk", "sub"), None),
            P(("blk", "sub"), None),
            P(("blk", "sub"), None),
            P(),
            P(),
            P(),
            P(),
            P(),
            P(),
            P(),
            P(),
            P(),
            P(),
            P(),
            P(),
        ),
        check_vma=False,
    )
```

```python
import functools
import math

import jax
import jax.numpy as jnp
from jax import lax
from jax.experimental import pallas as pl
from jax.experimental.pallas import tpu as pltpu
from jax.sharding import PartitionSpec as P

EPSILON = 1e-05


TILE = 512
CHUNK = 512
LANES = 128
SPARE = 8
VMEM_BYTES = 60 * 2**20


def dot(left, right):
    return jnp.dot(left, right, preferred_element_type=jnp.float32)


def dot_left(left, right):
    return lax.dot_general(
        left, right, (((0,), (0,)), ((), ())), preferred_element_type=jnp.float32
    )


def dot_right(left, right):
    return lax.dot_general(
        left, right, (((1,), (1,)), ((), ())), preferred_element_type=jnp.float32
    )


def split_low(values):
    high = values.astype(jnp.bfloat16)
    return high, (values - high.astype(jnp.float32)).astype(jnp.bfloat16)


def lay_rows(target, start, values):
    count, width = values.shape
    parts = width // LANES
    for j in range(parts):
        target[pl.ds(start * parts + j, count, stride=parts), :] = values[:, j * LANES : (j + 1) * LANES]


def read_rows(source, start, count, parts):
    return jnp.concatenate(
        [source[pl.ds(start * parts + j, count, stride=parts), :] for j in range(parts)], axis=1
    )


def load_table(wide, table, stage, sems):
    steps = wide.shape[0] // CHUNK

    def fetch(i, slot):
        return pltpu.make_async_copy(wide.at[pl.ds(i * CHUNK, CHUNK)], stage.at[slot], sems.at[slot])

    for i in range(3):
        fetch(i, i).start()

    def body(i, carry):
        slot = lax.rem(i, 4)

        @pl.when(i + 3 < steps)
        def _():
            fetch(i + 3, lax.rem(i + 3, 4)).start()

        fetch(i, slot).wait()

        def piece(k, carry):
            values = stage[slot, pl.ds(k * 64, 64), :].astype(jnp.float32)
            lay_rows(table, i * CHUNK + k * 64, values)
            return carry

        return lax.fori_loop(0, CHUNK // 64, piece, carry)

    lax.fori_loop(0, steps, body, 0)


def gather_rows(index, base, table, rows, parts):
    def body(i, carry):
        for u in range(16):
            slot = i * 16 + u
            place = index[base + slot]
            rows[pl.ds(pl.multiple_of(slot * parts, parts), parts), :] = table[
                pl.ds(pl.multiple_of(place * parts, parts), parts), :
            ]
        return carry

    lax.fori_loop(0, TILE // 16, body, 0)


def gather_inline(index, base, table, rows, parts):
    for slot in range(TILE):
        place = index[base + slot]
        rows[slot * parts : (slot + 1) * parts, :] = table[pl.ds(pl.multiple_of(place * parts, parts), parts), :]


def row_normal(values):
    average = jnp.mean(values, -1, keepdims=True)
    centred = values - average
    variance = jnp.mean(centred * centred, -1, keepdims=True)
    scale = lax.rsqrt(variance + EPSILON)
    return centred * scale, scale


def forward_kernel(
    count, recv, send, edge, wide, nodes, w_one, b_one, w_two, b_two, gain, shift,
    result, first, second, received, message,
    table, rows, stage, sems,
):
    step = pl.program_id(0)
    base = step * TILE
    width = nodes.shape[1]
    parts = width // LANES

    @pl.when(step == 0)
    def _():
        load_table(wide, table, stage, sems)
        gather_rows(recv, base, table, rows, parts)

    later = jnp.where(step + 1 < pl.num_programs(0), base + TILE, 0)
    received[...] = read_rows(rows, 0, TILE, parts).astype(jnp.bfloat16)
    gather_inline(recv, later, table, rows, parts)
    from_recv = received[...]
    lane = lax.broadcasted_iota(jnp.int32, (LANES, LANES), 1)
    chosen = []
    for i in range(TILE // LANES):
        column = jnp.broadcast_to(send[pl.ds(step * (TILE // LANES) + i, 1), :], (LANES, LANES)).T
        chosen.append(
            jnp.concatenate(
                [
                    jnp.where(column == lane + j * LANES, 1.0, 0.0).astype(jnp.bfloat16)
                    for j in range(nodes.shape[0] // LANES)
                ],
                axis=1,
            )
        )
    chosen = jnp.concatenate(chosen, axis=0)
    from_send = dot(chosen, nodes[...]).astype(jnp.bfloat16)
    pre = (
        dot(edge[...], w_one[:width])
        + dot(from_send, w_one[width : 2 * width])
        + dot(from_recv, w_one[2 * width :])
        + b_one[...]
    )
    first[...] = pre
    act = (pre * jax.nn.sigmoid(pre)).astype(jnp.bfloat16)
    post = dot(act, w_two[...]) + b_two[...]
    second[...] = post
    normal, _ = row_normal(post)
    branch = normal * gain[...] + shift[...]
    live = base + lax.broadcasted_iota(jnp.int32, (TILE, 1), 0) < count[0]
    outcome = edge[...].astype(jnp.float32) + jnp.where(live, branch, 0.0)
    result[...] = outcome
    message[...] = jnp.where(live, outcome, 0.0).astype(jnp.bfloat16)


def edge_forward(count, recv, send, edge, wide, nodes, w_one, b_one, w_two, b_two, gain, shift):
    edges, width = edge.shape
    steps = edges // TILE
    parts = width // LANES
    hold = pl.BlockSpec(memory_space=pltpu.VMEM)
    scalar = pl.BlockSpec(memory_space=pltpu.SMEM)
    tile = pl.BlockSpec((TILE, width), lambda i: (i, 0))
    return pl.pallas_call(
        forward_kernel,
        grid=(steps,),
        in_specs=[
            scalar, scalar, hold, tile,
            pl.BlockSpec(memory_space=pl.ANY), hold, hold, hold, hold, hold, hold, hold,
        ],
        out_specs=[tile] * 5,
        out_shape=[
            jax.ShapeDtypeStruct((edges, width), jnp.float32),
            jax.ShapeDtypeStruct((edges, width), jnp.float32),
            jax.ShapeDtypeStruct((edges, width), jnp.float32),
            jax.ShapeDtypeStruct((edges, width), jnp.bfloat16),
            jax.ShapeDtypeStruct((edges, width), jnp.bfloat16),
        ],
        scratch_shapes=[
            pltpu.VMEM((wide.shape[0] * parts + SPARE, LANES), jnp.float32),
            pltpu.VMEM((TILE * parts + SPARE, LANES), jnp.float32),
            pltpu.VMEM((4, CHUNK, width), jnp.bfloat16),
            pltpu.SemaphoreType.DMA((4,)),
        ],
        compiler_params=pltpu.CompilerParams(vmem_limit_bytes=VMEM_BYTES),
        cost_estimate=pl.CostEstimate(
            flops=20 * edges * width * width, bytes_accessed=40 * edges * width, transcendentals=2 * edges * width
        ),
        name="edge_forward",
    )(count, recv, send, edge, wide, nodes, w_one, b_one, w_two, b_two, gain, shift)


def backward_kernel(
    count, recv, send, cotangent, edge, received, first, second, wide, node_part, node_vectors, nodes, w_one, w_two, gain,
    grad, message, all_grads, vectors, sender_grad,
    table, rows, stage, sems, by_sender, grads, give_sem,
):
    step = pl.program_id(0)
    base = step * TILE
    width = nodes.shape[1]
    parts = width // LANES

    @pl.when(step == 0)
    def _():
        load_table(wide, table, stage, sems)
        grads[...] = jnp.zeros_like(grads)
        vectors[...] = node_vectors[...]
        by_sender[...] = jnp.zeros_like(by_sender)
        gather_rows(recv, base, table, rows, parts)

    live = base + lax.broadcasted_iota(jnp.int32, (TILE, 1), 0) < count[0]
    upstream = cotangent[...].astype(jnp.float32) + jnp.where(live, read_rows(rows, 0, TILE, parts), 0.0)
    grad[...] = upstream
    later = jnp.where(step + 1 < pl.num_programs(0), base + TILE, 0)
    gather_inline(recv, later, table, rows, parts)
    masked = jnp.where(live, upstream, 0.0)
    normal, scale = row_normal(second[...])
    vectors[2:3, :] += jnp.sum(masked * normal, 0, keepdims=True)
    vectors[3:4, :] += jnp.sum(masked, 0, keepdims=True)
    scaled = masked * gain[...]
    slope = jnp.mean(scaled * normal, -1, keepdims=True)
    grad_second = scale * (scaled - jnp.mean(scaled, -1, keepdims=True) - normal * slope)
    second_low = grad_second.astype(jnp.bfloat16)
    vectors[1:2, :] += jnp.sum(second_low.astype(jnp.float32), 0, keepdims=True)
    pre = first[...]
    logistic = jax.nn.sigmoid(pre)
    act = (pre * logistic).astype(jnp.bfloat16)
    grads[3 * width : 4 * width] += dot_left(act, second_low)
    grad_first = dot_right(second_low, w_two[...]) * (logistic * (1.0 + pre * (1.0 - logistic)))
    first_low = grad_first.astype(jnp.bfloat16)
    message[...] = first_low
    grads[:width] += dot_left(edge[...], first_low)
    grads[2 * width : 3 * width] += dot_left(received[...], first_low)
    node = lax.broadcasted_iota(jnp.int32, (nodes.shape[0], LANES), 0)
    chosen = jnp.concatenate(
        [
            jnp.where(node == send[pl.ds(step * (TILE // LANES) + i, 1), :], 1.0, 0.0).astype(jnp.bfloat16)
            for i in range(TILE // LANES)
        ],
        axis=1,
    )
    by_sender[...] += dot(chosen, first_low)
    grad[...] += dot_right(first_low, w_one[:width])

    @pl.when(step == pl.num_programs(0) - 1)
    def _():
        vectors[0:1, :] = jnp.sum(by_sender[...], 0, keepdims=True)
        high, rest = split_low(by_sender[...])
        grads[width : 2 * width] = dot_left(nodes[...], high) + dot_left(nodes[...], rest)
        give = pltpu.make_async_copy(grads, all_grads, give_sem)
        give.start()
        middle = w_one[width : 2 * width]
        sender_grad[...] = node_part[...] + dot_right(high, middle) + dot_right(rest, middle)
        give.wait()


def edge_backward(
    count, recv, send, cotangent, edge, received, first, second, wide, node_part, node_vectors, nodes,
    w_one, w_two, gain,
):
    edges, width = edge.shape
    steps = edges // TILE
    parts = width // LANES
    per_device = nodes.shape[0]
    hold = pl.BlockSpec(memory_space=pltpu.VMEM)
    scalar = pl.BlockSpec(memory_space=pltpu.SMEM)
    tile = pl.BlockSpec((TILE, width), lambda i: (i, 0))

    across = pl.BlockSpec(memory_space=pl.ANY)

    def whole(rows):
        return pl.BlockSpec((rows, width), lambda i: (0, 0))

    return pl.pallas_call(
        backward_kernel,
        grid=(steps,),
        in_specs=[
            scalar, scalar, hold, tile, tile, tile, tile, tile,
            across, hold, hold, hold, hold, hold, hold,
        ],
        out_specs=[
            tile, tile, across, whole(8), whole(per_device),
        ],
        out_shape=[
            jax.ShapeDtypeStruct((edges, width), jnp.float32),
            jax.ShapeDtypeStruct((edges, width), jnp.bfloat16),
            jax.ShapeDtypeStruct((4 * width, width), jnp.float32),
            jax.ShapeDtypeStruct((8, width), jnp.float32),
            jax.ShapeDtypeStruct((per_device, width), jnp.float32),
        ],
        scratch_shapes=[
            pltpu.VMEM((wide.shape[0] * parts + SPARE, LANES), jnp.float32),
            pltpu.VMEM((TILE * parts + SPARE, LANES), jnp.float32),
            pltpu.VMEM((4, CHUNK, width), jnp.bfloat16),
            pltpu.SemaphoreType.DMA((4,)),
            pltpu.VMEM((per_device, width), jnp.float32),
            pltpu.VMEM((4 * width, width), jnp.float32),
            pltpu.SemaphoreType.DMA,
        ],
        compiler_params=pltpu.CompilerParams(vmem_limit_bytes=VMEM_BYTES),
        cost_estimate=pl.CostEstimate(
            flops=24 * edges * width * width, bytes_accessed=40 * edges * width, transcendentals=2 * edges * width
        ),
        name="edge_backward",
    )(
        count, recv, send, cotangent, edge, received, first, second, wide,
        node_part, node_vectors, nodes, w_one, w_two, gain,
    )


MESH = pl.DeviceIdType.MESH
PIECES = 4
SPLIT = True
LOW = jnp.bfloat16
WIDE = jnp.float32


def places():
    groups = lax.axis_size("blk")
    group, sub = lax.axis_index("blk"), lax.axis_index("sub")
    odd = lax.rem(group, 2)
    along = groups // 2
    spot = group // 2
    beside = group + 1 - 2 * odd
    return dict(
        group=group,
        sub=sub,
        core=lax.rem(sub, 2),
        chip=sub // 2,
        odd=odd,
        spot=spot,
        along=along,
        sibling=sub + 1 - 2 * lax.rem(sub, 2),
        partner=lax.rem(sub + 2, 4),
        to_sibling=(group, sub + 1 - 2 * lax.rem(sub, 2)),
        to_partner=(group, lax.rem(sub + 2, 4)),
        to_beside=(beside, sub),
        to_onward=(lax.rem(group + 2 - 4 * odd + groups, groups), sub),
        to_source=(lax.rem(group - 2 + 4 * odd + groups, groups), sub),
        peers=[(2 * lax.rem(spot + k, along) + odd, sub) for k in range(1, along)],
        near=2 - 2 * odd,
        far=2 * odd,
    )


def meet(senders):
    barrier = pltpu.get_barrier_semaphore()
    for device in senders:
        pl.semaphore_signal(barrier, inc=1, device_id=device, device_id_type=MESH)
    pl.semaphore_wait(barrier, len(senders))


def meet_all():
    barrier = pltpu.get_barrier_semaphore()
    subs = lax.axis_size("sub")
    devices = lax.axis_size("blk") * subs
    here = lax.axis_index("blk") * subs + lax.axis_index("sub")

    def greet(k, carry):
        there = lax.rem(here + k, devices)
        pl.semaphore_signal(barrier, inc=1, device_id=(there // subs, lax.rem(there, subs)), device_id_type=MESH)
        return carry

    lax.fori_loop(1, devices, greet, 0)
    pl.semaphore_wait(barrier, devices - 1)


def remote(source, target, send, recv, device):
    return pltpu.make_async_remote_copy(
        src_ref=source, dst_ref=target, send_sem=send, recv_sem=recv, device_id=device, device_id_type=MESH
    )


def in_pieces(count, body):
    block = math.gcd(count, 128)

    def run(i, carry):
        body(pl.multiple_of(i * block, block), block)
        return carry

    lax.fori_loop(0, count // block, run, 0)


def padded_rows(rows):
    unit = 64 * lax.axis_size("blk")
    return -(-rows // unit) * unit


def streams_of(sources):
    unit = 64 * lax.axis_size("blk")
    streams = []
    for i, rows in enumerate(sources):
        first = -(-(rows // unit) // 2) * unit if SPLIT else rows
        streams.append((i, 0, first))
        if first < rows:
            streams.append((i, first, rows - first))
    return streams


def reducers_scratch(sources, width, along):
    return [ref for _, _, rows in streams_of(sources) for ref in reducer_scratch(rows, width, along)]


def reducers(at, sources, reduced, refs):
    made = []
    for i, (which, start, rows) in enumerate(streams_of([source.shape[0] for source in sources])):
        first = start + sum(source.shape[0] for source in sources[:which])
        made.append(reducer(at, sources[which], start, reduced, first, rows, i % 2 > 0, refs[i * 13 : i * 13 + 13]))
    return made, refs[len(made) * 13 :]


def reducer_scratch(rows, width, along):
    return [
        pltpu.VMEM((rows // 2, width), WIDE),
        pltpu.VMEM((rows // 2, width), WIDE),
        pltpu.VMEM((rows // 4, width), LOW),
        pltpu.VMEM((rows // 4, width), LOW),
        pltpu.VMEM((rows // 8, width), LOW),
        pltpu.VMEM((rows // 8, width), LOW),
        pltpu.VMEM((rows // 8, width), LOW),
        pltpu.VMEM((along - 1, rows // 8 // along, width), LOW),
        pltpu.SemaphoreType.DMA,
        pltpu.SemaphoreType.DMA((6,)),
        pltpu.SemaphoreType.DMA((6,)),
        pltpu.SemaphoreType.DMA((2, along - 1)),
        pltpu.SemaphoreType.DMA((2, along - 1)),
    ]


def reducer(at, grads, source_first, reduced, first, rows, swap, refs):
    (
        half, half_in, cross_out, cross_in, side_out, side_in, ring_out, ring_in,
        load_sem, step_send, step_recv, ring_send, ring_recv,
    ) = refs
    along, peers = at["along"], at["peers"]
    turns = [(at["chip"], at["to_partner"]), (at["odd"], at["to_beside"])]
    (bit_one, device_one), (bit_two, device_two) = turns[::-1] if swap else turns
    core, spot = at["core"], at["spot"]
    n_half, n_cross, n_side, n_ring = rows // 2, rows // 4, rows // 8, rows // 8 // along
    at_half = first + core * n_half
    at_cross = at_half + bit_one * n_cross
    at_side = at_cross + bit_two * n_side
    at_ring = at_side + spot * n_ring

    def span(start, count):
        return pl.ds(pl.multiple_of(start, 16), count)

    def step(kind):
        if kind == 0:
            other = span(source_first + (1 - core) * n_half, n_half)
            source, target, device = grads.at[other], half_in, at["to_sibling"]
        elif kind == 1:
            source, target, device = cross_out, cross_in, device_one
        elif kind == 2:
            source, target, device = side_out, side_in, device_two
        else:
            start, count, device = {
                3: (at_side, n_side, device_two),
                4: (at_cross, n_cross, device_one),
                5: (at_half, n_half, at["to_sibling"]),
            }[kind]
            source = target = reduced.at[span(start, count)]
        return remote(source, target, step_send.at[kind], step_recv.at[kind], device)

    def ring(kind, k):
        if kind == 0:
            source = ring_out.at[span(lax.rem(spot + k, along) * n_ring, n_ring)]
            target = ring_in.at[k - 1]
        else:
            source = target = reduced.at[span(at_ring, n_ring)]
        return remote(source, target, ring_send.at[kind, k - 1], ring_recv.at[kind, k - 1], peers[k - 1])

    load = pltpu.make_async_copy(grads.at[span(source_first + core * n_half, n_half)], half, load_sem)

    def start():
        step(0).start()
        load.start()

    def add_half():
        load.wait()
        step(0).wait_recv()
        other = (1 - bit_one) * n_cross

        def part(i, block):
            here = pl.ds(pl.multiple_of(other + i, block), block)
            cross_out[pl.ds(i, block), :] = (half[here, :] + half_in[here, :]).astype(LOW)

        in_pieces(n_cross, part)
        step(1).start()

    def add_cross():
        mine, other = bit_one * n_cross, (1 - bit_two) * n_side
        step(1).wait_recv()

        def part(i, block):
            there = pl.ds(pl.multiple_of(other + i, block), block)
            here = pl.ds(pl.multiple_of(mine + other + i, block), block)
            side_out[pl.ds(i, block), :] = (half[here, :] + half_in[here, :] + cross_in[there, :].astype(WIDE)).astype(LOW)

        in_pieces(n_side, part)
        step(2).start()

    def add_side():
        mine, kept = bit_one * n_cross, bit_two * n_side
        step(2).wait_recv()

        def part(i, block):
            there = pl.ds(pl.multiple_of(kept + i, block), block)
            here = pl.ds(pl.multiple_of(mine + kept + i, block), block)
            flat = pl.ds(i, block)
            value = half[here, :] + half_in[here, :] + cross_in[there, :].astype(WIDE) + side_in[flat, :].astype(WIDE)
            half[here, :] = value
            ring_out[flat, :] = value.astype(LOW)

        in_pieces(n_side, part)
        for k in range(1, along):
            ring(0, k).start()

    def add_ring():
        value = half[span(bit_one * n_cross + bit_two * n_side + spot * n_ring, n_ring), :]
        for k in range(1, along):
            ring(0, k).wait_recv()
            value = value + ring_in[k - 1].astype(WIDE)
        reduced[span(at_ring, n_ring), :] = value.astype(LOW)
        for k in range(1, along):
            ring(1, k).start()

    def share_side():
        for k in range(1, along):
            ring(1, k).wait_recv()
        step(3).start()

    def share_cross():
        step(3).wait_recv()
        step(4).start()

    def share_half():
        step(4).wait_recv()
        step(5).start()

    def last():
        step(5).wait_recv()

    def drain():
        for kind in range(6):
            step(kind).wait_send()
        for k in range(1, along):
            ring(0, k).wait_send()
            ring(1, k).wait_send()

    return [start, add_half, add_cross, add_side, add_ring, share_side, share_cross, share_half, last, drain]


def vector_scratch(shape, along):
    return [
        pltpu.VMEM((4, *shape), WIDE),
        pltpu.VMEM((2 + along, *shape), WIDE),
        pltpu.SemaphoreType.DMA((2 + along,)),
        pltpu.SemaphoreType.DMA((2 + along,)),
    ]


def vector_reducer(at, vectors, reduced, refs):
    held, held_in, send_sems, recv_sems = refs
    along = at["along"]
    devices = (at["to_sibling"], at["to_partner"], at["to_beside"], *at["peers"])

    def move(kind):
        return remote(held.at[min(kind, 3)], held_in.at[kind], send_sems.at[kind], recv_sems.at[kind], devices[kind])

    def start():
        held[0] = vectors[...]
        move(0).start()

    def turn(kind):
        def run():
            move(kind).wait_recv()
            held[kind + 1] = held[kind] + held_in[kind]
            for k in range(kind + 1, kind + 2 if kind < 2 else 2 + along):
                move(k).start()

        return run

    def last():
        value = held[3]
        for k in range(3, 2 + along):
            move(k).wait_recv()
            value = value + held_in[k]
        reduced[...] = value
        for k in range(2 + along):
            move(k).wait_send()

    return [start, turn(0), turn(1), turn(2), last]


def spread_moves(at, own, table, keep_sem, send_sems, recv_sems):
    sub, partner, near, far = at["sub"], at["partner"], at["near"], at["far"]
    to_sibling, to_partner, to_beside, to_onward = (
        at["to_sibling"], at["to_partner"], at["to_beside"], at["to_onward"]
    )
    size = own.shape[0] // PIECES

    def move(kind, piece):
        source, slot, device = {
            0: (None, (1, sub), to_partner),
            1: (None, (far, sub), to_beside),
            2: (None, (1, sub), to_sibling),
            3: ((1, partner), (far, partner), to_beside),
            4: ((1, partner), (1, partner), to_sibling),
            5: ((near, sub), (far, sub), to_onward),
            6: ((near, sub), (near, sub), to_sibling),
            7: ((near, partner), (far, partner), to_onward),
            8: ((near, partner), (near, partner), to_sibling),
            9: ((far, sub), (far, sub), to_sibling),
            10: ((far, partner), (far, partner), to_sibling),
            11: ((near, sub), (near, sub), to_partner),
            12: ((far, sub), (far, sub), to_partner),
        }[kind]
        source = own if source is None else table.at[source[0], source[1]]
        rows = pl.ds(piece * size, size)
        return remote(
            source.at[rows], table.at[slot[0], slot[1], rows],
            send_sems.at[kind, piece], recv_sems.at[kind, piece], device,
        )

    keep = pltpu.make_async_copy(own, table.at[1, sub], keep_sem)

    def start():
        for piece in range(PIECES):
            for kind in (0, 1, 2):
                move(kind, piece).start()
        keep.start()

    def relay(arrived, kinds, piece):
        move(arrived, piece).wait_recv()
        for kind in kinds:
            move(kind, piece).start()

    straight = range(PIECES - 2)

    def one(piece):
        relay(0, (3, 4) if piece in straight else (4,), piece)
        relay(1, (5, 6) if piece in straight else (5, 6, 11), piece)

    def two(piece):
        if piece in straight:
            relay(3, (7, 8), piece)
            relay(5, (9,), piece)
        else:
            relay(5, (9, 12), piece)
            relay(11, (8,), piece)

    def three(piece):
        if piece in straight:
            relay(7, (10,), piece)
        else:
            relay(12, (10,), piece)

    def drain():
        for kind in range(13):
            for piece in range(PIECES):
                if kind in ((11, 12) if piece in straight else (3, 7)):
                    continue
                if kind in (2, 4, 6, 8, 9, 10):
                    move(kind, piece).wait_recv()
                move(kind, piece).wait_send()
        keep.wait()

    return start, one, two, three, drain


def spread_scratch():
    return [
        pltpu.SemaphoreType.DMA,
        pltpu.SemaphoreType.DMA((13, PIECES)),
        pltpu.SemaphoreType.DMA((13, PIECES)),
    ]


HALVES = 2
ORDER = (
    (0, 1, 0), (0, 1, 1), (1, 1, 0), (0, 0, 0), (1, 1, 1), (0, 0, 1),
    (1, 0, 0), (2, 1, 0), (1, 0, 1), (2, 1, 1), (2, 0, 0), (2, 0, 1),
)


def collect_scratch(rows, width, edges):
    return [
        pltpu.VMEM((edges, width), LOW),
        pltpu.VMEM((2, 3, 2, rows, width), WIDE),
        pltpu.VMEM((3, 2, rows, width), WIDE),
        pltpu.VMEM((2, rows, width), LOW),
        pltpu.VMEM((2, rows, width), LOW),
        pltpu.VMEM((2, rows, width), LOW),
        pltpu.VMEM((2, rows, width), LOW),
        pltpu.VMEM((rows, width), LOW),
        pltpu.VMEM((rows, width), LOW),
        pltpu.SemaphoreType.DMA,
        pltpu.SemaphoreType.DMA((3, 2, HALVES)),
        pltpu.SemaphoreType.DMA((3, 2, HALVES)),
        pltpu.SemaphoreType.DMA((5, PIECES)),
        pltpu.SemaphoreType.DMA((5, PIECES)),
    ]


def collect_moves(at, index, messages, out, refs):
    (
        held, parts, landed, far_out, far_in, near_out, near_in, pair_out, pair_in,
        load_sem, give_sems, take_sems, send_sems, recv_sems,
    ) = refs
    sub, partner, sibling = at["sub"], at["partner"], at["sibling"]
    rows = out.shape[0]
    size = rows // PIECES
    part_rows = rows // HALVES
    load = pltpu.make_async_copy(messages, held, load_sem)

    def piece_of(ref, piece):
        return ref.at[pl.ds(piece * size, size)]

    def give(role, side, half):
        span = pl.ds(pl.multiple_of(half * part_rows, part_rows), part_rows)
        return remote(
            parts.at[0, role, side, span], landed.at[role, side, span],
            give_sems.at[role, side, half], take_sems.at[role, side, half], at["to_sibling"],
        )

    def hop(kind, piece):
        source, target, device = {
            0: (far_out.at[0], far_in.at[0], at["to_source"]),
            1: (far_out.at[1], far_in.at[1], at["to_source"]),
            2: (near_out.at[0], near_in.at[0], at["to_beside"]),
            3: (near_out.at[1], near_in.at[1], at["to_beside"]),
            4: (pair_out, pair_in, at["to_partner"]),
        }[kind]
        return remote(
            piece_of(source, piece), piece_of(target, piece),
            send_sems.at[kind, piece], recv_sems.at[kind, piece], device,
        )

    def add_messages(step):
        def pick(column):
            return lax.rem(sum(int(item[column]) << (2 * i) for i, item in enumerate(ORDER)) >> (2 * step), 4)

        role, side, half = pick(0), pick(1), pick(2)
        relation = jnp.where(role == 0, at["far"], jnp.where(role == 1, at["near"], 1))
        span = pl.ds(pl.multiple_of(half * part_rows, part_rows), part_rows)

        def whose(w, carry):
            first = jnp.where(w == 0, sibling, sub)
            target = lax.rem(first + 2 * side, 4)
            base = (relation * 4 + target) * rows + half * part_rows
            node = lax.broadcasted_iota(jnp.int32, (part_rows, LANES), 0) + base
            chosen = jnp.concatenate(
                [jnp.where(node == index[j : j + 1, :], 1.0, 0.0).astype(LOW) for j in range(index.shape[0])], axis=1
            )
            parts[w, role, side, span, :] = dot(chosen, held[...])
            return carry

        lax.fori_loop(0, 2, whose, 0)
        give(role, side, half).start()

    def local(role, side, piece):
        span = pl.ds(piece * size, size)
        return parts[1, role, side, span, :] + landed[role, side, span, :]

    def arrived(kind, ref, piece):
        hop(kind, piece).wait_recv()
        return ref[pl.ds(piece * size, size), :].astype(WIDE)

    def pieces(half):
        return range(half * PIECES // HALVES, (half + 1) * PIECES // HALVES)

    def far_step(side, half):
        give(0, side, half).wait_recv()
        for piece in pieces(half):
            far_out[side, pl.ds(piece * size, size), :] = local(0, side, piece).astype(LOW)
            hop(side, piece).start()

    def near_step(side, half):
        give(1, side, half).wait_recv()
        for piece in pieces(half):
            value = local(1, side, piece) + arrived(side, far_in.at[side], piece)
            near_out[side, pl.ds(piece * size, size), :] = value.astype(LOW)
            hop(2 + side, piece).start()

    def pair_step(half):
        give(2, 1, half).wait_recv()
        for piece in pieces(half):
            value = local(2, 1, piece) + arrived(3, near_in.at[1], piece)
            pair_out[pl.ds(piece * size, size), :] = value.astype(LOW)
            hop(4, piece).start()

    def last_step(half):
        give(2, 0, half).wait_recv()
        for piece in pieces(half):
            value = local(2, 0, piece) + arrived(2, near_in.at[0], piece) + arrived(4, pair_in, piece)
            out[pl.ds(piece * size, size), :] = value

    def drain():
        for item in ORDER:
            give(*item).wait_send()
        for kind in range(5):
            for piece in range(PIECES):
                hop(kind, piece).wait_send()

    events = {
        1: [lambda: far_step(1, 0)],
        2: [lambda: far_step(1, 1)],
        3: [lambda: near_step(1, 0)],
        4: [lambda: far_step(0, 0)],
        5: [lambda: near_step(1, 1), lambda: far_step(0, 1)],
        7: [lambda: near_step(0, 0), lambda: pair_step(0)],
        9: [lambda: near_step(0, 1), lambda: pair_step(1)],
    }

    def run(more):
        def step(i, carry):
            add_messages(i)
            for k in sorted(set(events) | set(more)):
                @pl.when(i == k)
                def _():
                    for event in events.get(k, []) + more.get(k, []):
                        event()

            return carry

        lax.fori_loop(0, len(ORDER), step, 0)
        for half in range(HALVES):
            last_step(half)

    return load, run, drain


def exchange_scratch(rows, width, devices):
    slab = width // devices * (rows // LANES)
    return [
        pltpu.VMEM((devices * slab, LANES), WIDE),
        pltpu.VMEM((devices * slab, LANES), LOW),
        pltpu.VMEM((devices, slab, LANES), LOW),
        pltpu.VMEM((slab, LANES), WIDE),
        pltpu.SemaphoreType.DMA((devices - 1,)),
        pltpu.SemaphoreType.DMA((devices - 1,)),
    ]


def exchange_moves(residual, out, refs):
    flat, packed, landed, opened, send_sems, recv_sems = refs
    subs = lax.axis_size("sub")
    devices = lax.axis_size("blk") * subs
    here = lax.axis_index("blk") * subs + lax.axis_index("sub")
    slab = landed.shape[1]
    channels = out.shape[0]
    parts = slab // channels
    nodes = parts * LANES

    def move(k):
        there = lax.rem(here + k, devices)
        return remote(
            packed.at[pl.ds(pl.multiple_of(there * slab, slab), slab)], landed.at[here],
            send_sems.at[k - 1], recv_sems.at[k - 1], (there // subs, lax.rem(there, subs)),
        )

    def start(values):
        lay_rows(flat, 0, values.T)

        def cast(i, block):
            packed[pl.ds(i, block), :] = flat[pl.ds(i, block), :].astype(LOW)

        in_pieces(flat.shape[0], cast)

        def send(k, carry):
            move(k).start()
            return carry

        lax.fori_loop(1, devices, send, 0)

    def open_slab(source, device):
        opened[...] = source.astype(WIDE)
        for j in range(parts):
            columns = pl.ds(pl.multiple_of(device * nodes + j * LANES, LANES), LANES)
            out[:, columns] = residual[:, columns] + opened[pl.ds(j, channels, stride=parts), :]

    def last():
        open_slab(packed[pl.ds(pl.multiple_of(here * slab, slab), slab), :], here)

        def take(k, carry):
            move(k).wait_recv()
            device = lax.rem(here - k + devices, devices)
            open_slab(landed[device], device)
            return carry

        lax.fori_loop(1, devices, take, 0)

        def sent(k, carry):
            move(k).wait_send()
            return carry

        lax.fori_loop(1, devices, sent, 0)

    return start, last


def finish_kernel(
    index, messages, edge_grads, node_grads, vectors, node_part, weight, residual,
    node_grad, one_out, two_out, three_out, four_out, reduced_vectors, total, reduced, out_sems, *refs,
):
    at = places()
    count = len(collect_scratch(64, 128, 64))
    load, run, drain = collect_moves(at, index, messages, total, refs[:count])
    load.start()
    meet_all()
    streams, refs = reducers(at, (edge_grads, node_grads), reduced, refs[count:])
    vector_steps = vector_reducer(at, vectors, reduced_vectors, refs[:4])
    exchange, receive = exchange_moves(residual, node_grad, refs[4:])
    for stream in streams:
        stream[0]()
    vector_steps[0]()
    load.wait()
    timetable = (
        (0, 1, (0,)), (1, 1, (1, 2, 3)), (4, 2, (0, 1)), (6, 2, (3, 2)), (6, 3, (1,)), (7, 3, (0,)), (8, 3, (3, 2)),
        (10, 4, (1, 0)), (11, 4, (3, 2)),
    )
    later = {1: [vector_steps[1]], 4: [vector_steps[2]], 7: [vector_steps[3]]}
    for when, hop, which in timetable:
        later.setdefault(when, []).extend(streams[i][hop] for i in which if i < len(streams))
    run(later)

    def hops(hop, which):
        for i in which:
            if i < len(streams):
                streams[i][hop]()

    hops(5, (1, 0))
    high, rest = split_low(total[...])
    exchange(node_part[...] + dot_right(high, weight[...]) + dot_right(rest, weight[...]))
    hops(5, (3, 2))
    hops(6, (1, 0, 3, 2))
    hops(7, range(4))
    receive()
    hops(8, range(4))
    width = total.shape[1]
    nodes_at = edge_grads.shape[0]
    copies = [
        pltpu.make_async_copy(reduced.at[pl.ds(first, target.shape[0])], target, out_sems.at[i])
        for i, (first, target) in enumerate((
            (0, one_out), (3 * width, two_out), (nodes_at, three_out), (nodes_at + 2 * width, four_out)
        ))
    ]
    for copy in copies:
        copy.start()
    vector_steps[4]()
    drain()
    for stream in streams:
        stream[9]()
    for copy in copies:
        copy.wait()


def finish(index, messages, edge_grads, node_grads, vectors, node_part, weight, residual, collective):
    rows, width = node_part.shape
    edges = messages.shape[0]
    sources = [edge_grads.shape[0], node_grads.shape[0]]
    along = lax.axis_size("blk") // 2
    devices = lax.axis_size("blk") * lax.axis_size("sub")
    hold = pl.BlockSpec(memory_space=pltpu.VMEM)
    across = pl.BlockSpec(memory_space=pl.ANY)
    return pl.pallas_call(
        finish_kernel,
        grid=(1,),
        in_specs=[
            hold, across, across, across, hold, hold, pl.BlockSpec((width, width), lambda i: (2, 0)), hold,
        ],
        out_specs=[hold] + [across] * 4 + [hold],
        out_shape=[
            jax.ShapeDtypeStruct(residual.shape, WIDE),
            jax.ShapeDtypeStruct((3 * width, width), LOW),
            jax.ShapeDtypeStruct((width, width), LOW),
            jax.ShapeDtypeStruct((2 * width, width), LOW),
            jax.ShapeDtypeStruct((width, width), LOW),
            jax.ShapeDtypeStruct(vectors.shape, WIDE),
        ],
        scratch_shapes=[
            pltpu.VMEM((rows, width), WIDE),
            pltpu.VMEM((sum(sources), width), LOW),
            pltpu.SemaphoreType.DMA((4,)),
            *collect_scratch(rows, width, edges),
            *reducers_scratch(sources, width, along),
            *vector_scratch(vectors.shape, along),
            *exchange_scratch(rows, width, devices),
        ],
        compiler_params=pltpu.CompilerParams(
            collective_id=collective, has_side_effects=True, vmem_limit_bytes=VMEM_BYTES
        ),
        name="finish_sums",
    )(index.reshape(edges // LANES, LANES), messages, edge_grads, node_grads, vectors, node_part, weight, residual)


def middle_kernel(
    index, messages, node_low, upstream, w_one, b_one, w_two, b_two, gain, shift, residual,
    table, node_part, node_out, grads, vectors, total, sent, *refs
):
    at = places()
    count = len(collect_scratch(64, 128, 64))
    load, run, drain = collect_moves(at, index, messages, total, refs[:count])
    load.start()
    meet_all()
    refs = refs[count:]
    start, one, two, three, end = spread_moves(at, sent, table, *refs[:3])
    exchange, receive = exchange_moves(residual, node_out, refs[3:])
    load.wait()
    run({})

    width = total.shape[1]
    low = total[...].astype(LOW)
    pre = dot(node_low[...], w_one[:width]) + dot(low, w_one[width:]) + b_one[...]
    logistic = jax.nn.sigmoid(pre)
    act = (pre * logistic).astype(LOW)
    normal, scale = row_normal(dot(act, w_two[...]) + b_two[...])
    given = upstream[...].T
    scaled = given * gain[...]
    slope = jnp.mean(scaled * normal, -1, keepdims=True)
    fourth = scale * (scaled - jnp.mean(scaled, -1, keepdims=True) - normal * slope)
    fourth_low = fourth.astype(LOW)
    third = dot_right(fourth_low, w_two[...]) * (logistic * (1.0 + pre * (1.0 - logistic)))
    third_low = third.astype(LOW)
    sent[...] = dot_right(third_low, w_one[width:]).astype(LOW)
    start()
    grads[:width] = dot_left(node_low[...], third_low)
    grads[width : 2 * width] = dot_left(low, third_low)
    grads[2 * width : 3 * width] = dot_left(act, fourth_low)
    vectors[...] = jnp.zeros_like(vectors)
    vectors[4:5] = jnp.sum(third_low.astype(WIDE), 0, keepdims=True)
    vectors[5:6] = jnp.sum(fourth_low.astype(WIDE), 0, keepdims=True)
    vectors[6:7] = jnp.sum(given * normal, 0, keepdims=True)
    vectors[7:8] = jnp.sum(given, 0, keepdims=True)
    node_part[...] = dot_right(third_low, w_one[:width])
    exchange(normal * gain[...] + shift[...])

    for stage in (one, two, three):
        for piece in range(PIECES):
            stage(piece)
    receive()
    end()
    drain()


def middle(index, messages, node_low, upstream, w_one, b_one, w_two, b_two, gain, shift, residual, collective):
    rows, width = node_low.shape
    edges = messages.shape[0]
    devices = lax.axis_size("blk") * lax.axis_size("sub")
    grad_rows = padded_rows(3 * width)
    hold = pl.BlockSpec(memory_space=pltpu.VMEM)
    across = pl.BlockSpec(memory_space=pl.ANY)
    table, node_part, node_out, grads, vectors = pl.pallas_call(
        middle_kernel,
        in_specs=[hold, across] + [hold] * 9,
        out_specs=[across] + [hold] * 4,
        out_shape=[
            jax.ShapeDtypeStruct((3, 4, rows, width), LOW),
            jax.ShapeDtypeStruct((rows, width), WIDE),
            jax.ShapeDtypeStruct(residual.shape, WIDE),
            jax.ShapeDtypeStruct((grad_rows, width), WIDE),
            jax.ShapeDtypeStruct((8, width), WIDE),
        ],
        scratch_shapes=[
            pltpu.VMEM((rows, width), WIDE),
            pltpu.VMEM((rows, width), LOW),
            *collect_scratch(rows, width, edges),
            *spread_scratch(),
            *exchange_scratch(rows, width, devices),
        ],
        compiler_params=pltpu.CompilerParams(
            collective_id=collective, has_side_effects=True, vmem_limit_bytes=VMEM_BYTES
        ),
        name="middle_nodes",
    )(
        index.reshape(edges // LANES, LANES), messages, node_low, upstream,
        w_one, b_one, w_two, b_two, gain, shift, residual,
    )
    return table.reshape(12 * rows, width), node_part, node_out, grads, vectors


def scatter_scratch(channels, nodes, devices):
    slab = channels * (nodes // LANES)
    return [
        pltpu.VMEM((devices * slab, LANES), WIDE),
        pltpu.VMEM((devices * slab, LANES), LOW),
        pltpu.VMEM((devices, slab, LANES), LOW),
        pltpu.VMEM((slab, LANES), WIDE),
        pltpu.VMEM((nodes // LANES * devices * channels, LANES), WIDE),
        pltpu.SemaphoreType.DMA((devices - 1,)),
        pltpu.SemaphoreType.DMA((devices - 1,)),
    ]


def scatter_moves(shard, refs):
    flat, packed, landed, opened, square, send_sems, recv_sems = refs
    subs = lax.axis_size("sub")
    devices = lax.axis_size("blk") * subs
    here = lax.axis_index("blk") * subs + lax.axis_index("sub")
    slab = landed.shape[1]
    channels = shard.shape[0]
    parts = slab // channels
    nodes = parts * LANES

    def move(k):
        there = lax.rem(here + k, devices)
        return remote(
            packed.at[pl.ds(pl.multiple_of(there * slab, slab), slab)], landed.at[here],
            send_sems.at[k - 1], recv_sems.at[k - 1], (there // subs, lax.rem(there, subs)),
        )

    def start():
        def pack(k, carry):
            device = lax.rem(here + k, devices)
            rows = pl.ds(pl.multiple_of(device * slab, slab), slab)
            for j in range(parts):
                columns = pl.ds(pl.multiple_of(device * nodes + j * LANES, LANES), LANES)
                flat[pl.ds(device * slab + j, channels, stride=parts), :] = shard[:, columns]
            packed[rows, :] = flat[rows, :].astype(LOW)
            return carry

        def send(k, carry):
            pack(k, carry)
            move(k).start()
            return carry

        lax.fori_loop(1, devices, send, 0)
        pack(0, 0)

    def open_slab(source, device):
        opened[...] = source.astype(WIDE)
        for j in range(parts):
            rows = pl.ds(pl.multiple_of((j * devices + device) * channels, channels), channels)
            square[rows, :] = opened[pl.ds(j, channels, stride=parts), :]

    def last(rows):
        open_slab(packed[pl.ds(pl.multiple_of(here * slab, slab), slab), :], here)

        def take(k, carry):
            move(k).wait_recv()
            device = lax.rem(here - k + devices, devices)
            open_slab(landed[device], device)
            return carry

        lax.fori_loop(1, devices, take, 0)
        width = devices * channels
        for j in range(parts):
            rows[j * LANES : (j + 1) * LANES, :] = square[j * width : (j + 1) * width, :].T.astype(LOW)

    def drain():
        def sent(k, carry):
            move(k).wait_send()
            return carry

        lax.fori_loop(1, devices, sent, 0)

    return start, last, drain


def begin_kernel(
    shard, later, senders, receivers, own, table, later_out, send_local, recv_wide, held, held_sem, slab_sems, *refs
):
    at = places()
    fetch = pltpu.make_async_copy(later, held, held_sem)
    fetch.start()
    meet_all()
    start, last, drain = scatter_moves(shard, refs[3:])
    start()
    last(own)
    begin, one, two, three, end = spread_moves(at, own, table, *refs[:3])
    begin()
    rows = own.shape[0]
    groups, subs = lax.axis_size("blk"), lax.axis_size("sub")
    send_local[...] = senders[...] - (at["group"] * subs + at["sub"]) * rows
    relative = lax.rem(receivers[...] // (rows * subs) - at["group"] + 1 + groups, groups)
    recv_wide[...] = relative * (rows * subs) + lax.rem(receivers[...], rows * subs)
    fetch.wait()
    devices, _, nodes = later_out.shape

    def slab(k):
        columns = pl.ds(pl.multiple_of(k * nodes, LANES), nodes)
        return pltpu.make_async_copy(held.at[:, columns], later_out.at[k], slab_sems.at[k])

    def give(k, carry):
        slab(k).start()
        return carry

    def given(k, carry):
        slab(k).wait()
        return carry

    lax.fori_loop(0, devices, give, 0)
    drain()
    for stage in (one, two, three):
        for piece in range(PIECES):
            stage(piece)
    lax.fori_loop(0, devices, given, 0)
    end()


def begin(shard, later, senders, receivers, rows, collective):
    channels, nodes = shard.shape
    devices = lax.axis_size("blk") * lax.axis_size("sub")
    width = channels * devices
    hold = pl.BlockSpec(memory_space=pltpu.VMEM)
    across = pl.BlockSpec(memory_space=pl.ANY)
    lines = (senders.shape[0] // LANES, LANES)
    own, table, later, send_local, recv_wide = pl.pallas_call(
        begin_kernel,
        in_specs=[hold, across, hold, hold],
        out_specs=[hold, across, across, hold, hold],
        out_shape=[
            jax.ShapeDtypeStruct((rows, width), LOW),
            jax.ShapeDtypeStruct((3, 4, rows, width), LOW),
            jax.ShapeDtypeStruct((devices, channels, rows), later.dtype),
            jax.ShapeDtypeStruct(lines, jnp.int32),
            jax.ShapeDtypeStruct(lines, jnp.int32),
        ],
        scratch_shapes=[
            pltpu.VMEM(later.shape, later.dtype),
            pltpu.SemaphoreType.DMA,
            pltpu.SemaphoreType.DMA((devices,)),
            *spread_scratch(),
            *scatter_scratch(channels, rows, devices),
        ],
        compiler_params=pltpu.CompilerParams(
            collective_id=collective, has_side_effects=True, vmem_limit_bytes=VMEM_BYTES
        ),
        name="begin_rows",
    )(shard, later, senders.reshape(lines), receivers.reshape(lines))
    return own, table.reshape(12 * rows, width), later, send_local, recv_wide


def release_kernel(count, *refs):
    for source, target in zip(refs[:count], refs[count:]):
        target[...] = source[...].astype(target.dtype)


def release(whole, reduced):
    arrays = [*whole, *reduced]
    steps = 2

    def spec(item, kept):
        rows, columns = item.shape
        if kept:
            return pl.BlockSpec((rows, columns // steps), lambda i: (0, i))
        return pl.BlockSpec((rows // steps, columns), lambda i: (i, 0))

    specs = [spec(item, i < len(whole)) for i, item in enumerate(arrays)]
    return pl.pallas_call(
        functools.partial(release_kernel, len(arrays)),
        grid=(steps,),
        in_specs=specs,
        out_specs=specs,
        out_shape=[jax.ShapeDtypeStruct(item.shape, WIDE) for item in arrays],
        compiler_params=pltpu.CompilerParams(vmem_limit_bytes=VMEM_BYTES),
        name="release_results",
    )(*arrays)


def shards(
    node_input,
    edge_input,
    senders,
    receivers,
    edge_count,
    edge_w_one,
    edge_b_one,
    edge_w_two,
    edge_b_two,
    edge_gain,
    edge_shift,
    node_w_one,
    node_b_one,
    node_w_two,
    node_b_two,
    node_gain,
    node_shift,
    node_cotangent,
    edge_cotangent,
):
    groups = lax.axis_size("blk")
    sub_count = lax.axis_size("sub")
    width = edge_input.shape[1]
    per_device = node_input.shape[1] // (groups * sub_count)
    node_low, wide_low, cotangent_later, send_local, recv_wide = begin(
        node_input, node_cotangent, senders, receivers, per_device, 0
    )
    node_upstream = lax.all_to_all(
        cotangent_later, ("blk", "sub"), split_axis=0, concat_axis=0, tiled=True
    ).reshape(width, per_device)
    recv_list = recv_wide.reshape(-1)
    edge_result, first_pre, second_pre, received, messages = edge_forward(
        edge_count, recv_list, send_local, edge_input, wide_low, node_low,
        edge_w_one, edge_b_one[None], edge_w_two, edge_b_two[None], edge_gain[None], edge_shift[None],
    )
    wide_grad, node_part, node_out, node_grads, node_vectors = middle(
        recv_list, messages, node_low, node_upstream, node_w_one, node_b_one[None], node_w_two, node_b_two[None],
        node_gain[None], node_shift[None], node_input, 1,
    )
    edge_grad, messages, edge_grads, vectors, node_part = edge_backward(
        edge_count, recv_list, send_local, edge_cotangent, edge_input, received, first_pre, second_pre,
        wide_grad, node_part, node_vectors, node_low, edge_w_one, edge_w_two, edge_gain[None],
    )
    node_grad, *summed, vectors = finish(
        recv_list, messages, edge_grads, node_grads, vectors, node_part, edge_w_one, node_cotangent, 3
    )
    node_out, node_grad, *summed = release((node_out, node_grad), summed)
    return (
        node_out,
        edge_result,
        node_grad,
        edge_grad,
        summed[0],
        vectors[0],
        summed[1],
        vectors[1],
        vectors[2],
        vectors[3],
        summed[2],
        vectors[4],
        summed[3],
        vectors[5],
        vectors[6],
        vectors[7],
    )


def solution(mesh):
    placed = (
        P(("blk", "sub"), None),
        P(("blk", "sub"), None),
        P(("blk", "sub")),
        P(("blk", "sub")),
        P(("blk", "sub")),
        P(),
        P(),
        P(),
        P(),
        P(),
        P(),
        P(),
        P(),
        P(),
        P(),
        P(),
        P(),
        P(("blk", "sub"), None),
        P(("blk", "sub"), None),
    )
    return jax.shard_map(
        shards,
        mesh=mesh,
        in_specs=placed,
        out_specs=(
            P(("blk", "sub"), None),
            P(("blk", "sub"), None),
            P(("blk", "sub"), None),
            P(("blk", "sub"), None),
            P(),
            P(),
            P(),
            P(),
            P(),
            P(),
            P(),
            P(),
            P(),
            P(),
            P(),
            P(),
        ),
        check_vma=False,
    )
```

```python
import functools
import math

import jax
import jax.numpy as jnp
from jax import lax
from jax.experimental import pallas as pl
from jax.experimental.pallas import tpu as pltpu
from jax.sharding import PartitionSpec as P

EPSILON = 1e-05


TILE = 512
CHUNK = 512
LANES = 128
SPARE = 8
VMEM_BYTES = 60 * 2**20


def dot(left, right):
    return jnp.dot(left, right, preferred_element_type=jnp.float32)


def dot_left(left, right):
    return lax.dot_general(
        left, right, (((0,), (0,)), ((), ())), preferred_element_type=jnp.float32
    )


def dot_right(left, right):
    return lax.dot_general(
        left, right, (((1,), (1,)), ((), ())), preferred_element_type=jnp.float32
    )


def split_low(values):
    high = values.astype(jnp.bfloat16)
    return high, (values - high.astype(jnp.float32)).astype(jnp.bfloat16)


def lay_rows(target, start, values):
    count, width = values.shape
    parts = width // LANES
    for j in range(parts):
        target[pl.ds(start * parts + j, count, stride=parts), :] = values[:, j * LANES : (j + 1) * LANES]


def read_rows(source, start, count, parts):
    return jnp.concatenate(
        [source[pl.ds(start * parts + j, count, stride=parts), :] for j in range(parts)], axis=1
    )


def load_table(wide, table, stage, sems):
    steps = wide.shape[0] // CHUNK

    def fetch(i, slot):
        return pltpu.make_async_copy(wide.at[pl.ds(i * CHUNK, CHUNK)], stage.at[slot], sems.at[slot])

    for i in range(3):
        fetch(i, i).start()

    def body(i, carry):
        slot = lax.rem(i, 4)

        @pl.when(i + 3 < steps)
        def _():
            fetch(i + 3, lax.rem(i + 3, 4)).start()

        fetch(i, slot).wait()

        def piece(k, carry):
            values = stage[slot, pl.ds(k * 64, 64), :].astype(jnp.float32)
            lay_rows(table, i * CHUNK + k * 64, values)
            return carry

        return lax.fori_loop(0, CHUNK // 64, piece, carry)

    lax.fori_loop(0, steps, body, 0)


def gather_rows(index, base, table, rows, parts):
    def body(i, carry):
        for u in range(16):
            slot = i * 16 + u
            place = index[base + slot]
            rows[pl.ds(pl.multiple_of(slot * parts, parts), parts), :] = table[
                pl.ds(pl.multiple_of(place * parts, parts), parts), :
            ]
        return carry

    lax.fori_loop(0, TILE // 16, body, 0)


def gather_inline(index, base, table, rows, parts):
    for slot in range(TILE):
        place = index[base + slot]
        rows[slot * parts : (slot + 1) * parts, :] = table[pl.ds(pl.multiple_of(place * parts, parts), parts), :]


def row_normal(values):
    average = jnp.mean(values, -1, keepdims=True)
    centred = values - average
    variance = jnp.mean(centred * centred, -1, keepdims=True)
    scale = lax.rsqrt(variance + EPSILON)
    return centred * scale, scale


def forward_kernel(
    count, recv, send, edge, wide, nodes, w_one, b_one, w_two, b_two, gain, shift,
    result, first, second, received, message,
    table, rows, stage, sems,
):
    step = pl.program_id(0)
    base = step * TILE
    width = nodes.shape[1]
    parts = width // LANES

    @pl.when(step == 0)
    def _():
        load_table(wide, table, stage, sems)
        gather_rows(recv, base, table, rows, parts)

    later = jnp.where(step + 1 < pl.num_programs(0), base + TILE, 0)
    received[...] = read_rows(rows, 0, TILE, parts).astype(jnp.bfloat16)
    gather_inline(recv, later, table, rows, parts)
    from_recv = received[...]
    lane = lax.broadcasted_iota(jnp.int32, (LANES, LANES), 1)
    chosen = []
    for i in range(TILE // LANES):
        column = jnp.broadcast_to(send[pl.ds(step * (TILE // LANES) + i, 1), :], (LANES, LANES)).T
        chosen.append(
            jnp.concatenate(
                [
                    jnp.where(column == lane + j * LANES, 1.0, 0.0).astype(jnp.bfloat16)
                    for j in range(nodes.shape[0] // LANES)
                ],
                axis=1,
            )
        )
    chosen = jnp.concatenate(chosen, axis=0)
    from_send = dot(chosen, nodes[...]).astype(jnp.bfloat16)
    pre = (
        dot(edge[...], w_one[:width])
        + dot(from_send, w_one[width : 2 * width])
        + dot(from_recv, w_one[2 * width :])
        + b_one[...]
    )
    first[...] = pre
    act = (pre * jax.nn.sigmoid(pre)).astype(jnp.bfloat16)
    post = dot(act, w_two[...]) + b_two[...]
    second[...] = post
    normal, _ = row_normal(post)
    branch = normal * gain[...] + shift[...]
    live = base + lax.broadcasted_iota(jnp.int32, (TILE, 1), 0) < count[0]
    outcome = edge[...].astype(jnp.float32) + jnp.where(live, branch, 0.0)
    result[...] = outcome
    message[...] = jnp.where(live, outcome, 0.0).astype(jnp.bfloat16)


def edge_forward(count, recv, send, edge, wide, nodes, w_one, b_one, w_two, b_two, gain, shift):
    edges, width = edge.shape
    steps = edges // TILE
    parts = width // LANES
    hold = pl.BlockSpec(memory_space=pltpu.VMEM)
    scalar = pl.BlockSpec(memory_space=pltpu.SMEM)
    tile = pl.BlockSpec((TILE, width), lambda i: (i, 0))
    return pl.pallas_call(
        forward_kernel,
        grid=(steps,),
        in_specs=[
            scalar, scalar, hold, tile,
            pl.BlockSpec(memory_space=pl.ANY), hold, hold, hold, hold, hold, hold, hold,
        ],
        out_specs=[tile] * 5,
        out_shape=[
            jax.ShapeDtypeStruct((edges, width), jnp.float32),
            jax.ShapeDtypeStruct((edges, width), jnp.float32),
            jax.ShapeDtypeStruct((edges, width), jnp.float32),
            jax.ShapeDtypeStruct((edges, width), jnp.bfloat16),
            jax.ShapeDtypeStruct((edges, width), jnp.bfloat16),
        ],
        scratch_shapes=[
            pltpu.VMEM((wide.shape[0] * parts + SPARE, LANES), jnp.float32),
            pltpu.VMEM((TILE * parts + SPARE, LANES), jnp.float32),
            pltpu.VMEM((4, CHUNK, width), jnp.bfloat16),
            pltpu.SemaphoreType.DMA((4,)),
        ],
        compiler_params=pltpu.CompilerParams(vmem_limit_bytes=VMEM_BYTES),
        cost_estimate=pl.CostEstimate(
            flops=20 * edges * width * width, bytes_accessed=40 * edges * width, transcendentals=2 * edges * width
        ),
        name="edge_forward",
    )(count, recv, send, edge, wide, nodes, w_one, b_one, w_two, b_two, gain, shift)


def backward_kernel(
    count, recv, send, cotangent, edge, received, first, second, wide, node_part, node_vectors, nodes, w_one, w_two, gain,
    grad, message, all_grads, vectors, sender_grad,
    table, rows, stage, sems, by_sender, grads, give_sem,
):
    step = pl.program_id(0)
    base = step * TILE
    width = nodes.shape[1]
    parts = width // LANES

    @pl.when(step == 0)
    def _():
        load_table(wide, table, stage, sems)
        grads[...] = jnp.zeros_like(grads)
        vectors[...] = node_vectors[...]
        by_sender[...] = jnp.zeros_like(by_sender)
        gather_rows(recv, base, table, rows, parts)

    live = base + lax.broadcasted_iota(jnp.int32, (TILE, 1), 0) < count[0]
    upstream = cotangent[...].astype(jnp.float32) + jnp.where(live, read_rows(rows, 0, TILE, parts), 0.0)
    grad[...] = upstream
    later = jnp.where(step + 1 < pl.num_programs(0), base + TILE, 0)
    gather_inline(recv, later, table, rows, parts)
    masked = jnp.where(live, upstream, 0.0)
    normal, scale = row_normal(second[...])
    vectors[2:3, :] += jnp.sum(masked * normal, 0, keepdims=True)
    vectors[3:4, :] += jnp.sum(masked, 0, keepdims=True)
    scaled = masked * gain[...]
    slope = jnp.mean(scaled * normal, -1, keepdims=True)
    grad_second = scale * (scaled - jnp.mean(scaled, -1, keepdims=True) - normal * slope)
    second_low = grad_second.astype(jnp.bfloat16)
    vectors[1:2, :] += jnp.sum(second_low.astype(jnp.float32), 0, keepdims=True)
    pre = first[...]
    logistic = jax.nn.sigmoid(pre)
    act = (pre * logistic).astype(jnp.bfloat16)
    grads[3 * width : 4 * width] += dot_left(act, second_low)
    grad_first = dot_right(second_low, w_two[...]) * (logistic * (1.0 + pre * (1.0 - logistic)))
    first_low = grad_first.astype(jnp.bfloat16)
    message[...] = first_low
    grads[:width] += dot_left(edge[...], first_low)
    grads[2 * width : 3 * width] += dot_left(received[...], first_low)
    node = lax.broadcasted_iota(jnp.int32, (nodes.shape[0], LANES), 0)
    chosen = jnp.concatenate(
        [
            jnp.where(node == send[pl.ds(step * (TILE // LANES) + i, 1), :], 1.0, 0.0).astype(jnp.bfloat16)
            for i in range(TILE // LANES)
        ],
        axis=1,
    )
    by_sender[...] += dot(chosen, first_low)
    grad[...] += dot_right(first_low, w_one[:width])

    @pl.when(step == pl.num_programs(0) - 1)
    def _():
        vectors[0:1, :] = jnp.sum(by_sender[...], 0, keepdims=True)
        high, rest = split_low(by_sender[...])
        grads[width : 2 * width] = dot_left(nodes[...], high) + dot_left(nodes[...], rest)
        give = pltpu.make_async_copy(grads, all_grads, give_sem)
        give.start()
        middle = w_one[width : 2 * width]
        sender_grad[...] = node_part[...] + dot_right(high, middle) + dot_right(rest, middle)
        give.wait()


def edge_backward(
    count, recv, send, cotangent, edge, received, first, second, wide, node_part, node_vectors, nodes,
    w_one, w_two, gain,
):
    edges, width = edge.shape
    steps = edges // TILE
    parts = width // LANES
    per_device = nodes.shape[0]
    hold = pl.BlockSpec(memory_space=pltpu.VMEM)
    scalar = pl.BlockSpec(memory_space=pltpu.SMEM)
    tile = pl.BlockSpec((TILE, width), lambda i: (i, 0))

    across = pl.BlockSpec(memory_space=pl.ANY)

    def whole(rows):
        return pl.BlockSpec((rows, width), lambda i: (0, 0))

    return pl.pallas_call(
        backward_kernel,
        grid=(steps,),
        in_specs=[
            scalar, scalar, hold, tile, tile, tile, tile, tile,
            across, hold, hold, hold, hold, hold, hold,
        ],
        out_specs=[
            tile, tile, across, whole(8), whole(per_device),
        ],
        out_shape=[
            jax.ShapeDtypeStruct((edges, width), jnp.float32),
            jax.ShapeDtypeStruct((edges, width), jnp.bfloat16),
            jax.ShapeDtypeStruct((4 * width, width), jnp.float32),
            jax.ShapeDtypeStruct((8, width), jnp.float32),
            jax.ShapeDtypeStruct((per_device, width), jnp.float32),
        ],
        scratch_shapes=[
            pltpu.VMEM((wide.shape[0] * parts + SPARE, LANES), jnp.float32),
            pltpu.VMEM((TILE * parts + SPARE, LANES), jnp.float32),
            pltpu.VMEM((4, CHUNK, width), jnp.bfloat16),
            pltpu.SemaphoreType.DMA((4,)),
            pltpu.VMEM((per_device, width), jnp.float32),
            pltpu.VMEM((4 * width, width), jnp.float32),
            pltpu.SemaphoreType.DMA,
        ],
        compiler_params=pltpu.CompilerParams(vmem_limit_bytes=VMEM_BYTES),
        cost_estimate=pl.CostEstimate(
            flops=24 * edges * width * width, bytes_accessed=40 * edges * width, transcendentals=2 * edges * width
        ),
        name="edge_backward",
    )(
        count, recv, send, cotangent, edge, received, first, second, wide,
        node_part, node_vectors, nodes, w_one, w_two, gain,
    )


MESH = pl.DeviceIdType.MESH
PIECES = 4
SPLIT = True
LOW = jnp.bfloat16
WIDE = jnp.float32


def places():
    groups = lax.axis_size("blk")
    group, sub = lax.axis_index("blk"), lax.axis_index("sub")
    odd = lax.rem(group, 2)
    along = groups // 2
    spot = group // 2
    beside = group + 1 - 2 * odd
    return dict(
        group=group,
        sub=sub,
        core=lax.rem(sub, 2),
        chip=sub // 2,
        odd=odd,
        spot=spot,
        along=along,
        sibling=sub + 1 - 2 * lax.rem(sub, 2),
        partner=lax.rem(sub + 2, 4),
        to_sibling=(group, sub + 1 - 2 * lax.rem(sub, 2)),
        to_partner=(group, lax.rem(sub + 2, 4)),
        to_beside=(beside, sub),
        to_onward=(lax.rem(group + 2 - 4 * odd + groups, groups), sub),
        to_source=(lax.rem(group - 2 + 4 * odd + groups, groups), sub),
        peers=[(2 * lax.rem(spot + k, along) + odd, sub) for k in range(1, along)],
        near=2 - 2 * odd,
        far=2 * odd,
    )


def meet(senders):
    barrier = pltpu.get_barrier_semaphore()
    for device in senders:
        pl.semaphore_signal(barrier, inc=1, device_id=device, device_id_type=MESH)
    pl.semaphore_wait(barrier, len(senders))


def meet_all():
    barrier = pltpu.get_barrier_semaphore()
    subs = lax.axis_size("sub")
    devices = lax.axis_size("blk") * subs
    here = lax.axis_index("blk") * subs + lax.axis_index("sub")

    def greet(k, carry):
        there = lax.rem(here + k, devices)
        pl.semaphore_signal(barrier, inc=1, device_id=(there // subs, lax.rem(there, subs)), device_id_type=MESH)
        return carry

    lax.fori_loop(1, devices, greet, 0)
    pl.semaphore_wait(barrier, devices - 1)


def remote(source, target, send, recv, device):
    return pltpu.make_async_remote_copy(
        src_ref=source, dst_ref=target, send_sem=send, recv_sem=recv, device_id=device, device_id_type=MESH
    )


def in_pieces(count, body):
    block = math.gcd(count, 128)

    def run(i, carry):
        body(pl.multiple_of(i * block, block), block)
        return carry

    lax.fori_loop(0, count // block, run, 0)


def padded_rows(rows):
    unit = 64 * lax.axis_size("blk")
    return -(-rows // unit) * unit


def streams_of(sources):
    unit = 64 * lax.axis_size("blk")
    streams = []
    for i, rows in enumerate(sources):
        first = -(-(rows // unit) // 2) * unit if SPLIT else rows
        streams.append((i, 0, first))
        if first < rows:
            streams.append((i, first, rows - first))
    return streams


def reducers_scratch(sources, width, along):
    return [ref for _, _, rows in streams_of(sources) for ref in reducer_scratch(rows, width, along)]


def reducers(at, sources, reduced, refs):
    made = []
    for i, (which, start, rows) in enumerate(streams_of([source.shape[0] for source in sources])):
        first = start + sum(source.shape[0] for source in sources[:which])
        made.append(reducer(at, sources[which], start, reduced, first, rows, i % 2 > 0, refs[i * 13 : i * 13 + 13]))
    return made, refs[len(made) * 13 :]


def reducer_scratch(rows, width, along):
    return [
        pltpu.VMEM((rows // 2, width), WIDE),
        pltpu.VMEM((rows // 2, width), WIDE),
        pltpu.VMEM((rows // 4, width), LOW),
        pltpu.VMEM((rows // 4, width), LOW),
        pltpu.VMEM((rows // 8, width), LOW),
        pltpu.VMEM((rows // 8, width), LOW),
        pltpu.VMEM((rows // 8, width), LOW),
        pltpu.VMEM((along - 1, rows // 8 // along, width), LOW),
        pltpu.SemaphoreType.DMA,
        pltpu.SemaphoreType.DMA((6,)),
        pltpu.SemaphoreType.DMA((6,)),
        pltpu.SemaphoreType.DMA((2, along - 1)),
        pltpu.SemaphoreType.DMA((2, along - 1)),
    ]


def reducer(at, grads, source_first, reduced, first, rows, swap, refs):
    (
        half, half_in, cross_out, cross_in, side_out, side_in, ring_out, ring_in,
        load_sem, step_send, step_recv, ring_send, ring_recv,
    ) = refs
    along, peers = at["along"], at["peers"]
    turns = [(at["chip"], at["to_partner"]), (at["odd"], at["to_beside"])]
    (bit_one, device_one), (bit_two, device_two) = turns[::-1] if swap else turns
    core, spot = at["core"], at["spot"]
    n_half, n_cross, n_side, n_ring = rows // 2, rows // 4, rows // 8, rows // 8 // along
    at_half = first + core * n_half
    at_cross = at_half + bit_one * n_cross
    at_side = at_cross + bit_two * n_side
    at_ring = at_side + spot * n_ring

    def span(start, count):
        return pl.ds(pl.multiple_of(start, 16), count)

    def step(kind):
        if kind == 0:
            other = span(source_first + (1 - core) * n_half, n_half)
            source, target, device = grads.at[other], half_in, at["to_sibling"]
        elif kind == 1:
            source, target, device = cross_out, cross_in, device_one
        elif kind == 2:
            source, target, device = side_out, side_in, device_two
        else:
            start, count, device = {
                3: (at_side, n_side, device_two),
                4: (at_cross, n_cross, device_one),
                5: (at_half, n_half, at["to_sibling"]),
            }[kind]
            source = target = reduced.at[span(start, count)]
        return remote(source, target, step_send.at[kind], step_recv.at[kind], device)

    def ring(kind, k):
        if kind == 0:
            source = ring_out.at[span(lax.rem(spot + k, along) * n_ring, n_ring)]
            target = ring_in.at[k - 1]
        else:
            source = target = reduced.at[span(at_ring, n_ring)]
        return remote(source, target, ring_send.at[kind, k - 1], ring_recv.at[kind, k - 1], peers[k - 1])

    load = pltpu.make_async_copy(grads.at[span(source_first + core * n_half, n_half)], half, load_sem)

    def start():
        step(0).start()
        load.start()

    def add_half():
        load.wait()
        step(0).wait_recv()
        other = (1 - bit_one) * n_cross

        def part(i, block):
            here = pl.ds(pl.multiple_of(other + i, block), block)
            cross_out[pl.ds(i, block), :] = (half[here, :] + half_in[here, :]).astype(LOW)

        in_pieces(n_cross, part)
        step(1).start()

    def add_cross():
        mine, other = bit_one * n_cross, (1 - bit_two) * n_side
        step(1).wait_recv()

        def part(i, block):
            there = pl.ds(pl.multiple_of(other + i, block), block)
            here = pl.ds(pl.multiple_of(mine + other + i, block), block)
            side_out[pl.ds(i, block), :] = (half[here, :] + half_in[here, :] + cross_in[there, :].astype(WIDE)).astype(LOW)

        in_pieces(n_side, part)
        step(2).start()

    def add_side():
        mine, kept = bit_one * n_cross, bit_two * n_side
        step(2).wait_recv()

        def part(i, block):
            there = pl.ds(pl.multiple_of(kept + i, block), block)
            here = pl.ds(pl.multiple_of(mine + kept + i, block), block)
            flat = pl.ds(i, block)
            value = half[here, :] + half_in[here, :] + cross_in[there, :].astype(WIDE) + side_in[flat, :].astype(WIDE)
            half[here, :] = value
            ring_out[flat, :] = value.astype(LOW)

        in_pieces(n_side, part)
        for k in range(1, along):
            ring(0, k).start()

    def add_ring():
        value = half[span(bit_one * n_cross + bit_two * n_side + spot * n_ring, n_ring), :]
        for k in range(1, along):
            ring(0, k).wait_recv()
            value = value + ring_in[k - 1].astype(WIDE)
        reduced[span(at_ring, n_ring), :] = value.astype(LOW)
        for k in range(1, along):
            ring(1, k).start()

    def share_side():
        for k in range(1, along):
            ring(1, k).wait_recv()
        step(3).start()

    def share_cross():
        step(3).wait_recv()
        step(4).start()

    def share_half():
        step(4).wait_recv()
        step(5).start()

    def last():
        step(5).wait_recv()

    def drain():
        for kind in range(6):
            step(kind).wait_send()
        for k in range(1, along):
            ring(0, k).wait_send()
            ring(1, k).wait_send()

    return [start, add_half, add_cross, add_side, add_ring, share_side, share_cross, share_half, last, drain]


def vector_scratch(shape, along):
    return [
        pltpu.VMEM((4, *shape), WIDE),
        pltpu.VMEM((2 + along, *shape), WIDE),
        pltpu.SemaphoreType.DMA((2 + along,)),
        pltpu.SemaphoreType.DMA((2 + along,)),
    ]


def vector_reducer(at, vectors, reduced, refs):
    held, held_in, send_sems, recv_sems = refs
    along = at["along"]
    devices = (at["to_sibling"], at["to_partner"], at["to_beside"], *at["peers"])

    def move(kind):
        return remote(held.at[min(kind, 3)], held_in.at[kind], send_sems.at[kind], recv_sems.at[kind], devices[kind])

    def start():
        held[0] = vectors[...]
        move(0).start()

    def turn(kind):
        def run():
            move(kind).wait_recv()
            held[kind + 1] = held[kind] + held_in[kind]
            for k in range(kind + 1, kind + 2 if kind < 2 else 2 + along):
                move(k).start()

        return run

    def last():
        value = held[3]
        for k in range(3, 2 + along):
            move(k).wait_recv()
            value = value + held_in[k]
        reduced[...] = value
        for k in range(2 + along):
            move(k).wait_send()

    return [start, turn(0), turn(1), turn(2), last]


def spread_moves(at, own, table, keep_sem, send_sems, recv_sems):
    sub, partner, near, far = at["sub"], at["partner"], at["near"], at["far"]
    to_sibling, to_partner, to_beside, to_onward = (
        at["to_sibling"], at["to_partner"], at["to_beside"], at["to_onward"]
    )
    size = own.shape[0] // PIECES

    def move(kind, piece):
        source, slot, device = {
            0: (None, (1, sub), to_partner),
            1: (None, (far, sub), to_beside),
            2: (None, (1, sub), to_sibling),
            3: ((1, partner), (far, partner), to_beside),
            4: ((1, partner), (1, partner), to_sibling),
            5: ((near, sub), (far, sub), to_onward),
            6: ((near, sub), (near, sub), to_sibling),
            7: ((near, partner), (far, partner), to_onward),
            8: ((near, partner), (near, partner), to_sibling),
            9: ((far, sub), (far, sub), to_sibling),
            10: ((far, partner), (far, partner), to_sibling),
            11: ((near, sub), (near, sub), to_partner),
            12: ((far, sub), (far, sub), to_partner),
        }[kind]
        source = own if source is None else table.at[source[0], source[1]]
        rows = pl.ds(piece * size, size)
        return remote(
            source.at[rows], table.at[slot[0], slot[1], rows],
            send_sems.at[kind, piece], recv_sems.at[kind, piece], device,
        )

    keep = pltpu.make_async_copy(own, table.at[1, sub], keep_sem)

    def start():
        for piece in range(PIECES):
            for kind in (0, 1, 2):
                move(kind, piece).start()
        keep.start()

    def relay(arrived, kinds, piece):
        move(arrived, piece).wait_recv()
        for kind in kinds:
            move(kind, piece).start()

    straight = range(PIECES - 2)

    def one(piece):
        relay(0, (3, 4) if piece in straight else (4,), piece)
        relay(1, (5, 6) if piece in straight else (5, 6, 11), piece)

    def two(piece):
        if piece in straight:
            relay(3, (7, 8), piece)
            relay(5, (9,), piece)
        else:
            relay(5, (9, 12), piece)
            relay(11, (8,), piece)

    def three(piece):
        if piece in straight:
            relay(7, (10,), piece)
        else:
            relay(12, (10,), piece)

    def drain():
        for kind in range(13):
            for piece in range(PIECES):
                if kind in ((11, 12) if piece in straight else (3, 7)):
                    continue
                if kind in (2, 4, 6, 8, 9, 10):
                    move(kind, piece).wait_recv()
                move(kind, piece).wait_send()
        keep.wait()

    return start, one, two, three, drain


def spread_scratch():
    return [
        pltpu.SemaphoreType.DMA,
        pltpu.SemaphoreType.DMA((13, PIECES)),
        pltpu.SemaphoreType.DMA((13, PIECES)),
    ]


HALVES = 2
ORDER = (
    (0, 1, 0), (0, 1, 1), (1, 1, 0), (0, 0, 0), (1, 1, 1), (0, 0, 1),
    (1, 0, 0), (2, 1, 0), (1, 0, 1), (2, 1, 1), (2, 0, 0), (2, 0, 1),
)


def collect_scratch(rows, width, edges):
    return [
        pltpu.VMEM((edges, width), LOW),
        pltpu.VMEM((2, 3, 2, rows, width), WIDE),
        pltpu.VMEM((3, 2, rows, width), WIDE),
        pltpu.VMEM((2, rows, width), LOW),
        pltpu.VMEM((2, rows, width), LOW),
        pltpu.VMEM((2, rows, width), LOW),
        pltpu.VMEM((2, rows, width), LOW),
        pltpu.VMEM((rows, width), LOW),
        pltpu.VMEM((rows, width), LOW),
        pltpu.SemaphoreType.DMA,
        pltpu.SemaphoreType.DMA((3, 2, HALVES)),
        pltpu.SemaphoreType.DMA((3, 2, HALVES)),
        pltpu.SemaphoreType.DMA((5, PIECES)),
        pltpu.SemaphoreType.DMA((5, PIECES)),
    ]


def collect_moves(at, index, messages, out, refs):
    (
        held, parts, landed, far_out, far_in, near_out, near_in, pair_out, pair_in,
        load_sem, give_sems, take_sems, send_sems, recv_sems,
    ) = refs
    sub, partner, sibling = at["sub"], at["partner"], at["sibling"]
    rows = out.shape[0]
    size = rows // PIECES
    part_rows = rows // HALVES
    load = pltpu.make_async_copy(messages, held, load_sem)

    def piece_of(ref, piece):
        return ref.at[pl.ds(piece * size, size)]

    def give(role, side, half):
        span = pl.ds(pl.multiple_of(half * part_rows, part_rows), part_rows)
        return remote(
            parts.at[0, role, side, span], landed.at[role, side, span],
            give_sems.at[role, side, half], take_sems.at[role, side, half], at["to_sibling"],
        )

    def hop(kind, piece):
        source, target, device = {
            0: (far_out.at[0], far_in.at[0], at["to_source"]),
            1: (far_out.at[1], far_in.at[1], at["to_source"]),
            2: (near_out.at[0], near_in.at[0], at["to_beside"]),
            3: (near_out.at[1], near_in.at[1], at["to_beside"]),
            4: (pair_out, pair_in, at["to_partner"]),
        }[kind]
        return remote(
            piece_of(source, piece), piece_of(target, piece),
            send_sems.at[kind, piece], recv_sems.at[kind, piece], device,
        )

    def add_messages(step):
        def pick(column):
            return lax.rem(sum(int(item[column]) << (2 * i) for i, item in enumerate(ORDER)) >> (2 * step), 4)

        role, side, half = pick(0), pick(1), pick(2)
        relation = jnp.where(role == 0, at["far"], jnp.where(role == 1, at["near"], 1))
        span = pl.ds(pl.multiple_of(half * part_rows, part_rows), part_rows)

        def whose(w, carry):
            first = jnp.where(w == 0, sibling, sub)
            target = lax.rem(first + 2 * side, 4)
            base = (relation * 4 + target) * rows + half * part_rows
            node = lax.broadcasted_iota(jnp.int32, (part_rows, LANES), 0) + base
            chosen = jnp.concatenate(
                [jnp.where(node == index[j : j + 1, :], 1.0, 0.0).astype(LOW) for j in range(index.shape[0])], axis=1
            )
            parts[w, role, side, span, :] = dot(chosen, held[...])
            return carry

        lax.fori_loop(0, 2, whose, 0)
        give(role, side, half).start()

    def local(role, side, piece):
        span = pl.ds(piece * size, size)
        return parts[1, role, side, span, :] + landed[role, side, span, :]

    def arrived(kind, ref, piece):
        hop(kind, piece).wait_recv()
        return ref[pl.ds(piece * size, size), :].astype(WIDE)

    def pieces(half):
        return range(half * PIECES // HALVES, (half + 1) * PIECES // HALVES)

    def far_step(side, half):
        give(0, side, half).wait_recv()
        for piece in pieces(half):
            far_out[side, pl.ds(piece * size, size), :] = local(0, side, piece).astype(LOW)
            hop(side, piece).start()

    def near_step(side, half):
        give(1, side, half).wait_recv()
        for piece in pieces(half):
            value = local(1, side, piece) + arrived(side, far_in.at[side], piece)
            near_out[side, pl.ds(piece * size, size), :] = value.astype(LOW)
            hop(2 + side, piece).start()

    def pair_step(half):
        give(2, 1, half).wait_recv()
        for piece in pieces(half):
            value = local(2, 1, piece) + arrived(3, near_in.at[1], piece)
            pair_out[pl.ds(piece * size, size), :] = value.astype(LOW)
            hop(4, piece).start()

    def last_step(half):
        give(2, 0, half).wait_recv()
        for piece in pieces(half):
            value = local(2, 0, piece) + arrived(2, near_in.at[0], piece) + arrived(4, pair_in, piece)
            out[pl.ds(piece * size, size), :] = value

    def drain():
        for item in ORDER:
            give(*item).wait_send()
        for kind in range(5):
            for piece in range(PIECES):
                hop(kind, piece).wait_send()

    events = {
        1: [lambda: far_step(1, 0)],
        2: [lambda: far_step(1, 1)],
        3: [lambda: near_step(1, 0)],
        4: [lambda: far_step(0, 0)],
        5: [lambda: near_step(1, 1), lambda: far_step(0, 1)],
        7: [lambda: near_step(0, 0), lambda: pair_step(0)],
        9: [lambda: near_step(0, 1), lambda: pair_step(1)],
    }

    def run(more):
        def step(i, carry):
            add_messages(i)
            for k in sorted(set(events) | set(more)):
                @pl.when(i == k)
                def _():
                    for event in events.get(k, []) + more.get(k, []):
                        event()

            return carry

        lax.fori_loop(0, len(ORDER), step, 0)
        for half in range(HALVES):
            last_step(half)

    return load, run, drain


def exchange_scratch(rows, width, devices):
    slab = width // devices * (rows // LANES)
    return [
        pltpu.VMEM((devices * slab, LANES), WIDE),
        pltpu.VMEM((devices * slab, LANES), LOW),
        pltpu.VMEM((devices, slab, LANES), LOW),
        pltpu.VMEM((slab, LANES), WIDE),
        pltpu.SemaphoreType.DMA((devices - 1,)),
        pltpu.SemaphoreType.DMA((devices - 1,)),
    ]


def exchange_moves(residual, out, refs):
    flat, packed, landed, opened, send_sems, recv_sems = refs
    subs = lax.axis_size("sub")
    devices = lax.axis_size("blk") * subs
    here = lax.axis_index("blk") * subs + lax.axis_index("sub")
    slab = landed.shape[1]
    channels = out.shape[0]
    parts = slab // channels
    nodes = parts * LANES

    def move(k):
        there = lax.rem(here + k, devices)
        return remote(
            packed.at[pl.ds(pl.multiple_of(there * slab, slab), slab)], landed.at[here],
            send_sems.at[k - 1], recv_sems.at[k - 1], (there // subs, lax.rem(there, subs)),
        )

    def start(values):
        lay_rows(flat, 0, values.T)

        def cast(i, block):
            packed[pl.ds(i, block), :] = flat[pl.ds(i, block), :].astype(LOW)

        in_pieces(flat.shape[0], cast)

        def send(k, carry):
            move(k).start()
            return carry

        lax.fori_loop(1, devices, send, 0)

    def open_slab(source, device):
        opened[...] = source.astype(WIDE)
        for j in range(parts):
            columns = pl.ds(pl.multiple_of(device * nodes + j * LANES, LANES), LANES)
            out[:, columns] = residual[:, columns] + opened[pl.ds(j, channels, stride=parts), :]

    def last():
        open_slab(packed[pl.ds(pl.multiple_of(here * slab, slab), slab), :], here)

        def take(k, carry):
            move(k).wait_recv()
            device = lax.rem(here - k + devices, devices)
            open_slab(landed[device], device)
            return carry

        lax.fori_loop(1, devices, take, 0)

        def sent(k, carry):
            move(k).wait_send()
            return carry

        lax.fori_loop(1, devices, sent, 0)

    return start, last


def finish_kernel(
    index, messages, edge_grads, node_grads, vectors, node_part, weight, residual,
    node_grad, one_out, two_out, three_out, four_out, reduced_vectors, total, reduced, out_sems, *refs,
):
    at = places()
    count = len(collect_scratch(64, 128, 64))
    load, run, drain = collect_moves(at, index, messages, total, refs[:count])
    load.start()
    meet_all()
    streams, refs = reducers(at, (edge_grads, node_grads), reduced, refs[count:])
    vector_steps = vector_reducer(at, vectors, reduced_vectors, refs[:4])
    exchange, receive = exchange_moves(residual, node_grad, refs[4:])
    for stream in streams:
        stream[0]()
    vector_steps[0]()
    load.wait()
    timetable = (
        (0, 1, (0,)), (1, 1, (1, 2, 3)), (4, 2, (0, 1)), (6, 2, (3, 2)), (6, 3, (1,)), (7, 3, (0,)), (8, 3, (3, 2)),
        (10, 4, (1, 0)), (11, 4, (3, 2)),
    )
    later = {1: [vector_steps[1]], 4: [vector_steps[2]], 7: [vector_steps[3]]}
    for when, hop, which in timetable:
        later.setdefault(when, []).extend(streams[i][hop] for i in which if i < len(streams))
    run(later)

    def hops(hop, which):
        for i in which:
            if i < len(streams):
                streams[i][hop]()

    hops(5, (1, 0))
    high, rest = split_low(total[...])
    exchange(node_part[...] + dot_right(high, weight[...]) + dot_right(rest, weight[...]))
    hops(5, (3, 2))
    hops(6, (1, 0, 3, 2))
    hops(7, range(4))
    receive()
    hops(8, range(4))
    width = total.shape[1]
    nodes_at = edge_grads.shape[0]
    copies = [
        pltpu.make_async_copy(reduced.at[pl.ds(first, target.shape[0])], target, out_sems.at[i])
        for i, (first, target) in enumerate((
            (0, one_out), (3 * width, two_out), (nodes_at, three_out), (nodes_at + 2 * width, four_out)
        ))
    ]
    for copy in copies:
        copy.start()
    vector_steps[4]()
    drain()
    for stream in streams:
        stream[9]()
    for copy in copies:
        copy.wait()


def finish(index, messages, edge_grads, node_grads, vectors, node_part, weight, residual, collective):
    rows, width = node_part.shape
    edges = messages.shape[0]
    sources = [edge_grads.shape[0], node_grads.shape[0]]
    along = lax.axis_size("blk") // 2
    devices = lax.axis_size("blk") * lax.axis_size("sub")
    hold = pl.BlockSpec(memory_space=pltpu.VMEM)
    across = pl.BlockSpec(memory_space=pl.ANY)
    return pl.pallas_call(
        finish_kernel,
        grid=(1,),
        in_specs=[
            hold, across, across, across, hold, hold, pl.BlockSpec((width, width), lambda i: (2, 0)), hold,
        ],
        out_specs=[hold] + [across] * 4 + [hold],
        out_shape=[
            jax.ShapeDtypeStruct(residual.shape, WIDE),
            jax.ShapeDtypeStruct((3 * width, width), LOW),
            jax.ShapeDtypeStruct((width, width), LOW),
            jax.ShapeDtypeStruct((2 * width, width), LOW),
            jax.ShapeDtypeStruct((width, width), LOW),
            jax.ShapeDtypeStruct(vectors.shape, WIDE),
        ],
        scratch_shapes=[
            pltpu.VMEM((rows, width), WIDE),
            pltpu.VMEM((sum(sources), width), LOW),
            pltpu.SemaphoreType.DMA((4,)),
            *collect_scratch(rows, width, edges),
            *reducers_scratch(sources, width, along),
            *vector_scratch(vectors.shape, along),
            *exchange_scratch(rows, width, devices),
        ],
        compiler_params=pltpu.CompilerParams(
            collective_id=collective, has_side_effects=True, vmem_limit_bytes=VMEM_BYTES
        ),
        name="finish_sums",
    )(index.reshape(edges // LANES, LANES), messages, edge_grads, node_grads, vectors, node_part, weight, residual)


def middle_kernel(
    index, messages, node_low, upstream, w_one, b_one, w_two, b_two, gain, shift, residual,
    table, node_part, node_out, grads, vectors, total, sent, *refs
):
    at = places()
    count = len(collect_scratch(64, 128, 64))
    load, run, drain = collect_moves(at, index, messages, total, refs[:count])
    load.start()
    meet_all()
    refs = refs[count:]
    start, one, two, three, end = spread_moves(at, sent, table, *refs[:3])
    exchange, receive = exchange_moves(residual, node_out, refs[3:])
    load.wait()
    run({})

    width = total.shape[1]
    low = total[...].astype(LOW)
    pre = dot(node_low[...], w_one[:width]) + dot(low, w_one[width:]) + b_one[...]
    logistic = jax.nn.sigmoid(pre)
    act = (pre * logistic).astype(LOW)
    normal, scale = row_normal(dot(act, w_two[...]) + b_two[...])
    given = upstream[...].T
    scaled = given * gain[...]
    slope = jnp.mean(scaled * normal, -1, keepdims=True)
    fourth = scale * (scaled - jnp.mean(scaled, -1, keepdims=True) - normal * slope)
    fourth_low = fourth.astype(LOW)
    third = dot_right(fourth_low, w_two[...]) * (logistic * (1.0 + pre * (1.0 - logistic)))
    third_low = third.astype(LOW)
    sent[...] = dot_right(third_low, w_one[width:]).astype(LOW)
    start()
    grads[:width] = dot_left(node_low[...], third_low)
    grads[width : 2 * width] = dot_left(low, third_low)
    grads[2 * width : 3 * width] = dot_left(act, fourth_low)
    vectors[...] = jnp.zeros_like(vectors)
    vectors[4:5] = jnp.sum(third_low.astype(WIDE), 0, keepdims=True)
    vectors[5:6] = jnp.sum(fourth_low.astype(WIDE), 0, keepdims=True)
    vectors[6:7] = jnp.sum(given * normal, 0, keepdims=True)
    vectors[7:8] = jnp.sum(given, 0, keepdims=True)
    node_part[...] = dot_right(third_low, w_one[:width])
    exchange(normal * gain[...] + shift[...])

    for stage in (one, two, three):
        for piece in range(PIECES):
            stage(piece)
    receive()
    end()
    drain()


def middle(index, messages, node_low, upstream, w_one, b_one, w_two, b_two, gain, shift, residual, collective):
    rows, width = node_low.shape
    edges = messages.shape[0]
    devices = lax.axis_size("blk") * lax.axis_size("sub")
    grad_rows = padded_rows(3 * width)
    hold = pl.BlockSpec(memory_space=pltpu.VMEM)
    across = pl.BlockSpec(memory_space=pl.ANY)
    table, node_part, node_out, grads, vectors = pl.pallas_call(
        middle_kernel,
        in_specs=[hold, across] + [hold] * 9,
        out_specs=[across] + [hold] * 4,
        out_shape=[
            jax.ShapeDtypeStruct((3, 4, rows, width), LOW),
            jax.ShapeDtypeStruct((rows, width), WIDE),
            jax.ShapeDtypeStruct(residual.shape, WIDE),
            jax.ShapeDtypeStruct((grad_rows, width), WIDE),
            jax.ShapeDtypeStruct((8, width), WIDE),
        ],
        scratch_shapes=[
            pltpu.VMEM((rows, width), WIDE),
            pltpu.VMEM((rows, width), LOW),
            *collect_scratch(rows, width, edges),
            *spread_scratch(),
            *exchange_scratch(rows, width, devices),
        ],
        compiler_params=pltpu.CompilerParams(
            collective_id=collective, has_side_effects=True, vmem_limit_bytes=VMEM_BYTES
        ),
        name="middle_nodes",
    )(
        index.reshape(edges // LANES, LANES), messages, node_low, upstream,
        w_one, b_one, w_two, b_two, gain, shift, residual,
    )
    return table.reshape(12 * rows, width), node_part, node_out, grads, vectors


def scatter_scratch(channels, nodes, devices):
    slab = channels * (nodes // LANES)
    return [
        pltpu.VMEM((devices * slab, LANES), WIDE),
        pltpu.VMEM((devices * slab, LANES), LOW),
        pltpu.VMEM((devices, slab, LANES), LOW),
        pltpu.VMEM((slab, LANES), WIDE),
        pltpu.VMEM((nodes // LANES * devices * channels, LANES), WIDE),
        pltpu.SemaphoreType.DMA((devices - 1,)),
        pltpu.SemaphoreType.DMA((devices - 1,)),
    ]


def scatter_moves(shard, refs):
    flat, packed, landed, opened, square, send_sems, recv_sems = refs
    subs = lax.axis_size("sub")
    devices = lax.axis_size("blk") * subs
    here = lax.axis_index("blk") * subs + lax.axis_index("sub")
    slab = landed.shape[1]
    channels = shard.shape[0]
    parts = slab // channels
    nodes = parts * LANES

    def move(k):
        there = lax.rem(here + k, devices)
        return remote(
            packed.at[pl.ds(pl.multiple_of(there * slab, slab), slab)], landed.at[here],
            send_sems.at[k - 1], recv_sems.at[k - 1], (there // subs, lax.rem(there, subs)),
        )

    def start():
        def pack(k, carry):
            device = lax.rem(here + k, devices)
            rows = pl.ds(pl.multiple_of(device * slab, slab), slab)
            for j in range(parts):
                columns = pl.ds(pl.multiple_of(device * nodes + j * LANES, LANES), LANES)
                flat[pl.ds(device * slab + j, channels, stride=parts), :] = shard[:, columns]
            packed[rows, :] = flat[rows, :].astype(LOW)
            return carry

        def send(k, carry):
            pack(k, carry)
            move(k).start()
            return carry

        lax.fori_loop(1, devices, send, 0)
        pack(0, 0)

    def open_slab(source, device):
        opened[...] = source.astype(WIDE)
        for j in range(parts):
            rows = pl.ds(pl.multiple_of((j * devices + device) * channels, channels), channels)
            square[rows, :] = opened[pl.ds(j, channels, stride=parts), :]

    def last(rows):
        open_slab(packed[pl.ds(pl.multiple_of(here * slab, slab), slab), :], here)

        def take(k, carry):
            move(k).wait_recv()
            device = lax.rem(here - k + devices, devices)
            open_slab(landed[device], device)
            return carry

        lax.fori_loop(1, devices, take, 0)
        width = devices * channels
        for j in range(parts):
            rows[j * LANES : (j + 1) * LANES, :] = square[j * width : (j + 1) * width, :].T.astype(LOW)

    def drain():
        def sent(k, carry):
            move(k).wait_send()
            return carry

        lax.fori_loop(1, devices, sent, 0)

    return start, last, drain


def begin_kernel(
    shard, later, senders, receivers, own, table, later_out, send_local, recv_wide, held, held_sem, slab_sems, *refs
):
    at = places()
    fetch = pltpu.make_async_copy(later, held, held_sem)
    fetch.start()
    meet_all()
    start, last, drain = scatter_moves(shard, refs[3:])
    start()
    last(own)
    begin, one, two, three, end = spread_moves(at, own, table, *refs[:3])
    begin()
    rows = own.shape[0]
    groups, subs = lax.axis_size("blk"), lax.axis_size("sub")
    send_local[...] = senders[...] - (at["group"] * subs + at["sub"]) * rows
    relative = lax.rem(receivers[...] // (rows * subs) - at["group"] + 1 + groups, groups)
    recv_wide[...] = relative * (rows * subs) + lax.rem(receivers[...], rows * subs)
    fetch.wait()
    devices, _, nodes = later_out.shape

    def slab(k):
        columns = pl.ds(pl.multiple_of(k * nodes, LANES), nodes)
        return pltpu.make_async_copy(held.at[:, columns], later_out.at[k], slab_sems.at[k])

    def give(k, carry):
        slab(k).start()
        return carry

    def given(k, carry):
        slab(k).wait()
        return carry

    lax.fori_loop(0, devices, give, 0)
    drain()
    for stage in (one, two, three):
        for piece in range(PIECES):
            stage(piece)
    lax.fori_loop(0, devices, given, 0)
    end()


def begin(shard, later, senders, receivers, rows, collective):
    channels, nodes = shard.shape
    devices = lax.axis_size("blk") * lax.axis_size("sub")
    width = channels * devices
    hold = pl.BlockSpec(memory_space=pltpu.VMEM)
    across = pl.BlockSpec(memory_space=pl.ANY)
    lines = (senders.shape[0] // LANES, LANES)
    own, table, later, send_local, recv_wide = pl.pallas_call(
        begin_kernel,
        in_specs=[hold, across, hold, hold],
        out_specs=[hold, across, across, hold, hold],
        out_shape=[
            jax.ShapeDtypeStruct((rows, width), LOW),
            jax.ShapeDtypeStruct((3, 4, rows, width), LOW),
            jax.ShapeDtypeStruct((devices, channels, rows), later.dtype),
            jax.ShapeDtypeStruct(lines, jnp.int32),
            jax.ShapeDtypeStruct(lines, jnp.int32),
        ],
        scratch_shapes=[
            pltpu.VMEM(later.shape, later.dtype),
            pltpu.SemaphoreType.DMA,
            pltpu.SemaphoreType.DMA((devices,)),
            *spread_scratch(),
            *scatter_scratch(channels, rows, devices),
        ],
        compiler_params=pltpu.CompilerParams(
            collective_id=collective, has_side_effects=True, vmem_limit_bytes=VMEM_BYTES
        ),
        name="begin_rows",
    )(shard, later, senders.reshape(lines), receivers.reshape(lines))
    return own, table.reshape(12 * rows, width), later, send_local, recv_wide


def release_kernel(count, vectors, *refs):
    for source, target in zip(refs[:count], refs[count : 2 * count]):
        target[...] = source[...].astype(target.dtype)

    @pl.when(pl.program_id(0) == 0)
    def _():
        for i, target in enumerate(refs[2 * count :]):
            target[...] = vectors[i : i + 1, :]


def release(whole, reduced, vectors):
    arrays = [*whole, *reduced]
    steps = 2

    def spec(item, kept):
        rows, columns = item.shape
        if kept:
            return pl.BlockSpec((rows, columns // steps), lambda i: (0, i))
        return pl.BlockSpec((rows // steps, columns), lambda i: (i, 0))

    specs = [spec(item, i < len(whole)) for i, item in enumerate(arrays)]
    return pl.pallas_call(
        functools.partial(release_kernel, len(arrays)),
        grid=(steps,),
        in_specs=[pl.BlockSpec(vectors.shape, lambda i: (0, 0))] + specs,
        out_specs=specs + [pl.BlockSpec((1, vectors.shape[1]), lambda i: (0, 0))] * vectors.shape[0],
        out_shape=[jax.ShapeDtypeStruct(item.shape, WIDE) for item in arrays]
        + [jax.ShapeDtypeStruct((1, vectors.shape[1]), WIDE)] * vectors.shape[0],
        compiler_params=pltpu.CompilerParams(vmem_limit_bytes=VMEM_BYTES),
        name="release_results",
    )(vectors, *arrays)


def shards(
    node_input,
    edge_input,
    senders,
    receivers,
    edge_count,
    edge_w_one,
    edge_b_one,
    edge_w_two,
    edge_b_two,
    edge_gain,
    edge_shift,
    node_w_one,
    node_b_one,
    node_w_two,
    node_b_two,
    node_gain,
    node_shift,
    node_cotangent,
    edge_cotangent,
):
    groups = lax.axis_size("blk")
    sub_count = lax.axis_size("sub")
    width = edge_input.shape[1]
    per_device = node_input.shape[1] // (groups * sub_count)
    node_low, wide_low, cotangent_later, send_local, recv_wide = begin(
        node_input, node_cotangent, senders, receivers, per_device, 0
    )
    node_upstream = lax.all_to_all(
        cotangent_later, ("blk", "sub"), split_axis=0, concat_axis=0, tiled=True
    ).reshape(width, per_device)
    recv_list = recv_wide.reshape(-1)
    edge_result, first_pre, second_pre, received, messages = edge_forward(
        edge_count, recv_list, send_local, edge_input, wide_low, node_low,
        edge_w_one, edge_b_one[None], edge_w_two, edge_b_two[None], edge_gain[None], edge_shift[None],
    )
    wide_grad, node_part, node_out, node_grads, node_vectors = middle(
        recv_list, messages, node_low, node_upstream, node_w_one, node_b_one[None], node_w_two, node_b_two[None],
        node_gain[None], node_shift[None], node_input, 1,
    )
    edge_grad, messages, edge_grads, vectors, node_part = edge_backward(
        edge_count, recv_list, send_local, edge_cotangent, edge_input, received, first_pre, second_pre,
        wide_grad, node_part, node_vectors, node_low, edge_w_one, edge_w_two, edge_gain[None],
    )
    node_grad, *summed, vectors = finish(
        recv_list, messages, edge_grads, node_grads, vectors, node_part, edge_w_one, node_cotangent, 3
    )
    node_out, node_grad, *rest = release((node_out, node_grad), summed, vectors)
    summed, vectors = rest[:4], [row.reshape(width) for row in rest[4:]]
    return (
        node_out,
        edge_result,
        node_grad,
        edge_grad,
        summed[0],
        vectors[0],
        summed[1],
        vectors[1],
        vectors[2],
        vectors[3],
        summed[2],
        vectors[4],
        summed[3],
        vectors[5],
        vectors[6],
        vectors[7],
    )


def solution(mesh):
    placed = (
        P(("blk", "sub"), None),
        P(("blk", "sub"), None),
        P(("blk", "sub")),
        P(("blk", "sub")),
        P(("blk", "sub")),
        P(),
        P(),
        P(),
        P(),
        P(),
        P(),
        P(),
        P(),
        P(),
        P(),
        P(),
        P(),
        P(("blk", "sub"), None),
        P(("blk", "sub"), None),
    )
    return jax.shard_map(
        shards,
        mesh=mesh,
        in_specs=placed,
        out_specs=(
            P(("blk", "sub"), None),
            P(("blk", "sub"), None),
            P(("blk", "sub"), None),
            P(("blk", "sub"), None),
            P(),
            P(),
            P(),
            P(),
            P(),
            P(),
            P(),
            P(),
            P(),
            P(),
            P(),
            P(),
        ),
        check_vma=False,
    )
```
